32 devices in a mesh: head: 2 (over y), blk: 16 (over z, x, core).
Axes of the slice: x: 2, y: 2, z: 4, core: 2. Of those that a mesh axis runs over, the one named last changes fastest.
Arguments:
- tokens: bfloat16 [4096, 1536], P(('head', 'blk')), may hold values from -6 to 6
- cotangent: bfloat16 [4096, 1536], P(('head', 'blk')), may hold values from -6 to 6
- seq_lengths: int32 [3], replicated, may hold values from 1 to 2048, 4096 in all
- piece_order: int32 [32], replicated, may hold values from 0 to 31, each once
- routes: int32 [4096, 6], P(('head', 'blk')), may hold values from 0 to 15, all different within a row; in each aligned block of 128 rows (0 to 127, 128 to 255, ...) at most 64 rows name the same one
- norm1_gain: bfloat16 [1536], P(('head', 'blk')), may hold values from 0.5 to 1.5
- w_query: bfloat16 [1536, 1536], P(('head', 'blk')), may hold values from -0.15625 to 0.15625
- w_key: bfloat16 [1536, 512], P(('head', 'blk')), may hold values from -0.15625 to 0.15625
- w_value: bfloat16 [1536, 512], P(('head', 'blk')), may hold values from -0.15625 to 0.15625
- w_out: bfloat16 [1536, 1536], P(('head', 'blk')), may hold values from -1.75 to 1.75
- norm2_gain: bfloat16 [1536], P(('head', 'blk')), may hold values from 0.5 to 1.5
- w_router: bfloat16 [1536, 16], P(('head', 'blk')), may hold values from -0.078125 to 0.078125
- shared_up: bfloat16 [1536, 2048], P(('head', 'blk')), may hold values from -0.15625 to 0.15625
- shared_down: bfloat16 [1024, 1536], P(('head', 'blk')), may hold values from -0.1875 to 0.1875
- expert_up: bfloat16 [16, 1536, 1024], P('blk', 'head'), may hold values from -0.15625 to 0.15625
- expert_down: bfloat16 [16, 512, 1536], P('blk', None, 'head'), may hold values from -0.25 to 0.25
Outputs:
- output: bfloat16 [4096, 1536], P(('head', 'blk'))
- input_grad: float32 [4096, 1536], P(('head', 'blk'))
- norm1_gain_grad: float32 [1536], P(('head', 'blk'))
- w_query_grad: float32 [1536, 1536], P(('head', 'blk'))
- w_key_grad: float32 [1536, 512], P(('head', 'blk'))
- w_value_grad: float32 [1536, 512], P(('head', 'blk'))
- w_out_grad: float32 [1536, 1536], P(('head', 'blk'))
- norm2_gain_grad: float32 [1536], P(('head', 'blk'))
- w_router_grad: float32 [1536, 16], P(('head', 'blk'))
- shared_up_grad: float32 [1536, 2048], P(('head', 'blk'))
- shared_down_grad: float32 [1024, 1536], P(('head', 'blk'))
- expert_up_grad: float32 [16, 1536, 1024], P('blk', 'head')
- expert_down_grad: float32 [16, 512, 1536], P('blk', None, 'head')
The draws below stay inside these ranges and needn't reach their ends.
Inputs may be any that keep to these rules, and one draw needn't show every extreme that they name: `routes`: every row names 6 different experts. Among the 128 rows of one device no expert is named more than 64 times; in every draw some device names some expert exactly 64 times. `seq_lengths`: the lengths sum to 4096; the largest is exactly 2048. Each number appears once: dealt piece p holds the stream positions piece_order[p] * 128 to piece_order[p] * 128 + 127.
All inputs are finite; a program needn't handle non-finite values.
Results may differ from the reference program's by a relative error of at most 0.025.
Values may be sent and summed in bfloat16 or wider, within the bound.
A program may use at most 256 MiB of HBM per device.

```python
import math
import jax
import jax.numpy as jnp
import numpy as np
from jax import lax

D = 1536
H = 12
KVH = 4
HD = 128
EF = 512
SF = 1024
TOP = 6
TOK_DEV = 128
PIECE = 128
TOKENS = 4096
LMAX = 2048
NSEQ = 3
PIECES = 32
EXPERTS = 16
CAP = 64
DEVICES = 32


def level_of(own_key, dims, split, smallest, largest):
    def one(axis_at, shards_of):
        heights = jax.random.uniform(jax.random.fold_in(jax.random.fold_in(own_key, 6), axis_at), (shards_of,), jnp.float32, smallest / len(split), largest / len(split))
        return jnp.repeat(jnp.exp(heights), dims[axis_at] // shards_of).reshape((-1,) + (1,) * (len(dims) - axis_at - 1))

    factor_of = one(*split[0])
    for cut in split[1:]:
        factor_of = factor_of * one(*cut)
    return factor_of


def split_up(amount, total, reach, skew):
    weights = [(1 << 20) // math.isqrt(rank ** skew) + 1 for rank in range(2, amount + 1)]
    rest, given = total - reach - (amount - 1), [1] * (amount - 1)
    while rest > 0:
        movable = [i for i in range(amount - 1) if given[i] < reach]
        whole, left = sum([weights[i] for i in movable]), rest
        for i in movable:
            addition = min(reach - given[i], max(1, left * weights[i] // whole), rest)
            given[i] = given[i] + addition
            rest = rest - addition
    return np.array([reach] + given)


def uneven(rng, count, total, bound, slope):
    if count == 2:
        one = jax.random.randint(rng, (), max(1, total - bound), min(bound, total - 1) + 1)
        return jnp.stack([one, total - one])
    tallies = jnp.asarray(split_up(count, total, bound, slope), jnp.int32)
    couples = (count - 1) // 2
    source_of, receiver = tallies[1:1 + 2 * couples:2], tallies[2:2 + 2 * couples:2]
    slack = jnp.minimum(source_of - 1, bound - receiver)
    moved = jax.random.randint(jax.random.fold_in(rng, 1), (couples,), 0, 1 << 20) % (slack + 1)
    tallies = tallies.at[1:1 + 2 * couples:2].set(source_of - moved).at[2:2 + 2 * couples:2].set(receiver + moved)
    return tallies[jax.random.permutation(jax.random.fold_in(rng, 2), count)]


def deal_out(own_key, own, number, rows, number_of, top, most, slope):
    sequence = jax.random.permutation(own_key, number_of)
    crowded, usual = shares(number_of, rows * top, most, slope, True), shares(number_of, rows * top, most, slope, False)
    places = jnp.arange(number_of)

    def named(tallies, turn):
        used = int((tallies > 0).sum())
        fixed = max(1, used // 4)
        passed = fixed + (places - fixed + turn * (used - fixed)) % max(1, number_of - fixed)
        return jnp.zeros((number_of,), jnp.int32).at[sequence[jnp.where(places < fixed, places, passed)]].set(jnp.asarray(tallies, jnp.int32))

    tallies = jnp.where(number % 4 == 0, named(crowded, number // 4), named(usual, number - number // 4 - 1))
    mixed = jax.random.permutation(jax.random.fold_in(own, 3), number_of)
    giver, taker = mixed[0:number_of // 2 * 2:2], mixed[1:number_of // 2 * 2:2]
    slack = jnp.minimum(tallies[giver] - 1, most - tallies[taker]) // 2
    slack = jnp.where((giver == sequence[0]) | (taker == sequence[0]) | (tallies[taker] == 0), 0, jnp.maximum(slack, 0))
    passed = jax.random.randint(jax.random.fold_in(own, 4), (number_of // 2,), 0, 1 << 20) % (slack + 1)
    tallies = tallies.at[giver].add(-passed).at[taker].add(passed)
    items = jnp.searchsorted(jnp.cumsum(tallies), jnp.arange(rows * top), side="right").astype(jnp.int32)
    table = items.reshape(top, rows).T
    table = table[jax.random.permutation(jax.random.fold_in(own, 1), rows)]
    turn = jax.random.randint(jax.random.fold_in(own, 2), (rows, 1), 0, top)
    return jnp.take_along_axis(table, (jnp.arange(top)[None, :] + turn) % top, axis=1)


def shares(amount, total, bound, slope, full):
    weights = [(1 << 20) // math.isqrt(standing ** slope) + 1 for standing in range(1, amount + 1)]
    largest = bound if full else min(bound, max(-(-total // amount), total * weights[0] // sum(weights)))
    least = 1 if total - largest >= amount - 1 else 0
    counts, spare = [largest] + [least] * (amount - 1), total - largest - least * (amount - 1)
    while spare > 0:
        movable = [i for i in range(1, amount) if counts[i] < largest] or [i for i in range(1, amount) if counts[i] < bound]
        mass, left = sum([weights[i] for i in movable]), spare
        for i in movable:
            more = min(bound - counts[i], max(1, left * weights[i] // mass), spare)
            counts[i] = counts[i] + more
            spare = spare - more
    return np.array(counts)


def gaussian(own_key, extent, deviation, reach, pieces=(), kind=jnp.bfloat16):
    array = deviation * jax.random.normal(own_key, extent, jnp.float32)
    if pieces:
        array = array * level_of(own_key, extent, pieces, -0.22, 0.18)
    return jnp.clip(array, -reach, reach).astype(kind)


def setup_inputs(seed: int = 0) -> dict:
    arg_keys = jax.random.split(jax.random.key(seed), 17)
    tokens = gaussian(arg_keys[0], (TOKENS, D), 1.0, 6.0, ((0, 32),))
    cotangent = gaussian(arg_keys[1], (TOKENS, D), 1.0, 6.0, ((0, 32),))
    seq_lengths = uneven(arg_keys[2], NSEQ, TOKENS, LMAX, 2).astype(jnp.int32)
    piece_order = jax.random.permutation(arg_keys[3], PIECES).astype(jnp.int32)
    routes_keys = jax.random.split(jax.random.fold_in(arg_keys[4], 1), TOKENS // TOK_DEV)
    routes_turns = jax.random.permutation(jax.random.fold_in(arg_keys[4], 3), TOKENS // TOK_DEV)
    routes = jax.vmap(lambda own, number: deal_out(jax.random.fold_in(arg_keys[4], 2), own, number, TOK_DEV, EXPERTS, TOP, CAP, 2))(routes_keys, routes_turns).reshape((TOKENS, TOP))
    norm1_gain = jnp.clip(1.0 + 0.1 * jax.random.normal(arg_keys[5], (D,), jnp.float32), 0.5, 1.5).astype(jnp.bfloat16)
    w_query = gaussian(arg_keys[6], (D, H * HD), D ** -0.5, 0.15625, ((0, 32),))
    w_key = gaussian(arg_keys[7], (D, KVH * HD), D ** -0.5, 0.15625, ((0, 32),))
    w_value = gaussian(arg_keys[8], (D, KVH * HD), D ** -0.5, 0.15625, ((0, 32),))
    w_out = gaussian(arg_keys[9], (H * HD, D), (H * HD // 128) ** -0.5, 1.75, ((0, 32),))
    norm2_gain = jnp.clip(1.0 + 0.1 * jax.random.normal(arg_keys[10], (D,), jnp.float32), 0.5, 1.5).astype(jnp.bfloat16)
    w_router = gaussian(arg_keys[11], (D, EXPERTS), (4 * D) ** -0.5, 0.078125, ((0, 32),))
    shared_up = gaussian(arg_keys[12], (D, 2 * SF), D ** -0.5, 0.15625, ((0, 32),))
    shared_down = gaussian(arg_keys[13], (SF, D), SF ** -0.5, 0.1875, ((0, 32),))
    expert_up = gaussian(arg_keys[14], (EXPERTS, D, 2 * EF), D ** -0.5, 0.15625, ((0, 16), (1, 2)))
    expert_down = gaussian(arg_keys[15], (EXPERTS, EF, D), EF ** -0.5, 0.25, ((0, 16), (2, 2)))
    return {"tokens": tokens, "cotangent": cotangent, "seq_lengths": seq_lengths, "piece_order": piece_order, "routes": routes, "norm1_gain": norm1_gain, "w_query": w_query, "w_key": w_key, "w_value": w_value, "w_out": w_out, "norm2_gain": norm2_gain, "w_router": w_router, "shared_up": shared_up, "shared_down": shared_down, "expert_up": expert_up, "expert_down": expert_down}


epsilon = 1e-05
neg_big = -1e+30
highest = lax.Precision.HIGHEST

@jax.custom_vjp
def low(v):
    return lax.optimization_barrier(v.astype(jnp.bfloat16)).astype(jnp.float32)

@jax.custom_vjp
def low_back(v):
    return v

def low_keep(v):
    return (low(v), None)

def low_pass(kept, grad):
    return (grad,)

def back_keep(v):
    return (v, None)

def back_low(kept, grad):
    return (low(grad),)
low.defvjp(low_keep, low_pass)
low_back.defvjp(back_keep, back_low)

def matmul(former, latter):
    return jnp.dot(former, latter, precision=highest, preferred_element_type=jnp.float32)

def rms_norm(values, norm_gain):
    return values * lax.rsqrt(lax.optimization_barrier(jnp.mean(values * values, axis=1, keepdims=True)) + epsilon) * norm_gain

def silu_pair(both_parts, half_width):
    return jax.nn.silu(both_parts[:, :half_width]) * both_parts[:, half_width:]

def reference(tokens, cotangent, seq_lengths, piece_order, routes, norm1_gain, w_query, w_key, w_value, w_out, norm2_gain, w_router, shared_up, shared_down, expert_up, expert_down):
    row_ids = jnp.arange(TOKENS, dtype=jnp.int32)
    position = (piece_order[row_ids // PIECE] * PIECE + row_ids % PIECE).astype(jnp.int32)
    seq_ends = jnp.cumsum(seq_lengths).astype(jnp.int32)
    member = lax.optimization_barrier(jnp.sum((seq_ends[None, :] <= position[:, None]).astype(jnp.int32), axis=1)).astype(jnp.int32)
    route_hot = (routes[:, :, None] == jnp.arange(EXPERTS, dtype=jnp.int32)[None, None, :]).astype(jnp.int32)
    per_device = route_hot.reshape(DEVICES, TOK_DEV * TOP, EXPERTS)
    running_count = jnp.cumsum(per_device, axis=1).astype(jnp.int32)
    earlier = lax.optimization_barrier(jnp.sum((running_count - per_device) * per_device, axis=2)).astype(jnp.int32).reshape(TOKENS, TOP)
    column = ((row_ids // TOK_DEV)[:, None] * CAP + earlier).astype(jnp.int32)
    owners = jnp.broadcast_to(row_ids[:, None], (TOKENS, TOP)).astype(jnp.int32)
    slot_table = jnp.full((EXPERTS, DEVICES * CAP), TOKENS, jnp.int32).at[routes, column].set(owners)
    block_rows = min(512, TOKENS)
    blocks = TOKENS // block_rows
    groups = KVH
    repeats = H // KVH
    score_scale = HD ** (-0.5)

    def attend(queries, key_rows, value_rows):
        query_heads = queries.reshape(blocks, block_rows, groups, repeats, HD)
        key_heads = key_rows.reshape(TOKENS, groups, HD)
        value_heads = value_rows.reshape(TOKENS, groups, HD)

        def one_block(block_args):
            query_part, pos_part, member_part = block_args
            scores = low_back(jnp.einsum('qgrh,kgh->qgrk', query_part, key_heads, precision=highest) * score_scale)
            allowed = (member_part[:, None] == member[None, :]) & (position[None, :] <= pos_part[:, None])
            masked = jnp.where(allowed[:, None, None, :], scores, neg_big)
            weights = low(jax.nn.softmax(masked, axis=-1))
            return jnp.einsum('qgrk,kgh->qgrh', weights, value_heads, precision=highest)
        result = lax.map(jax.checkpoint(one_block), (query_heads, position.reshape(blocks, block_rows), member.reshape(blocks, block_rows)))
        return result.reshape(TOKENS, H * HD)

    def forward(inputs, gain_one, query_w, key_w, value_w, out_w, gain_two, router_w, up_w, down_w, experts_in, experts_out):
        normed_one = low(rms_norm(inputs, gain_one))
        queries = low(low_back(matmul(normed_one, query_w)))
        key_rows = low(low_back(matmul(normed_one, key_w)))
        value_rows = low(low_back(matmul(normed_one, value_w)))
        attended = low(low_back(attend(queries, key_rows, value_rows)))
        hidden_res = inputs + low_back(matmul(attended, out_w))
        normed_two = low(rms_norm(hidden_res, gain_two))
        logits = low_back(matmul(normed_two, router_w))
        gate_probs = jax.nn.softmax(jnp.take_along_axis(logits, routes, axis=1), axis=1)
        shared_act = low(silu_pair(low_back(matmul(normed_two, up_w)), SF))
        shared_sum = low_back(matmul(shared_act, down_w))
        padded = jnp.concatenate([normed_two, jnp.zeros((1, D), normed_two.dtype)], axis=0)
        expert_rows = low_back(padded[slot_table])

        def one_expert(block_args):
            rows_in, weight_in, weight_out = block_args
            activated = low(silu_pair(low_back(matmul(rows_in, weight_in)), EF))
            return matmul(activated, weight_out)
        results = low(low_back(lax.map(jax.checkpoint(one_expert), (expert_rows, experts_in, experts_out))))
        picked = results[routes, column]
        routed_sum = lax.optimization_barrier(jnp.sum(gate_probs[:, :, None] * picked, axis=1))
        return hidden_res + routed_sum + shared_sum
    float_args = tuple((array_in.astype(jnp.float32) for array_in in (tokens, norm1_gain, w_query, w_key, w_value, w_out, norm2_gain, w_router, shared_up, shared_down, expert_up, expert_down)))
    output, pullback = jax.vjp(forward, *float_args)
    gradients = pullback(cotangent.astype(jnp.float32))
    return (output.astype(jnp.bfloat16), gradients[0], gradients[1], gradients[2], gradients[3], gradients[4], gradients[5], gradients[6], gradients[7], gradients[8], gradients[9], gradients[10], gradients[11])
```

```python
import functools

import jax
import jax.numpy as jnp
from jax import lax
from jax.experimental import pallas as pl
from jax.experimental.pallas import tpu as pltpu
from jax.sharding import PartitionSpec as P

MESH = pl.DeviceIdType.MESH


def ring_place(chip, chips):
    odd = chip % 2
    return (chip // 2) * (1 - odd) + (chips - 1 - chip // 2) * odd


def ring_chip(place, chips):
    high = place // (chips // 2)
    return 2 * place * (1 - high) + (2 * (chips - 1 - place) + 1) * high


def ring_info(chips):
    blk = lax.axis_index("blk")
    chip, core = blk // 2, blk % 2
    place = ring_place(chip, chips)

    def at(step):
        return ring_chip((place + step + chips) % chips, chips) * 2 + core

    return blk, core, at, blk + 1 - 2 * core


def pieces_of(shape):
    if len(shape) == 3:
        return [(0, None), (1, None)]
    rows = shape[0]
    if rows >= 32 and rows % 16 == 0:
        cut = (rows // 2 + 15) // 16 * 16
        return [(0, cut), (cut, rows - cut)]
    return [(0, rows)]


def part_in(ref, piece):
    start, size = piece
    return ref.at[start] if size is None else ref.at[pl.ds(start, size)]


def part_out(ref, piece, b):
    start, size = piece
    return ref.at[start, b] if size is None else ref.at[b, pl.ds(start, size)]


def ag_kernel(count, chips, plans, *refs):
    ins, outs = refs[:count], refs[count : 2 * count]
    right_sem, left_sem, sib_sem, sright, sleft, ssib, own_sem = refs[2 * count :]
    blk, core, at, sib = ring_info(chips)
    right, left = at(1), at(-1)
    barrier = pltpu.get_barrier_semaphore()
    for other in (right, left, sib):
        pl.semaphore_signal(barrier, inc=1, device_id={"blk": other}, device_id_type=MESH)
    pl.semaphore_wait(barrier, 3)
    half = chips // 2
    started = []

    def send(src, dst, ssem, rsem, dev):
        copy = pltpu.make_async_remote_copy(
            src_ref=src, dst_ref=dst, send_sem=ssem, recv_sem=rsem,
            device_id={"blk": dev}, device_id_type=MESH)
        copy.start()
        started.append(copy)
        return copy

    chunks = []
    for k in range(count):
        for i, piece in enumerate(plans[k]):
            chunks.append((len(chunks), k, piece, half - (i % 2), half - 1 + (i % 2)))
    copies = {}
    locals_ = []
    for c, k, piece, rh, lh in chunks:
        src = part_in(ins[k], piece)
        dst = part_out(outs[k], piece, blk)
        if rh >= 1:
            copies[c, "r", 1] = send(src, dst, sright.at[c, 0], right_sem.at[c, 0], right)
        if lh >= 1:
            copies[c, "l", 1] = send(src, dst, sleft.at[c, 0], left_sem.at[c, 0], left)
        copies[c, "s", 0] = send(src, dst, ssib.at[c, 0], sib_sem.at[c, 0], sib)
        own = pltpu.make_async_copy(src, dst, own_sem.at[c])
        own.start()
        locals_.append(own)
    for s in range(1, half + 1):
        for c, k, piece, rh, lh in chunks:
            if s <= rh:
                copies[c, "r", s].wait_recv()
                b = at(-s)
                blockref = part_out(outs[k], piece, b)
                if s < rh:
                    copies[c, "r", s + 1] = send(blockref, blockref, sright.at[c, s], right_sem.at[c, s], right)
                copies[c, "sr", s] = send(blockref, blockref, ssib.at[c, s], sib_sem.at[c, s], sib)
            if s <= lh:
                copies[c, "l", s].wait_recv()
                b = at(s)
                blockref = part_out(outs[k], piece, b)
                if s < lh:
                    copies[c, "l", s + 1] = send(blockref, blockref, sleft.at[c, s], left_sem.at[c, s], left)
                copies[c, "sl", s] = send(blockref, blockref, ssib.at[c, half + s], sib_sem.at[c, half + s], sib)
    for (c, d, s), copy in copies.items():
        if d in ("s", "sr", "sl"):
            copy.wait_recv()
    for copy in started:
        copy.wait_send()
    for copy in locals_:
        copy.wait()


def all_gather_blk(arrays, blks, collective_id, vmem=False):
    chips = blks // 2
    count = len(arrays)
    plans = [pieces_of(a.shape) for a in arrays]
    n = sum(len(p) for p in plans)
    half = chips // 2
    shapes = [
        jax.ShapeDtypeStruct((a.shape[0], blks) + a.shape[1:] if a.ndim == 3 else (blks,) + a.shape, a.dtype)
        for a in arrays
    ]
    dma = pltpu.SemaphoreType.DMA
    space = pltpu.VMEM if vmem else pl.ANY
    return pl.pallas_call(
        functools.partial(ag_kernel, count, chips, plans),
        out_shape=shapes,
        in_specs=[pl.BlockSpec(memory_space=space)] * count,
        out_specs=[pl.BlockSpec(memory_space=space)] * count,
        scratch_shapes=[
            dma((n, half)), dma((n, half)), dma((n, 2 * half + 1)),
            dma((n, half)), dma((n, half)), dma((n, 2 * half + 1)), dma((n,)),
        ],
        compiler_params=pltpu.CompilerParams(collective_id=collective_id, has_side_effects=True,
            vmem_limit_bytes=(60 << 20) if vmem else None),
    )(*arrays)


def rs_kernel(count, chips, plans, *refs):
    xs, outs = refs[:count], refs[count : 2 * count]
    rest = refs[2 * count :]
    n = sum(len(p) for p in plans)
    ys, rs, ls = rest[:n], rest[n : 2 * n], rest[2 * n : 3 * n]
    right_sem, left_sem, sib_sem, sright, sleft, ssib = rest[3 * n :]
    blk, core, at, sib = ring_info(chips)
    right, left = at(1), at(-1)
    barrier = pltpu.get_barrier_semaphore()
    for other in (right, left, sib):
        pl.semaphore_signal(barrier, inc=1, device_id={"blk": other}, device_id_type=MESH)
    pl.semaphore_wait(barrier, 3)
    half = chips // 2
    started = []

    def send(src, dst, ssem, rsem, dev):
        copy = pltpu.make_async_remote_copy(
            src_ref=src, dst_ref=dst, send_sem=ssem, recv_sem=rsem,
            device_id={"blk": dev}, device_id_type=MESH)
        copy.start()
        started.append(copy)
        return copy

    chunks = []
    for k in range(count):
        for i, piece in enumerate(plans[k]):
            chunks.append((len(chunks), k, piece, half - (i % 2), half - 1 + (i % 2)))
    order = []
    for d in range(half, 0, -1):
        order += [d, -d] if d < half else [d]
    order.append(0)
    sibs = {}
    for j, d in enumerate(order):
        there = at(d) + 1 - 2 * core
        for c, k, piece, rh, lh in chunks:
            sibs[c, d] = send(part_out(xs[k], piece, there), ys[c].at[j], ssib.at[c, j], sib_sem.at[c, j], sib)
    ready = set()

    def blocks(rows, body):
        step = 16 if rows % 16 == 0 else rows

        @pl.loop(0, rows // step)
        def _(i):
            body(pl.ds(pl.multiple_of(i * step, step), step))

    def mine(c, k, piece, d):
        j = order.index(d)
        if (c, d) not in ready:
            sibs[c, d].wait_recv()
            ready.add((c, d))
        return j

    copies = {}

    def join(c, k, piece, d, into, recv):
        j = mine(c, k, piece, d)
        x = part_out(xs[k], piece, at(d))
        rows = x.shape[0]

        def body(w):
            total = x[w].astype(jnp.float32) + ys[c][j, w].astype(jnp.float32)
            if recv is not None:
                total = total + recv[w].astype(jnp.float32)
            into[w] = total.astype(into.dtype)

        blocks(rows, body)

    for s in range(1, half + 1):
        for c, k, piece, rh, lh in chunks:
            for way, hops, buf, sem, ssem, dev in (
                (1, rh, rs[c], right_sem, sright, right),
                (-1, lh, ls[c], left_sem, sleft, left),
            ):
                if s > hops:
                    continue
                if s == 1:
                    j = order.index(way * hops if way * hops in order else hops)
                    join(c, k, piece, order[j], ys[c].at[j], None)
                    src = ys[c].at[j]
                else:
                    copies[c, way, s - 1].wait_recv()
                    d = way * (hops - s + 1)
                    src = buf.at[s - 2]
                    join(c, k, piece, d, src, src)
                copies[c, way, s] = send(src, buf.at[s - 1], ssem.at[c, s - 1], sem.at[c, s - 1], dev)
    for c, k, piece, rh, lh in chunks:
        if rh >= 1:
            copies[c, 1, rh].wait_recv()
        if lh >= 1:
            copies[c, -1, lh].wait_recv()
        j = mine(c, k, piece, 0)
        x = part_out(xs[k], piece, blk)
        target = part_in(outs[k], piece)

        def body(w, x=x, c=c, j=j, rh=rh, lh=lh, target=target):
            total = x[w].astype(jnp.float32) + ys[c][j, w].astype(jnp.float32)
            if rh >= 1:
                total = total + rs[c][rh - 1, w].astype(jnp.float32)
            if lh >= 1:
                total = total + ls[c][lh - 1, w].astype(jnp.float32)
            target[w] = total.astype(target.dtype)

        blocks(x.shape[0], body)
    for copy in started:
        copy.wait_send()


def reduce_scatter_blk(arrays, blks, collective_id, out_dtypes):
    chips = blks // 2
    half = chips // 2
    count = len(arrays)
    shapes = [a.shape[1:] if a.ndim == 3 else (2,) + a.shape[2:] for a in arrays]
    plans = [pieces_of(s) for s in shapes]
    dma = pltpu.SemaphoreType.DMA
    ys, rs = [], []
    for s, plan in zip(shapes, plans):
        for start, size in plan:
            rows = s[1] if size is None else size
            ys.append(pltpu.VMEM((chips, rows, s[-1]), jnp.bfloat16))
            rs.append(pltpu.VMEM((half, rows, s[-1]), jnp.bfloat16))
    n = len(ys)
    return pl.pallas_call(
        functools.partial(rs_kernel, count, chips, plans),
        out_shape=[jax.ShapeDtypeStruct(s, t) for s, t in zip(shapes, out_dtypes)],
        in_specs=[pl.BlockSpec(memory_space=pltpu.VMEM)] * count,
        out_specs=[pl.BlockSpec(memory_space=pltpu.VMEM)] * count,
        scratch_shapes=ys + rs + rs + [
            dma((n, half)), dma((n, half)), dma((n, chips)),
            dma((n, half)), dma((n, half)), dma((n, chips)),
        ],
        compiler_params=pltpu.CompilerParams(collective_id=collective_id, has_side_effects=True,
            vmem_limit_bytes=60 << 20),
    )(*arrays)


H = 12
KVH = 4
HD = 128
TOP = 6
PIECE = 128
EPS = 1e-05
NEG = -1e30
F32 = jnp.float32
BF16 = jnp.bfloat16


def dot(a, b):
    return jnp.dot(a, b, preferred_element_type=F32)


def dot_first(a, b):
    return lax.dot_general(a, b, (((0,), (0,)), ((), ())), preferred_element_type=F32)


def dot_last(a, b):
    return lax.dot_general(a, b, (((1,), (1,)), ((), ())), preferred_element_type=F32)


def inv_scale(values):
    return lax.rsqrt(jnp.mean(values * values, axis=1, keepdims=True) + EPS)


def norm_back(values, scaler, gain, upstream):
    normed = values * scaler
    gain_grad = jnp.sum(upstream * normed, axis=0)
    scaled = upstream * gain
    grad = scaler * (scaled - normed * jnp.mean(scaled * normed, axis=1, keepdims=True))
    return grad, gain_grad


def gated_grad(act_grad, gate, lift):
    sig = jax.nn.sigmoid(gate)
    return jnp.concatenate(
        [act_grad * lift * sig * (1.0 + gate * (1.0 - sig)), act_grad * gate * sig], axis=1
    ).astype(BF16)


def swap(array):
    return lax.ppermute(array, "head", [(0, 1), (1, 0)])


def key_span(places_ref, ends_ref, i):
    place = places_ref[i]
    start = jnp.int32(0)
    for e in range(ends_ref.shape[0]):
        start = jnp.where(ends_ref[e] <= place * PIECE, ends_ref[e], start)
    return start // PIECE, place


def key_chunk(slots_ref, first, pieces, *refs):
    last = slots_ref.shape[0] - 1
    slots = [slots_ref[jnp.minimum(first + k, last)] for k in range(pieces)]
    return slots, [jnp.concatenate([ref[s] for s in slots], axis=0) for ref in refs]


def stacked(ref, i, repeats):
    return jnp.concatenate(
        [ref[pl.ds(i * PIECE, PIECE), pl.ds(r * HD, HD)] for r in range(repeats)], axis=0)


def seen(ends_ref, place, first, keys, cols):
    own = place * PIECE + lax.broadcasted_iota(jnp.int32, (1, cols), 1) % PIECE
    start = jnp.zeros((1, cols), jnp.int32)
    for e in range(ends_ref.shape[0]):
        start = jnp.where(ends_ref[e] <= own, ends_ref[e], start)
    there = first * PIECE + lax.broadcasted_iota(jnp.int32, (keys, 1), 0)
    return (there <= own) & (there >= start)


CHUNK = 4


def forward_kernel(repeats, slots_ref, places_ref, ends_ref, q_ref, k_ref, v_ref, low_ref, full_ref, lse_ref):
    cols = repeats * PIECE
    for i in range(q_ref.shape[0] // PIECE):
        lo, place = key_span(places_ref, ends_ref, i)
        q = stacked(q_ref, i, repeats)

        def step(n, carry, lo=lo, place=place, q=q):
            top, total, acc = carry
            first = lo + n * CHUNK
            _, (k, v) = key_chunk(slots_ref, first, CHUNK, k_ref, v_ref)
            scores = dot_last(k, q) * HD**-0.5
            scores = jnp.where(seen(ends_ref, place, first, CHUNK * PIECE, cols), scores, NEG)
            new = jnp.maximum(top, jnp.max(scores, axis=0, keepdims=True))
            weights = jnp.exp(scores - new)
            factor = jnp.exp(top - new)
            total = total * factor + jnp.sum(weights, axis=0, keepdims=True)
            return new, total, acc * factor + dot_first(v, weights.astype(BF16))

        top, total, acc = lax.fori_loop(
            0, (place - lo) // CHUNK + 1, step,
            (jnp.full((1, cols), NEG, F32), jnp.zeros((1, cols), F32), jnp.zeros((HD, cols), F32)))
        out = jnp.swapaxes(acc / total, 0, 1)
        lse_ref[0, pl.ds(i, 1), :] = top + jnp.log(total)
        for r in range(repeats):
            part = out[r * PIECE : (r + 1) * PIECE]
            full_ref[pl.ds(i * PIECE, PIECE), pl.ds(r * HD, HD)] = part
            low_ref[pl.ds(i * PIECE, PIECE), pl.ds(r * HD, HD)] = part.astype(BF16)


def attention_forward(query, kv, where):
    rows, pieces = query.shape[0], kv.shape[0]
    groups = kv.shape[2] // (2 * HD)
    wide = query.shape[1] // groups
    repeats = wide // HD
    spec = pl.BlockSpec((rows, wide), lambda g, *_: (0, g))
    return pl.pallas_call(
        functools.partial(forward_kernel, repeats),
        grid_spec=pltpu.PrefetchScalarGridSpec(
            num_scalar_prefetch=3,
            grid=(groups,),
            in_specs=[
                spec,
                pl.BlockSpec((pieces, PIECE, HD), lambda g, *_: (0, 0, g)),
                pl.BlockSpec((pieces, PIECE, HD), lambda g, *_: (0, 0, groups + g)),
            ],
            out_specs=[spec, spec, pl.BlockSpec((1, rows // PIECE, repeats * PIECE), lambda g, *_: (g, 0, 0))],
        ),
        out_shape=[
            jax.ShapeDtypeStruct(query.shape, BF16),
            jax.ShapeDtypeStruct(query.shape, F32),
            jax.ShapeDtypeStruct((groups, rows // PIECE, repeats * PIECE), F32),
        ],
        compiler_params=pltpu.CompilerParams(vmem_limit_bytes=48 << 20),
    )(*where, query, kv, kv)


def backward_kernel(
    repeats, slots_ref, places_ref, ends_ref, q_ref, k_ref, v_ref, full_ref, grad_ref, lse_ref,
    dq_ref, dk_ref, dv_ref, key_acc, value_acc,
):
    cols = repeats * PIECE
    key_acc[...] = jnp.zeros_like(key_acc)
    value_acc[...] = jnp.zeros_like(value_acc)
    for i in range(q_ref.shape[0] // PIECE):
        lo, place = key_span(places_ref, ends_ref, i)
        q, grad = stacked(q_ref, i, repeats), stacked(grad_ref, i, repeats)
        product = grad.astype(F32) * stacked(full_ref, i, repeats)
        delta = jnp.sum(jnp.swapaxes(product, 0, 1), axis=0, keepdims=True)
        lse = lse_ref[0, pl.ds(i, 1), :]

        def step(n, dq, lo=lo, place=place, q=q, grad=grad, delta=delta, lse=lse):
            first = lo + n * CHUNK
            slots, (k, v) = key_chunk(slots_ref, first, CHUNK, k_ref, v_ref)
            scores = dot_last(k, q) * HD**-0.5
            weights = jnp.where(
                seen(ends_ref, place, first, CHUNK * PIECE, cols), jnp.exp(scores - lse), 0.0)
            back = (weights * (dot_last(v, grad) - delta)).astype(BF16)
            dk = dot(back, q)
            dv = dot(weights.astype(BF16), grad)
            for j, s in enumerate(slots):
                key_acc[s] += dk[j * PIECE : (j + 1) * PIECE]
                value_acc[s] += dv[j * PIECE : (j + 1) * PIECE]
            return dq + dot_first(k, back)

        dq = lax.fori_loop(0, (place - lo) // CHUNK + 1, step, jnp.zeros((HD, cols), F32))
        out = (jnp.swapaxes(dq, 0, 1) * HD**-0.5).astype(BF16)
        for r in range(repeats):
            dq_ref[pl.ds(i * PIECE, PIECE), pl.ds(r * HD, HD)] = out[r * PIECE : (r + 1) * PIECE]
    dk_ref[...] = (key_acc[...] * HD**-0.5).astype(BF16)
    dv_ref[...] = value_acc[...].astype(BF16)


def attention_backward(query, kv, full, lse, grad, where):
    rows, pieces = query.shape[0], kv.shape[0]
    groups = kv.shape[2] // (2 * HD)
    wide = query.shape[1] // groups
    repeats = wide // HD
    spec = pl.BlockSpec((rows, wide), lambda g, *_: (0, g))
    block = pl.BlockSpec((pieces, PIECE, HD), lambda g, *_: (0, 0, g))
    half = jax.ShapeDtypeStruct((pieces, PIECE, groups * HD), BF16)
    return pl.pallas_call(
        functools.partial(backward_kernel, repeats),
        grid_spec=pltpu.PrefetchScalarGridSpec(
            num_scalar_prefetch=3,
            grid=(groups,),
            in_specs=[
                spec, block, pl.BlockSpec((pieces, PIECE, HD), lambda g, *_: (0, 0, groups + g)), spec, spec,
                pl.BlockSpec((1, rows // PIECE, repeats * PIECE), lambda g, *_: (g, 0, 0)),
            ],
            out_specs=[spec, block, block],
            scratch_shapes=[pltpu.VMEM((pieces, PIECE, HD), F32)] * 2,
        ),
        out_shape=[jax.ShapeDtypeStruct(query.shape, BF16), half, half],
        compiler_params=pltpu.CompilerParams(vmem_limit_bytes=60 << 20),
    )(*where, query, kv, kv, full, grad, lse)


def shards(
    tokens, cotangent, seq_lengths, piece_order, routes, norm1_gain, w_query, w_key, w_value, w_out,
    norm2_gain, w_router, shared_up, shared_down, expert_up, expert_down,
):
    blks = lax.axis_size("blk")
    h, b = lax.axis_index("head"), lax.axis_index("blk")
    rows, width = tokens.shape
    experts = blks
    capacity = rows * TOP * 4 // (3 * blks)
    dense_rows = w_query.shape[0]

    def pair(own, other):
        return jnp.where(h == 0, jnp.stack([own, other]), jnp.stack([other, own]))

    def half(w, i, parts=1):
        size = w.shape[1] // (2 * parts)
        cut = lax.dynamic_slice_in_dim(w.reshape(w.shape[0], parts, 2 * size), i * size, size, 2)
        return cut.reshape(w.shape[0], parts * size)

    def pick(stacked, i):
        return lax.dynamic_index_in_dim(stacked, i, 0, keepdims=False)

    def columns(i):
        return jnp.concatenate([half(w_query, i), half(w_key, i), half(w_value, i)], axis=1)

    small = jnp.concatenate(
        [w_router, norm1_gain[:, None], norm2_gain[:, None],
         jnp.zeros((dense_rows, -(experts + 2) % 128), BF16)], axis=1)
    lanes = small.shape[1]
    first = pair(
        jnp.concatenate([columns(h), small], axis=1),
        swap(jnp.concatenate([columns(1 - h), small], axis=1)),
    )
    tokens_pair = pair(tokens, swap(tokens))
    cotangent_pair = pair(cotangent, swap(cotangent)).reshape(2 * rows, width)
    up_pair = pair(half(shared_up, h, 2), swap(half(shared_up, 1 - h, 2)))
    expert_in = pair(expert_up[0], swap(expert_up[0])).reshape(width, -1)
    other_down = swap(expert_down[0])
    expert_out = jnp.where(
        h == 0,
        jnp.concatenate([expert_down[0], other_down], axis=1),
        jnp.concatenate([other_down, expert_down[0]], axis=1),
    )
    gathered = all_gather_blk([first], blks, 0)[0].reshape(width, -1)
    qw = w_query.shape[1] // 2
    kw = w_key.shape[1] // 2
    full_qkv = gathered[:, : qw + 2 * kw]
    full_router = gathered[:, qw + 2 * kw : qw + 2 * kw + experts]
    gain_first = gathered[:, qw + 2 * kw + experts].astype(F32)
    gain_second = gathered[:, qw + 2 * kw + experts + 1].astype(F32)

    inputs_pair = tokens_pair.reshape(2 * rows, width).astype(F32)
    normed_one = (inputs_pair * inv_scale(inputs_pair) * gain_first).astype(BF16)
    qkv = dot(normed_one, full_qkv).astype(BF16)
    query = qkv[:, :qw]
    kv = all_gather_blk([qkv[:, qw:]], blks, 1)[0].reshape(-1, PIECE, 2 * kw)

    places = jnp.swapaxes(piece_order.reshape(2, blks), 0, 1).reshape(-1)
    order = jnp.arange(2 * blks, dtype=jnp.int32)
    slots = jnp.sum(jnp.where(places[None, :] == order[:, None], order[None, :], 0), axis=1)
    where = (slots, lax.dynamic_slice_in_dim(places, 2 * b, 2), jnp.cumsum(seq_lengths))
    attended, attended_full, lse = attention_forward(query, kv, where)

    up_all, out_all, down_all, cot_all = all_gather_blk([up_pair, w_out, shared_down, cotangent], blks, 2)
    full_up = up_all.reshape(width, -1)
    full_out = out_all.reshape(-1, width)
    full_down = down_all.reshape(-1, width)
    shared_width = full_down.shape[0]

    mixed = dot(attended, full_out).reshape(2, rows, width)
    inputs = tokens.astype(F32)
    resid = inputs + (pick(mixed, h) + swap(pick(mixed, 1 - h).astype(BF16)).astype(F32))
    scaler_two = inv_scale(resid)
    normed_two = (resid * scaler_two * gain_second).astype(BF16)
    normed_pair = pair(normed_two, swap(normed_two)).reshape(2 * rows, width)

    logits = dot(normed_two, full_router)
    hot = routes[:, :, None] == jnp.arange(experts, dtype=jnp.int32)[None, None, :]
    mask = jnp.any(hot, axis=1)
    masked = jnp.where(mask, logits, NEG)
    raised = jnp.where(mask, jnp.exp(masked - jnp.max(masked, axis=1, keepdims=True)), 0.0)
    gates = raised / jnp.sum(raised, axis=1, keepdims=True)
    extra = jnp.concatenate(
        [gates.astype(BF16), mask.astype(BF16), jnp.zeros((rows, -2 * experts % 128), BF16)], axis=1)

    ext = all_gather_blk([jnp.concatenate([normed_two, extra], axis=1)], blks, 3)[0]
    norm_all = ext[:, :, :width]
    gate_here = lax.dynamic_index_in_dim(ext, width + b, 2, keepdims=False).astype(F32)
    mask_here = lax.dynamic_index_in_dim(ext, width + experts + b, 2, keepdims=False).astype(F32)
    rank = jnp.cumsum(mask_here, axis=1) - mask_here
    slots = jnp.arange(capacity, dtype=F32)
    deal = ((rank[:, None, :] == slots[None, :, None]) & (mask_here[:, None, :] > 0)).astype(BF16)
    deal_gate = deal * gate_here[:, None, :].astype(BF16)

    def to_slots(dealer, array):
        moved = jnp.einsum("bst,btd->bsd", dealer, array, preferred_element_type=F32)
        return moved.astype(BF16).reshape(blks * capacity, width)

    def to_rows(dealer, array):
        return jnp.einsum(
            "bst,bsd->btd", dealer, array.reshape(blks, capacity, width), preferred_element_type=F32)

    expert_rows = to_slots(deal, norm_all)
    both = dot(expert_rows, expert_in)
    ew = expert_out.shape[0]
    gate_part, up_part = both[:, :ew], both[:, ew:]
    activated = (jax.nn.silu(gate_part) * up_part).astype(BF16)
    result = dot(activated, expert_out).astype(BF16)
    result_rows = to_rows(deal, result)
    gate_grad = jnp.sum(result_rows * cot_all.astype(F32), axis=2, keepdims=True)
    routed = (result_rows * gate_here[:, :, None]).astype(BF16)
    slot_grad = to_slots(deal_gate, cot_all)
    act_grad = dot_last(slot_grad, expert_out)
    both_grad = gated_grad(act_grad, gate_part, up_part)
    rows_back = to_rows(deal, dot_last(both_grad, expert_in).astype(BF16)).astype(BF16)
    lane = jnp.arange(128 * (-(-2 * experts // 128)), dtype=jnp.int32)
    grad_high = gate_grad.astype(BF16)
    grad_low = (gate_grad - grad_high.astype(F32)).astype(BF16)
    grad_lanes = jnp.where(lane == b, grad_high, jnp.where(lane == b + experts, grad_low, jnp.zeros((), BF16)))
    home = reduce_scatter_blk([jnp.concatenate([rows_back, grad_lanes], axis=2)], blks, 4, [F32])[0]
    routed_sum = reduce_scatter_blk([routed], blks, 5, [F32])[0]
    dwn = dot_first(activated, slot_grad)
    dup = dot_first(expert_rows, both_grad).reshape(2, width // 2, -1)
    dwn = jnp.stack([dwn[:, : width // 2], dwn[:, width // 2 :]])
    expert_up_grad = pick(dup, h) + swap(pick(dup, 1 - h).astype(BF16)).astype(F32)
    expert_down_grad = pick(dwn, h) + swap(pick(dwn, 1 - h).astype(BF16)).astype(F32)

    shared_both = dot(normed_pair, full_up)
    shared_gate, shared_lift = shared_both[:, :shared_width], shared_both[:, shared_width:]
    shared_act = (jax.nn.silu(shared_gate) * shared_lift).astype(BF16)
    shared_sum = dot(shared_act, full_down).reshape(2, rows, width)
    shared_down_part = dot_first(shared_act, cotangent_pair)
    shared_grad = gated_grad(dot_last(cotangent_pair, full_down), shared_gate, shared_lift)
    shared_up_part = dot_first(normed_pair, shared_grad)
    shared_back = dot_last(shared_grad, full_up).reshape(2, rows, width)
    output = (
        resid + routed_sum + pick(shared_sum, h) + swap(pick(shared_sum, 1 - h).astype(BF16)).astype(F32)
    ).astype(BF16)

    dgate = home[:, width : width + experts] + home[:, width + experts : width + 2 * experts]
    weighted = gates * dgate
    logit_grad = (weighted - gates * jnp.sum(weighted, axis=1, keepdims=True)).astype(BF16)
    router_part = dot_first(normed_two, logit_grad)
    norm_two_grad = (
        home[:, :width] + dot_last(logit_grad, full_router)
        + pick(shared_back, h) + swap(pick(shared_back, 1 - h).astype(BF16)).astype(F32)
    )
    back, gain_two_part = norm_back(resid, scaler_two, gain_second, norm_two_grad)
    hidden_grad = cotangent.astype(F32) + back
    hidden_low = hidden_grad.astype(BF16)
    hidden_pair = pair(hidden_low, swap(hidden_low)).reshape(2 * rows, width)
    out_part = dot_first(attended, hidden_pair)
    mixed_grad = dot_last(hidden_pair, full_out).astype(BF16)
    query_grad, *kv_parts = attention_backward(query, kv, attended_full, lse, mixed_grad, where)
    kv_grads = reduce_scatter_blk([part.reshape(blks, 2 * rows, kw) for part in kv_parts], blks, 6, [BF16] * 2)
    qkv_grad = jnp.concatenate([query_grad, *kv_grads], axis=1)
    norm_one_part = dot_last(qkv_grad, full_qkv).reshape(2, rows, width)
    norm_one_grad = pick(norm_one_part, h) + swap(pick(norm_one_part, 1 - h).astype(BF16)).astype(F32)
    extra_grad, gain_one_part = norm_back(inputs, inv_scale(inputs), gain_first, norm_one_grad)
    input_grad = hidden_grad + extra_grad
    qkv_part = dot_first(normed_one, qkv_grad)
    small_part = jnp.concatenate(
        [router_part, gain_one_part[:, None], gain_two_part[:, None],
         jnp.zeros((width, lanes - experts - 2), F32)], axis=1)

    def by_rows(part):
        return part.astype(BF16).reshape(2, blks, dense_rows, -1)

    qkv_sum, up_sum, out_sum, down_sum, small_sum = reduce_scatter_blk(
        [by_rows(qkv_part), by_rows(shared_up_part),
         out_part.astype(BF16).reshape(blks, dense_rows, width),
         shared_down_part.astype(BF16).reshape(blks, -1, width), by_rows(small_part)],
        blks, 7, [BF16, BF16, F32, F32, F32])
    there = swap(jnp.concatenate([pick(qkv_sum, 1 - h), pick(up_sum, 1 - h)], axis=1)).astype(F32)
    here = jnp.concatenate([pick(qkv_sum, h), pick(up_sum, h)], axis=1).astype(F32)
    small_sum = pick(small_sum, h) + swap(pick(small_sum, 1 - h))

    def whole(start, size):
        return jnp.where(
            h == 0,
            jnp.concatenate([here[:, start : start + size], there[:, start : start + size]], axis=1),
            jnp.concatenate([there[:, start : start + size], here[:, start : start + size]], axis=1))

    top = qw + 2 * kw
    sw = shared_width
    up_grad = jnp.concatenate([whole(top, sw), whole(top + sw, sw)], axis=1)
    return (
        output, input_grad, small_sum[:, experts], whole(0, qw), whole(qw, kw), whole(qw + kw, kw),
        out_sum, small_sum[:, experts + 1], small_sum[:, :experts], up_grad, down_sum,
        expert_up_grad[None], expert_down_grad[None],
    )


def solution(mesh):
    both = P(("head", "blk"), None)
    flat = P(("head", "blk"))
    up, down = P("blk", "head", None), P("blk", None, "head")
    return jax.shard_map(
        shards,
        mesh=mesh,
        in_specs=(both, both, P(), P(), both, flat, both, both, both, both, flat, both, both, both, up, down),
        out_specs=(both, both, flat, both, both, both, both, flat, both, both, both, up, down),
        check_vma=False,
    )
```

```python
import functools

import jax
import jax.numpy as jnp
from jax import lax
from jax.experimental import pallas as pl
from jax.experimental.pallas import tpu as pltpu
from jax.sharding import PartitionSpec as P

MESH = pl.DeviceIdType.MESH


def ring_place(chip, chips):
    odd = chip % 2
    return (chip // 2) * (1 - odd) + (chips - 1 - chip // 2) * odd


def ring_chip(place, chips):
    high = place // (chips // 2)
    return 2 * place * (1 - high) + (2 * (chips - 1 - place) + 1) * high


def ring_info(chips):
    blk = lax.axis_index("blk")
    chip, core = blk // 2, blk % 2
    place = ring_place(chip, chips)

    def at(step):
        return ring_chip((place + step + chips) % chips, chips) * 2 + core

    return blk, core, at, blk + 1 - 2 * core


def pieces_of(shape):
    if len(shape) == 3:
        return [(0, None), (1, None)]
    rows = shape[0]
    if rows >= 32 and rows % 16 == 0:
        cut = (rows // 2 + 15) // 16 * 16
        return [(0, cut), (cut, rows - cut)]
    return [(0, rows)]


def part_in(ref, piece):
    start, size = piece
    return ref.at[start] if size is None else ref.at[pl.ds(start, size)]


def part_out(ref, piece, b):
    start, size = piece
    return ref.at[start, b] if size is None else ref.at[b, pl.ds(start, size)]


def ag_kernel(count, chips, plans, *refs):
    ins, outs = refs[:count], refs[count : 2 * count]
    right_sem, left_sem, sib_sem, sright, sleft, ssib, own_sem = refs[2 * count :]
    blk, core, at, sib = ring_info(chips)
    right, left = at(1), at(-1)
    barrier = pltpu.get_barrier_semaphore()
    for other in (right, left, sib):
        pl.semaphore_signal(barrier, inc=1, device_id={"blk": other}, device_id_type=MESH)
    pl.semaphore_wait(barrier, 3)
    half = chips // 2
    started = []

    def send(src, dst, ssem, rsem, dev):
        copy = pltpu.make_async_remote_copy(
            src_ref=src, dst_ref=dst, send_sem=ssem, recv_sem=rsem,
            device_id={"blk": dev}, device_id_type=MESH)
        copy.start()
        started.append(copy)
        return copy

    chunks = []
    for k in range(count):
        for i, piece in enumerate(plans[k]):
            chunks.append((len(chunks), k, piece, half - (i % 2), half - 1 + (i % 2)))
    copies = {}
    locals_ = []
    for c, k, piece, rh, lh in chunks:
        src = part_in(ins[k], piece)
        dst = part_out(outs[k], piece, blk)
        if rh >= 1:
            copies[c, "r", 1] = send(src, dst, sright.at[c, 0], right_sem.at[c, 0], right)
        if lh >= 1:
            copies[c, "l", 1] = send(src, dst, sleft.at[c, 0], left_sem.at[c, 0], left)
        copies[c, "s", 0] = send(src, dst, ssib.at[c, 0], sib_sem.at[c, 0], sib)
        own = pltpu.make_async_copy(src, dst, own_sem.at[c])
        own.start()
        locals_.append(own)
    for s in range(1, half + 1):
        for c, k, piece, rh, lh in chunks:
            if s <= rh:
                copies[c, "r", s].wait_recv()
                b = at(-s)
                blockref = part_out(outs[k], piece, b)
                if s < rh:
                    copies[c, "r", s + 1] = send(blockref, blockref, sright.at[c, s], right_sem.at[c, s], right)
                copies[c, "sr", s] = send(blockref, blockref, ssib.at[c, s], sib_sem.at[c, s], sib)
            if s <= lh:
                copies[c, "l", s].wait_recv()
                b = at(s)
                blockref = part_out(outs[k], piece, b)
                if s < lh:
                    copies[c, "l", s + 1] = send(blockref, blockref, sleft.at[c, s], left_sem.at[c, s], left)
                copies[c, "sl", s] = send(blockref, blockref, ssib.at[c, half + s], sib_sem.at[c, half + s], sib)
    for (c, d, s), copy in copies.items():
        if d in ("s", "sr", "sl"):
            copy.wait_recv()
    for copy in started:
        copy.wait_send()
    for copy in locals_:
        copy.wait()


def all_gather_blk(arrays, blks, collective_id, vmem=False):
    chips = blks // 2
    count = len(arrays)
    plans = [pieces_of(a.shape) for a in arrays]
    n = sum(len(p) for p in plans)
    half = chips // 2
    shapes = [
        jax.ShapeDtypeStruct((a.shape[0], blks) + a.shape[1:] if a.ndim == 3 else (blks,) + a.shape, a.dtype)
        for a in arrays
    ]
    dma = pltpu.SemaphoreType.DMA
    space = pltpu.VMEM if vmem else pl.ANY
    return pl.pallas_call(
        functools.partial(ag_kernel, count, chips, plans),
        out_shape=shapes,
        in_specs=[pl.BlockSpec(memory_space=space)] * count,
        out_specs=[pl.BlockSpec(memory_space=space)] * count,
        scratch_shapes=[
            dma((n, half)), dma((n, half)), dma((n, 2 * half + 1)),
            dma((n, half)), dma((n, half)), dma((n, 2 * half + 1)), dma((n,)),
        ],
        compiler_params=pltpu.CompilerParams(collective_id=collective_id, has_side_effects=True,
            vmem_limit_bytes=(60 << 20) if vmem else None),
    )(*arrays)


def rs_kernel(count, chips, plans, *refs):
    xs, outs = refs[:count], refs[count : 2 * count]
    rest = refs[2 * count :]
    n = sum(len(p) for p in plans)
    ys, rs, ls = rest[:n], rest[n : 2 * n], rest[2 * n : 3 * n]
    right_sem, left_sem, sib_sem, sright, sleft, ssib = rest[3 * n :]
    blk, core, at, sib = ring_info(chips)
    right, left = at(1), at(-1)
    barrier = pltpu.get_barrier_semaphore()
    for other in (right, left, sib):
        pl.semaphore_signal(barrier, inc=1, device_id={"blk": other}, device_id_type=MESH)
    pl.semaphore_wait(barrier, 3)
    half = chips // 2
    started = []

    def send(src, dst, ssem, rsem, dev):
        copy = pltpu.make_async_remote_copy(
            src_ref=src, dst_ref=dst, send_sem=ssem, recv_sem=rsem,
            device_id={"blk": dev}, device_id_type=MESH)
        copy.start()
        started.append(copy)
        return copy

    chunks = []
    for k in range(count):
        for i, piece in enumerate(plans[k]):
            chunks.append((len(chunks), k, piece, half - (i % 2), half - 1 + (i % 2)))
    order = []
    for d in range(half, 0, -1):
        order += [d, -d] if d < half else [d]
    order.append(0)
    sibs = {}
    for j, d in enumerate(order):
        there = at(d) + 1 - 2 * core
        for c, k, piece, rh, lh in chunks:
            sibs[c, d] = send(part_out(xs[k], piece, there), ys[c].at[j], ssib.at[c, j], sib_sem.at[c, j], sib)
    ready = set()

    def blocks(rows, body):
        step = 16 if rows % 16 == 0 else rows

        @pl.loop(0, rows // step)
        def _(i):
            body(pl.ds(pl.multiple_of(i * step, step), step))

    def mine(c, k, piece, d):
        j = order.index(d)
        if (c, d) not in ready:
            sibs[c, d].wait_recv()
            ready.add((c, d))
        return j

    copies = {}

    def join(c, k, piece, d, into, recv):
        j = mine(c, k, piece, d)
        x = part_out(xs[k], piece, at(d))
        rows = x.shape[0]

        def body(w):
            total = x[w].astype(jnp.float32) + ys[c][j, w].astype(jnp.float32)
            if recv is not None:
                total = total + recv[w].astype(jnp.float32)
            into[w] = total.astype(into.dtype)

        blocks(rows, body)

    for s in range(1, half + 1):
        for c, k, piece, rh, lh in chunks:
            for way, hops, buf, sem, ssem, dev in (
                (1, rh, rs[c], right_sem, sright, right),
                (-1, lh, ls[c], left_sem, sleft, left),
            ):
                if s > hops:
                    continue
                if s == 1:
                    j = order.index(way * hops if way * hops in order else hops)
                    join(c, k, piece, order[j], ys[c].at[j], None)
                    src = ys[c].at[j]
                else:
                    copies[c, way, s - 1].wait_recv()
                    d = way * (hops - s + 1)
                    src = buf.at[s - 2]
                    join(c, k, piece, d, src, src)
                copies[c, way, s] = send(src, buf.at[s - 1], ssem.at[c, s - 1], sem.at[c, s - 1], dev)
    for c, k, piece, rh, lh in chunks:
        if rh >= 1:
            copies[c, 1, rh].wait_recv()
        if lh >= 1:
            copies[c, -1, lh].wait_recv()
        j = mine(c, k, piece, 0)
        x = part_out(xs[k], piece, blk)
        target = part_in(outs[k], piece)

        def body(w, x=x, c=c, j=j, rh=rh, lh=lh, target=target):
            total = x[w].astype(jnp.float32) + ys[c][j, w].astype(jnp.float32)
            if rh >= 1:
                total = total + rs[c][rh - 1, w].astype(jnp.float32)
            if lh >= 1:
                total = total + ls[c][lh - 1, w].astype(jnp.float32)
            target[w] = total.astype(target.dtype)

        blocks(x.shape[0], body)
    for copy in started:
        copy.wait_send()


def reduce_scatter_blk(arrays, blks, collective_id, out_dtypes):
    chips = blks // 2
    half = chips // 2
    count = len(arrays)
    shapes = [a.shape[1:] if a.ndim == 3 else (2,) + a.shape[2:] for a in arrays]
    plans = [pieces_of(s) for s in shapes]
    dma = pltpu.SemaphoreType.DMA
    ys, rs = [], []
    for s, plan in zip(shapes, plans):
        for start, size in plan:
            rows = s[1] if size is None else size
            ys.append(pltpu.VMEM((chips, rows, s[-1]), jnp.bfloat16))
            rs.append(pltpu.VMEM((half, rows, s[-1]), jnp.bfloat16))
    n = len(ys)
    return pl.pallas_call(
        functools.partial(rs_kernel, count, chips, plans),
        out_shape=[jax.ShapeDtypeStruct(s, t) for s, t in zip(shapes, out_dtypes)],
        in_specs=[pl.BlockSpec(memory_space=pltpu.VMEM)] * count,
        out_specs=[pl.BlockSpec(memory_space=pltpu.VMEM)] * count,
        scratch_shapes=ys + rs + rs + [
            dma((n, half)), dma((n, half)), dma((n, chips)),
            dma((n, half)), dma((n, half)), dma((n, chips)),
        ],
        compiler_params=pltpu.CompilerParams(collective_id=collective_id, has_side_effects=True,
            vmem_limit_bytes=60 << 20),
    )(*arrays)


H = 12
KVH = 4
HD = 128
TOP = 6
PIECE = 128
EPS = 1e-05
NEG = -1e30
F32 = jnp.float32
BF16 = jnp.bfloat16


def dot(a, b):
    return jnp.dot(a, b, preferred_element_type=F32)


def dot_first(a, b):
    return lax.dot_general(a, b, (((0,), (0,)), ((), ())), preferred_element_type=F32)


def dot_last(a, b):
    return lax.dot_general(a, b, (((1,), (1,)), ((), ())), preferred_element_type=F32)


def inv_scale(values):
    return lax.rsqrt(jnp.mean(values * values, axis=1, keepdims=True) + EPS)


def norm_back(values, scaler, gain, upstream):
    normed = values * scaler
    gain_grad = jnp.sum(upstream * normed, axis=0)
    scaled = upstream * gain
    grad = scaler * (scaled - normed * jnp.mean(scaled * normed, axis=1, keepdims=True))
    return grad, gain_grad


def gated_grad(act_grad, gate, lift):
    sig = jax.nn.sigmoid(gate)
    return jnp.concatenate(
        [act_grad * lift * sig * (1.0 + gate * (1.0 - sig)), act_grad * gate * sig], axis=1
    ).astype(BF16)


def swap(array):
    return lax.ppermute(array, "head", [(0, 1), (1, 0)])


def key_span(places_ref, ends_ref, i):
    place = places_ref[i]
    start = jnp.int32(0)
    for e in range(ends_ref.shape[0]):
        start = jnp.where(ends_ref[e] <= place * PIECE, ends_ref[e], start)
    return start // PIECE, place


def key_chunk(slots_ref, first, pieces, *refs):
    last = slots_ref.shape[0] - 1
    slots = [slots_ref[jnp.minimum(first + k, last)] for k in range(pieces)]
    return slots, [jnp.concatenate([ref[s] for s in slots], axis=0) for ref in refs]


def stacked(ref, i, repeats):
    return jnp.concatenate(
        [ref[pl.ds(i * PIECE, PIECE), pl.ds(r * HD, HD)] for r in range(repeats)], axis=0)


def seen(ends_ref, place, first, keys, cols):
    own = place * PIECE + lax.broadcasted_iota(jnp.int32, (1, cols), 1) % PIECE
    start = jnp.zeros((1, cols), jnp.int32)
    for e in range(ends_ref.shape[0]):
        start = jnp.where(ends_ref[e] <= own, ends_ref[e], start)
    there = first * PIECE + lax.broadcasted_iota(jnp.int32, (keys, 1), 0)
    return (there <= own) & (there >= start)


CHUNK = 4


def forward_kernel(repeats, slots_ref, places_ref, ends_ref, q_ref, k_ref, v_ref, low_ref, full_ref, lse_ref):
    cols = repeats * PIECE
    for i in range(q_ref.shape[0] // PIECE):
        lo, place = key_span(places_ref, ends_ref, i)
        q = stacked(q_ref, i, repeats)

        def step(n, carry, lo=lo, place=place, q=q):
            top, total, acc = carry
            first = lo + n * CHUNK
            _, (k, v) = key_chunk(slots_ref, first, CHUNK, k_ref, v_ref)
            scores = dot_last(k, q) * HD**-0.5
            scores = jnp.where(seen(ends_ref, place, first, CHUNK * PIECE, cols), scores, NEG)
            new = jnp.maximum(top, jnp.max(scores, axis=0, keepdims=True))
            weights = jnp.exp(scores - new)
            factor = jnp.exp(top - new)
            total = total * factor + jnp.sum(weights, axis=0, keepdims=True)
            return new, total, acc * factor + dot_first(v, weights.astype(BF16))

        top, total, acc = lax.fori_loop(
            0, (place - lo) // CHUNK + 1, step,
            (jnp.full((1, cols), NEG, F32), jnp.zeros((1, cols), F32), jnp.zeros((HD, cols), F32)))
        out = jnp.swapaxes(acc / total, 0, 1)
        lse_ref[0, pl.ds(i, 1), :] = top + jnp.log(total)
        for r in range(repeats):
            part = out[r * PIECE : (r + 1) * PIECE]
            full_ref[pl.ds(i * PIECE, PIECE), pl.ds(r * HD, HD)] = part
            low_ref[pl.ds(i * PIECE, PIECE), pl.ds(r * HD, HD)] = part.astype(BF16)


def attention_forward(query, kv, where):
    rows, pieces = query.shape[0], kv.shape[0]
    groups = kv.shape[2] // (2 * HD)
    wide = query.shape[1] // groups
    repeats = wide // HD
    spec = pl.BlockSpec((rows, wide), lambda g, *_: (0, g))
    return pl.pallas_call(
        functools.partial(forward_kernel, repeats),
        grid_spec=pltpu.PrefetchScalarGridSpec(
            num_scalar_prefetch=3,
            grid=(groups,),
            in_specs=[
                spec,
                pl.BlockSpec((pieces, PIECE, HD), lambda g, *_: (0, 0, g)),
                pl.BlockSpec((pieces, PIECE, HD), lambda g, *_: (0, 0, groups + g)),
            ],
            out_specs=[spec, spec, pl.BlockSpec((1, rows // PIECE, repeats * PIECE), lambda g, *_: (g, 0, 0))],
        ),
        out_shape=[
            jax.ShapeDtypeStruct(query.shape, BF16),
            jax.ShapeDtypeStruct(query.shape, F32),
            jax.ShapeDtypeStruct((groups, rows // PIECE, repeats * PIECE), F32),
        ],
        compiler_params=pltpu.CompilerParams(vmem_limit_bytes=48 << 20),
    )(*where, query, kv, kv)


def backward_kernel(
    repeats, slots_ref, places_ref, ends_ref, q_ref, k_ref, v_ref, full_ref, grad_ref, lse_ref,
    dq_ref, dk_ref, dv_ref, key_acc, value_acc,
):
    cols = repeats * PIECE
    key_acc[...] = jnp.zeros_like(key_acc)
    value_acc[...] = jnp.zeros_like(value_acc)
    for i in range(q_ref.shape[0] // PIECE):
        lo, place = key_span(places_ref, ends_ref, i)
        q, grad = stacked(q_ref, i, repeats), stacked(grad_ref, i, repeats)
        product = grad.astype(F32) * stacked(full_ref, i, repeats)
        delta = jnp.sum(jnp.swapaxes(product, 0, 1), axis=0, keepdims=True)
        lse = lse_ref[0, pl.ds(i, 1), :]

        def step(n, dq, lo=lo, place=place, q=q, grad=grad, delta=delta, lse=lse):
            first = lo + n * CHUNK
            slots, (k, v) = key_chunk(slots_ref, first, CHUNK, k_ref, v_ref)
            scores = dot_last(k, q) * HD**-0.5
            weights = jnp.where(
                seen(ends_ref, place, first, CHUNK * PIECE, cols), jnp.exp(scores - lse), 0.0)
            back = (weights * (dot_last(v, grad) - delta)).astype(BF16)
            dk = dot(back, q)
            dv = dot(weights.astype(BF16), grad)
            for j, s in enumerate(slots):
                key_acc[s] += dk[j * PIECE : (j + 1) * PIECE]
                value_acc[s] += dv[j * PIECE : (j + 1) * PIECE]
            return dq + dot_first(k, back)

        dq = lax.fori_loop(0, (place - lo) // CHUNK + 1, step, jnp.zeros((HD, cols), F32))
        out = (jnp.swapaxes(dq, 0, 1) * HD**-0.5).astype(BF16)
        for r in range(repeats):
            dq_ref[pl.ds(i * PIECE, PIECE), pl.ds(r * HD, HD)] = out[r * PIECE : (r + 1) * PIECE]
    dk_ref[...] = (key_acc[...] * HD**-0.5).astype(BF16)
    dv_ref[...] = value_acc[...].astype(BF16)


def attention_backward(query, kv, full, lse, grad, where):
    rows, pieces = query.shape[0], kv.shape[0]
    groups = kv.shape[2] // (2 * HD)
    wide = query.shape[1] // groups
    repeats = wide // HD
    spec = pl.BlockSpec((rows, wide), lambda g, *_: (0, g))
    block = pl.BlockSpec((pieces, PIECE, HD), lambda g, *_: (0, 0, g))
    half = jax.ShapeDtypeStruct((pieces, PIECE, groups * HD), BF16)
    return pl.pallas_call(
        functools.partial(backward_kernel, repeats),
        grid_spec=pltpu.PrefetchScalarGridSpec(
            num_scalar_prefetch=3,
            grid=(groups,),
            in_specs=[
                spec, block, pl.BlockSpec((pieces, PIECE, HD), lambda g, *_: (0, 0, groups + g)), spec, spec,
                pl.BlockSpec((1, rows // PIECE, repeats * PIECE), lambda g, *_: (g, 0, 0)),
            ],
            out_specs=[spec, block, block],
            scratch_shapes=[pltpu.VMEM((pieces, PIECE, HD), F32)] * 2,
        ),
        out_shape=[jax.ShapeDtypeStruct(query.shape, BF16), half, half],
        compiler_params=pltpu.CompilerParams(vmem_limit_bytes=60 << 20),
    )(*where, query, kv, kv, full, grad, lse)


def tiles(total, size, body):
    if total == size:
        body(pl.ds(0, size))
    else:

        @pl.loop(0, total // size)
        def _(i):
            body(pl.ds(pl.multiple_of(i * size, size), size))


def shifted(c, by):
    if isinstance(c.start, int):
        return pl.ds(c.start + by, c.size)
    return pl.ds(pl.multiple_of(c.start + by, c.size), c.size)


def expert_kernel(
    chips, experts, ext_ref, in_ref, out_ref, cot_ref,
    home_ref, routed_ref, din_ref, dout_ref,
    ext, cot, rows_x, rows_dy, rows_act, rows_dab, both, result, back, deal, gate,
    own_d, own_o, stage_d, stage_o, sib_d, sib_o, right_d, right_o, left_d, left_o,
    copy_sem, cot_sem, ag_r, ag_l, ag_sr, ag_sl, ss_r, ss_l, ss_sr, ss_sl,
    ex_sem, ss_ex, rs_r, rs_l, ss_rr, ss_rl,
):
    blk, core, at, sib = ring_info(chips)
    right, left = at(1), at(-1)
    half = chips // 2
    rows, wide = ext_ref.shape
    width = in_ref.shape[0]
    hidden = out_ref.shape[0]
    slots = rows_x.shape[0] // chips
    cut = rows // 2
    upper, lower = pl.ds(0, cut), pl.ds(cut, cut)

    barrier = pltpu.get_barrier_semaphore()
    for other in (right, left, sib):
        pl.semaphore_signal(barrier, inc=1, device_id={"blk": other}, device_id_type=MESH)
    pl.semaphore_wait(barrier, 3)

    def remote(src, dst, ssem, rsem, dev):
        return pltpu.make_async_remote_copy(
            src_ref=src, dst_ref=dst, send_sem=ssem, recv_sem=rsem,
            device_id={"blk": dev}, device_id_type=MESH)

    def hop_right(part, k, s):
        ref = ext.at[at(1 - s), part]
        return remote(ref, ref, ss_r.at[k, s], ag_r.at[k, s], right)

    def hop_left(part, k, s):
        ref = ext.at[at(s - 1), part]
        return remote(ref, ref, ss_l.at[k, s], ag_l.at[k, s], left)

    def over_right(part, k, s):
        ref = ext.at[at(-s), part]
        return remote(ref, ref, ss_sr.at[k, s], ag_sr.at[k, s], sib)

    def over_left(part, k, s):
        ref = ext.at[at(s), part]
        return remote(ref, ref, ss_sl.at[k, s], ag_sl.at[k, s], sib)

    def cot_copy(g, j):
        there = at(-g) if j == 0 else at(g + 1)
        slot = lax.rem(g, 2)
        return pltpu.make_async_copy(
            cot_ref.at[pl.ds(there - core, 2)], cot.at[slot, j], cot_sem.at[slot, j])

    def place_of(g, j):
        return at(-g) if j == 0 else at(g + 1)

    def exchange_d(g, j):
        return remote(stage_d.at[j], sib_d.at[lax.div(place_of(g, j), 2)], ss_ex.at[0, j, g], ex_sem.at[0, j, g], sib)

    def exchange_o(g, j):
        return remote(stage_o.at[j], sib_o.at[lax.div(place_of(g, j), 2)], ss_ex.at[1, j, g], ex_sem.at[1, j, g], sib)

    mine = pltpu.make_async_copy(ext_ref, ext.at[blk], copy_sem)
    mine.start()
    cot_copy(0, 0).start()
    cot_copy(0, 1).start()
    mine.wait()
    for k, part in ((0, upper), (1, lower)):
        hop_right(part, k, 1).start()
        hop_left(part, k, 1).start()
        over_right(part, k, 0).start()

    triangle = lax.broadcasted_iota(jnp.int32, (rows, rows), 0) > lax.broadcasted_iota(jnp.int32, (rows, rows), 1)
    triangle = triangle.astype(BF16)
    lane = lax.broadcasted_iota(jnp.int32, (rows, 128), 1)

    @pl.loop(0, half)
    def _(g):
        s = g + 1
        hop_right(upper, 0, s).wait_recv()

        @pl.when(s < half)
        def _():
            hop_right(upper, 0, s + 1).start()

        over_right(upper, 0, s).start()
        hop_left(lower, 1, s).wait_recv()

        @pl.when(s < half)
        def _():
            hop_left(lower, 1, s + 1).start()

        over_left(lower, 1, s).start()

        @pl.when(s < half)
        def _():
            hop_right(lower, 1, s).wait_recv()

            @pl.when(s < half - 1)
            def _():
                hop_right(lower, 1, s + 1).start()

            over_right(lower, 1, s).start()
            hop_left(upper, 0, s).wait_recv()

            @pl.when(s < half - 1)
            def _():
                hop_left(upper, 0, s + 1).start()

            over_left(upper, 0, s).start()

        over_right(upper, 0, g).wait_recv()
        over_right(lower, 1, g).wait_recv()
        over_left(lower, 1, s).wait_recv()

        @pl.when(s < half)
        def _():
            over_left(upper, 0, s).wait_recv()

        @pl.when(s == half)
        def _():
            over_right(upper, 0, s).wait_recv()

        cot_copy(g, 0).wait()
        cot_copy(g, 1).wait()

        @pl.when(s < half)
        def _():
            cot_copy(g + 1, 0).start()
            cot_copy(g + 1, 1).start()

        turn = lax.rem(g, 2)
        group = pl.ds(pl.multiple_of(g * 2 * slots, 2 * slots), 2 * slots)
        firsts = (at(-g) - core, at(g + 1) - core)
        for j in range(2):
            for i in range(2):
                lanes = ext[firsts[j] + i, :, pl.ds(width, 128)].astype(F32)
                chosen = jnp.sum(jnp.where(lane == experts + blk, lanes, 0.0), axis=1, keepdims=True)
                weight = jnp.sum(jnp.where(lane == blk, lanes, 0.0), axis=1, keepdims=True)
                chosen = jnp.broadcast_to(chosen, (rows, 128))
                rank = dot(triangle, chosen.astype(BF16)) + i * (slots // 2)
                spread = jnp.where((rank == lane.astype(F32)) & (chosen > 0.5), 1.0, 0.0)
                deal[j, i] = spread.astype(BF16)
                gate[j, i] = jnp.broadcast_to(weight, (rows, 128))
            where = pl.ds(pl.multiple_of(g * 2 * slots + j * slots, slots), slots)

            def pick_rows(c, j=j, where=where):
                taken = dot_first(deal[j, 0], ext[firsts[j], :, c]) + dot_first(deal[j, 1], ext[firsts[j] + 1, :, c])
                rows_x[where, c] = taken.astype(BF16)
                scaled = [(deal[j, i] * gate[j, i].astype(BF16)) for i in range(2)]
                taken = dot_first(scaled[0], cot[turn, j, 0, :, c]) + dot_first(scaled[1], cot[turn, j, 1, :, c])
                rows_dy[where, c] = taken.astype(BF16)

            tiles(width, 512, pick_rows)

        def hidden_tile(c):
            high = shifted(c, hidden)
            x = rows_x[group]
            gate_part = dot(x, in_ref[:, c])
            lift = dot(x, in_ref[:, high])
            both[:, c] = gate_part
            both[:, high] = lift
            rows_act[group, c] = (jax.nn.silu(gate_part) * lift).astype(BF16)

        tiles(hidden, 256, hidden_tile)

        def result_tile(c):
            result[:, c] = dot(rows_act[group], out_ref[:, c]).astype(BF16)

        tiles(width, 512, result_tile)

        def grad_tile(c):
            high = shifted(c, hidden)
            da = dot_last(rows_dy[group], out_ref[c, :])
            gate_part, lift = both[:, c], both[:, high]
            sig = jax.nn.sigmoid(gate_part)
            rows_dab[group, c] = (da * lift * sig * (1.0 + gate_part * (1.0 - sig))).astype(BF16)
            rows_dab[group, high] = (da * gate_part * sig).astype(BF16)

        tiles(hidden, 256, grad_tile)

        def back_tile(c):
            back[:, c] = dot_last(rows_dab[group], in_ref[c, :]).astype(BF16)

        tiles(width, 512, back_tile)

        @pl.when(g > 0)
        def _():
            for j in range(2):
                exchange_d(g - 1, j).wait_send()
                exchange_o(g - 1, j).wait_send()

        for j in range(2):
            chip = lax.div(firsts[j], 2)
            for which, to_d, to_o in (
                (core, own_d.at[chip], own_o.at[chip]),
                (1 - core, stage_d.at[j], stage_o.at[j]),
            ):
                part = pl.ds(j * slots, slots)
                dealer = deal[j, which]
                share = gate[j, which]
                total = jnp.zeros((rows, 1), F32)
                for t in range(width // 512):
                    c = pl.ds(t * 512, 512)
                    home_rows = dot(dealer, result[part, c])
                    to_o[:, c] = (home_rows * share[:, :1]).astype(BF16)
                    total = total + jnp.sum(
                        home_rows * cot[turn, j, which, :, c].astype(F32), axis=1, keepdims=True)
                    to_d[:, c] = dot(dealer, back[part, c]).astype(BF16)
                high = total.astype(BF16).astype(F32)
                lanes = jnp.where(lane == blk, high, jnp.where(lane == experts + blk, total - high, 0.0))
                to_d[:, pl.ds(width, 128)] = lanes.astype(BF16)
            exchange_d(g, j).start()
            exchange_o(g, j).start()

    arrays = ((0, own_d, sib_d, right_d, left_d, home_ref), (1, own_o, sib_o, right_o, left_o, routed_ref))
    arrived = set()

    def join(a, own, other, d, part, into, received):
        g, j = (d - 1, 1) if d > 0 else (-d, 0)
        if (a, g, j) not in arrived:
            arrived.add((a, g, j))
            (exchange_d, exchange_o)[a](g, j).wait_recv()
        chip = lax.div(at(d), 2)

        def add(c):
            total = own[chip, c].astype(F32) + other[chip, c].astype(F32)
            for ref in received:
                total = total + ref[c].astype(F32)
            into[c] = total.astype(into.dtype)

        @pl.loop(0, cut // 16)
        def _(i):
            add(pl.ds(pl.multiple_of(part.start + i * 16, 16), 16))

    def pass_right(a, src, buf, k, part, s):
        return remote(src.at[part], buf.at[s - 1, part], ss_rr.at[a, k, s], rs_r.at[a, k, s], right)

    def pass_left(a, src, buf, k, part, s):
        return remote(src.at[part], buf.at[s - 1, part], ss_rl.at[a, k, s], rs_l.at[a, k, s], left)

    ways = (
        (0, upper, 1, half), (1, lower, -1, half), (1, lower, 1, half - 1), (0, upper, -1, half - 1),
    )
    sent = []
    for s in range(1, half + 1):
        for a, own, other, to_right, to_left, _ in arrays:
            for k, part, way, hops in ways:
                if s > hops:
                    continue
                make, buf = (pass_right, to_right) if way > 0 else (pass_left, to_left)
                d = way * (hops - s + 1)
                if d == -half:
                    d = half
                if s == 1:
                    src = own.at[lax.div(at(d), 2)]
                    join(a, own, other, d, part, src, ())
                else:
                    src = buf.at[s - 2]
                    make(a, src, buf, k, part, s - 1).wait_recv()
                    join(a, own, other, d, part, src, (src,))
                copy = make(a, src, buf, k, part, s)
                copy.start()
                sent.append(copy)
        if s < half:
            each = width // 256 // (half - 1)

            @pl.loop((s - 1) * each, s * each)
            def _(i):
                c = pl.ds(pl.multiple_of(i * 256, 256), 256)
                din_ref[c, :] = dot_first(rows_x[:, c], rows_dab[...]).astype(BF16)
        else:

            def weight_tile(c):
                dout_ref[c, :] = dot_first(rows_act[:, c], rows_dy[...]).astype(BF16)

            tiles(hidden, 256, weight_tile)
    for a, own, other, to_right, to_left, into in arrays:
        for k, part in ((0, upper), (1, lower)):
            last_right, last_left = half - k, half - 1 + k
            pass_right(a, own.at[0], to_right, k, part, last_right).wait_recv()
            pass_left(a, own.at[0], to_left, k, part, last_left).wait_recv()
            join(a, own, other, 0, part, into, (to_right.at[last_right - 1], to_left.at[last_left - 1]))
    for copy in sent:
        copy.wait_send()
    for j in range(2):
        exchange_d(half - 1, j).wait_send()
        exchange_o(half - 1, j).wait_send()
    for k, part in ((0, upper), (1, lower)):
        over_right(part, k, 0).wait_send()
        for s in range(1, half + 1):
            if s <= half - k:
                hop_right(part, k, s).wait_send()
                over_right(part, k, s).wait_send()
            if s <= half - 1 + k:
                hop_left(part, k, s).wait_send()
                over_left(part, k, s).wait_send()


def experts_fused(ext, expert_in, expert_out, cot_all, blks, capacity, collective_id):
    chips, half = blks // 2, blks // 4
    rows, wide = ext.shape
    width, hidden = expert_in.shape[0], expert_out.shape[0]
    count = blks * capacity
    group = 4 * capacity
    dma = pltpu.SemaphoreType.DMA
    vmem = pl.BlockSpec(memory_space=pltpu.VMEM)
    anywhere = pl.BlockSpec(memory_space=pl.ANY)

    def low(*shape):
        return pltpu.VMEM(shape, BF16)

    return pl.pallas_call(
        functools.partial(expert_kernel, chips, blks),
        out_shape=[
            jax.ShapeDtypeStruct((rows, wide), F32), jax.ShapeDtypeStruct((rows, width), F32),
            jax.ShapeDtypeStruct(expert_in.shape, BF16), jax.ShapeDtypeStruct(expert_out.shape, BF16),
        ],
        in_specs=[anywhere, vmem, vmem, anywhere],
        out_specs=[vmem] * 4,
        scratch_shapes=[
            low(blks, rows, wide), low(2, 2, 2, rows, width),
            low(count, width), low(count, width), low(count, hidden), low(count, 2 * hidden),
            pltpu.VMEM((group, 2 * hidden), F32), low(group, width), low(group, width),
            low(2, 2, rows, 128), pltpu.VMEM((2, 2, rows, 128), F32),
            low(chips, rows, wide), low(chips, rows, width), low(2, rows, wide), low(2, rows, width),
            low(chips, rows, wide), low(chips, rows, width),
            low(half, rows, wide), low(half, rows, width), low(half, rows, wide), low(half, rows, width),
            dma(()), dma((2, 2)),
            dma((2, half + 1)), dma((2, half + 1)), dma((2, half + 1)), dma((2, half + 1)),
            dma((2, half + 1)), dma((2, half + 1)), dma((2, half + 1)), dma((2, half + 1)),
            dma((2, 2, half)), dma((2, 2, half)),
            dma((2, 2, half + 1)), dma((2, 2, half + 1)), dma((2, 2, half + 1)), dma((2, 2, half + 1)),
        ],
        compiler_params=pltpu.CompilerParams(
            collective_id=collective_id, has_side_effects=True, vmem_limit_bytes=62 << 20),
    )(ext, expert_in, expert_out, cot_all)


def experts_plain(own_ext, expert_in, expert_out, cot_all, blks, capacity, collective_id):
    b = lax.axis_index("blk")
    experts, width = blks, expert_in.shape[0]
    rows = own_ext.shape[0]
    ext = all_gather_blk([own_ext], blks, collective_id)[0]
    norm_all = ext[:, :, :width]
    gate_here = lax.dynamic_index_in_dim(ext, width + b, 2, keepdims=False).astype(F32)
    mask_here = lax.dynamic_index_in_dim(ext, width + experts + b, 2, keepdims=False).astype(F32)
    rank = jnp.cumsum(mask_here, axis=1) - mask_here
    slots = jnp.arange(capacity, dtype=F32)
    deal = ((rank[:, None, :] == slots[None, :, None]) & (mask_here[:, None, :] > 0)).astype(BF16)
    deal_gate = deal * gate_here[:, None, :].astype(BF16)

    def to_slots(dealer, array):
        moved = jnp.einsum("bst,btd->bsd", dealer, array, preferred_element_type=F32)
        return moved.astype(BF16).reshape(blks * capacity, width)

    def to_rows(dealer, array):
        return jnp.einsum(
            "bst,bsd->btd", dealer, array.reshape(blks, capacity, width), preferred_element_type=F32)

    expert_rows = to_slots(deal, norm_all)
    both = dot(expert_rows, expert_in)
    ew = expert_out.shape[0]
    gate_part, up_part = both[:, :ew], both[:, ew:]
    activated = (jax.nn.silu(gate_part) * up_part).astype(BF16)
    result = dot(activated, expert_out).astype(BF16)
    result_rows = to_rows(deal, result)
    gate_grad = jnp.sum(result_rows * cot_all.astype(F32), axis=2, keepdims=True)
    routed = (result_rows * gate_here[:, :, None]).astype(BF16)
    slot_grad = to_slots(deal_gate, cot_all)
    act_grad = dot_last(slot_grad, expert_out)
    both_grad = gated_grad(act_grad, gate_part, up_part)
    rows_back = to_rows(deal, dot_last(both_grad, expert_in).astype(BF16)).astype(BF16)
    lane = jnp.arange(128 * (-(-2 * experts // 128)), dtype=jnp.int32)
    grad_high = gate_grad.astype(BF16)
    grad_low = (gate_grad - grad_high.astype(F32)).astype(BF16)
    grad_lanes = jnp.where(lane == b, grad_high, jnp.where(lane == b + experts, grad_low, jnp.zeros((), BF16)))
    dwn = dot_first(activated, slot_grad).astype(BF16)
    dup = dot_first(expert_rows, both_grad).astype(BF16)
    home = reduce_scatter_blk([jnp.concatenate([rows_back, grad_lanes], axis=2)], blks, collective_id + 1, [F32])[0]
    routed_sum = reduce_scatter_blk([routed], blks, collective_id + 2, [F32])[0]
    return home, routed_sum, dup, dwn


def shards(
    tokens, cotangent, seq_lengths, piece_order, routes, norm1_gain, w_query, w_key, w_value, w_out,
    norm2_gain, w_router, shared_up, shared_down, expert_up, expert_down,
):
    blks = lax.axis_size("blk")
    h, b = lax.axis_index("head"), lax.axis_index("blk")
    rows, width = tokens.shape
    experts = blks
    capacity = rows * TOP * 4 // (3 * blks)
    dense_rows = w_query.shape[0]

    def pair(own, other):
        return jnp.where(h == 0, jnp.stack([own, other]), jnp.stack([other, own]))

    def half(w, i, parts=1):
        size = w.shape[1] // (2 * parts)
        cut = lax.dynamic_slice_in_dim(w.reshape(w.shape[0], parts, 2 * size), i * size, size, 2)
        return cut.reshape(w.shape[0], parts * size)

    def pick(stacked, i):
        return lax.dynamic_index_in_dim(stacked, i, 0, keepdims=False)

    def columns(i):
        return jnp.concatenate([half(w_query, i), half(w_key, i), half(w_value, i)], axis=1)

    small = jnp.concatenate(
        [w_router, norm1_gain[:, None], norm2_gain[:, None],
         jnp.zeros((dense_rows, -(experts + 2) % 128), BF16)], axis=1)
    lanes = small.shape[1]
    first = pair(
        jnp.concatenate([columns(h), small], axis=1),
        swap(jnp.concatenate([columns(1 - h), small], axis=1)),
    )
    tokens_pair = pair(tokens, swap(tokens))
    cotangent_pair = pair(cotangent, swap(cotangent)).reshape(2 * rows, width)
    up_pair = pair(half(shared_up, h, 2), swap(half(shared_up, 1 - h, 2)))
    expert_in = pair(expert_up[0], swap(expert_up[0])).reshape(width, -1)
    other_down = swap(expert_down[0])
    expert_out = jnp.where(
        h == 0,
        jnp.concatenate([expert_down[0], other_down], axis=1),
        jnp.concatenate([other_down, expert_down[0]], axis=1),
    )
    gathered = all_gather_blk([first], blks, 0)[0].reshape(width, -1)
    qw = w_query.shape[1] // 2
    kw = w_key.shape[1] // 2
    full_qkv = gathered[:, : qw + 2 * kw]
    full_router = gathered[:, qw + 2 * kw : qw + 2 * kw + experts]
    gain_first = gathered[:, qw + 2 * kw + experts].astype(F32)
    gain_second = gathered[:, qw + 2 * kw + experts + 1].astype(F32)

    inputs_pair = tokens_pair.reshape(2 * rows, width).astype(F32)
    normed_one = (inputs_pair * inv_scale(inputs_pair) * gain_first).astype(BF16)
    qkv = dot(normed_one, full_qkv).astype(BF16)
    query = qkv[:, :qw]
    kv = all_gather_blk([qkv[:, qw:]], blks, 1)[0].reshape(-1, PIECE, 2 * kw)

    places = jnp.swapaxes(piece_order.reshape(2, blks), 0, 1).reshape(-1)
    order = jnp.arange(2 * blks, dtype=jnp.int32)
    slots = jnp.sum(jnp.where(places[None, :] == order[:, None], order[None, :], 0), axis=1)
    where = (slots, lax.dynamic_slice_in_dim(places, 2 * b, 2), jnp.cumsum(seq_lengths))
    attended, attended_full, lse = attention_forward(query, kv, where)

    up_all, out_all, down_all, cot_all = all_gather_blk([up_pair, w_out, shared_down, cotangent], blks, 2)
    full_up = up_all.reshape(width, -1)
    full_out = out_all.reshape(-1, width)
    full_down = down_all.reshape(-1, width)
    shared_width = full_down.shape[0]

    mixed = dot(attended, full_out).reshape(2, rows, width)
    inputs = tokens.astype(F32)
    resid = inputs + (pick(mixed, h) + swap(pick(mixed, 1 - h).astype(BF16)).astype(F32))
    scaler_two = inv_scale(resid)
    normed_two = (resid * scaler_two * gain_second).astype(BF16)
    normed_pair = pair(normed_two, swap(normed_two)).reshape(2 * rows, width)

    logits = dot(normed_two, full_router)
    hot = routes[:, :, None] == jnp.arange(experts, dtype=jnp.int32)[None, None, :]
    mask = jnp.any(hot, axis=1)
    masked = jnp.where(mask, logits, NEG)
    raised = jnp.where(mask, jnp.exp(masked - jnp.max(masked, axis=1, keepdims=True)), 0.0)
    gates = raised / jnp.sum(raised, axis=1, keepdims=True)
    extra = jnp.concatenate(
        [gates.astype(BF16), mask.astype(BF16), jnp.zeros((rows, -2 * experts % 128), BF16)], axis=1)

    ext = jnp.concatenate([normed_two, extra], axis=1)
    fits = blks == 16 and rows == 128 and 2 * capacity == 128 and width % 768 == 0
    experts_run = experts_fused if fits else experts_plain
    home, routed_sum, dup, dwn = experts_run(ext, expert_in, expert_out, cot_all, blks, capacity, 3)
    dup = dup.reshape(2, width // 2, -1)
    dwn = jnp.stack([dwn[:, : width // 2], dwn[:, width // 2 :]])
    expert_up_grad = pick(dup, h).astype(F32) + swap(pick(dup, 1 - h)).astype(F32)
    expert_down_grad = pick(dwn, h).astype(F32) + swap(pick(dwn, 1 - h)).astype(F32)

    shared_both = dot(normed_pair, full_up)
    shared_gate, shared_lift = shared_both[:, :shared_width], shared_both[:, shared_width:]
    shared_act = (jax.nn.silu(shared_gate) * shared_lift).astype(BF16)
    shared_sum = dot(shared_act, full_down).reshape(2, rows, width)
    shared_down_part = dot_first(shared_act, cotangent_pair)
    shared_grad = gated_grad(dot_last(cotangent_pair, full_down), shared_gate, shared_lift)
    shared_up_part = dot_first(normed_pair, shared_grad)
    shared_back = dot_last(shared_grad, full_up).reshape(2, rows, width)
    output = (
        resid + routed_sum + pick(shared_sum, h) + swap(pick(shared_sum, 1 - h).astype(BF16)).astype(F32)
    ).astype(BF16)

    dgate = home[:, width : width + experts] + home[:, width + experts : width + 2 * experts]
    weighted = gates * dgate
    logit_grad = (weighted - gates * jnp.sum(weighted, axis=1, keepdims=True)).astype(BF16)
    router_part = dot_first(normed_two, logit_grad)
    norm_two_grad = (
        home[:, :width] + dot_last(logit_grad, full_router)
        + pick(shared_back, h) + swap(pick(shared_back, 1 - h).astype(BF16)).astype(F32)
    )
    back, gain_two_part = norm_back(resid, scaler_two, gain_second, norm_two_grad)
    hidden_grad = cotangent.astype(F32) + back
    hidden_low = hidden_grad.astype(BF16)
    hidden_pair = pair(hidden_low, swap(hidden_low)).reshape(2 * rows, width)
    out_part = dot_first(attended, hidden_pair)
    mixed_grad = dot_last(hidden_pair, full_out).astype(BF16)
    query_grad, *kv_parts = attention_backward(query, kv, attended_full, lse, mixed_grad, where)
    kv_grads = reduce_scatter_blk([part.reshape(blks, 2 * rows, kw) for part in kv_parts], blks, 6, [BF16] * 2)
    qkv_grad = jnp.concatenate([query_grad, *kv_grads], axis=1)
    norm_one_part = dot_last(qkv_grad, full_qkv).reshape(2, rows, width)
    norm_one_grad = pick(norm_one_part, h) + swap(pick(norm_one_part, 1 - h).astype(BF16)).astype(F32)
    extra_grad, gain_one_part = norm_back(inputs, inv_scale(inputs), gain_first, norm_one_grad)
    input_grad = hidden_grad + extra_grad
    qkv_part = dot_first(normed_one, qkv_grad)
    small_part = jnp.concatenate(
        [router_part, gain_one_part[:, None], gain_two_part[:, None],
         jnp.zeros((width, lanes - experts - 2), F32)], axis=1)

    def by_rows(part):
        return part.astype(BF16).reshape(2, blks, dense_rows, -1)

    qkv_sum, up_sum, out_sum, down_sum, small_sum = reduce_scatter_blk(
        [by_rows(qkv_part), by_rows(shared_up_part),
         out_part.astype(BF16).reshape(blks, dense_rows, width),
         shared_down_part.astype(BF16).reshape(blks, -1, width), by_rows(small_part)],
        blks, 7, [BF16, BF16, F32, F32, F32])
    there = swap(jnp.concatenate([pick(qkv_sum, 1 - h), pick(up_sum, 1 - h)], axis=1)).astype(F32)
    here = jnp.concatenate([pick(qkv_sum, h), pick(up_sum, h)], axis=1).astype(F32)
    small_sum = pick(small_sum, h) + swap(pick(small_sum, 1 - h))

    def whole(start, size):
        return jnp.where(
            h == 0,
            jnp.concatenate([here[:, start : start + size], there[:, start : start + size]], axis=1),
            jnp.concatenate([there[:, start : start + size], here[:, start : start + size]], axis=1))

    top = qw + 2 * kw
    sw = shared_width
    up_grad = jnp.concatenate([whole(top, sw), whole(top + sw, sw)], axis=1)
    return (
        output, input_grad, small_sum[:, experts], whole(0, qw), whole(qw, kw), whole(qw + kw, kw),
        out_sum, small_sum[:, experts + 1], small_sum[:, :experts], up_grad, down_sum,
        expert_up_grad[None], expert_down_grad[None],
    )


def solution(mesh):
    both = P(("head", "blk"), None)
    flat = P(("head", "blk"))
    up, down = P("blk", "head", None), P("blk", None, "head")
    return jax.shard_map(
        shards,
        mesh=mesh,
        in_specs=(both, both, P(), P(), both, flat, both, both, both, both, flat, both, both, both, up, down),
        out_specs=(both, both, flat, both, both, both, both, flat, both, both, both, up, down),
        check_vma=False,
    )
```

```python
import functools

import jax
import jax.numpy as jnp
from jax import lax
from jax.experimental import pallas as pl
from jax.experimental.pallas import tpu as pltpu
from jax.sharding import PartitionSpec as P

MESH = pl.DeviceIdType.MESH


def ring_place(chip, chips):
    odd = chip % 2
    return (chip // 2) * (1 - odd) + (chips - 1 - chip // 2) * odd


def ring_chip(place, chips):
    high = place // (chips // 2)
    return 2 * place * (1 - high) + (2 * (chips - 1 - place) + 1) * high


def ring_info(chips):
    blk = lax.axis_index("blk")
    chip, core = blk // 2, blk % 2
    place = ring_place(chip, chips)

    def at(step):
        return ring_chip((place + step + chips) % chips, chips) * 2 + core

    return blk, core, at, blk + 1 - 2 * core


def pieces_of(shape):
    if len(shape) == 3:
        return [(0, None), (1, None)]
    rows = shape[0]
    if rows >= 32 and rows % 16 == 0:
        cut = (rows // 2 + 15) // 16 * 16
        return [(0, cut), (cut, rows - cut)]
    return [(0, rows)]


def part_in(ref, piece):
    start, size = piece
    return ref.at[start] if size is None else ref.at[pl.ds(start, size)]


def part_out(ref, piece, b):
    start, size = piece
    return ref.at[start, b] if size is None else ref.at[b, pl.ds(start, size)]


def ag_kernel(count, chips, plans, *refs):
    ins, outs = refs[:count], refs[count : 2 * count]
    right_sem, left_sem, sib_sem, sright, sleft, ssib, own_sem = refs[2 * count :]
    blk, core, at, sib = ring_info(chips)
    right, left = at(1), at(-1)
    barrier = pltpu.get_barrier_semaphore()
    for other in (right, left, sib):
        pl.semaphore_signal(barrier, inc=1, device_id={"blk": other}, device_id_type=MESH)
    pl.semaphore_wait(barrier, 3)
    half = chips // 2
    started = []

    def send(src, dst, ssem, rsem, dev):
        copy = pltpu.make_async_remote_copy(
            src_ref=src, dst_ref=dst, send_sem=ssem, recv_sem=rsem,
            device_id={"blk": dev}, device_id_type=MESH)
        copy.start()
        started.append(copy)
        return copy

    chunks = []
    for k in range(count):
        for i, piece in enumerate(plans[k]):
            chunks.append((len(chunks), k, piece, half - (i % 2), half - 1 + (i % 2)))
    copies = {}
    locals_ = []
    for c, k, piece, rh, lh in chunks:
        src = part_in(ins[k], piece)
        dst = part_out(outs[k], piece, blk)
        if rh >= 1:
            copies[c, "r", 1] = send(src, dst, sright.at[c, 0], right_sem.at[c, 0], right)
        if lh >= 1:
            copies[c, "l", 1] = send(src, dst, sleft.at[c, 0], left_sem.at[c, 0], left)
        copies[c, "s", 0] = send(src, dst, ssib.at[c, 0], sib_sem.at[c, 0], sib)
        own = pltpu.make_async_copy(src, dst, own_sem.at[c])
        own.start()
        locals_.append(own)
    for s in range(1, half + 1):
        for c, k, piece, rh, lh in chunks:
            if s <= rh:
                copies[c, "r", s].wait_recv()
                b = at(-s)
                blockref = part_out(outs[k], piece, b)
                if s < rh:
                    copies[c, "r", s + 1] = send(blockref, blockref, sright.at[c, s], right_sem.at[c, s], right)
                copies[c, "sr", s] = send(blockref, blockref, ssib.at[c, s], sib_sem.at[c, s], sib)
            if s <= lh:
                copies[c, "l", s].wait_recv()
                b = at(s)
                blockref = part_out(outs[k], piece, b)
                if s < lh:
                    copies[c, "l", s + 1] = send(blockref, blockref, sleft.at[c, s], left_sem.at[c, s], left)
                copies[c, "sl", s] = send(blockref, blockref, ssib.at[c, half + s], sib_sem.at[c, half + s], sib)
    for (c, d, s), copy in copies.items():
        if d in ("s", "sr", "sl"):
            copy.wait_recv()
    for copy in started:
        copy.wait_send()
    for copy in locals_:
        copy.wait()


def all_gather_blk(arrays, blks, collective_id, vmem=False):
    chips = blks // 2
    count = len(arrays)
    plans = [pieces_of(a.shape) for a in arrays]
    n = sum(len(p) for p in plans)
    half = chips // 2
    shapes = [
        jax.ShapeDtypeStruct((a.shape[0], blks) + a.shape[1:] if a.ndim == 3 else (blks,) + a.shape, a.dtype)
        for a in arrays
    ]
    dma = pltpu.SemaphoreType.DMA
    space = pltpu.VMEM if vmem else pl.ANY
    return pl.pallas_call(
        functools.partial(ag_kernel, count, chips, plans),
        out_shape=shapes,
        in_specs=[pl.BlockSpec(memory_space=space)] * count,
        out_specs=[pl.BlockSpec(memory_space=space)] * count,
        scratch_shapes=[
            dma((n, half)), dma((n, half)), dma((n, 2 * half + 1)),
            dma((n, half)), dma((n, half)), dma((n, 2 * half + 1)), dma((n,)),
        ],
        compiler_params=pltpu.CompilerParams(collective_id=collective_id, has_side_effects=True,
            vmem_limit_bytes=(60 << 20) if vmem else None),
    )(*arrays)


def rs_kernel(count, chips, plans, *refs):
    xs, outs = refs[:count], refs[count : 2 * count]
    rest = refs[2 * count :]
    n = sum(len(p) for p in plans)
    ys, rs, ls = rest[:n], rest[n : 2 * n], rest[2 * n : 3 * n]
    right_sem, left_sem, sib_sem, sright, sleft, ssib = rest[3 * n :]
    blk, core, at, sib = ring_info(chips)
    right, left = at(1), at(-1)
    barrier = pltpu.get_barrier_semaphore()
    for other in (right, left, sib):
        pl.semaphore_signal(barrier, inc=1, device_id={"blk": other}, device_id_type=MESH)
    pl.semaphore_wait(barrier, 3)
    half = chips // 2
    started = []

    def send(src, dst, ssem, rsem, dev):
        copy = pltpu.make_async_remote_copy(
            src_ref=src, dst_ref=dst, send_sem=ssem, recv_sem=rsem,
            device_id={"blk": dev}, device_id_type=MESH)
        copy.start()
        started.append(copy)
        return copy

    chunks = []
    for k in range(count):
        for i, piece in enumerate(plans[k]):
            chunks.append((len(chunks), k, piece, half - (i % 2), half - 1 + (i % 2)))
    order = []
    for d in range(half, 0, -1):
        order += [d, -d] if d < half else [d]
    order.append(0)
    sibs = {}
    for j, d in enumerate(order):
        there = at(d) + 1 - 2 * core
        for c, k, piece, rh, lh in chunks:
            sibs[c, d] = send(part_out(xs[k], piece, there), ys[c].at[j], ssib.at[c, j], sib_sem.at[c, j], sib)
    ready = set()

    def blocks(rows, body):
        step = 16 if rows % 16 == 0 else rows

        @pl.loop(0, rows // step)
        def _(i):
            body(pl.ds(pl.multiple_of(i * step, step), step))

    def mine(c, k, piece, d):
        j = order.index(d)
        if (c, d) not in ready:
            sibs[c, d].wait_recv()
            ready.add((c, d))
        return j

    copies = {}

    def join(c, k, piece, d, into, recv):
        j = mine(c, k, piece, d)
        x = part_out(xs[k], piece, at(d))
        rows = x.shape[0]

        def body(w):
            total = x[w].astype(jnp.float32) + ys[c][j, w].astype(jnp.float32)
            if recv is not None:
                total = total + recv[w].astype(jnp.float32)
            into[w] = total.astype(into.dtype)

        blocks(rows, body)

    for s in range(1, half + 1):
        for c, k, piece, rh, lh in chunks:
            for way, hops, buf, sem, ssem, dev in (
                (1, rh, rs[c], right_sem, sright, right),
                (-1, lh, ls[c], left_sem, sleft, left),
            ):
                if s > hops:
                    continue
                if s == 1:
                    j = order.index(way * hops if way * hops in order else hops)
                    join(c, k, piece, order[j], ys[c].at[j], None)
                    src = ys[c].at[j]
                else:
                    copies[c, way, s - 1].wait_recv()
                    d = way * (hops - s + 1)
                    src = buf.at[s - 2]
                    join(c, k, piece, d, src, src)
                copies[c, way, s] = send(src, buf.at[s - 1], ssem.at[c, s - 1], sem.at[c, s - 1], dev)
    for c, k, piece, rh, lh in chunks:
        if rh >= 1:
            copies[c, 1, rh].wait_recv()
        if lh >= 1:
            copies[c, -1, lh].wait_recv()
        j = mine(c, k, piece, 0)
        x = part_out(xs[k], piece, blk)
        target = part_in(outs[k], piece)

        def body(w, x=x, c=c, j=j, rh=rh, lh=lh, target=target):
            total = x[w].astype(jnp.float32) + ys[c][j, w].astype(jnp.float32)
            if rh >= 1:
                total = total + rs[c][rh - 1, w].astype(jnp.float32)
            if lh >= 1:
                total = total + ls[c][lh - 1, w].astype(jnp.float32)
            target[w] = total.astype(target.dtype)

        blocks(x.shape[0], body)
    for copy in started:
        copy.wait_send()


def reduce_scatter_blk(arrays, blks, collective_id, out_dtypes):
    chips = blks // 2
    half = chips // 2
    count = len(arrays)
    shapes = [a.shape[1:] if a.ndim == 3 else (2,) + a.shape[2:] for a in arrays]
    plans = [pieces_of(s) for s in shapes]
    dma = pltpu.SemaphoreType.DMA
    ys, rs = [], []
    for s, plan in zip(shapes, plans):
        for start, size in plan:
            rows = s[1] if size is None else size
            ys.append(pltpu.VMEM((chips, rows, s[-1]), jnp.bfloat16))
            rs.append(pltpu.VMEM((half, rows, s[-1]), jnp.bfloat16))
    n = len(ys)
    return pl.pallas_call(
        functools.partial(rs_kernel, count, chips, plans),
        out_shape=[jax.ShapeDtypeStruct(s, t) for s, t in zip(shapes, out_dtypes)],
        in_specs=[pl.BlockSpec(memory_space=pltpu.VMEM)] * count,
        out_specs=[pl.BlockSpec(memory_space=pltpu.VMEM)] * count,
        scratch_shapes=ys + rs + rs + [
            dma((n, half)), dma((n, half)), dma((n, chips)),
            dma((n, half)), dma((n, half)), dma((n, chips)),
        ],
        compiler_params=pltpu.CompilerParams(collective_id=collective_id, has_side_effects=True,
            vmem_limit_bytes=60 << 20),
    )(*arrays)


H = 12
KVH = 4
HD = 128
TOP = 6
PIECE = 128
EPS = 1e-05
NEG = -1e30
F32 = jnp.float32
BF16 = jnp.bfloat16


def dot(a, b):
    return jnp.dot(a, b, preferred_element_type=F32)


def dot_first(a, b):
    return lax.dot_general(a, b, (((0,), (0,)), ((), ())), preferred_element_type=F32)


def dot_last(a, b):
    return lax.dot_general(a, b, (((1,), (1,)), ((), ())), preferred_element_type=F32)


def inv_scale(values):
    return lax.rsqrt(jnp.mean(values * values, axis=1, keepdims=True) + EPS)


def norm_back(values, scaler, gain, upstream):
    normed = values * scaler
    gain_grad = jnp.sum(upstream * normed, axis=0)
    scaled = upstream * gain
    grad = scaler * (scaled - normed * jnp.mean(scaled * normed, axis=1, keepdims=True))
    return grad, gain_grad


def gated_grad(act_grad, gate, lift):
    sig = jax.nn.sigmoid(gate)
    return jnp.concatenate(
        [act_grad * lift * sig * (1.0 + gate * (1.0 - sig)), act_grad * gate * sig], axis=1
    ).astype(BF16)


def swap(array):
    return lax.ppermute(array, "head", [(0, 1), (1, 0)])


def key_span(places_ref, ends_ref, i):
    place = places_ref[i]
    start = jnp.int32(0)
    for e in range(ends_ref.shape[0]):
        start = jnp.where(ends_ref[e] <= place * PIECE, ends_ref[e], start)
    return start // PIECE, place


def key_chunk(slots_ref, first, pieces, *refs):
    last = slots_ref.shape[0] - 1
    slots = [slots_ref[jnp.clip(first + k, 0, last)] for k in range(pieces)]
    return slots, [jnp.concatenate([ref[s] for s in slots], axis=0) for ref in refs]


def stacked(ref, i, repeats):
    return jnp.concatenate(
        [ref[pl.ds(i * PIECE, PIECE), pl.ds(r * HD, HD)] for r in range(repeats)], axis=0)


def seen(ends_ref, place, first, keys, cols):
    own = place * PIECE + lax.broadcasted_iota(jnp.int32, (1, cols), 1) % PIECE
    start = jnp.zeros((1, cols), jnp.int32)
    for e in range(ends_ref.shape[0]):
        start = jnp.where(ends_ref[e] <= own, ends_ref[e], start)
    there = first * PIECE + lax.broadcasted_iota(jnp.int32, (keys, 1), 0)
    return (there <= own) & (there >= start)


CHUNK = 4


def forward_kernel(repeats, slots_ref, places_ref, ends_ref, q_ref, k_ref, v_ref, low_ref, full_ref, lse_ref):
    cols = repeats * PIECE
    for i in range(q_ref.shape[0] // PIECE):
        lo, place = key_span(places_ref, ends_ref, i)
        q = stacked(q_ref, i, repeats)

        def step(n, carry, lo=lo, place=place, q=q):
            top, total, acc = carry
            first = lo + n * CHUNK
            _, (k, v) = key_chunk(slots_ref, first, CHUNK, k_ref, v_ref)
            scores = dot_last(k, q) * HD**-0.5
            scores = jnp.where(seen(ends_ref, place, first, CHUNK * PIECE, cols), scores, NEG)
            new = jnp.maximum(top, jnp.max(scores, axis=0, keepdims=True))
            weights = jnp.exp(scores - new)
            factor = jnp.exp(top - new)
            total = total * factor + jnp.sum(weights, axis=0, keepdims=True)
            return new, total, acc * factor + dot_first(v, weights.astype(BF16))

        top, total, acc = lax.fori_loop(
            0, (place - lo) // CHUNK + 1, step,
            (jnp.full((1, cols), NEG, F32), jnp.zeros((1, cols), F32), jnp.zeros((HD, cols), F32)))
        out = jnp.swapaxes(acc / total, 0, 1)
        lse_ref[0, pl.ds(i, 1), :] = top + jnp.log(total)
        for r in range(repeats):
            part = out[r * PIECE : (r + 1) * PIECE]
            full_ref[pl.ds(i * PIECE, PIECE), pl.ds(r * HD, HD)] = part
            low_ref[pl.ds(i * PIECE, PIECE), pl.ds(r * HD, HD)] = part.astype(BF16)


def attention_forward(query, kv, where):
    rows, pieces = query.shape[0], kv.shape[0]
    groups = kv.shape[2] // (2 * HD)
    wide = query.shape[1] // groups
    repeats = wide // HD
    spec = pl.BlockSpec((rows, wide), lambda g, *_: (0, g))
    return pl.pallas_call(
        functools.partial(forward_kernel, repeats),
        grid_spec=pltpu.PrefetchScalarGridSpec(
            num_scalar_prefetch=3,
            grid=(groups,),
            in_specs=[
                spec,
                pl.BlockSpec((pieces, PIECE, HD), lambda g, *_: (0, 0, g)),
                pl.BlockSpec((pieces, PIECE, HD), lambda g, *_: (0, 0, groups + g)),
            ],
            out_specs=[spec, spec, pl.BlockSpec((1, rows // PIECE, repeats * PIECE), lambda g, *_: (g, 0, 0))],
        ),
        out_shape=[
            jax.ShapeDtypeStruct(query.shape, BF16),
            jax.ShapeDtypeStruct(query.shape, F32),
            jax.ShapeDtypeStruct((groups, rows // PIECE, repeats * PIECE), F32),
        ],
        compiler_params=pltpu.CompilerParams(vmem_limit_bytes=48 << 20),
    )(*where, query, kv, kv)


def backward_kernel(
    repeats, slots_ref, places_ref, ends_ref, q_ref, k_ref, v_ref, full_ref, grad_ref, lse_ref,
    dq_ref, dk_ref, dv_ref, key_acc, value_acc,
):
    cols = repeats * PIECE
    key_acc[...] = jnp.zeros_like(key_acc)
    value_acc[...] = jnp.zeros_like(value_acc)
    for i in range(q_ref.shape[0] // PIECE):
        lo, place = key_span(places_ref, ends_ref, i)
        q, grad = stacked(q_ref, i, repeats), stacked(grad_ref, i, repeats)
        product = grad.astype(F32) * stacked(full_ref, i, repeats)
        delta = jnp.sum(jnp.swapaxes(product, 0, 1), axis=0, keepdims=True)
        lse = lse_ref[0, pl.ds(i, 1), :]

        def step(n, dq, lo=lo, place=place, q=q, grad=grad, delta=delta, lse=lse):
            first = lo + n * CHUNK
            slots, (k, v) = key_chunk(slots_ref, first, CHUNK, k_ref, v_ref)
            scores = dot_last(k, q) * HD**-0.5
            weights = jnp.where(
                seen(ends_ref, place, first, CHUNK * PIECE, cols), jnp.exp(scores - lse), 0.0)
            back = (weights * (dot_last(v, grad) - delta)).astype(BF16)
            dk = dot(back, q)
            dv = dot(weights.astype(BF16), grad)
            for j, s in enumerate(slots):
                key_acc[s] += dk[j * PIECE : (j + 1) * PIECE]
                value_acc[s] += dv[j * PIECE : (j + 1) * PIECE]
            return dq + dot_first(k, back)

        dq = lax.fori_loop(0, (place - lo) // CHUNK + 1, step, jnp.zeros((HD, cols), F32))
        out = (jnp.swapaxes(dq, 0, 1) * HD**-0.5).astype(BF16)
        for r in range(repeats):
            dq_ref[pl.ds(i * PIECE, PIECE), pl.ds(r * HD, HD)] = out[r * PIECE : (r + 1) * PIECE]
    dk_ref[...] = (key_acc[...] * HD**-0.5).astype(BF16)
    dv_ref[...] = value_acc[...].astype(BF16)


def attention_backward(query, kv, full, lse, grad, where):
    rows, pieces = query.shape[0], kv.shape[0]
    groups = kv.shape[2] // (2 * HD)
    wide = query.shape[1] // groups
    repeats = wide // HD
    spec = pl.BlockSpec((rows, wide), lambda g, *_: (0, g))
    block = pl.BlockSpec((pieces, PIECE, HD), lambda g, *_: (0, 0, g))
    half = jax.ShapeDtypeStruct((pieces, PIECE, groups * HD), BF16)
    return pl.pallas_call(
        functools.partial(backward_kernel, repeats),
        grid_spec=pltpu.PrefetchScalarGridSpec(
            num_scalar_prefetch=3,
            grid=(groups,),
            in_specs=[
                spec, block, pl.BlockSpec((pieces, PIECE, HD), lambda g, *_: (0, 0, groups + g)), spec, spec,
                pl.BlockSpec((1, rows // PIECE, repeats * PIECE), lambda g, *_: (g, 0, 0)),
            ],
            out_specs=[spec, block, block],
            scratch_shapes=[pltpu.VMEM((pieces, PIECE, HD), F32)] * 2,
        ),
        out_shape=[jax.ShapeDtypeStruct(query.shape, BF16), half, half],
        compiler_params=pltpu.CompilerParams(vmem_limit_bytes=60 << 20),
    )(*where, query, kv, kv, full, grad, lse)


def tiles(total, size, body):
    if total == size:
        body(pl.ds(0, size))
    else:

        @pl.loop(0, total // size)
        def _(i):
            body(pl.ds(pl.multiple_of(i * size, size), size))


def shifted(c, by):
    if isinstance(c.start, int):
        return pl.ds(c.start + by, c.size)
    return pl.ds(pl.multiple_of(c.start + by, c.size), c.size)


def expert_kernel(
    chips, experts, ext_ref, up_own, up_other, down_own, down_other, cot_ref,
    home_ref, routed_ref, din_ref, dout_ref, norm_pair,
    in_ref, out_ref, ext, cot, rows_x, rows_dy, rows_act, rows_dab, both, result, back, deal, gate,
    own_d, own_o, stage_d, stage_o, sib_d, sib_o, right_d, right_o, left_d, left_o,
    copy_sem, cot_sem, ag_r, ag_l, ag_sr, ag_sl, ss_r, ss_l, ss_sr, ss_sl,
    ex_sem, ss_ex, rs_r, rs_l, ss_rr, ss_rl, weight_sem, pair_sem,
):
    blk, core, at, sib = ring_info(chips)
    h = lax.axis_index("head")
    right, left = at(1), at(-1)
    half = chips // 2
    rows, wide = ext_ref.shape
    width = in_ref.shape[0]
    hidden = out_ref.shape[0]
    slots = rows_x.shape[0] // chips
    cut = rows // 2
    upper, lower = pl.ds(0, cut), pl.ds(cut, cut)

    barrier = pltpu.get_barrier_semaphore()
    for other in (right, left, sib):
        pl.semaphore_signal(barrier, inc=1, device_id={"blk": other}, device_id_type=MESH)
    pl.semaphore_signal(barrier, inc=1, device_id={"head": 1 - h}, device_id_type=MESH)
    pl.semaphore_wait(barrier, 4)

    def remote(src, dst, ssem, rsem, dev):
        return pltpu.make_async_remote_copy(
            src_ref=src, dst_ref=dst, send_sem=ssem, recv_sem=rsem,
            device_id={"blk": dev}, device_id_type=MESH)

    def hop_right(part, k, s):
        ref = ext.at[at(1 - s), part]
        return remote(ref, ref, ss_r.at[k, s], ag_r.at[k, s], right)

    def hop_left(part, k, s):
        ref = ext.at[at(s - 1), part]
        return remote(ref, ref, ss_l.at[k, s], ag_l.at[k, s], left)

    def over_right(part, k, s):
        ref = ext.at[at(-s), part]
        return remote(ref, ref, ss_sr.at[k, s], ag_sr.at[k, s], sib)

    def over_left(part, k, s):
        ref = ext.at[at(s), part]
        return remote(ref, ref, ss_sl.at[k, s], ag_sl.at[k, s], sib)

    def cot_copy(g, j):
        there = at(-g) if j == 0 else at(g + 1)
        slot = lax.rem(g, 2)
        return pltpu.make_async_copy(
            cot_ref.at[pl.ds(there - core, 2)], cot.at[slot, j], cot_sem.at[slot, j])

    def place_of(g, j):
        return at(-g) if j == 0 else at(g + 1)

    def exchange_d(g, j):
        return remote(stage_d.at[j], sib_d.at[lax.div(place_of(g, j), 2)], ss_ex.at[0, j, g], ex_sem.at[0, j, g], sib)

    def exchange_o(g, j):
        return remote(stage_o.at[j], sib_o.at[lax.div(place_of(g, j), 2)], ss_ex.at[1, j, g], ex_sem.at[1, j, g], sib)

    mine = pltpu.make_async_copy(ext_ref, ext.at[blk], copy_sem)
    mine.start()
    cot_copy(0, 0).start()
    cot_copy(0, 1).start()
    weights = []
    for i, (up, down) in ((h, (up_own, down_own)), (1 - h, (up_other, down_other))):
        size = up.shape[0]
        start = pl.multiple_of(i * size, size)
        weights.append((up, in_ref.at[pl.ds(start, size)]))
        weights.append((down, out_ref.at[:, pl.ds(start, size)]))
    weights = [pltpu.make_async_copy(a, b, weight_sem.at[i]) for i, (a, b) in enumerate(weights)]
    for copy in weights:
        copy.start()
    mine.wait()
    for k, part in ((0, upper), (1, lower)):
        hop_right(part, k, 1).start()
        hop_left(part, k, 1).start()
        over_right(part, k, 0).start()
    own_norm = ext.at[blk, :, pl.ds(0, width)]
    keep = pltpu.make_async_copy(own_norm, norm_pair.at[h], pair_sem.at[0])
    keep.start()
    swapped = pltpu.make_async_remote_copy(
        src_ref=own_norm, dst_ref=norm_pair.at[h], send_sem=pair_sem.at[1], recv_sem=pair_sem.at[2],
        device_id={"head": 1 - h}, device_id_type=MESH)
    swapped.start()
    for copy in weights:
        copy.wait()

    triangle = lax.broadcasted_iota(jnp.int32, (rows, rows), 0) > lax.broadcasted_iota(jnp.int32, (rows, rows), 1)
    triangle = triangle.astype(BF16)
    lane = lax.broadcasted_iota(jnp.int32, (rows, 128), 1)

    @pl.loop(0, half)
    def _(g):
        s = g + 1
        hop_right(upper, 0, s).wait_recv()

        @pl.when(s < half)
        def _():
            hop_right(upper, 0, s + 1).start()

        over_right(upper, 0, s).start()
        hop_left(lower, 1, s).wait_recv()

        @pl.when(s < half)
        def _():
            hop_left(lower, 1, s + 1).start()

        over_left(lower, 1, s).start()

        @pl.when(s < half)
        def _():
            hop_right(lower, 1, s).wait_recv()

            @pl.when(s < half - 1)
            def _():
                hop_right(lower, 1, s + 1).start()

            over_right(lower, 1, s).start()
            hop_left(upper, 0, s).wait_recv()

            @pl.when(s < half - 1)
            def _():
                hop_left(upper, 0, s + 1).start()

            over_left(upper, 0, s).start()

        over_right(upper, 0, g).wait_recv()
        over_right(lower, 1, g).wait_recv()
        over_left(lower, 1, s).wait_recv()

        @pl.when(s < half)
        def _():
            over_left(upper, 0, s).wait_recv()

        @pl.when(s == half)
        def _():
            over_right(upper, 0, s).wait_recv()

        cot_copy(g, 0).wait()
        cot_copy(g, 1).wait()

        @pl.when(s < half)
        def _():
            cot_copy(g + 1, 0).start()
            cot_copy(g + 1, 1).start()

        turn = lax.rem(g, 2)
        group = pl.ds(pl.multiple_of(g * 2 * slots, 2 * slots), 2 * slots)
        firsts = (at(-g) - core, at(g + 1) - core)
        for j in range(2):
            for i in range(2):
                lanes = ext[firsts[j] + i, :, pl.ds(width, 128)].astype(F32)
                chosen = jnp.sum(jnp.where(lane == experts + blk, lanes, 0.0), axis=1, keepdims=True)
                weight = jnp.sum(jnp.where(lane == blk, lanes, 0.0), axis=1, keepdims=True)
                chosen = jnp.broadcast_to(chosen, (rows, 128))
                rank = dot(triangle, chosen.astype(BF16)) + i * (slots // 2)
                spread = jnp.where((rank == lane.astype(F32)) & (chosen > 0.5), 1.0, 0.0)
                deal[j, i] = spread.astype(BF16)
                gate[j, i] = jnp.broadcast_to(weight, (rows, 128))
            where = pl.ds(pl.multiple_of(g * 2 * slots + j * slots, slots), slots)

            def pick_rows(c, j=j, where=where):
                taken = dot_first(deal[j, 0], ext[firsts[j], :, c]) + dot_first(deal[j, 1], ext[firsts[j] + 1, :, c])
                rows_x[where, c] = taken.astype(BF16)
                scaled = [(deal[j, i] * gate[j, i].astype(BF16)) for i in range(2)]
                taken = dot_first(scaled[0], cot[turn, j, 0, :, c]) + dot_first(scaled[1], cot[turn, j, 1, :, c])
                rows_dy[where, c] = taken.astype(BF16)

            tiles(width, 512, pick_rows)

        def hidden_tile(c):
            high = shifted(c, hidden)
            x = rows_x[group]
            gate_part = dot(x, in_ref[:, c])
            lift = dot(x, in_ref[:, high])
            both[:, c] = gate_part
            both[:, high] = lift
            rows_act[group, c] = (jax.nn.silu(gate_part) * lift).astype(BF16)

        tiles(hidden, 256, hidden_tile)

        def result_tile(c):
            result[:, c] = dot(rows_act[group], out_ref[:, c]).astype(BF16)

        tiles(width, 512, result_tile)

        def grad_tile(c):
            high = shifted(c, hidden)
            da = dot_last(rows_dy[group], out_ref[c, :])
            gate_part, lift = both[:, c], both[:, high]
            sig = jax.nn.sigmoid(gate_part)
            rows_dab[group, c] = (da * lift * sig * (1.0 + gate_part * (1.0 - sig))).astype(BF16)
            rows_dab[group, high] = (da * gate_part * sig).astype(BF16)

        tiles(hidden, 256, grad_tile)

        def back_tile(c):
            back[:, c] = dot_last(rows_dab[group], in_ref[c, :]).astype(BF16)

        tiles(width, 512, back_tile)

        @pl.when(g > 0)
        def _():
            for j in range(2):
                exchange_d(g - 1, j).wait_send()
                exchange_o(g - 1, j).wait_send()

        for j in range(2):
            chip = lax.div(firsts[j], 2)
            for which, to_d, to_o in (
                (core, own_d.at[chip], own_o.at[chip]),
                (1 - core, stage_d.at[j], stage_o.at[j]),
            ):
                part = pl.ds(j * slots, slots)
                dealer = deal[j, which]
                share = gate[j, which]
                total = jnp.zeros((rows, 1), F32)
                for t in range(width // 512):
                    c = pl.ds(t * 512, 512)
                    home_rows = dot(dealer, result[part, c])
                    to_o[:, c] = (home_rows * share[:, :1]).astype(BF16)
                    total = total + jnp.sum(
                        home_rows * cot[turn, j, which, :, c].astype(F32), axis=1, keepdims=True)
                    to_d[:, c] = dot(dealer, back[part, c]).astype(BF16)
                high = total.astype(BF16).astype(F32)
                lanes = jnp.where(lane == blk, high, jnp.where(lane == experts + blk, total - high, 0.0))
                to_d[:, pl.ds(width, 128)] = lanes.astype(BF16)
            exchange_d(g, j).start()
            exchange_o(g, j).start()

    arrays = ((0, own_d, sib_d, right_d, left_d, home_ref), (1, own_o, sib_o, right_o, left_o, routed_ref))
    arrived = set()

    def join(a, own, other, d, part, into, received):
        g, j = (d - 1, 1) if d > 0 else (-d, 0)
        if (a, g, j) not in arrived:
            arrived.add((a, g, j))
            (exchange_d, exchange_o)[a](g, j).wait_recv()
        chip = lax.div(at(d), 2)

        def add(c):
            total = own[chip, c].astype(F32) + other[chip, c].astype(F32)
            for ref in received:
                total = total + ref[c].astype(F32)
            into[c] = total.astype(into.dtype)

        @pl.loop(0, cut // 16)
        def _(i):
            add(pl.ds(pl.multiple_of(part.start + i * 16, 16), 16))

    def pass_right(a, src, buf, k, part, s):
        return remote(src.at[part], buf.at[s - 1, part], ss_rr.at[a, k, s], rs_r.at[a, k, s], right)

    def pass_left(a, src, buf, k, part, s):
        return remote(src.at[part], buf.at[s - 1, part], ss_rl.at[a, k, s], rs_l.at[a, k, s], left)

    ways = (
        (0, upper, 1, half), (1, lower, -1, half), (1, lower, 1, half - 1), (0, upper, -1, half - 1),
    )
    sent = []
    for s in range(1, half + 1):
        for a, own, other, to_right, to_left, _ in arrays:
            for k, part, way, hops in ways:
                if s > hops:
                    continue
                make, buf = (pass_right, to_right) if way > 0 else (pass_left, to_left)
                d = way * (hops - s + 1)
                if d == -half:
                    d = half
                if s == 1:
                    src = own.at[lax.div(at(d), 2)]
                    join(a, own, other, d, part, src, ())
                else:
                    src = buf.at[s - 2]
                    make(a, src, buf, k, part, s - 1).wait_recv()
                    join(a, own, other, d, part, src, (src,))
                copy = make(a, src, buf, k, part, s)
                copy.start()
                sent.append(copy)
        if s < half:
            each = width // 256 // (half - 1)

            @pl.loop((s - 1) * each, s * each)
            def _(i):
                c = pl.ds(pl.multiple_of(i * 256, 256), 256)
                din_ref[c, :] = dot_first(rows_x[:, c], rows_dab[...]).astype(BF16)
        else:

            def weight_tile(c):
                dout_ref[c, :] = dot_first(rows_act[:, c], rows_dy[...]).astype(BF16)

            tiles(hidden, 256, weight_tile)
    for a, own, other, to_right, to_left, into in arrays:
        for k, part in ((0, upper), (1, lower)):
            last_right, last_left = half - k, half - 1 + k
            pass_right(a, own.at[0], to_right, k, part, last_right).wait_recv()
            pass_left(a, own.at[0], to_left, k, part, last_left).wait_recv()
            join(a, own, other, 0, part, into, (to_right.at[last_right - 1], to_left.at[last_left - 1]))
    keep.wait()
    swapped.wait()
    for copy in sent:
        copy.wait_send()
    for j in range(2):
        exchange_d(half - 1, j).wait_send()
        exchange_o(half - 1, j).wait_send()
    for k, part in ((0, upper), (1, lower)):
        over_right(part, k, 0).wait_send()
        for s in range(1, half + 1):
            if s <= half - k:
                hop_right(part, k, s).wait_send()
                over_right(part, k, s).wait_send()
            if s <= half - 1 + k:
                hop_left(part, k, s).wait_send()
                over_left(part, k, s).wait_send()


def experts_fused(ext, weights, cot_all, blks, capacity, collective_id):
    chips, half = blks // 2, blks // 4
    rows, wide = ext.shape
    width, hidden = 2 * weights[0].shape[0], weights[2].shape[0]
    count = blks * capacity
    group = 4 * capacity
    dma = pltpu.SemaphoreType.DMA
    vmem = pl.BlockSpec(memory_space=pltpu.VMEM)
    anywhere = pl.BlockSpec(memory_space=pl.ANY)

    def low(*shape):
        return pltpu.VMEM(shape, BF16)

    return pl.pallas_call(
        functools.partial(expert_kernel, chips, blks),
        out_shape=[
            jax.ShapeDtypeStruct((rows, wide), F32), jax.ShapeDtypeStruct((rows, width), F32),
            jax.ShapeDtypeStruct((width, 2 * hidden), BF16), jax.ShapeDtypeStruct((hidden, width), BF16),
            jax.ShapeDtypeStruct((2, rows, width), BF16),
        ],
        in_specs=[anywhere] * 6,
        out_specs=[vmem] * 4 + [anywhere],
        scratch_shapes=[
            low(width, 2 * hidden), low(hidden, width),
            low(blks, rows, wide), low(2, 2, 2, rows, width),
            low(count, width), low(count, width), low(count, hidden), low(count, 2 * hidden),
            pltpu.VMEM((group, 2 * hidden), F32), low(group, width), low(group, width),
            low(2, 2, rows, 128), pltpu.VMEM((2, 2, rows, 128), F32),
            low(chips, rows, wide), low(chips, rows, width), low(2, rows, wide), low(2, rows, width),
            low(chips, rows, wide), low(chips, rows, width),
            low(half, rows, wide), low(half, rows, width), low(half, rows, wide), low(half, rows, width),
            dma(()), dma((2, 2)),
            dma((2, half + 1)), dma((2, half + 1)), dma((2, half + 1)), dma((2, half + 1)),
            dma((2, half + 1)), dma((2, half + 1)), dma((2, half + 1)), dma((2, half + 1)),
            dma((2, 2, half)), dma((2, 2, half)),
            dma((2, 2, half + 1)), dma((2, 2, half + 1)), dma((2, 2, half + 1)), dma((2, 2, half + 1)),
            dma((4,)), dma((3,)),
        ],
        compiler_params=pltpu.CompilerParams(
            collective_id=collective_id, has_side_effects=True, vmem_limit_bytes=62 << 20),
    )(ext, *weights, cot_all)


class Ring:
    def __init__(self, info, chips, chunks, first, sems):
        self.blk, self.at, self.sib = info
        self.half = chips // 2
        self.chunks, self.first = chunks, first
        self.send_r, self.recv_r, self.send_l, self.recv_l, self.send_s, self.recv_s = sems

    def hops(self, c):
        return self.half - c % 2, self.half - 1 + c % 2

    def copy(self, ref, ssem, rsem, dev):
        return pltpu.make_async_remote_copy(
            src_ref=ref, dst_ref=ref, send_sem=ssem, recv_sem=rsem,
            device_id={"blk": dev}, device_id_type=MESH)

    def right(self, c, s):
        i = self.first + c
        return self.copy(self.chunks[c](self.at(1 - s)), self.send_r.at[i, s], self.recv_r.at[i, s], self.at(1))

    def left(self, c, s):
        i = self.first + c
        return self.copy(self.chunks[c](self.at(s - 1)), self.send_l.at[i, s], self.recv_l.at[i, s], self.at(-1))

    def over(self, c, d):
        i, k = self.first + c, d + self.half
        return self.copy(self.chunks[c](self.at(d)), self.send_s.at[i, k], self.recv_s.at[i, k], self.sib)

    def start(self, c):
        self.right(c, 1).start()
        self.left(c, 1).start()
        self.over(c, 0).start()

    def step(self, s):
        for c in range(len(self.chunks)):
            rh, lh = self.hops(c)
            if s <= rh:
                self.right(c, s).wait_recv()
                if s < rh:
                    self.right(c, s + 1).start()
                self.over(c, -s).start()
            if s <= lh:
                self.left(c, s).wait_recv()
                if s < lh:
                    self.left(c, s + 1).start()
                self.over(c, s).start()

    def end(self):
        for c in range(len(self.chunks)):
            rh, lh = self.hops(c)
            for d in range(-rh, lh + 1):
                self.over(c, d).wait_recv()

    def flush(self):
        for c in range(len(self.chunks)):
            rh, lh = self.hops(c)
            for s in range(1, rh + 1):
                self.right(c, s).wait_send()
            for s in range(1, lh + 1):
                self.left(c, s).wait_send()
            for d in range(-rh, lh + 1):
                self.over(c, d).wait_send()


def front_kernel(
    chips, experts,
    slots_ref, places_ref, ends_ref, lanes_ref, tokens, cotangent, w_query, w_key, w_value, small, w_out,
    shared_up, shared_down, expert_up, expert_down,
    n1, query, kv, first_w, out_w, up_w, down_w, cot, cot_pair, expert_in, expert_out,
    low, full, lse, resid, ext, gates, turned,
    pair, to_other, from_other,
    send_r, recv_r, send_l, recv_l, send_s, recv_s, own_sem, y_send, y_recv,
):
    h = lax.axis_index("head")
    blk, core, at, sib = ring_info(chips)
    half = chips // 2
    rows, width = tokens.shape
    qw, kw = w_query.shape[1] // 2, w_key.shape[1] // 2
    sw = shared_up.shape[1] // 4
    barrier = pltpu.get_barrier_semaphore()
    for other in (at(1), at(-1), sib):
        pl.semaphore_signal(barrier, inc=1, device_id={"blk": other}, device_id_type=MESH)
    pl.semaphore_signal(barrier, inc=1, device_id={"head": 1 - h}, device_id_type=MESH)
    pl.semaphore_wait(barrier, 4)

    def lanes_of(start, size):
        return pl.ds(pl.multiple_of(start, 128), size)

    def halves(i, j):
        return [
            (w_query.at[:, lanes_of(i * qw, qw)], first_w.at[j, blk, :, pl.ds(0, qw)]),
            (w_key.at[:, lanes_of(i * kw, kw)], first_w.at[j, blk, :, pl.ds(qw, kw)]),
            (w_value.at[:, lanes_of(i * kw, kw)], first_w.at[j, blk, :, pl.ds(qw + kw, kw)]),
            (small, first_w.at[j, blk, :, pl.ds(qw + 2 * kw, small.shape[1])]),
            (tokens, pair.at[j]),
            (shared_up.at[:, lanes_of(i * sw, sw)], up_w.at[j, blk, :, pl.ds(0, sw)]),
            (shared_up.at[:, lanes_of((2 + i) * sw, sw)], up_w.at[j, blk, :, pl.ds(sw, sw)]),
            (cotangent, cot_pair.at[j]),
        ]

    whole = [(expert_up, expert_in), (expert_down, expert_out)]

    own = [pltpu.make_async_copy(a, b, own_sem.at[i]) for i, (a, b) in enumerate(halves(h, h))]
    own.append(pltpu.make_async_copy(w_out, out_w.at[blk], own_sem.at[len(own)]))
    own.append(pltpu.make_async_copy(shared_down, down_w.at[blk], own_sem.at[len(own)]))
    own.append(pltpu.make_async_copy(cotangent, cot.at[blk], own_sem.at[len(own)]))
    swaps = [
        pltpu.make_async_remote_copy(
            src_ref=a, dst_ref=b, send_sem=y_send.at[i], recv_sem=y_recv.at[i],
            device_id={"head": 1 - h}, device_id_type=MESH)
        for i, (a, b) in enumerate(halves(1 - h, h) + whole)
    ]
    for i in range(5):
        swaps[i].start()
    for i in (0, 1, 2, 3, 8, 4):
        own[i].start()

    info = (blk, at, sib)
    sems = (send_r, recv_r, send_l, recv_l, send_s, recv_s)

    def row_cuts(ref, *sizes):
        start, chunks = 0, []
        for size in sizes:
            chunks.append(lambda b, start=start, size=size: ref.at[b, pl.ds(start, size)])
            start += size
        return chunks

    ring_w = Ring(info, chips, [lambda b: first_w.at[h, b], lambda b: first_w.at[1 - h, b]], 0, sems)
    out_rows, down_rows = w_out.shape[0], shared_down.shape[0]
    ring_o = Ring(info, chips, row_cuts(out_w, 32, out_rows - 32), 2, sems)
    ring_kv = Ring(info, chips, [lambda b: kv.at[2 * b], lambda b: kv.at[2 * b + 1]], 4, sems)
    ring_u = Ring(info, chips, [lambda b: up_w.at[h, b], lambda b: up_w.at[1 - h, b]], 6, sems)
    ring_d = Ring(info, chips, row_cuts(down_w, down_rows // 2, down_rows // 2), 8, sems)
    ring_c = Ring(info, chips, row_cuts(cot, rows // 2, rows // 2), 10, sems)

    for i in (0, 1, 2, 3):
        own[i].wait()
    ring_w.start(0)
    own[8].wait()
    for i in range(4):
        swaps[i].wait_recv()
    ring_w.start(1)
    ring_o.start(0)
    ring_o.start(1)
    for i in (5, 6, 9, 10, 7):
        own[i].start()
    for i in range(5, 10):
        swaps[i].start()
    for s in range(1, half + 1):
        ring_w.step(s)
        ring_o.step(s)
    ring_w.end()
    own[4].wait()
    swaps[4].wait_recv()

    small_cols = first_w[:, :, :, pl.ds(qw + 2 * kw, 128)].reshape(width, 128)
    turned[...] = jnp.swapaxes(small_cols.astype(F32), 0, 1)

    @pl.loop(0, 2 * rows // 64)
    def _(i):
        x = pair[lax.div(i, rows // 64), pl.ds(pl.multiple_of(lax.rem(i, rows // 64) * 64, 64), 64), :].astype(F32)
        scaled = x * lax.rsqrt(jnp.mean(x * x, axis=1, keepdims=True) + EPS) * turned[pl.ds(experts, 1), :]
        n1[pl.ds(pl.multiple_of(i * 64, 64), 64), :] = scaled.astype(BF16)

    def project(start, size):
        weights = first_w[:, :, :, pl.ds(start, size)].reshape(width, size)
        return dot(n1[...], weights).astype(BF16)

    for t in range(2 * kw // 256):
        part = project(qw + t * 256, 256)
        for i in range(2):
            kv[2 * blk + i, :, pl.ds(t * 256, 256)] = part[i * rows : (i + 1) * rows]
    ring_kv.start(0)
    ring_kv.start(1)
    for t in range(qw // 256):
        query[:, pl.ds(t * 256, 256)] = project(t * 256, 256)
    for i in (5, 6, 9, 10):
        own[i].wait()
    swaps[5].wait_recv()
    swaps[6].wait_recv()
    for s in range(1, half + 1):
        ring_kv.step(s)
        if s == half - 1:
            for ring in (ring_u, ring_d, ring_c):
                ring.start(0)
                ring.start(1)
    ring_kv.end()

    groups, repeats = kw // HD, qw // kw
    cols = repeats * PIECE
    pieces = slots_ref.shape[0]
    need = pieces // 2 + 1
    chunk = 6
    chunks = -(-need // chunk)
    later = [(ring_u, 1), (ring_d, 1), (ring_c, 1), (ring_u, 2), (ring_d, 2), (ring_c, 2)]
    turns = 0
    for i in range(2):
        place = places_ref[i]
        for g in range(groups):
            q = jnp.concatenate(
                [query[pl.ds(i * PIECE, PIECE), pl.ds((g * repeats + r) * HD, HD)] for r in range(repeats)], axis=0)

            def step(n, carry, place=place, g=g, q=q):
                top, total, acc = carry
                first = place + 1 - chunks * chunk + n * chunk
                _, (k, v) = key_chunk(
                    slots_ref, first, chunk, kv.at[:, :, pl.ds(g * HD, HD)], kv.at[:, :, pl.ds((groups + g) * HD, HD)])
                scores = dot_last(k, q) * HD**-0.5
                scores = jnp.where(seen(ends_ref, place, first, chunk * PIECE, cols), scores, NEG)
                new = jnp.maximum(top, jnp.max(scores, axis=0, keepdims=True))
                weights = jnp.exp(scores - new)
                factor = jnp.exp(top - new)
                total = total * factor + jnp.sum(weights, axis=0, keepdims=True)
                return new, total, acc * factor + dot_first(v, weights.astype(BF16))

            top, total, acc = lax.fori_loop(
                0, chunks, step,
                (jnp.full((1, cols), NEG, F32), jnp.zeros((1, cols), F32), jnp.zeros((HD, cols), F32)))
            out = jnp.swapaxes(acc / total, 0, 1)
            lse[g, pl.ds(i, 1), :] = top + jnp.log(total)
            for r in range(repeats):
                part = out[r * PIECE : (r + 1) * PIECE]
                full[pl.ds(i * PIECE, PIECE), pl.ds((g * repeats + r) * HD, HD)] = part
                low[pl.ds(i * PIECE, PIECE), pl.ds((g * repeats + r) * HD, HD)] = part.astype(BF16)
            turns += 1
            if turns % 2 == 0:
                for ring, s in later[:3]:
                    ring.step(s)
                later = later[3:]

    ring_o.end()
    theirs = pl.ds(pl.multiple_of((1 - h) * rows, rows), rows)
    ours = pl.ds(pl.multiple_of(h * rows, rows), rows)

    def mixed(where, c):
        return dot(low[where, :], out_w[:, :, c].reshape(qw, c.size))

    for t in range(width // 512):
        c = pl.ds(t * 512, 512)
        to_other[:, c] = mixed(theirs, c).astype(BF16)
    swap_mixed = pltpu.make_async_remote_copy(
        src_ref=to_other, dst_ref=from_other, send_sem=y_send.at[10], recv_sem=y_recv.at[10],
        device_id={"head": 1 - h}, device_id_type=MESH)
    swap_mixed.start()
    for t in range(width // 512):
        c = pl.ds(t * 512, 512)
        resid[:, c] = pair[h, :, c].astype(F32) + mixed(ours, c)
    for ring in (ring_u, ring_d, ring_c):
        ring.step(3)
    swap_mixed.wait_recv()

    @pl.loop(0, rows // 32)
    def _(i):
        part = pl.ds(pl.multiple_of(i * 32, 32), 32)
        x = resid[part, :] + from_other[part, :].astype(F32)
        resid[part, :] = x
        scaled = x * lax.rsqrt(jnp.mean(x * x, axis=1, keepdims=True) + EPS) * turned[pl.ds(experts + 1, 1), :]
        ext[part, pl.ds(0, width)] = scaled.astype(BF16)

    logits = dot_last(ext[:, pl.ds(0, width)], turned[...].astype(BF16))
    mask = lanes_ref[:, pl.ds(0, 128)]
    masked = jnp.where(mask > 0.5, logits, NEG)
    raised = jnp.where(mask > 0.5, jnp.exp(masked - jnp.max(masked, axis=1, keepdims=True)), 0.0)
    probs = raised / jnp.sum(raised, axis=1, keepdims=True)
    gates[...] = probs
    ext[:, pl.ds(width, 128)] = (probs + lanes_ref[:, pl.ds(128, 128)]).astype(BF16)
    for ring in (ring_u, ring_d, ring_c):
        ring.step(4)
    own[7].wait()
    for i in (7, 8, 9):
        swaps[i].wait_recv()
    for ring in (ring_u, ring_d, ring_c):
        ring.end()
    for ring in (ring_w, ring_o, ring_kv, ring_u, ring_d, ring_c):
        ring.flush()
    for copy in swaps:
        copy.wait_send()
    swap_mixed.wait_send()


def front_fused(
    tokens, cotangent, where, mask, w_query, w_key, w_value, small, w_out, shared_up, shared_down,
    expert_up, expert_down, blks, collective_id,
):
    chips, half = blks // 2, blks // 4
    rows, width = tokens.shape
    dense = w_query.shape[0]
    qw, kw, sw = w_query.shape[1] // 2, w_key.shape[1] // 2, shared_up.shape[1] // 4
    groups, repeats = kw // HD, qw // kw
    lanes = jnp.concatenate(
        [jnp.pad(mask, ((0, 0), (0, 128 - blks))), jnp.pad(mask, ((0, 0), (blks, 128 - 2 * blks)))], axis=1).astype(F32)
    dma = pltpu.SemaphoreType.DMA
    vmem = pl.BlockSpec(memory_space=pltpu.VMEM)
    anywhere = pl.BlockSpec(memory_space=pl.ANY)
    smem = pl.BlockSpec(memory_space=pltpu.SMEM)
    out = [
        ((2 * rows, width), BF16, vmem), ((2 * rows, qw), BF16, vmem), ((2 * blks, rows, 2 * kw), BF16, vmem),
        ((2, blks, dense, qw + 2 * kw + small.shape[1]), BF16, vmem), ((blks, w_out.shape[0], width), BF16, vmem),
        ((2, blks, dense, 2 * sw), BF16, anywhere), ((blks, shared_down.shape[0], width), BF16, anywhere),
        ((blks, rows, width), BF16, anywhere), ((2, rows, width), BF16, anywhere),
        (expert_up.shape, BF16, anywhere), (expert_down.shape, BF16, anywhere),
        ((2 * rows, qw), BF16, vmem), ((2 * rows, qw), F32, vmem), ((groups, 2, repeats * PIECE), F32, vmem),
        ((rows, width), F32, vmem), ((rows, width + 128), BF16, vmem), ((rows, 128), F32, vmem), ((128, width), F32, vmem),
    ]
    ring = [dma((12, half + 1))] * 4 + [dma((12, 2 * half + 1))] * 2
    (
        n1, query, kv, first_w, out_w, up_w, down_w, cot, cot_pair, expert_in, expert_out,
        low, full, lse, resid, ext, gates, turned,
    ) = pl.pallas_call(
        functools.partial(front_kernel, chips, blks),
        out_shape=[jax.ShapeDtypeStruct(s, t) for s, t, _ in out],
        in_specs=[smem] * 3 + [vmem, anywhere, vmem] + [anywhere] * 5 + [vmem] * 2 + [anywhere] * 2,
        out_specs=[space for _, _, space in out],
        scratch_shapes=[pltpu.VMEM((2, rows, width), BF16), pltpu.VMEM((rows, width), BF16), pltpu.VMEM((rows, width), BF16)]
        + ring + [dma((11,)), dma((11,)), dma((11,))],
        compiler_params=pltpu.CompilerParams(
            collective_id=collective_id, has_side_effects=True, vmem_limit_bytes=56 << 20),
    )(*where, lanes, tokens, cotangent, w_query, w_key, w_value, small, w_out, shared_up, shared_down, expert_up, expert_down)
    return (
        n1, query, kv, first_w.reshape(width, -1)[:, : qw + 2 * kw], out_w.reshape(-1, width),
        up_w.reshape(width, -1), down_w.reshape(-1, width), cot, cot_pair.reshape(2 * rows, width),
        expert_in, expert_out, low, full, lse, resid, ext, gates[:, :blks],
        turned[:blks].astype(BF16), turned[blks], turned[blks + 1])


def experts_plain(own_ext, weights, cot_all, blks, capacity, collective_id):
    h, b = lax.axis_index("head"), lax.axis_index("blk")
    own_up, other_up, own_down, other_down = weights
    expert_in = pair(own_up, other_up).reshape(2 * own_up.shape[0], -1)
    expert_out = jnp.where(
        h == 0,
        jnp.concatenate([own_down, other_down], axis=1),
        jnp.concatenate([other_down, own_down], axis=1),
    )
    normed = own_ext[:, : expert_in.shape[0]]
    normed_pair = pair(normed, swap(normed))
    experts, width = blks, expert_in.shape[0]
    rows = own_ext.shape[0]
    ext = all_gather_blk([own_ext], blks, collective_id)[0]
    norm_all = ext[:, :, :width]
    gate_here = lax.dynamic_index_in_dim(ext, width + b, 2, keepdims=False).astype(F32)
    mask_here = lax.dynamic_index_in_dim(ext, width + experts + b, 2, keepdims=False).astype(F32)
    rank = jnp.cumsum(mask_here, axis=1) - mask_here
    slots = jnp.arange(capacity, dtype=F32)
    deal = ((rank[:, None, :] == slots[None, :, None]) & (mask_here[:, None, :] > 0)).astype(BF16)
    deal_gate = deal * gate_here[:, None, :].astype(BF16)

    def to_slots(dealer, array):
        moved = jnp.einsum("bst,btd->bsd", dealer, array, preferred_element_type=F32)
        return moved.astype(BF16).reshape(blks * capacity, width)

    def to_rows(dealer, array):
        return jnp.einsum(
            "bst,bsd->btd", dealer, array.reshape(blks, capacity, width), preferred_element_type=F32)

    expert_rows = to_slots(deal, norm_all)
    both = dot(expert_rows, expert_in)
    ew = expert_out.shape[0]
    gate_part, up_part = both[:, :ew], both[:, ew:]
    activated = (jax.nn.silu(gate_part) * up_part).astype(BF16)
    result = dot(activated, expert_out).astype(BF16)
    result_rows = to_rows(deal, result)
    gate_grad = jnp.sum(result_rows * cot_all.astype(F32), axis=2, keepdims=True)
    routed = (result_rows * gate_here[:, :, None]).astype(BF16)
    slot_grad = to_slots(deal_gate, cot_all)
    act_grad = dot_last(slot_grad, expert_out)
    both_grad = gated_grad(act_grad, gate_part, up_part)
    rows_back = to_rows(deal, dot_last(both_grad, expert_in).astype(BF16)).astype(BF16)
    lane = jnp.arange(128 * (-(-2 * experts // 128)), dtype=jnp.int32)
    grad_high = gate_grad.astype(BF16)
    grad_low = (gate_grad - grad_high.astype(F32)).astype(BF16)
    grad_lanes = jnp.where(lane == b, grad_high, jnp.where(lane == b + experts, grad_low, jnp.zeros((), BF16)))
    dwn = dot_first(activated, slot_grad).astype(BF16)
    dup = dot_first(expert_rows, both_grad).astype(BF16)
    home = reduce_scatter_blk([jnp.concatenate([rows_back, grad_lanes], axis=2)], blks, collective_id + 1, [F32])[0]
    routed_sum = reduce_scatter_blk([routed], blks, collective_id + 2, [F32])[0]
    return home, routed_sum, dup, dwn, normed_pair


def pair(own, other):
    return jnp.where(lax.axis_index("head") == 0, jnp.stack([own, other]), jnp.stack([other, own]))


def half(w, i, parts=1):
    size = w.shape[1] // (2 * parts)
    cut = lax.dynamic_slice_in_dim(w.reshape(w.shape[0], parts, 2 * size), i * size, size, 2)
    return cut.reshape(w.shape[0], parts * size)


def pick(stacked, i):
    return lax.dynamic_index_in_dim(stacked, i, 0, keepdims=False)


def front_plain(
    tokens, cotangent, where, mask, w_query, w_key, w_value, small, w_out, shared_up, shared_down,
    expert_up, expert_down, blks, collective_id,
):
    h = lax.axis_index("head")
    rows, width = tokens.shape
    experts = blks

    def columns(i):
        return jnp.concatenate([half(w_query, i), half(w_key, i), half(w_value, i)], axis=1)

    first = pair(
        jnp.concatenate([columns(h), small], axis=1),
        swap(jnp.concatenate([columns(1 - h), small], axis=1)),
    )
    tokens_pair = pair(tokens, swap(tokens))
    cotangent_pair = pair(cotangent, swap(cotangent)).reshape(2 * rows, width)
    up_pair = pair(half(shared_up, h, 2), swap(half(shared_up, 1 - h, 2)))
    other_up, other_down = swap(expert_up), swap(expert_down)
    gathered = all_gather_blk([first], blks, collective_id)[0].reshape(width, -1)
    qw = w_query.shape[1] // 2
    kw = w_key.shape[1] // 2
    full_qkv = gathered[:, : qw + 2 * kw]
    full_router = gathered[:, qw + 2 * kw : qw + 2 * kw + experts]
    gain_first = gathered[:, qw + 2 * kw + experts].astype(F32)
    gain_second = gathered[:, qw + 2 * kw + experts + 1].astype(F32)

    inputs_pair = tokens_pair.reshape(2 * rows, width).astype(F32)
    normed_one = (inputs_pair * inv_scale(inputs_pair) * gain_first).astype(BF16)
    qkv = dot(normed_one, full_qkv).astype(BF16)
    query = qkv[:, :qw]
    kv = all_gather_blk([qkv[:, qw:]], blks, collective_id + 1)[0].reshape(-1, PIECE, 2 * kw)

    attended, attended_full, lse = attention_forward(query, kv, where)

    up_all, out_all, down_all, cot_all = all_gather_blk([up_pair, w_out, shared_down, cotangent], blks, collective_id + 2)
    full_up = up_all.reshape(width, -1)
    full_out = out_all.reshape(-1, width)
    full_down = down_all.reshape(-1, width)

    mixed = dot(attended, full_out).reshape(2, rows, width)
    inputs = tokens.astype(F32)
    resid = inputs + (pick(mixed, h) + swap(pick(mixed, 1 - h).astype(BF16)).astype(F32))
    scaler_two = inv_scale(resid)
    normed_two = (resid * scaler_two * gain_second).astype(BF16)

    logits = dot(normed_two, full_router)
    masked = jnp.where(mask, logits, NEG)
    raised = jnp.where(mask, jnp.exp(masked - jnp.max(masked, axis=1, keepdims=True)), 0.0)
    gates = raised / jnp.sum(raised, axis=1, keepdims=True)
    extra = jnp.concatenate(
        [gates.astype(BF16), mask.astype(BF16), jnp.zeros((rows, -2 * experts % 128), BF16)], axis=1)
    ext = jnp.concatenate([normed_two, extra], axis=1)
    return (
        normed_one, query, kv, full_qkv, full_out, full_up, full_down, cot_all, cotangent_pair, other_up, other_down,
        attended, attended_full, lse, resid, ext, gates, full_router.T, gain_first, gain_second)


def shards(
    tokens, cotangent, seq_lengths, piece_order, routes, norm1_gain, w_query, w_key, w_value, w_out,
    norm2_gain, w_router, shared_up, shared_down, expert_up, expert_down,
):
    blks = lax.axis_size("blk")
    h, b = lax.axis_index("head"), lax.axis_index("blk")
    rows, width = tokens.shape
    experts = blks
    capacity = rows * TOP * 4 // (3 * blks)
    dense_rows = w_query.shape[0]

    small = jnp.concatenate(
        [w_router, norm1_gain[:, None], norm2_gain[:, None],
         jnp.zeros((dense_rows, -(experts + 2) % 128), BF16)], axis=1)
    lanes = small.shape[1]
    places = jnp.swapaxes(piece_order.reshape(2, blks), 0, 1).reshape(-1)
    order = jnp.arange(2 * blks, dtype=jnp.int32)
    slots = jnp.sum(jnp.where(places[None, :] == order[:, None], order[None, :], 0), axis=1)
    where = (slots, lax.dynamic_slice_in_dim(places, 2 * b, 2), jnp.cumsum(seq_lengths))
    hot = routes[:, :, None] == jnp.arange(experts, dtype=jnp.int32)[None, None, :]
    mask = jnp.any(hot, axis=1)
    fits = blks == 16 and rows == 128 and 2 * capacity == 128 and width % 768 == 0 and dense_rows == 48
    front = front_fused if fits else front_plain
    (
        normed_one, query, kv, full_qkv, full_out, full_up, full_down, cot_all, cotangent_pair, other_up, other_down,
        attended, attended_full, lse, resid, ext, gates, router_rows, gain_first, gain_second,
    ) = front(
        tokens, cotangent, where, mask, w_query, w_key, w_value, small, w_out, shared_up, shared_down,
        expert_up[0], expert_down[0], blks, 0)
    qw, kw = w_query.shape[1] // 2, w_key.shape[1] // 2
    shared_width = full_down.shape[0]
    inputs = tokens.astype(F32)
    scaler_two = inv_scale(resid)
    normed_two = ext[:, :width]

    experts_run = experts_fused if fits else experts_plain
    home, routed_sum, dup, dwn, normed_pair = experts_run(
        ext, (expert_up[0], other_up, expert_down[0], other_down), cot_all, blks, capacity, 3)
    normed_pair = normed_pair.reshape(2 * rows, width)
    shared_both = dot(normed_pair, full_up)
    shared_gate, shared_lift = shared_both[:, :shared_width], shared_both[:, shared_width:]
    shared_act = (jax.nn.silu(shared_gate) * shared_lift).astype(BF16)
    shared_sum = dot(shared_act, full_down).reshape(2, rows, width)
    shared_down_part = dot_first(shared_act, cotangent_pair)
    shared_grad = gated_grad(dot_last(cotangent_pair, full_down), shared_gate, shared_lift)
    shared_up_part = dot_first(normed_pair, shared_grad)
    shared_back = dot_last(shared_grad, full_up).reshape(2, rows, width)
    output = (
        resid + routed_sum + pick(shared_sum, h) + swap(pick(shared_sum, 1 - h).astype(BF16)).astype(F32)
    ).astype(BF16)

    dgate = home[:, width : width + experts] + home[:, width + experts : width + 2 * experts]
    weighted = gates * dgate
    logit_grad = (weighted - gates * jnp.sum(weighted, axis=1, keepdims=True)).astype(BF16)
    router_part = dot_first(normed_two, logit_grad)
    norm_two_grad = (
        home[:, :width] + dot(logit_grad, router_rows)
        + pick(shared_back, h) + swap(pick(shared_back, 1 - h).astype(BF16)).astype(F32)
    )
    back, gain_two_part = norm_back(resid, scaler_two, gain_second, norm_two_grad)
    hidden_grad = cotangent.astype(F32) + back
    hidden_low = hidden_grad.astype(BF16)
    hidden_pair = pair(hidden_low, swap(hidden_low)).reshape(2 * rows, width)
    out_part = dot_first(attended, hidden_pair)
    mixed_grad = dot_last(hidden_pair, full_out).astype(BF16)
    query_grad, *kv_parts = attention_backward(query, kv, attended_full, lse, mixed_grad, where)
    dup, dwn, query_grad = lax.optimization_barrier((dup, dwn, query_grad))
    dup = dup.reshape(2, width // 2, -1)
    dwn = jnp.stack([dwn[:, : width // 2], dwn[:, width // 2 :]])
    expert_up_grad = pick(dup, h).astype(F32) + swap(pick(dup, 1 - h)).astype(F32)
    expert_down_grad = pick(dwn, h).astype(F32) + swap(pick(dwn, 1 - h)).astype(F32)
    kv_grads = reduce_scatter_blk([part.reshape(blks, 2 * rows, kw) for part in kv_parts], blks, 6, [BF16] * 2)
    qkv_grad = jnp.concatenate([query_grad, *kv_grads], axis=1)
    norm_one_part = dot_last(qkv_grad, full_qkv).reshape(2, rows, width)
    norm_one_grad = pick(norm_one_part, h) + swap(pick(norm_one_part, 1 - h).astype(BF16)).astype(F32)
    extra_grad, gain_one_part = norm_back(inputs, inv_scale(inputs), gain_first, norm_one_grad)
    input_grad = hidden_grad + extra_grad
    qkv_part = dot_first(normed_one, qkv_grad)
    small_part = jnp.concatenate(
        [router_part, gain_one_part[:, None], gain_two_part[:, None],
         jnp.zeros((width, lanes - experts - 2), F32)], axis=1)

    def by_rows(part):
        return part.astype(BF16).reshape(2, blks, dense_rows, -1)

    qkv_sum, up_sum, out_sum, down_sum, small_sum = reduce_scatter_blk(
        [by_rows(qkv_part), by_rows(shared_up_part),
         out_part.astype(BF16).reshape(blks, dense_rows, width),
         shared_down_part.astype(BF16).reshape(blks, -1, width), by_rows(small_part)],
        blks, 7, [BF16, BF16, F32, F32, F32])
    there = swap(jnp.concatenate([pick(qkv_sum, 1 - h), pick(up_sum, 1 - h)], axis=1)).astype(F32)
    here = jnp.concatenate([pick(qkv_sum, h), pick(up_sum, h)], axis=1).astype(F32)
    small_sum = pick(small_sum, h) + swap(pick(small_sum, 1 - h))

    def whole(start, size):
        return jnp.where(
            h == 0,
            jnp.concatenate([here[:, start : start + size], there[:, start : start + size]], axis=1),
            jnp.concatenate([there[:, start : start + size], here[:, start : start + size]], axis=1))

    top = qw + 2 * kw
    sw = shared_width
    up_grad = jnp.concatenate([whole(top, sw), whole(top + sw, sw)], axis=1)
    return (
        output, input_grad, small_sum[:, experts], whole(0, qw), whole(qw, kw), whole(qw + kw, kw),
        out_sum, small_sum[:, experts + 1], small_sum[:, :experts], up_grad, down_sum,
        expert_up_grad[None], expert_down_grad[None],
    )


def solution(mesh):
    both = P(("head", "blk"), None)
    flat = P(("head", "blk"))
    up, down = P("blk", "head", None), P("blk", None, "head")
    return jax.shard_map(
        shards,
        mesh=mesh,
        in_specs=(both, both, P(), P(), both, flat, both, both, both, both, flat, both, both, both, up, down),
        out_specs=(both, both, flat, both, both, both, both, flat, both, both, both, up, down),
        check_vma=False,
    )
```

```python
import functools

import jax
import jax.numpy as jnp
from jax import lax
from jax.experimental import pallas as pl
from jax.experimental.pallas import tpu as pltpu
from jax.sharding import PartitionSpec as P

MESH = pl.DeviceIdType.MESH


def ring_place(chip, chips):
    odd = chip % 2
    return (chip // 2) * (1 - odd) + (chips - 1 - chip // 2) * odd


def ring_chip(place, chips):
    high = place // (chips // 2)
    return 2 * place * (1 - high) + (2 * (chips - 1 - place) + 1) * high


def ring_info(chips):
    blk = lax.axis_index("blk")
    chip, core = blk // 2, blk % 2
    place = ring_place(chip, chips)

    def at(step):
        return ring_chip((place + step + chips) % chips, chips) * 2 + core

    return blk, core, at, blk + 1 - 2 * core


def pieces_of(shape):
    if len(shape) == 3:
        return [(0, None), (1, None)]
    rows = shape[0]
    if rows >= 32 and rows % 16 == 0:
        cut = (rows // 2 + 15) // 16 * 16
        return [(0, cut), (cut, rows - cut)]
    return [(0, rows)]


def part_in(ref, piece):
    start, size = piece
    return ref.at[start] if size is None else ref.at[pl.ds(start, size)]


def part_out(ref, piece, b):
    start, size = piece
    return ref.at[start, b] if size is None else ref.at[b, pl.ds(start, size)]


def ag_kernel(count, chips, plans, *refs):
    ins, outs = refs[:count], refs[count : 2 * count]
    right_sem, left_sem, sib_sem, sright, sleft, ssib, own_sem = refs[2 * count :]
    blk, core, at, sib = ring_info(chips)
    right, left = at(1), at(-1)
    barrier = pltpu.get_barrier_semaphore()
    for other in (right, left, sib):
        pl.semaphore_signal(barrier, inc=1, device_id={"blk": other}, device_id_type=MESH)
    pl.semaphore_wait(barrier, 3)
    half = chips // 2
    started = []

    def send(src, dst, ssem, rsem, dev):
        copy = pltpu.make_async_remote_copy(
            src_ref=src, dst_ref=dst, send_sem=ssem, recv_sem=rsem,
            device_id={"blk": dev}, device_id_type=MESH)
        copy.start()
        started.append(copy)
        return copy

    chunks = []
    for k in range(count):
        for i, piece in enumerate(plans[k]):
            chunks.append((len(chunks), k, piece, half - (i % 2), half - 1 + (i % 2)))
    copies = {}
    locals_ = []
    for c, k, piece, rh, lh in chunks:
        src = part_in(ins[k], piece)
        dst = part_out(outs[k], piece, blk)
        if rh >= 1:
            copies[c, "r", 1] = send(src, dst, sright.at[c, 0], right_sem.at[c, 0], right)
        if lh >= 1:
            copies[c, "l", 1] = send(src, dst, sleft.at[c, 0], left_sem.at[c, 0], left)
        copies[c, "s", 0] = send(src, dst, ssib.at[c, 0], sib_sem.at[c, 0], sib)
        own = pltpu.make_async_copy(src, dst, own_sem.at[c])
        own.start()
        locals_.append(own)
    for s in range(1, half + 1):
        for c, k, piece, rh, lh in chunks:
            if s <= rh:
                copies[c, "r", s].wait_recv()
                b = at(-s)
                blockref = part_out(outs[k], piece, b)
                if s < rh:
                    copies[c, "r", s + 1] = send(blockref, blockref, sright.at[c, s], right_sem.at[c, s], right)
                copies[c, "sr", s] = send(blockref, blockref, ssib.at[c, s], sib_sem.at[c, s], sib)
            if s <= lh:
                copies[c, "l", s].wait_recv()
                b = at(s)
                blockref = part_out(outs[k], piece, b)
                if s < lh:
                    copies[c, "l", s + 1] = send(blockref, blockref, sleft.at[c, s], left_sem.at[c, s], left)
                copies[c, "sl", s] = send(blockref, blockref, ssib.at[c, half + s], sib_sem.at[c, half + s], sib)
    for (c, d, s), copy in copies.items():
        if d in ("s", "sr", "sl"):
            copy.wait_recv()
    for copy in started:
        copy.wait_send()
    for copy in locals_:
        copy.wait()


def all_gather_blk(arrays, blks, collective_id, vmem=False):
    chips = blks // 2
    count = len(arrays)
    plans = [pieces_of(a.shape) for a in arrays]
    n = sum(len(p) for p in plans)
    half = chips // 2
    shapes = [
        jax.ShapeDtypeStruct((a.shape[0], blks) + a.shape[1:] if a.ndim == 3 else (blks,) + a.shape, a.dtype)
        for a in arrays
    ]
    dma = pltpu.SemaphoreType.DMA
    space = pltpu.VMEM if vmem else pl.ANY
    return pl.pallas_call(
        functools.partial(ag_kernel, count, chips, plans),
        out_shape=shapes,
        in_specs=[pl.BlockSpec(memory_space=space)] * count,
        out_specs=[pl.BlockSpec(memory_space=space)] * count,
        scratch_shapes=[
            dma((n, half)), dma((n, half)), dma((n, 2 * half + 1)),
            dma((n, half)), dma((n, half)), dma((n, 2 * half + 1)), dma((n,)),
        ],
        compiler_params=pltpu.CompilerParams(collective_id=collective_id, has_side_effects=True,
            vmem_limit_bytes=(60 << 20) if vmem else None),
    )(*arrays)


def rs_kernel(count, chips, plans, *refs):
    xs, outs = refs[:count], refs[count : 2 * count]
    rest = refs[2 * count :]
    n = sum(len(p) for p in plans)
    ys, rs, ls = rest[:n], rest[n : 2 * n], rest[2 * n : 3 * n]
    right_sem, left_sem, sib_sem, sright, sleft, ssib = rest[3 * n :]
    blk, core, at, sib = ring_info(chips)
    right, left = at(1), at(-1)
    barrier = pltpu.get_barrier_semaphore()
    for other in (right, left, sib):
        pl.semaphore_signal(barrier, inc=1, device_id={"blk": other}, device_id_type=MESH)
    pl.semaphore_wait(barrier, 3)
    half = chips // 2
    started = []

    def send(src, dst, ssem, rsem, dev):
        copy = pltpu.make_async_remote_copy(
            src_ref=src, dst_ref=dst, send_sem=ssem, recv_sem=rsem,
            device_id={"blk": dev}, device_id_type=MESH)
        copy.start()
        started.append(copy)
        return copy

    chunks = []
    for k in range(count):
        for i, piece in enumerate(plans[k]):
            chunks.append((len(chunks), k, piece, half - (i % 2), half - 1 + (i % 2)))
    order = []
    for d in range(half, 0, -1):
        order += [d, -d] if d < half else [d]
    order.append(0)
    sibs = {}
    for j, d in enumerate(order):
        there = at(d) + 1 - 2 * core
        for c, k, piece, rh, lh in chunks:
            sibs[c, d] = send(part_out(xs[k], piece, there), ys[c].at[j], ssib.at[c, j], sib_sem.at[c, j], sib)
    ready = set()

    def blocks(rows, body):
        step = 16 if rows % 16 == 0 else rows

        @pl.loop(0, rows // step)
        def _(i):
            body(pl.ds(pl.multiple_of(i * step, step), step))

    def mine(c, k, piece, d):
        j = order.index(d)
        if (c, d) not in ready:
            sibs[c, d].wait_recv()
            ready.add((c, d))
        return j

    copies = {}

    def join(c, k, piece, d, into, recv):
        j = mine(c, k, piece, d)
        x = part_out(xs[k], piece, at(d))
        rows = x.shape[0]

        def body(w):
            total = x[w].astype(jnp.float32) + ys[c][j, w].astype(jnp.float32)
            if recv is not None:
                total = total + recv[w].astype(jnp.float32)
            into[w] = total.astype(into.dtype)

        blocks(rows, body)

    for s in range(1, half + 1):
        for c, k, piece, rh, lh in chunks:
            for way, hops, buf, sem, ssem, dev in (
                (1, rh, rs[c], right_sem, sright, right),
                (-1, lh, ls[c], left_sem, sleft, left),
            ):
                if s > hops:
                    continue
                if s == 1:
                    j = order.index(way * hops if way * hops in order else hops)
                    join(c, k, piece, order[j], ys[c].at[j], None)
                    src = ys[c].at[j]
                else:
                    copies[c, way, s - 1].wait_recv()
                    d = way * (hops - s + 1)
                    src = buf.at[s - 2]
                    join(c, k, piece, d, src, src)
                copies[c, way, s] = send(src, buf.at[s - 1], ssem.at[c, s - 1], sem.at[c, s - 1], dev)
    for c, k, piece, rh, lh in chunks:
        if rh >= 1:
            copies[c, 1, rh].wait_recv()
        if lh >= 1:
            copies[c, -1, lh].wait_recv()
        j = mine(c, k, piece, 0)
        x = part_out(xs[k], piece, blk)
        target = part_in(outs[k], piece)

        def body(w, x=x, c=c, j=j, rh=rh, lh=lh, target=target):
            total = x[w].astype(jnp.float32) + ys[c][j, w].astype(jnp.float32)
            if rh >= 1:
                total = total + rs[c][rh - 1, w].astype(jnp.float32)
            if lh >= 1:
                total = total + ls[c][lh - 1, w].astype(jnp.float32)
            target[w] = total.astype(target.dtype)

        blocks(x.shape[0], body)
    for copy in started:
        copy.wait_send()


def reduce_scatter_blk(arrays, blks, collective_id, out_dtypes):
    chips = blks // 2
    half = chips // 2
    count = len(arrays)
    shapes = [a.shape[1:] if a.ndim == 3 else (2,) + a.shape[2:] for a in arrays]
    plans = [pieces_of(s) for s in shapes]
    dma = pltpu.SemaphoreType.DMA
    ys, rs = [], []
    for s, plan in zip(shapes, plans):
        for start, size in plan:
            rows = s[1] if size is None else size
            ys.append(pltpu.VMEM((chips, rows, s[-1]), jnp.bfloat16))
            rs.append(pltpu.VMEM((half, rows, s[-1]), jnp.bfloat16))
    n = len(ys)
    return pl.pallas_call(
        functools.partial(rs_kernel, count, chips, plans),
        out_shape=[jax.ShapeDtypeStruct(s, t) for s, t in zip(shapes, out_dtypes)],
        in_specs=[pl.BlockSpec(memory_space=pltpu.VMEM)] * count,
        out_specs=[pl.BlockSpec(memory_space=pltpu.VMEM)] * count,
        scratch_shapes=ys + rs + rs + [
            dma((n, half)), dma((n, half)), dma((n, chips)),
            dma((n, half)), dma((n, half)), dma((n, chips)),
        ],
        compiler_params=pltpu.CompilerParams(collective_id=collective_id, has_side_effects=True,
            vmem_limit_bytes=60 << 20),
    )(*arrays)


H = 12
KVH = 4
HD = 128
TOP = 6
PIECE = 128
EPS = 1e-05
NEG = -1e30
F32 = jnp.float32
BF16 = jnp.bfloat16


def dot(a, b):
    return jnp.dot(a, b, preferred_element_type=F32)


def dot_first(a, b):
    return lax.dot_general(a, b, (((0,), (0,)), ((), ())), preferred_element_type=F32)


def dot_last(a, b):
    return lax.dot_general(a, b, (((1,), (1,)), ((), ())), preferred_element_type=F32)


def inv_scale(values):
    return lax.rsqrt(jnp.mean(values * values, axis=1, keepdims=True) + EPS)


def norm_back(values, scaler, gain, upstream):
    normed = values * scaler
    gain_grad = jnp.sum(upstream * normed, axis=0)
    scaled = upstream * gain
    grad = scaler * (scaled - normed * jnp.mean(scaled * normed, axis=1, keepdims=True))
    return grad, gain_grad


def gated_grad(act_grad, gate, lift):
    sig = jax.nn.sigmoid(gate)
    return jnp.concatenate(
        [act_grad * lift * sig * (1.0 + gate * (1.0 - sig)), act_grad * gate * sig], axis=1
    ).astype(BF16)


def swap(array):
    return lax.ppermute(array, "head", [(0, 1), (1, 0)])


def key_span(places_ref, ends_ref, i):
    place = places_ref[i]
    start = jnp.int32(0)
    for e in range(ends_ref.shape[0]):
        start = jnp.where(ends_ref[e] <= place * PIECE, ends_ref[e], start)
    return start // PIECE, place


def key_chunk(slots_ref, first, pieces, *refs):
    last = slots_ref.shape[0] - 1
    slots = [slots_ref[jnp.clip(first + k, 0, last)] for k in range(pieces)]
    return slots, [jnp.concatenate([ref[s] for s in slots], axis=0) for ref in refs]


def stacked(ref, i, repeats):
    return jnp.concatenate(
        [ref[pl.ds(i * PIECE, PIECE), pl.ds(r * HD, HD)] for r in range(repeats)], axis=0)


def seen(ends_ref, place, first, keys, cols):
    own = place * PIECE + lax.broadcasted_iota(jnp.int32, (1, cols), 1) % PIECE
    start = jnp.zeros((1, cols), jnp.int32)
    for e in range(ends_ref.shape[0]):
        start = jnp.where(ends_ref[e] <= own, ends_ref[e], start)
    there = first * PIECE + lax.broadcasted_iota(jnp.int32, (keys, 1), 0)
    return (there <= own) & (there >= start)


CHUNK = 4


def forward_kernel(repeats, slots_ref, places_ref, ends_ref, q_ref, k_ref, v_ref, low_ref, full_ref, lse_ref):
    cols = repeats * PIECE
    for i in range(q_ref.shape[0] // PIECE):
        lo, place = key_span(places_ref, ends_ref, i)
        q = stacked(q_ref, i, repeats)

        def step(n, carry, lo=lo, place=place, q=q):
            top, total, acc = carry
            first = lo + n * CHUNK
            _, (k, v) = key_chunk(slots_ref, first, CHUNK, k_ref, v_ref)
            scores = dot_last(k, q) * HD**-0.5
            scores = jnp.where(seen(ends_ref, place, first, CHUNK * PIECE, cols), scores, NEG)
            new = jnp.maximum(top, jnp.max(scores, axis=0, keepdims=True))
            weights = jnp.exp(scores - new)
            factor = jnp.exp(top - new)
            total = total * factor + jnp.sum(weights, axis=0, keepdims=True)
            return new, total, acc * factor + dot_first(v, weights.astype(BF16))

        top, total, acc = lax.fori_loop(
            0, (place - lo) // CHUNK + 1, step,
            (jnp.full((1, cols), NEG, F32), jnp.zeros((1, cols), F32), jnp.zeros((HD, cols), F32)))
        out = jnp.swapaxes(acc / total, 0, 1)
        lse_ref[0, pl.ds(i, 1), :] = top + jnp.log(total)
        for r in range(repeats):
            part = out[r * PIECE : (r + 1) * PIECE]
            full_ref[pl.ds(i * PIECE, PIECE), pl.ds(r * HD, HD)] = part
            low_ref[pl.ds(i * PIECE, PIECE), pl.ds(r * HD, HD)] = part.astype(BF16)


def attention_forward(query, kv, where):
    rows, pieces = query.shape[0], kv.shape[0]
    groups = kv.shape[2] // (2 * HD)
    wide = query.shape[1] // groups
    repeats = wide // HD
    spec = pl.BlockSpec((rows, wide), lambda g, *_: (0, g))
    return pl.pallas_call(
        functools.partial(forward_kernel, repeats),
        grid_spec=pltpu.PrefetchScalarGridSpec(
            num_scalar_prefetch=3,
            grid=(groups,),
            in_specs=[
                spec,
                pl.BlockSpec((pieces, PIECE, HD), lambda g, *_: (0, 0, g)),
                pl.BlockSpec((pieces, PIECE, HD), lambda g, *_: (0, 0, groups + g)),
            ],
            out_specs=[spec, spec, pl.BlockSpec((1, rows // PIECE, repeats * PIECE), lambda g, *_: (g, 0, 0))],
        ),
        out_shape=[
            jax.ShapeDtypeStruct(query.shape, BF16),
            jax.ShapeDtypeStruct(query.shape, F32),
            jax.ShapeDtypeStruct((groups, rows // PIECE, repeats * PIECE), F32),
        ],
        compiler_params=pltpu.CompilerParams(vmem_limit_bytes=48 << 20),
    )(*where, query, kv, kv)


def backward_kernel(
    repeats, slots_ref, places_ref, ends_ref, q_ref, k_ref, v_ref, full_ref, grad_ref, lse_ref,
    dq_ref, dk_ref, dv_ref, key_acc, value_acc,
):
    cols = repeats * PIECE
    key_acc[...] = jnp.zeros_like(key_acc)
    value_acc[...] = jnp.zeros_like(value_acc)
    for i in range(q_ref.shape[0] // PIECE):
        lo, place = key_span(places_ref, ends_ref, i)
        q, grad = stacked(q_ref, i, repeats), stacked(grad_ref, i, repeats)
        product = grad.astype(F32) * stacked(full_ref, i, repeats)
        delta = jnp.sum(jnp.swapaxes(product, 0, 1), axis=0, keepdims=True)
        lse = lse_ref[0, pl.ds(i, 1), :]

        def step(n, dq, lo=lo, place=place, q=q, grad=grad, delta=delta, lse=lse):
            first = lo + n * CHUNK
            slots, (k, v) = key_chunk(slots_ref, first, CHUNK, k_ref, v_ref)
            scores = dot_last(k, q) * HD**-0.5
            weights = jnp.where(
                seen(ends_ref, place, first, CHUNK * PIECE, cols), jnp.exp(scores - lse), 0.0)
            back = (weights * (dot_last(v, grad) - delta)).astype(BF16)
            dk = dot(back, q)
            dv = dot(weights.astype(BF16), grad)
            for j, s in enumerate(slots):
                key_acc[s] += dk[j * PIECE : (j + 1) * PIECE]
                value_acc[s] += dv[j * PIECE : (j + 1) * PIECE]
            return dq + dot_first(k, back)

        dq = lax.fori_loop(0, (place - lo) // CHUNK + 1, step, jnp.zeros((HD, cols), F32))
        out = (jnp.swapaxes(dq, 0, 1) * HD**-0.5).astype(BF16)
        for r in range(repeats):
            dq_ref[pl.ds(i * PIECE, PIECE), pl.ds(r * HD, HD)] = out[r * PIECE : (r + 1) * PIECE]
    dk_ref[...] = (key_acc[...] * HD**-0.5).astype(BF16)
    dv_ref[...] = value_acc[...].astype(BF16)


def attention_backward(query, kv, full, lse, grad, where):
    rows, pieces = query.shape[0], kv.shape[0]
    groups = kv.shape[2] // (2 * HD)
    wide = query.shape[1] // groups
    repeats = wide // HD
    spec = pl.BlockSpec((rows, wide), lambda g, *_: (0, g))
    block = pl.BlockSpec((pieces, PIECE, HD), lambda g, *_: (0, 0, g))
    half = jax.ShapeDtypeStruct((pieces, PIECE, groups * HD), BF16)
    return pl.pallas_call(
        functools.partial(backward_kernel, repeats),
        grid_spec=pltpu.PrefetchScalarGridSpec(
            num_scalar_prefetch=3,
            grid=(groups,),
            in_specs=[
                spec, block, pl.BlockSpec((pieces, PIECE, HD), lambda g, *_: (0, 0, groups + g)), spec, spec,
                pl.BlockSpec((1, rows // PIECE, repeats * PIECE), lambda g, *_: (g, 0, 0)),
            ],
            out_specs=[spec, block, block],
            scratch_shapes=[pltpu.VMEM((pieces, PIECE, HD), F32)] * 2,
        ),
        out_shape=[jax.ShapeDtypeStruct(query.shape, BF16), half, half],
        compiler_params=pltpu.CompilerParams(vmem_limit_bytes=60 << 20),
    )(*where, query, kv, kv, full, grad, lse)


def tiles(total, size, body):
    if total == size:
        body(pl.ds(0, size))
    else:

        @pl.loop(0, total // size)
        def _(i):
            body(pl.ds(pl.multiple_of(i * size, size), size))


def shifted(c, by):
    if isinstance(c.start, int):
        return pl.ds(c.start + by, c.size)
    return pl.ds(pl.multiple_of(c.start + by, c.size), c.size)


def expert_kernel(
    chips, experts, ext_ref, up_own, up_other, down_own, down_other, cot_ref,
    shared_up, shared_down, cot_pair, cot_own, resid, gates, turned, low, full_out,
    output, hidden_grad, mixed_grad, out_part, up_part, down_part, din, dout, row_part, norm_pair,
    home_ref, routed_ref, din_ref, dout_ref, shared_act, shared_dab, hid, from_back, from_sum,
    in_ref, out_ref, ext, cot, rows_x, rows_dy, rows_act, rows_dab, both, result, back, deal, gate,
    own_d, own_o, stage_d, stage_o, sib_d, sib_o, right_d, right_o, left_d, left_o,
    copy_sem, cot_sem, ag_r, ag_l, ag_sr, ag_sl, ss_r, ss_l, ss_sr, ss_sl,
    ex_sem, ss_ex, rs_r, rs_l, ss_rr, ss_rl, weight_sem, pair_sem, load_sem, y_send, y_recv,
):
    blk, core, at, sib = ring_info(chips)
    h = lax.axis_index("head")
    right, left = at(1), at(-1)
    half = chips // 2
    rows, wide = ext_ref.shape
    width = in_ref.shape[0]
    hidden = out_ref.shape[0]
    slots = rows_x.shape[0] // chips
    cut = rows // 2
    upper, lower = pl.ds(0, cut), pl.ds(cut, cut)

    barrier = pltpu.get_barrier_semaphore()
    for other in (right, left, sib):
        pl.semaphore_signal(barrier, inc=1, device_id={"blk": other}, device_id_type=MESH)
    pl.semaphore_signal(barrier, inc=1, device_id={"head": 1 - h}, device_id_type=MESH)
    pl.semaphore_wait(barrier, 4)

    def remote(src, dst, ssem, rsem, dev):
        return pltpu.make_async_remote_copy(
            src_ref=src, dst_ref=dst, send_sem=ssem, recv_sem=rsem,
            device_id={"blk": dev}, device_id_type=MESH)

    def hop_right(part, k, s):
        ref = ext.at[at(1 - s), part]
        return remote(ref, ref, ss_r.at[k, s], ag_r.at[k, s], right)

    def hop_left(part, k, s):
        ref = ext.at[at(s - 1), part]
        return remote(ref, ref, ss_l.at[k, s], ag_l.at[k, s], left)

    def over_right(part, k, s):
        ref = ext.at[at(-s), part]
        return remote(ref, ref, ss_sr.at[k, s], ag_sr.at[k, s], sib)

    def over_left(part, k, s):
        ref = ext.at[at(s), part]
        return remote(ref, ref, ss_sl.at[k, s], ag_sl.at[k, s], sib)

    def cot_copy(g, j):
        there = at(-g) if j == 0 else at(g + 1)
        slot = lax.rem(g, 2)
        return pltpu.make_async_copy(
            cot_ref.at[pl.ds(there - core, 2)], cot.at[slot, j], cot_sem.at[slot, j])

    def place_of(g, j):
        return at(-g) if j == 0 else at(g + 1)

    def exchange_d(g, j):
        return remote(stage_d.at[j], sib_d.at[lax.div(place_of(g, j), 2)], ss_ex.at[0, j, g], ex_sem.at[0, j, g], sib)

    def exchange_o(g, j):
        return remote(stage_o.at[j], sib_o.at[lax.div(place_of(g, j), 2)], ss_ex.at[1, j, g], ex_sem.at[1, j, g], sib)

    mine = pltpu.make_async_copy(ext_ref, ext.at[blk], copy_sem)
    mine.start()
    cot_copy(0, 0).start()
    cot_copy(0, 1).start()
    weights = []
    for i, (up, down) in ((h, (up_own, down_own)), (1 - h, (up_other, down_other))):
        size = up.shape[0]
        start = pl.multiple_of(i * size, size)
        weights.append((up, in_ref.at[pl.ds(start, size)]))
        weights.append((down, out_ref.at[:, pl.ds(start, size)]))
    weights = [pltpu.make_async_copy(a, b, weight_sem.at[i]) for i, (a, b) in enumerate(weights)]
    for copy in weights:
        copy.start()
    mine.wait()
    for k, part in ((0, upper), (1, lower)):
        hop_right(part, k, 1).start()
        hop_left(part, k, 1).start()
        over_right(part, k, 0).start()
    own_norm = ext.at[blk, :, pl.ds(0, width)]
    keep = pltpu.make_async_copy(own_norm, norm_pair.at[h], pair_sem.at[0])
    keep.start()
    swapped = pltpu.make_async_remote_copy(
        src_ref=own_norm, dst_ref=norm_pair.at[h], send_sem=pair_sem.at[1], recv_sem=pair_sem.at[2],
        device_id={"head": 1 - h}, device_id_type=MESH)
    swapped.start()
    for copy in weights:
        copy.wait()

    triangle = lax.broadcasted_iota(jnp.int32, (rows, rows), 0) > lax.broadcasted_iota(jnp.int32, (rows, rows), 1)
    triangle = triangle.astype(BF16)
    lane = lax.broadcasted_iota(jnp.int32, (rows, 128), 1)

    @pl.loop(0, half)
    def _(g):
        s = g + 1
        hop_right(upper, 0, s).wait_recv()

        @pl.when(s < half)
        def _():
            hop_right(upper, 0, s + 1).start()

        over_right(upper, 0, s).start()
        hop_left(lower, 1, s).wait_recv()

        @pl.when(s < half)
        def _():
            hop_left(lower, 1, s + 1).start()

        over_left(lower, 1, s).start()

        @pl.when(s < half)
        def _():
            hop_right(lower, 1, s).wait_recv()

            @pl.when(s < half - 1)
            def _():
                hop_right(lower, 1, s + 1).start()

            over_right(lower, 1, s).start()
            hop_left(upper, 0, s).wait_recv()

            @pl.when(s < half - 1)
            def _():
                hop_left(upper, 0, s + 1).start()

            over_left(upper, 0, s).start()

        over_right(upper, 0, g).wait_recv()
        over_right(lower, 1, g).wait_recv()
        over_left(lower, 1, s).wait_recv()

        @pl.when(s < half)
        def _():
            over_left(upper, 0, s).wait_recv()

        @pl.when(s == half)
        def _():
            over_right(upper, 0, s).wait_recv()

        cot_copy(g, 0).wait()
        cot_copy(g, 1).wait()

        @pl.when(s < half)
        def _():
            cot_copy(g + 1, 0).start()
            cot_copy(g + 1, 1).start()

        turn = lax.rem(g, 2)
        group = pl.ds(pl.multiple_of(g * 2 * slots, 2 * slots), 2 * slots)
        firsts = (at(-g) - core, at(g + 1) - core)
        for j in range(2):
            for i in range(2):
                lanes = ext[firsts[j] + i, :, pl.ds(width, 128)].astype(F32)
                chosen = jnp.sum(jnp.where(lane == experts + blk, lanes, 0.0), axis=1, keepdims=True)
                weight = jnp.sum(jnp.where(lane == blk, lanes, 0.0), axis=1, keepdims=True)
                chosen = jnp.broadcast_to(chosen, (rows, 128))
                rank = dot(triangle, chosen.astype(BF16)) + i * (slots // 2)
                spread = jnp.where((rank == lane.astype(F32)) & (chosen > 0.5), 1.0, 0.0)
                deal[j, i] = spread.astype(BF16)
                gate[j, i] = jnp.broadcast_to(weight, (rows, 128))
            where = pl.ds(pl.multiple_of(g * 2 * slots + j * slots, slots), slots)

            def pick_rows(c, j=j, where=where):
                taken = dot_first(deal[j, 0], ext[firsts[j], :, c]) + dot_first(deal[j, 1], ext[firsts[j] + 1, :, c])
                rows_x[where, c] = taken.astype(BF16)
                scaled = [(deal[j, i] * gate[j, i].astype(BF16)) for i in range(2)]
                taken = dot_first(scaled[0], cot[turn, j, 0, :, c]) + dot_first(scaled[1], cot[turn, j, 1, :, c])
                rows_dy[where, c] = taken.astype(BF16)

            tiles(width, 512, pick_rows)

        def hidden_tile(c):
            high = shifted(c, hidden)
            x = rows_x[group]
            gate_part = dot(x, in_ref[:, c])
            lift = dot(x, in_ref[:, high])
            both[:, c] = gate_part
            both[:, high] = lift
            rows_act[group, c] = (jax.nn.silu(gate_part) * lift).astype(BF16)

        tiles(hidden, 256, hidden_tile)

        def result_tile(c):
            result[:, c] = dot(rows_act[group], out_ref[:, c]).astype(BF16)

        tiles(width, 512, result_tile)

        def grad_tile(c):
            high = shifted(c, hidden)
            da = dot_last(rows_dy[group], out_ref[c, :])
            gate_part, lift = both[:, c], both[:, high]
            sig = jax.nn.sigmoid(gate_part)
            rows_dab[group, c] = (da * lift * sig * (1.0 + gate_part * (1.0 - sig))).astype(BF16)
            rows_dab[group, high] = (da * gate_part * sig).astype(BF16)

        tiles(hidden, 256, grad_tile)

        def back_tile(c):
            back[:, c] = dot_last(rows_dab[group], in_ref[c, :]).astype(BF16)

        tiles(width, 512, back_tile)

        @pl.when(g > 0)
        def _():
            for j in range(2):
                exchange_d(g - 1, j).wait_send()
                exchange_o(g - 1, j).wait_send()

        for j in range(2):
            chip = lax.div(firsts[j], 2)
            for which, to_d, to_o in (
                (core, own_d.at[chip], own_o.at[chip]),
                (1 - core, stage_d.at[j], stage_o.at[j]),
            ):
                part = pl.ds(j * slots, slots)
                dealer = deal[j, which]
                share = gate[j, which]
                total = jnp.zeros((rows, 1), F32)
                for t in range(width // 512):
                    c = pl.ds(t * 512, 512)
                    home_rows = dot(dealer, result[part, c])
                    to_o[:, c] = (home_rows * share[:, :1]).astype(BF16)
                    total = total + jnp.sum(
                        home_rows * cot[turn, j, which, :, c].astype(F32), axis=1, keepdims=True)
                    to_d[:, c] = dot(dealer, back[part, c]).astype(BF16)
                high = total.astype(BF16).astype(F32)
                lanes = jnp.where(lane == blk, high, jnp.where(lane == experts + blk, total - high, 0.0))
                to_d[:, pl.ds(width, 128)] = lanes.astype(BF16)
            exchange_d(g, j).start()
            exchange_o(g, j).start()

    arrays = ((0, own_d, sib_d, right_d, left_d, home_ref), (1, own_o, sib_o, right_o, left_o, routed_ref))
    arrived = set()

    def join(a, own, other, d, part, into, received):
        g, j = (d - 1, 1) if d > 0 else (-d, 0)
        if (a, g, j) not in arrived:
            arrived.add((a, g, j))
            (exchange_d, exchange_o)[a](g, j).wait_recv()
        chip = lax.div(at(d), 2)

        def add(c):
            total = own[chip, c].astype(F32) + other[chip, c].astype(F32)
            for ref in received:
                total = total + ref[c].astype(F32)
            into[c] = total.astype(into.dtype)

        @pl.loop(0, cut // 16)
        def _(i):
            add(pl.ds(pl.multiple_of(part.start + i * 16, 16), 16))

    def pass_right(a, src, buf, k, part, s):
        return remote(src.at[part], buf.at[s - 1, part], ss_rr.at[a, k, s], rs_r.at[a, k, s], right)

    def pass_left(a, src, buf, k, part, s):
        return remote(src.at[part], buf.at[s - 1, part], ss_rl.at[a, k, s], rs_l.at[a, k, s], left)

    ways = (
        (0, upper, 1, half), (1, lower, -1, half), (1, lower, 1, half - 1), (0, upper, -1, half - 1),
    )
    sent = []

    def scatter_step(a, s):
        _, own, other, to_right, to_left, _ = arrays[a]
        for k, part, way, hops in ways:
            if s > hops:
                continue
            make, buf = (pass_right, to_right) if way > 0 else (pass_left, to_left)
            d = way * (hops - s + 1)
            if d == -half:
                d = half
            if s == 1:
                src = own.at[lax.div(at(d), 2)]
                join(a, own, other, d, part, src, ())
            else:
                src = buf.at[s - 2]
                make(a, src, buf, k, part, s - 1).wait_recv()
                join(a, own, other, d, part, src, (src,))
            copy = make(a, src, buf, k, part, s)
            copy.start()
            sent.append(copy)

    def scatter_finish(a):
        _, own, other, to_right, to_left, into = arrays[a]
        for k, part in ((0, upper), (1, lower)):
            last_right, last_left = half - k, half - 1 + k
            pass_right(a, own.at[0], to_right, k, part, last_right).wait_recv()
            pass_left(a, own.at[0], to_left, k, part, last_left).wait_recv()
            join(a, own, other, 0, part, into, (to_right.at[last_right - 1], to_left.at[last_left - 1]))

    loads = 0

    def move(src, dst):
        nonlocal loads
        copy = pltpu.make_async_copy(src, dst, load_sem.at[loads])
        loads += 1
        copy.start()
        return copy

    def cross(i, src, dst):
        return pltpu.make_async_remote_copy(
            src_ref=src, dst_ref=dst, send_sem=y_send.at[i], recv_sem=y_recv.at[i],
            device_id={"head": 1 - h}, device_id_type=MESH)

    theirs = pl.ds(pl.multiple_of((1 - h) * rows, rows), rows)
    ours = pl.ds(pl.multiple_of(h * rows, rows), rows)
    keep.wait()
    swapped.wait()
    shared_loads = [
        move(shared_up, in_ref), move(shared_down, out_ref), move(cot_pair, back),
        move(norm_pair.at[0], result.at[pl.ds(0, rows)]), move(norm_pair.at[1], result.at[pl.ds(rows, rows)])]
    scatter_step(0, 1)

    def weight_in(c):
        din_ref[c, :] = dot_first(rows_x[:, c], rows_dab[...]).astype(BF16)

    tiles(width, 256, weight_in)
    din_out = move(din_ref, din)
    load_out = move(full_out, rows_x.at[pl.ds(0, low.shape[1])])
    scatter_step(0, 2)
    scatter_step(1, 1)

    for copy in shared_loads:
        copy.wait()

    def shared_tile(c):
        high = shifted(c, hidden)
        gate_part = dot(result[...], in_ref[:, c])
        lift = dot(result[...], in_ref[:, high])
        sig = jax.nn.sigmoid(gate_part)
        shared_act[:, c] = (gate_part * sig * lift).astype(BF16)
        da = dot_last(back[...], out_ref[c, :])
        shared_dab[:, c] = (da * lift * sig * (1.0 + gate_part * (1.0 - sig))).astype(BF16)
        shared_dab[:, high] = (da * gate_part * sig).astype(BF16)

    tiles(hidden, 256, shared_tile)
    to_back, to_sum = cot.at[0, 0, 0], cot.at[0, 0, 1]

    def back_part(c):
        to_back[:, c] = dot_last(shared_dab[theirs, :], in_ref[c, :]).astype(BF16)

    tiles(width, 512, back_part)
    swap_back = cross(0, to_back, from_back)
    swap_back.start()

    def weight_out(c):
        dout_ref[c, :] = dot_first(rows_act[:, c], rows_dy[...]).astype(BF16)

    tiles(hidden, 256, weight_out)
    dout_out = move(dout_ref, dout)
    scatter_step(0, 3)
    scatter_step(1, 2)

    def sum_part(c):
        to_sum[:, c] = dot(shared_act[theirs, :], out_ref[:, c]).astype(BF16)

    tiles(width, 512, sum_part)
    swap_sum = cross(1, to_sum, from_sum)
    swap_sum.start()
    din_out.wait()

    def shared_in(c):
        din_ref[c, :] = dot_first(result[:, c], shared_dab[...]).astype(BF16)

    tiles(width, 256, shared_in)
    up_out = move(din_ref, up_part)
    scatter_step(0, 4)
    scatter_step(1, 3)
    dout_out.wait()

    def shared_out(c):
        dout_ref[c, :] = dot_first(shared_act[:, c], back[...]).astype(BF16)

    tiles(hidden, 256, shared_out)
    down_out = move(dout_ref, down_part)
    swap_back.wait_recv()
    scatter_finish(0)

    lanes = home_ref[:, pl.ds(width, 128)].astype(BF16)
    row_id = lax.broadcasted_iota(jnp.int32, (128, 128), 0)
    col_id = lax.broadcasted_iota(jnp.int32, (128, 128), 1)
    fold = jnp.where((row_id == col_id) | (row_id == col_id + experts), 1.0, 0.0).astype(BF16)
    weighted = gates[...] * dot(lanes, fold)
    logit_grad = (weighted - gates[...] * jnp.sum(weighted, axis=1, keepdims=True)).astype(BF16)
    short = logit_grad[:, : turned.shape[0]]

    def norm_part(c):
        hidden_grad[:, c] = (
            home_ref[:, c] + from_back[:, c].astype(F32) + dot_last(shared_dab[ours, :], in_ref[c, :])
            + dot(short, turned[:, c].astype(BF16)))
        row_part[:, c] = dot_first(logit_grad, ext[blk, :, c])

    tiles(width, 512, norm_part)

    def norm_rows(n, total):
        part = pl.ds(pl.multiple_of(n * 32, 32), 32)
        x, up = resid[part, :], hidden_grad[part, :]
        scaler = lax.rsqrt(jnp.mean(x * x, axis=1, keepdims=True) + EPS)
        normed = x * scaler
        scaled = up * turned[pl.ds(experts + 1, 1), :]
        grad = cot_own[part, :].astype(F32) + scaler * (
            scaled - normed * jnp.mean(scaled * normed, axis=1, keepdims=True))
        hidden_grad[part, :] = grad
        hid[h, part, :] = grad.astype(BF16)
        return total + jnp.sum(up * normed, axis=0, keepdims=True)

    gain = lax.fori_loop(0, rows // 32, norm_rows, jnp.zeros((1, width), F32))
    swap_hid = cross(2, hid.at[h], hid.at[h])
    swap_hid.start()
    row_part[pl.ds(experts + 1, 1), :] = gain
    load_out.wait()
    inner = low.shape[1]
    full = rows_x.at[pl.ds(0, inner)]

    def mixed_tile(who, where):
        for t in range(inner // 256):
            c = pl.ds(t * 256, 256)
            mixed_grad[where, c] = dot_last(hid[who], full[c, :]).astype(BF16)

    mixed_tile(h, ours)
    scatter_step(1, 4)
    swap_hid.wait_recv()
    mixed_tile(1 - h, theirs)

    def out_tile(c):
        rows_dy[c, :] = (
            dot_first(low[pl.ds(0, rows), c], hid[0]) + dot_first(low[pl.ds(rows, rows), c], hid[1])).astype(BF16)

    for t in range(inner // 256):
        out_tile(pl.ds(t * 256, 256))
    part_out = move(rows_dy.at[pl.ds(0, inner)], out_part)
    swap_sum.wait_recv()
    scatter_finish(1)

    def output_tile(c):
        output[:, c] = (
            resid[:, c] + routed_ref[:, c] + from_sum[:, c].astype(F32)
            + dot(shared_act[ours, :], out_ref[:, c])).astype(BF16)

    tiles(width, 512, output_tile)
    for copy in (swap_back, swap_sum, swap_hid):
        copy.wait_send()
    for copy in (up_out, down_out, part_out):
        copy.wait()
    for copy in sent:
        copy.wait_send()
    for j in range(2):
        exchange_d(half - 1, j).wait_send()
        exchange_o(half - 1, j).wait_send()
    for k, part in ((0, upper), (1, lower)):
        over_right(part, k, 0).wait_send()
        for s in range(1, half + 1):
            if s <= half - k:
                hop_right(part, k, s).wait_send()
                over_right(part, k, s).wait_send()
            if s <= half - 1 + k:
                hop_left(part, k, s).wait_send()
                over_left(part, k, s).wait_send()


def experts_fused(
    ext, weights, cot_all, shared, cot_pair, cot_own, resid, gates, turned, low, full_out, blks, capacity, collective_id,
):
    chips, half = blks // 2, blks // 4
    rows, wide = ext.shape
    width, hidden = 2 * weights[0].shape[0], weights[2].shape[0]
    count = blks * capacity
    group = 4 * capacity
    inner = low.shape[1]
    dma = pltpu.SemaphoreType.DMA
    vmem = pl.BlockSpec(memory_space=pltpu.VMEM)
    anywhere = pl.BlockSpec(memory_space=pl.ANY)

    def bf16(*shape):
        return pltpu.VMEM(shape, BF16)

    def f32(*shape):
        return pltpu.VMEM(shape, F32)

    out = [
        ((rows, width), BF16, vmem), ((rows, width), F32, vmem), ((2 * rows, inner), BF16, vmem),
        ((inner, width), BF16, anywhere), ((width, 2 * hidden), BF16, anywhere), ((hidden, width), BF16, anywhere),
        ((width, 2 * hidden), BF16, anywhere), ((hidden, width), BF16, anywhere), ((128, width), F32, vmem),
        ((2, rows, width), BF16, anywhere),
    ]
    return pl.pallas_call(
        functools.partial(expert_kernel, chips, blks),
        out_shape=[jax.ShapeDtypeStruct(s, t) for s, t, _ in out],
        in_specs=[anywhere] * 9 + [vmem] * 5 + [anywhere],
        out_specs=[space for _, _, space in out],
        scratch_shapes=[
            f32(rows, wide), f32(rows, width), bf16(width, 2 * hidden), bf16(hidden, width),
            bf16(2 * rows, hidden), bf16(2 * rows, 2 * hidden), bf16(2, rows, width), bf16(rows, width), bf16(rows, width),
            bf16(width, 2 * hidden), bf16(hidden, width),
            bf16(blks, rows, wide), bf16(2, 2, 2, rows, width),
            bf16(count, width), bf16(count, width), bf16(count, hidden), bf16(count, 2 * hidden),
            f32(group, 2 * hidden), bf16(group, width), bf16(group, width),
            bf16(2, 2, rows, 128), f32(2, 2, rows, 128),
            bf16(chips, rows, wide), bf16(chips, rows, width), bf16(2, rows, wide), bf16(2, rows, width),
            bf16(chips, rows, wide), bf16(chips, rows, width),
            bf16(half, rows, wide), bf16(half, rows, width), bf16(half, rows, wide), bf16(half, rows, width),
            dma(()), dma((2, 2)),
        ] + [dma((2, half + 1))] * 8 + [dma((2, 2, half))] * 2 + [dma((2, 2, half + 1))] * 4
        + [dma((4,)), dma((3,)), dma((11,)), dma((3,)), dma((3,))],
        compiler_params=pltpu.CompilerParams(
            collective_id=collective_id, has_side_effects=True, vmem_limit_bytes=63 << 20),
    )(ext, *weights, cot_all, *shared, cot_pair, cot_own, resid, gates, turned, low, full_out)


class Ring:
    def __init__(self, info, chips, chunks, first, sems):
        self.blk, self.at, self.sib = info
        self.half = chips // 2
        self.chunks, self.first = chunks, first
        self.send_r, self.recv_r, self.send_l, self.recv_l, self.send_s, self.recv_s = sems

    def hops(self, c):
        return self.half - c % 2, self.half - 1 + c % 2

    def copy(self, ref, ssem, rsem, dev):
        return pltpu.make_async_remote_copy(
            src_ref=ref, dst_ref=ref, send_sem=ssem, recv_sem=rsem,
            device_id={"blk": dev}, device_id_type=MESH)

    def right(self, c, s):
        i = self.first + c
        return self.copy(self.chunks[c](self.at(1 - s)), self.send_r.at[i, s], self.recv_r.at[i, s], self.at(1))

    def left(self, c, s):
        i = self.first + c
        return self.copy(self.chunks[c](self.at(s - 1)), self.send_l.at[i, s], self.recv_l.at[i, s], self.at(-1))

    def over(self, c, d):
        i, k = self.first + c, d + self.half
        return self.copy(self.chunks[c](self.at(d)), self.send_s.at[i, k], self.recv_s.at[i, k], self.sib)

    def start(self, c):
        self.right(c, 1).start()
        self.left(c, 1).start()
        self.over(c, 0).start()

    def step(self, s):
        for c in range(len(self.chunks)):
            rh, lh = self.hops(c)
            if s <= rh:
                self.right(c, s).wait_recv()
                if s < rh:
                    self.right(c, s + 1).start()
                self.over(c, -s).start()
            if s <= lh:
                self.left(c, s).wait_recv()
                if s < lh:
                    self.left(c, s + 1).start()
                self.over(c, s).start()

    def end(self):
        for c in range(len(self.chunks)):
            rh, lh = self.hops(c)
            for d in range(-rh, lh + 1):
                self.over(c, d).wait_recv()

    def flush(self):
        for c in range(len(self.chunks)):
            rh, lh = self.hops(c)
            for s in range(1, rh + 1):
                self.right(c, s).wait_send()
            for s in range(1, lh + 1):
                self.left(c, s).wait_send()
            for d in range(-rh, lh + 1):
                self.over(c, d).wait_send()


def front_kernel(
    chips, experts,
    slots_ref, places_ref, ends_ref, lanes_ref, tokens, cotangent, w_query, w_key, w_value, small, w_out,
    shared_up, shared_down, expert_up, expert_down,
    n1, query, kv, first_w, out_w, up_w, down_w, cot, cot_pair, expert_in, expert_out,
    low, full, lse, resid, ext, gates, short,
    turned, pair, to_other, from_other,
    send_r, recv_r, send_l, recv_l, send_s, recv_s, own_sem, y_send, y_recv,
):
    h = lax.axis_index("head")
    blk, core, at, sib = ring_info(chips)
    half = chips // 2
    rows, width = tokens.shape
    qw, kw = w_query.shape[1] // 2, w_key.shape[1] // 2
    sw = shared_up.shape[1] // 4
    barrier = pltpu.get_barrier_semaphore()
    for other in (at(1), at(-1), sib):
        pl.semaphore_signal(barrier, inc=1, device_id={"blk": other}, device_id_type=MESH)
    pl.semaphore_signal(barrier, inc=1, device_id={"head": 1 - h}, device_id_type=MESH)
    pl.semaphore_wait(barrier, 4)

    def lanes_of(start, size):
        return pl.ds(pl.multiple_of(start, 128), size)

    def halves(i, j):
        return [
            (w_query.at[:, lanes_of(i * qw, qw)], first_w.at[j, blk, :, pl.ds(0, qw)]),
            (w_key.at[:, lanes_of(i * kw, kw)], first_w.at[j, blk, :, pl.ds(qw, kw)]),
            (w_value.at[:, lanes_of(i * kw, kw)], first_w.at[j, blk, :, pl.ds(qw + kw, kw)]),
            (small, first_w.at[j, blk, :, pl.ds(qw + 2 * kw, small.shape[1])]),
            (tokens, pair.at[j]),
            (shared_up.at[:, lanes_of(i * sw, sw)], up_w.at[j, blk, :, pl.ds(0, sw)]),
            (shared_up.at[:, lanes_of((2 + i) * sw, sw)], up_w.at[j, blk, :, pl.ds(sw, sw)]),
            (cotangent, cot_pair.at[j]),
        ]

    whole = [(expert_up, expert_in), (expert_down, expert_out)]

    own = [pltpu.make_async_copy(a, b, own_sem.at[i]) for i, (a, b) in enumerate(halves(h, h))]
    own.append(pltpu.make_async_copy(w_out, out_w.at[blk], own_sem.at[len(own)]))
    own.append(pltpu.make_async_copy(shared_down, down_w.at[blk], own_sem.at[len(own)]))
    own.append(pltpu.make_async_copy(cotangent, cot.at[blk], own_sem.at[len(own)]))
    swaps = [
        pltpu.make_async_remote_copy(
            src_ref=a, dst_ref=b, send_sem=y_send.at[i], recv_sem=y_recv.at[i],
            device_id={"head": 1 - h}, device_id_type=MESH)
        for i, (a, b) in enumerate(halves(1 - h, h) + whole)
    ]
    for i in range(5):
        swaps[i].start()
    for i in (0, 1, 2, 3, 8, 4):
        own[i].start()

    info = (blk, at, sib)
    sems = (send_r, recv_r, send_l, recv_l, send_s, recv_s)

    def row_cuts(ref, *sizes):
        start, chunks = 0, []
        for size in sizes:
            chunks.append(lambda b, start=start, size=size: ref.at[b, pl.ds(start, size)])
            start += size
        return chunks

    ring_w = Ring(info, chips, [lambda b: first_w.at[h, b], lambda b: first_w.at[1 - h, b]], 0, sems)
    out_rows, down_rows = w_out.shape[0], shared_down.shape[0]
    ring_o = Ring(info, chips, row_cuts(out_w, 32, out_rows - 32), 2, sems)
    ring_kv = Ring(info, chips, [lambda b: kv.at[2 * b], lambda b: kv.at[2 * b + 1]], 4, sems)
    ring_u = Ring(info, chips, [lambda b: up_w.at[h, b], lambda b: up_w.at[1 - h, b]], 6, sems)
    ring_d = Ring(info, chips, row_cuts(down_w, down_rows // 2, down_rows // 2), 8, sems)
    ring_c = Ring(info, chips, row_cuts(cot, rows // 2, rows // 2), 10, sems)

    for i in (0, 1, 2, 3):
        own[i].wait()
    ring_w.start(0)
    own[8].wait()
    for i in range(4):
        swaps[i].wait_recv()
    ring_w.start(1)
    ring_o.start(0)
    ring_o.start(1)
    for i in (5, 6, 9, 10, 7):
        own[i].start()
    for i in range(5, 10):
        swaps[i].start()
    for s in range(1, half + 1):
        ring_w.step(s)
        ring_o.step(s)
    ring_w.end()
    own[4].wait()
    swaps[4].wait_recv()

    small_cols = first_w[:, :, :, pl.ds(qw + 2 * kw, 128)].reshape(width, 128)
    turned[...] = jnp.swapaxes(small_cols.astype(F32), 0, 1)
    short[...] = turned[pl.ds(0, short.shape[0]), :]

    @pl.loop(0, 2 * rows // 64)
    def _(i):
        x = pair[lax.div(i, rows // 64), pl.ds(pl.multiple_of(lax.rem(i, rows // 64) * 64, 64), 64), :].astype(F32)
        scaled = x * lax.rsqrt(jnp.mean(x * x, axis=1, keepdims=True) + EPS) * turned[pl.ds(experts, 1), :]
        n1[pl.ds(pl.multiple_of(i * 64, 64), 64), :] = scaled.astype(BF16)

    def project(start, size):
        weights = first_w[:, :, :, pl.ds(start, size)].reshape(width, size)
        return dot(n1[...], weights).astype(BF16)

    for t in range(2 * kw // 256):
        part = project(qw + t * 256, 256)
        for i in range(2):
            kv[2 * blk + i, :, pl.ds(t * 256, 256)] = part[i * rows : (i + 1) * rows]
    ring_kv.start(0)
    ring_kv.start(1)
    for t in range(qw // 256):
        query[:, pl.ds(t * 256, 256)] = project(t * 256, 256)
    for i in (5, 6, 9, 10):
        own[i].wait()
    swaps[5].wait_recv()
    swaps[6].wait_recv()
    for s in range(1, half + 1):
        ring_kv.step(s)
        if s == half - 1:
            for ring in (ring_u, ring_d, ring_c):
                ring.start(0)
                ring.start(1)
    ring_kv.end()

    groups, repeats = kw // HD, qw // kw
    cols = repeats * PIECE
    pieces = slots_ref.shape[0]
    need = pieces // 2 + 1
    chunk = 6
    chunks = -(-need // chunk)
    later = [(ring_u, 1), (ring_d, 1), (ring_c, 1), (ring_u, 2), (ring_d, 2), (ring_c, 2)]
    turns = 0
    for i in range(2):
        place = places_ref[i]
        for g in range(groups):
            q = jnp.concatenate(
                [query[pl.ds(i * PIECE, PIECE), pl.ds((g * repeats + r) * HD, HD)] for r in range(repeats)], axis=0)

            def step(n, carry, place=place, g=g, q=q):
                top, total, acc = carry
                first = place + 1 - chunks * chunk + n * chunk
                _, (k, v) = key_chunk(
                    slots_ref, first, chunk, kv.at[:, :, pl.ds(g * HD, HD)], kv.at[:, :, pl.ds((groups + g) * HD, HD)])
                scores = dot_last(k, q) * HD**-0.5
                scores = jnp.where(seen(ends_ref, place, first, chunk * PIECE, cols), scores, NEG)
                new = jnp.maximum(top, jnp.max(scores, axis=0, keepdims=True))
                weights = jnp.exp(scores - new)
                factor = jnp.exp(top - new)
                total = total * factor + jnp.sum(weights, axis=0, keepdims=True)
                return new, total, acc * factor + dot_first(v, weights.astype(BF16))

            top, total, acc = lax.fori_loop(
                0, chunks, step,
                (jnp.full((1, cols), NEG, F32), jnp.zeros((1, cols), F32), jnp.zeros((HD, cols), F32)))
            out = jnp.swapaxes(acc / total, 0, 1)
            lse[g, pl.ds(i, 1), :] = top + jnp.log(total)
            for r in range(repeats):
                part = out[r * PIECE : (r + 1) * PIECE]
                full[pl.ds(i * PIECE, PIECE), pl.ds((g * repeats + r) * HD, HD)] = part
                low[pl.ds(i * PIECE, PIECE), pl.ds((g * repeats + r) * HD, HD)] = part.astype(BF16)
            turns += 1
            if turns % 2 == 0:
                for ring, s in later[:3]:
                    ring.step(s)
                later = later[3:]

    ring_o.end()
    theirs = pl.ds(pl.multiple_of((1 - h) * rows, rows), rows)
    ours = pl.ds(pl.multiple_of(h * rows, rows), rows)

    def mixed(where, c):
        return dot(low[where, :], out_w[:, :, c].reshape(qw, c.size))

    for t in range(width // 512):
        c = pl.ds(t * 512, 512)
        to_other[:, c] = mixed(theirs, c).astype(BF16)
    swap_mixed = pltpu.make_async_remote_copy(
        src_ref=to_other, dst_ref=from_other, send_sem=y_send.at[10], recv_sem=y_recv.at[10],
        device_id={"head": 1 - h}, device_id_type=MESH)
    swap_mixed.start()
    for t in range(width // 512):
        c = pl.ds(t * 512, 512)
        resid[:, c] = pair[h, :, c].astype(F32) + mixed(ours, c)
    for ring in (ring_u, ring_d, ring_c):
        ring.step(3)
    swap_mixed.wait_recv()

    @pl.loop(0, rows // 32)
    def _(i):
        part = pl.ds(pl.multiple_of(i * 32, 32), 32)
        x = resid[part, :] + from_other[part, :].astype(F32)
        resid[part, :] = x
        scaled = x * lax.rsqrt(jnp.mean(x * x, axis=1, keepdims=True) + EPS) * turned[pl.ds(experts + 1, 1), :]
        ext[part, pl.ds(0, width)] = scaled.astype(BF16)

    logits = dot_last(ext[:, pl.ds(0, width)], turned[...].astype(BF16))
    mask = lanes_ref[:, pl.ds(0, 128)]
    masked = jnp.where(mask > 0.5, logits, NEG)
    raised = jnp.where(mask > 0.5, jnp.exp(masked - jnp.max(masked, axis=1, keepdims=True)), 0.0)
    probs = raised / jnp.sum(raised, axis=1, keepdims=True)
    gates[...] = probs
    ext[:, pl.ds(width, 128)] = (probs + lanes_ref[:, pl.ds(128, 128)]).astype(BF16)
    for ring in (ring_u, ring_d, ring_c):
        ring.step(4)
    own[7].wait()
    for i in (7, 8, 9):
        swaps[i].wait_recv()
    for ring in (ring_u, ring_d, ring_c):
        ring.end()
    for ring in (ring_w, ring_o, ring_kv, ring_u, ring_d, ring_c):
        ring.flush()
    for copy in swaps:
        copy.wait_send()
    swap_mixed.wait_send()


def front_fused(
    tokens, cotangent, where, mask, w_query, w_key, w_value, small, w_out, shared_up, shared_down,
    expert_up, expert_down, blks, collective_id,
):
    chips, half = blks // 2, blks // 4
    rows, width = tokens.shape
    dense = w_query.shape[0]
    qw, kw, sw = w_query.shape[1] // 2, w_key.shape[1] // 2, shared_up.shape[1] // 4
    groups, repeats = kw // HD, qw // kw
    lanes = jnp.concatenate(
        [jnp.pad(mask, ((0, 0), (0, 128 - blks))), jnp.pad(mask, ((0, 0), (blks, 128 - 2 * blks)))], axis=1).astype(F32)
    dma = pltpu.SemaphoreType.DMA
    vmem = pl.BlockSpec(memory_space=pltpu.VMEM)
    anywhere = pl.BlockSpec(memory_space=pl.ANY)
    smem = pl.BlockSpec(memory_space=pltpu.SMEM)
    out = [
        ((2 * rows, width), BF16, vmem), ((2 * rows, qw), BF16, vmem), ((2 * blks, rows, 2 * kw), BF16, vmem),
        ((2, blks, dense, qw + 2 * kw + small.shape[1]), BF16, vmem), ((blks, w_out.shape[0], width), BF16, vmem),
        ((2, blks, dense, 2 * sw), BF16, anywhere), ((blks, shared_down.shape[0], width), BF16, anywhere),
        ((blks, rows, width), BF16, anywhere), ((2, rows, width), BF16, anywhere),
        (expert_up.shape, BF16, anywhere), (expert_down.shape, BF16, anywhere),
        ((2 * rows, qw), BF16, vmem), ((2 * rows, qw), F32, vmem), ((groups, 2, repeats * PIECE), F32, vmem),
        ((rows, width), F32, vmem), ((rows, width + 128), BF16, vmem), ((rows, 128), F32, vmem), ((blks + 8, width), F32, vmem),
    ]
    ring = [dma((12, half + 1))] * 4 + [dma((12, 2 * half + 1))] * 2
    (
        n1, query, kv, first_w, out_w, up_w, down_w, cot, cot_pair, expert_in, expert_out,
        low, full, lse, resid, ext, gates, turned,
    ) = pl.pallas_call(
        functools.partial(front_kernel, chips, blks),
        out_shape=[jax.ShapeDtypeStruct(s, t) for s, t, _ in out],
        in_specs=[smem] * 3 + [vmem, anywhere, vmem] + [anywhere] * 5 + [vmem] * 2 + [anywhere] * 2,
        out_specs=[space for _, _, space in out],
        scratch_shapes=[
            pltpu.VMEM((128, width), F32), pltpu.VMEM((2, rows, width), BF16), pltpu.VMEM((rows, width), BF16), pltpu.VMEM((rows, width), BF16)]
        + ring + [dma((11,)), dma((11,)), dma((11,))],
        compiler_params=pltpu.CompilerParams(
            collective_id=collective_id, has_side_effects=True, vmem_limit_bytes=56 << 20),
    )(*where, lanes, tokens, cotangent, w_query, w_key, w_value, small, w_out, shared_up, shared_down, expert_up, expert_down)
    return (
        n1, query, kv, first_w.reshape(width, -1)[:, : qw + 2 * kw], out_w.reshape(-1, width),
        up_w.reshape(width, -1), down_w.reshape(-1, width), cot, cot_pair.reshape(2 * rows, width),
        expert_in, expert_out, low, full, lse, resid, ext, gates,
        None, None, None, (first_w, turned))


class Scatter:
    def __init__(self, info, chips, chunks, first, sems):
        self.core, self.at, self.sib = info
        self.half = chips // 2
        self.chunks, self.first = chunks, first
        self.ex_s, self.ex_r, self.right_s, self.right_r, self.left_s, self.left_r = sems
        self.there, self.sent = set(), []

    def remote(self, src, dst, ssem, rsem, dev):
        return pltpu.make_async_remote_copy(
            src_ref=src, dst_ref=dst, send_sem=ssem, recv_sem=rsem,
            device_id={"blk": dev}, device_id_type=MESH)

    def over(self, c, d):
        own, other = self.chunks[c][:2]
        i, k = self.first + c, d + self.half
        place = self.at(d)
        return self.remote(
            own(place + 1 - 2 * self.core), other.at[lax.div(place, 2)], self.ex_s.at[i, k], self.ex_r.at[i, k], self.sib)

    def exchange(self):
        for d in sorted(range(1 - self.half, self.half + 1), key=lambda d: (-abs(d), -d)):
            for c in range(len(self.chunks)):
                copy = self.over(c, d)
                copy.start()
                self.sent.append(copy)

    def join(self, c, d, into, received):
        own, other = self.chunks[c][:2]
        if (c, d) not in self.there:
            self.there.add((c, d))
            self.over(c, d).wait_recv()
        place = self.at(d)
        mine, theirs = own(place), other.at[lax.div(place, 2)]
        rows = mine.shape[0]

        @pl.loop(0, rows // 16)
        def _(i):
            w = pl.ds(pl.multiple_of(i * 16, 16), 16)
            total = mine[w].astype(F32) + theirs[w].astype(F32)
            for ref in received:
                total = total + ref[w].astype(F32)
            into[w] = total.astype(into.dtype)

    def hop(self, c, way, src, s):
        i = self.first + c
        if way > 0:
            return self.remote(
                src, self.chunks[c][2].at[s - 1], self.right_s.at[i, s], self.right_r.at[i, s], self.at(1))
        return self.remote(
            src, self.chunks[c][3].at[s - 1], self.left_s.at[i, s], self.left_r.at[i, s], self.at(-1))

    def hops(self, c, way):
        return self.half - c % 2 if way > 0 else self.half - 1 + c % 2

    def step(self, s):
        for c, (own, _, right, left) in enumerate(self.chunks):
            for way in (1, -1):
                hops = self.hops(c, way)
                if s > hops:
                    continue
                d = way * (hops - s + 1)
                d = self.half if d == -self.half else d
                if s == 1:
                    src = self.chunks[c][1].at[lax.div(self.at(d), 2)]
                    self.join(c, d, src, ())
                else:
                    src = (right if way > 0 else left).at[s - 2]
                    self.hop(c, way, src, s - 1).wait_recv()
                    self.join(c, d, src, (src,))
                copy = self.hop(c, way, src, s)
                copy.start()
                self.sent.append(copy)

    def finish(self, outs):
        for c, (own, _, right, left) in enumerate(self.chunks):
            lasts = []
            for way, buf in ((1, right), (-1, left)):
                hops = self.hops(c, way)
                self.hop(c, way, own(self.at(0)), hops).wait_recv()
                lasts.append(buf.at[hops - 1])
            self.join(c, 0, outs[c], lasts)

    def flush(self):
        for copy in self.sent:
            copy.wait_send()


def tail_kernel(
    chips, experts,
    dk, dv, dq, n1, first_w, tokens, hidden_grad, turned, out_part, up_part, down_part, row_part, din, dout,
    input_grad, query_grad, key_grad, value_grad, out_grad, up_grad, down_grad, small_grad, other_up, other_down,
    kv_sum, qkv_part, qkv_sum, up_sum, small_part, small_sum, to_other, from_other, qkv_from, up_from, small_from,
    *rest,
):
    h = lax.axis_index("head")
    blk, core, at, sib = ring_info(chips)
    half = chips // 2
    rows, width = tokens.shape
    qw, kw = dq.shape[1], dk.shape[2]
    top = qw + 2 * kw
    dense = first_w.shape[2]
    sw = up_part.shape[3] // 2
    count = 14
    others, rights, lefts = rest[:count], rest[count : 2 * count], rest[2 * count : 3 * count]
    sems, (y_send, y_recv) = rest[3 * count : 3 * count + 6], rest[3 * count + 6 :]
    barrier = pltpu.get_barrier_semaphore()
    for other in (at(1), at(-1), sib):
        pl.semaphore_signal(barrier, inc=1, device_id={"blk": other}, device_id_type=MESH)
    pl.semaphore_signal(barrier, inc=1, device_id={"head": 1 - h}, device_id_type=MESH)
    pl.semaphore_wait(barrier, 4)

    def cross(i, src, dst):
        return pltpu.make_async_remote_copy(
            src_ref=src, dst_ref=dst, send_sem=y_send.at[i], recv_sem=y_recv.at[i],
            device_id={"head": 1 - h}, device_id_type=MESH)

    info = (core, at, sib)

    def scatter(first, owns):
        chunks = [(own, others[first + i], rights[first + i], lefts[first + i]) for i, own in enumerate(owns)]
        return Scatter(info, chips, chunks, first, sems)

    def pieces_at(ref, i):
        return lambda b: ref.at[2 * b + i]

    def source_at(ref, i):
        return lambda b: ref.at[i, b]

    def rows_at(ref, start, size):
        return lambda b: ref.at[b, pl.ds(start, size)]

    out_rows, down_rows = out_part.shape[1], down_part.shape[1]
    kv_ring = scatter(0, [pieces_at(dk, 0), pieces_at(dk, 1), pieces_at(dv, 0), pieces_at(dv, 1)])
    rest_ring = scatter(4, [
        source_at(up_part, 0), source_at(up_part, 1), rows_at(out_part, 0, 32), rows_at(out_part, 32, out_rows - 32),
        rows_at(down_part, 0, down_rows // 2), rows_at(down_part, down_rows // 2, down_rows // 2)])
    qkv_ring = scatter(10, [source_at(qkv_part, 0), source_at(qkv_part, 1)])
    small_ring = scatter(12, [source_at(small_part, 0), source_at(small_part, 1)])

    kv_ring.exchange()
    rest_ring.exchange()
    size = width // 2
    start = pl.multiple_of((1 - h) * size, 128)
    swap_up = cross(0, din.at[pl.ds(start, size)], other_up)
    swap_down = cross(1, dout.at[:, pl.ds(start, size)], other_down)
    for s in range(1, half + 1):
        kv_ring.step(s)
        if s == half - 1:
            rest_ring.step(1)
    kv_ring.finish([kv_sum.at[i, pl.ds(j * rows, rows)] for i in range(2) for j in range(2)])

    theirs = pl.ds(pl.multiple_of((1 - h) * rows, rows), rows)
    ours = pl.ds(pl.multiple_of(h * rows, rows), rows)
    step = 8 * dense

    def norm_grad(where, i, t):
        def part(a, first, n):
            return dot_last(a, first_w[i, pl.ds(t * 8, 8), :, pl.ds(first, n)].reshape(step, n))

        return part(dq[where, :], 0, qw) + part(kv_sum[0, where, :], qw, kw) + part(kv_sum[1, where, :], qw + kw, kw)

    spans = [(i, t, pl.ds(i * (width // 2) + t * step, step)) for i in range(2) for t in range(width // (2 * step))]
    for i, t, c in spans:
        to_other[:, c] = norm_grad(theirs, i, t).astype(BF16)
    swap_norm = cross(2, to_other, from_other)
    swap_norm.start()
    swap_up.start()
    swap_down.start()
    for i, t, c in spans:
        lhs = n1[:, c]
        for first, n, rhs in ((0, qw, dq[...]), (qw, kw, kv_sum[0]), (qw + kw, kw, kv_sum[1])):
            part = dot_first(lhs, rhs).astype(BF16)
            qkv_part[i, pl.ds(t * 8, 8), :, pl.ds(first, n)] = part.reshape(8, dense, n)
    qkv_ring.exchange()
    rest_ring.step(2)
    qkv_ring.step(1)
    for i, t, c in spans:
        input_grad[:, c] = norm_grad(ours, i, t)
    swap_norm.wait_recv()
    rest_ring.step(3)
    qkv_ring.step(2)

    def norm_rows(n, total):
        part = pl.ds(pl.multiple_of(n * 32, 32), 32)
        x = tokens[part, :].astype(F32)
        up = input_grad[part, :] + from_other[part, :].astype(F32)
        scaler = lax.rsqrt(jnp.mean(x * x, axis=1, keepdims=True) + EPS)
        normed = x * scaler
        scaled = up * turned[pl.ds(experts, 1), :]
        back = scaler * (scaled - normed * jnp.mean(scaled * normed, axis=1, keepdims=True))
        input_grad[part, :] = hidden_grad[part, :] + back
        return total + jnp.sum(up * normed, axis=0, keepdims=True)

    gain = lax.fori_loop(0, rows // 32, norm_rows, jnp.zeros((1, width), F32))
    ids = lax.broadcasted_iota(jnp.int32, (128, 1), 0)
    turned_part = jnp.swapaxes(row_part[...] + jnp.where(ids == experts, gain, 0.0), 0, 1)
    small_part[...] = turned_part.astype(BF16).reshape(small_part.shape)
    small_ring.exchange()
    small_ring.step(1)
    rest_ring.step(4)
    qkv_ring.step(3)
    small_ring.step(2)
    up_views = [up_sum.at[0], up_sum.at[1]]
    rest_ring.finish(up_views + [
        out_grad.at[pl.ds(0, 32)], out_grad.at[pl.ds(32, out_rows - 32)],
        down_grad.at[pl.ds(0, down_rows // 2)], down_grad.at[pl.ds(down_rows // 2, down_rows // 2)]])
    swap_sum = cross(3, up_sum.at[1 - h], up_from)
    swap_sum.start()
    qkv_ring.step(4)
    small_ring.step(3)
    qkv_ring.finish([qkv_sum.at[0], qkv_sum.at[1]])
    swap_qkv = cross(4, qkv_sum.at[1 - h], qkv_from)
    swap_qkv.start()
    small_ring.step(4)
    small_ring.finish([small_sum.at[0], small_sum.at[1]])
    swap_small = cross(5, small_sum.at[1 - h], small_from)
    swap_small.start()

    def place(ref, source, first, n, base=0):
        for who, part in ((h, source[0]), (1 - h, source[1])):
            ref[:, pl.ds(pl.multiple_of(base + who * n, 128), n)] = part[:, pl.ds(first, n)].astype(F32)

    swap_sum.wait_recv()
    ups = (up_sum.at[h], up_from)
    place(up_grad, ups, 0, sw)
    place(up_grad, ups, sw, sw, 2 * sw)
    swap_qkv.wait_recv()
    sums = (qkv_sum.at[h], qkv_from)
    place(query_grad, sums, 0, qw)
    place(key_grad, sums, qw, kw)
    place(value_grad, sums, qw + kw, kw)
    swap_small.wait_recv()
    small_grad[...] = small_sum[h] + small_from[...]
    for ring in (kv_ring, rest_ring, qkv_ring, small_ring):
        ring.flush()
    for copy in (swap_norm, swap_up, swap_down, swap_sum, swap_qkv, swap_small):
        copy.wait_send()
    swap_up.wait_recv()
    swap_down.wait_recv()


def tail_fused(
    dk, dv, dq, n1, first_w, tokens, hidden_grad, turned, out_part, up_part, down_part, row_part, din, dout,
    blks, collective_id,
):
    chips, half = blks // 2, blks // 4
    rows, width = tokens.shape
    qw, kw = dq.shape[1], dk.shape[2]
    top = qw + 2 * kw
    dense = first_w.shape[2]
    out_rows, down_rows, up_wide = out_part.shape[1], down_part.shape[1], up_part.shape[3]
    dma = pltpu.SemaphoreType.DMA
    vmem = pl.BlockSpec(memory_space=pltpu.VMEM)
    anywhere = pl.BlockSpec(memory_space=pl.ANY)
    shapes = [(rows, kw)] * 4 + [(dense, up_wide)] * 2 + [(32, width), (out_rows - 32, width)]
    shapes += [(down_rows // 2, width)] * 2 + [(dense, top)] * 2 + [(dense, 128)] * 2
    others = [pltpu.VMEM((chips,) + s, BF16) for s in shapes]
    slots = [pltpu.VMEM((half,) + s, BF16) for s in shapes]
    n = len(shapes)

    def f32(*shape):
        return jax.ShapeDtypeStruct(shape, F32)

    def low(*shape):
        return pltpu.VMEM(shape, BF16)

    return pl.pallas_call(
        functools.partial(tail_kernel, chips, blks),
        out_shape=[
            f32(rows, width), f32(dense, 2 * qw), f32(dense, 2 * kw), f32(dense, 2 * kw), f32(out_rows, width),
            f32(dense, 2 * up_wide), f32(down_rows, width), f32(dense, 128),
            jax.ShapeDtypeStruct((din.shape[0] // 2, din.shape[1]), BF16),
            jax.ShapeDtypeStruct((dout.shape[0], dout.shape[1] // 2), BF16),
        ],
        in_specs=[vmem] * 12 + [anywhere] * 2,
        out_specs=[vmem] * 8 + [anywhere] * 2,
        scratch_shapes=[
            low(2, 2 * rows, kw), low(2, blks, dense, top), low(2, dense, top), low(2, dense, up_wide),
            low(2, blks, dense, 128), pltpu.VMEM((2, dense, 128), F32), low(rows, width), low(rows, width),
            low(dense, top), low(dense, up_wide), pltpu.VMEM((dense, 128), F32),
        ] + others + slots + slots + [dma((n, 2 * half + 1))] * 2 + [dma((n, half + 1))] * 4 + [dma((6,)), dma((6,))],
        compiler_params=pltpu.CompilerParams(
            collective_id=collective_id, has_side_effects=True, vmem_limit_bytes=62 << 20),
    )(dk, dv, dq, n1, first_w, tokens, hidden_grad, turned, out_part, up_part, down_part, row_part, din, dout)


def experts_plain(own_ext, weights, cot_all, blks, capacity, collective_id):
    h, b = lax.axis_index("head"), lax.axis_index("blk")
    own_up, other_up, own_down, other_down = weights
    expert_in = pair(own_up, other_up).reshape(2 * own_up.shape[0], -1)
    expert_out = jnp.where(
        h == 0,
        jnp.concatenate([own_down, other_down], axis=1),
        jnp.concatenate([other_down, own_down], axis=1),
    )
    normed = own_ext[:, : expert_in.shape[0]]
    normed_pair = pair(normed, swap(normed))
    experts, width = blks, expert_in.shape[0]
    rows = own_ext.shape[0]
    ext = all_gather_blk([own_ext], blks, collective_id)[0]
    norm_all = ext[:, :, :width]
    gate_here = lax.dynamic_index_in_dim(ext, width + b, 2, keepdims=False).astype(F32)
    mask_here = lax.dynamic_index_in_dim(ext, width + experts + b, 2, keepdims=False).astype(F32)
    rank = jnp.cumsum(mask_here, axis=1) - mask_here
    slots = jnp.arange(capacity, dtype=F32)
    deal = ((rank[:, None, :] == slots[None, :, None]) & (mask_here[:, None, :] > 0)).astype(BF16)
    deal_gate = deal * gate_here[:, None, :].astype(BF16)

    def to_slots(dealer, array):
        moved = jnp.einsum("bst,btd->bsd", dealer, array, preferred_element_type=F32)
        return moved.astype(BF16).reshape(blks * capacity, width)

    def to_rows(dealer, array):
        return jnp.einsum(
            "bst,bsd->btd", dealer, array.reshape(blks, capacity, width), preferred_element_type=F32)

    expert_rows = to_slots(deal, norm_all)
    both = dot(expert_rows, expert_in)
    ew = expert_out.shape[0]
    gate_part, up_part = both[:, :ew], both[:, ew:]
    activated = (jax.nn.silu(gate_part) * up_part).astype(BF16)
    result = dot(activated, expert_out).astype(BF16)
    result_rows = to_rows(deal, result)
    gate_grad = jnp.sum(result_rows * cot_all.astype(F32), axis=2, keepdims=True)
    routed = (result_rows * gate_here[:, :, None]).astype(BF16)
    slot_grad = to_slots(deal_gate, cot_all)
    act_grad = dot_last(slot_grad, expert_out)
    both_grad = gated_grad(act_grad, gate_part, up_part)
    rows_back = to_rows(deal, dot_last(both_grad, expert_in).astype(BF16)).astype(BF16)
    lane = jnp.arange(128 * (-(-2 * experts // 128)), dtype=jnp.int32)
    grad_high = gate_grad.astype(BF16)
    grad_low = (gate_grad - grad_high.astype(F32)).astype(BF16)
    grad_lanes = jnp.where(lane == b, grad_high, jnp.where(lane == b + experts, grad_low, jnp.zeros((), BF16)))
    dwn = dot_first(activated, slot_grad).astype(BF16)
    dup = dot_first(expert_rows, both_grad).astype(BF16)
    home = reduce_scatter_blk([jnp.concatenate([rows_back, grad_lanes], axis=2)], blks, collective_id + 1, [F32])[0]
    routed_sum = reduce_scatter_blk([routed], blks, collective_id + 2, [F32])[0]
    return home, routed_sum, dup, dwn, normed_pair


def pair(own, other):
    return jnp.where(lax.axis_index("head") == 0, jnp.stack([own, other]), jnp.stack([other, own]))


def half(w, i, parts=1):
    size = w.shape[1] // (2 * parts)
    cut = lax.dynamic_slice_in_dim(w.reshape(w.shape[0], parts, 2 * size), i * size, size, 2)
    return cut.reshape(w.shape[0], parts * size)


def pick(stacked, i):
    return lax.dynamic_index_in_dim(stacked, i, 0, keepdims=False)


def front_plain(
    tokens, cotangent, where, mask, w_query, w_key, w_value, small, w_out, shared_up, shared_down,
    expert_up, expert_down, blks, collective_id,
):
    h = lax.axis_index("head")
    rows, width = tokens.shape
    experts = blks

    def columns(i):
        return jnp.concatenate([half(w_query, i), half(w_key, i), half(w_value, i)], axis=1)

    first = pair(
        jnp.concatenate([columns(h), small], axis=1),
        swap(jnp.concatenate([columns(1 - h), small], axis=1)),
    )
    tokens_pair = pair(tokens, swap(tokens))
    cotangent_pair = pair(cotangent, swap(cotangent)).reshape(2 * rows, width)
    up_pair = pair(half(shared_up, h, 2), swap(half(shared_up, 1 - h, 2)))
    other_up, other_down = swap(expert_up), swap(expert_down)
    gathered = all_gather_blk([first], blks, collective_id)[0].reshape(width, -1)
    qw = w_query.shape[1] // 2
    kw = w_key.shape[1] // 2
    full_qkv = gathered[:, : qw + 2 * kw]
    full_router = gathered[:, qw + 2 * kw : qw + 2 * kw + experts]
    gain_first = gathered[:, qw + 2 * kw + experts].astype(F32)
    gain_second = gathered[:, qw + 2 * kw + experts + 1].astype(F32)

    inputs_pair = tokens_pair.reshape(2 * rows, width).astype(F32)
    normed_one = (inputs_pair * inv_scale(inputs_pair) * gain_first).astype(BF16)
    qkv = dot(normed_one, full_qkv).astype(BF16)
    query = qkv[:, :qw]
    kv = all_gather_blk([qkv[:, qw:]], blks, collective_id + 1)[0].reshape(-1, PIECE, 2 * kw)

    attended, attended_full, lse = attention_forward(query, kv, where)

    up_all, out_all, down_all, cot_all = all_gather_blk([up_pair, w_out, shared_down, cotangent], blks, collective_id + 2)
    full_up = up_all.reshape(width, -1)
    full_out = out_all.reshape(-1, width)
    full_down = down_all.reshape(-1, width)

    mixed = dot(attended, full_out).reshape(2, rows, width)
    inputs = tokens.astype(F32)
    resid = inputs + (pick(mixed, h) + swap(pick(mixed, 1 - h).astype(BF16)).astype(F32))
    scaler_two = inv_scale(resid)
    normed_two = (resid * scaler_two * gain_second).astype(BF16)

    logits = dot(normed_two, full_router)
    masked = jnp.where(mask, logits, NEG)
    raised = jnp.where(mask, jnp.exp(masked - jnp.max(masked, axis=1, keepdims=True)), 0.0)
    gates = raised / jnp.sum(raised, axis=1, keepdims=True)
    extra = jnp.concatenate(
        [gates.astype(BF16), mask.astype(BF16), jnp.zeros((rows, -2 * experts % 128), BF16)], axis=1)
    ext = jnp.concatenate([normed_two, extra], axis=1)
    return (
        normed_one, query, kv, full_qkv, full_out, full_up, full_down, cot_all, cotangent_pair, other_up, other_down,
        attended, attended_full, lse, resid, ext, gates, full_router.T, gain_first, gain_second, None)


def shards(
    tokens, cotangent, seq_lengths, piece_order, routes, norm1_gain, w_query, w_key, w_value, w_out,
    norm2_gain, w_router, shared_up, shared_down, expert_up, expert_down,
):
    blks = lax.axis_size("blk")
    h, b = lax.axis_index("head"), lax.axis_index("blk")
    rows, width = tokens.shape
    experts = blks
    capacity = rows * TOP * 4 // (3 * blks)
    dense_rows = w_query.shape[0]

    small = jnp.concatenate(
        [w_router, norm1_gain[:, None], norm2_gain[:, None],
         jnp.zeros((dense_rows, -(experts + 2) % 128), BF16)], axis=1)
    lanes = small.shape[1]
    places = jnp.swapaxes(piece_order.reshape(2, blks), 0, 1).reshape(-1)
    order = jnp.arange(2 * blks, dtype=jnp.int32)
    slots = jnp.sum(jnp.where(places[None, :] == order[:, None], order[None, :], 0), axis=1)
    where = (slots, lax.dynamic_slice_in_dim(places, 2 * b, 2), jnp.cumsum(seq_lengths))
    hot = routes[:, :, None] == jnp.arange(experts, dtype=jnp.int32)[None, None, :]
    mask = jnp.any(hot, axis=1)
    fits = blks == 16 and rows == 128 and 2 * capacity == 128 and width % 768 == 0 and dense_rows == 48
    front = front_fused if fits else front_plain
    (
        normed_one, query, kv, full_qkv, full_out, full_up, full_down, cot_all, cotangent_pair, other_up, other_down,
        attended, attended_full, lse, resid, ext, gates, router_rows, gain_first, gain_second, kept,
    ) = front(
        tokens, cotangent, where, mask, w_query, w_key, w_value, small, w_out, shared_up, shared_down,
        expert_up[0], expert_down[0], blks, 0)
    qw, kw = w_query.shape[1] // 2, w_key.shape[1] // 2
    shared_width = full_down.shape[0]
    inputs = tokens.astype(F32)
    if fits:
        (
            output, hidden_grad, mixed_grad, out_part, shared_up_part, shared_down_part, dup, dwn, row_part, _,
        ) = experts_fused(
            ext, (expert_up[0], other_up, expert_down[0], other_down), cot_all, (full_up, full_down), cotangent_pair,
            cotangent, resid, gates, kept[1], attended, full_out, blks, capacity, 3)
        query_grad, *kv_parts = attention_backward(query, kv, attended_full, lse, mixed_grad, where)
        (
            input_grad, w_query_grad, w_key_grad, w_value_grad, out_sum, up_grad, down_sum, small_sum, add_up, add_down,
        ) = tail_fused(
            *kv_parts, query_grad, normed_one, kept[0], tokens, hidden_grad, kept[1],
            out_part.reshape(blks, dense_rows, width),
            shared_up_part.reshape(2, blks, dense_rows, -1),
            shared_down_part.reshape(blks, -1, width), row_part, dup, dwn, blks, 6)
        size = width // 2
        expert_up_grad = lax.dynamic_slice_in_dim(dup, h * size, size, 0).astype(F32) + add_up.astype(F32)
        expert_down_grad = lax.dynamic_slice_in_dim(dwn, h * size, size, 1).astype(F32) + add_down.astype(F32)
        return (
            output, input_grad, small_sum[:, experts], w_query_grad, w_key_grad, w_value_grad,
            out_sum, small_sum[:, experts + 1], small_sum[:, :experts], up_grad, down_sum,
            expert_up_grad[None], expert_down_grad[None],
        )
    scaler_two = inv_scale(resid)
    normed_two = ext[:, :width]

    home, routed_sum, dup, dwn, normed_pair = experts_plain(
        ext, (expert_up[0], other_up, expert_down[0], other_down), cot_all, blks, capacity, 3)
    normed_pair = normed_pair.reshape(2 * rows, width)
    shared_both = dot(normed_pair, full_up)
    shared_gate, shared_lift = shared_both[:, :shared_width], shared_both[:, shared_width:]
    shared_act = (jax.nn.silu(shared_gate) * shared_lift).astype(BF16)
    shared_sum = dot(shared_act, full_down).reshape(2, rows, width)
    shared_down_part = dot_first(shared_act, cotangent_pair)
    shared_grad = gated_grad(dot_last(cotangent_pair, full_down), shared_gate, shared_lift)
    shared_up_part = dot_first(normed_pair, shared_grad)
    shared_back = dot_last(shared_grad, full_up).reshape(2, rows, width)
    output = (
        resid + routed_sum + pick(shared_sum, h) + swap(pick(shared_sum, 1 - h).astype(BF16)).astype(F32)
    ).astype(BF16)

    dgate = home[:, width : width + experts] + home[:, width + experts : width + 2 * experts]
    weighted = gates * dgate
    logit_grad = (weighted - gates * jnp.sum(weighted, axis=1, keepdims=True)).astype(BF16)
    norm_two_grad = (
        home[:, :width] + dot(logit_grad, router_rows)
        + pick(shared_back, h) + swap(pick(shared_back, 1 - h).astype(BF16)).astype(F32)
    )
    back, gain_two_part = norm_back(resid, scaler_two, gain_second, norm_two_grad)
    hidden_grad = cotangent.astype(F32) + back
    hidden_low = hidden_grad.astype(BF16)
    hidden_pair = pair(hidden_low, swap(hidden_low)).reshape(2 * rows, width)
    out_part = dot_first(attended, hidden_pair)
    mixed_grad = dot_last(hidden_pair, full_out).astype(BF16)
    query_grad, *kv_parts = attention_backward(query, kv, attended_full, lse, mixed_grad, where)
    router_part = dot_first(normed_two, logit_grad)
    dup, dwn, query_grad = lax.optimization_barrier((dup, dwn, query_grad))
    dup = dup.reshape(2, width // 2, -1)
    dwn = jnp.stack([dwn[:, : width // 2], dwn[:, width // 2 :]])
    expert_up_grad = pick(dup, h).astype(F32) + swap(pick(dup, 1 - h)).astype(F32)
    expert_down_grad = pick(dwn, h).astype(F32) + swap(pick(dwn, 1 - h)).astype(F32)
    kv_grads = reduce_scatter_blk([part.reshape(blks, 2 * rows, kw) for part in kv_parts], blks, 6, [BF16] * 2)
    qkv_grad = jnp.concatenate([query_grad, *kv_grads], axis=1)
    norm_one_part = dot_last(qkv_grad, full_qkv).reshape(2, rows, width)
    norm_one_grad = pick(norm_one_part, h) + swap(pick(norm_one_part, 1 - h).astype(BF16)).astype(F32)
    extra_grad, gain_one_part = norm_back(inputs, inv_scale(inputs), gain_first, norm_one_grad)
    input_grad = hidden_grad + extra_grad
    qkv_part = dot_first(normed_one, qkv_grad)
    small_part = jnp.concatenate(
        [router_part, gain_one_part[:, None], gain_two_part[:, None],
         jnp.zeros((width, lanes - experts - 2), F32)], axis=1)

    def by_rows(part):
        return part.astype(BF16).reshape(2, blks, dense_rows, -1)

    qkv_sum, up_sum, out_sum, down_sum, small_sum = reduce_scatter_blk(
        [by_rows(qkv_part), by_rows(shared_up_part),
         out_part.astype(BF16).reshape(blks, dense_rows, width),
         shared_down_part.astype(BF16).reshape(blks, -1, width), by_rows(small_part)],
        blks, 7, [BF16, BF16, F32, F32, F32])
    there = swap(jnp.concatenate([pick(qkv_sum, 1 - h), pick(up_sum, 1 - h)], axis=1)).astype(F32)
    here = jnp.concatenate([pick(qkv_sum, h), pick(up_sum, h)], axis=1).astype(F32)
    small_sum = pick(small_sum, h) + swap(pick(small_sum, 1 - h))

    def whole(start, size):
        return jnp.where(
            h == 0,
            jnp.concatenate([here[:, start : start + size], there[:, start : start + size]], axis=1),
            jnp.concatenate([there[:, start : start + size], here[:, start : start + size]], axis=1))

    top = qw + 2 * kw
    sw = shared_width
    up_grad = jnp.concatenate([whole(top, sw), whole(top + sw, sw)], axis=1)
    return (
        output, input_grad, small_sum[:, experts], whole(0, qw), whole(qw, kw), whole(qw + kw, kw),
        out_sum, small_sum[:, experts + 1], small_sum[:, :experts], up_grad, down_sum,
        expert_up_grad[None], expert_down_grad[None],
    )


def solution(mesh):
    both = P(("head", "blk"), None)
    flat = P(("head", "blk"))
    up, down = P("blk", "head", None), P("blk", None, "head")
    return jax.shard_map(
        shards,
        mesh=mesh,
        in_specs=(both, both, P(), P(), both, flat, both, both, both, both, flat, both, both, both, up, down),
        out_specs=(both, both, flat, both, both, both, both, flat, both, both, both, up, down),
        check_vma=False,
    )
```

```python
import functools

import jax
import jax.numpy as jnp
from jax import lax
from jax.experimental import pallas as pl
from jax.experimental.pallas import tpu as pltpu
from jax.sharding import PartitionSpec as P

MESH = pl.DeviceIdType.MESH


def ring_place(chip, chips):
    odd = chip % 2
    return (chip // 2) * (1 - odd) + (chips - 1 - chip // 2) * odd


def ring_chip(place, chips):
    high = place // (chips // 2)
    return 2 * place * (1 - high) + (2 * (chips - 1 - place) + 1) * high


def ring_info(chips):
    blk = lax.axis_index("blk")
    chip, core = blk // 2, blk % 2
    place = ring_place(chip, chips)

    def at(step):
        return ring_chip((place + step + chips) % chips, chips) * 2 + core

    return blk, core, at, blk + 1 - 2 * core


def pieces_of(shape):
    if len(shape) == 3:
        return [(0, None), (1, None)]
    rows = shape[0]
    if rows >= 32 and rows % 16 == 0:
        cut = (rows // 2 + 15) // 16 * 16
        return [(0, cut), (cut, rows - cut)]
    return [(0, rows)]


def part_in(ref, piece):
    start, size = piece
    return ref.at[start] if size is None else ref.at[pl.ds(start, size)]


def part_out(ref, piece, b):
    start, size = piece
    return ref.at[start, b] if size is None else ref.at[b, pl.ds(start, size)]


def ag_kernel(count, chips, plans, *refs):
    ins, outs = refs[:count], refs[count : 2 * count]
    right_sem, left_sem, sib_sem, sright, sleft, ssib, own_sem = refs[2 * count :]
    blk, core, at, sib = ring_info(chips)
    right, left = at(1), at(-1)
    barrier = pltpu.get_barrier_semaphore()
    for other in (right, left, sib):
        pl.semaphore_signal(barrier, inc=1, device_id={"blk": other}, device_id_type=MESH)
    pl.semaphore_wait(barrier, 3)
    half = chips // 2
    started = []

    def send(src, dst, ssem, rsem, dev):
        copy = pltpu.make_async_remote_copy(
            src_ref=src, dst_ref=dst, send_sem=ssem, recv_sem=rsem,
            device_id={"blk": dev}, device_id_type=MESH)
        copy.start()
        started.append(copy)
        return copy

    chunks = []
    for k in range(count):
        for i, piece in enumerate(plans[k]):
            chunks.append((len(chunks), k, piece, half - (i % 2), half - 1 + (i % 2)))
    copies = {}
    locals_ = []
    for c, k, piece, rh, lh in chunks:
        src = part_in(ins[k], piece)
        dst = part_out(outs[k], piece, blk)
        if rh >= 1:
            copies[c, "r", 1] = send(src, dst, sright.at[c, 0], right_sem.at[c, 0], right)
        if lh >= 1:
            copies[c, "l", 1] = send(src, dst, sleft.at[c, 0], left_sem.at[c, 0], left)
        copies[c, "s", 0] = send(src, dst, ssib.at[c, 0], sib_sem.at[c, 0], sib)
        own = pltpu.make_async_copy(src, dst, own_sem.at[c])
        own.start()
        locals_.append(own)
    for s in range(1, half + 1):
        for c, k, piece, rh, lh in chunks:
            if s <= rh:
                copies[c, "r", s].wait_recv()
                b = at(-s)
                blockref = part_out(outs[k], piece, b)
                if s < rh:
                    copies[c, "r", s + 1] = send(blockref, blockref, sright.at[c, s], right_sem.at[c, s], right)
                copies[c, "sr", s] = send(blockref, blockref, ssib.at[c, s], sib_sem.at[c, s], sib)
            if s <= lh:
                copies[c, "l", s].wait_recv()
                b = at(s)
                blockref = part_out(outs[k], piece, b)
                if s < lh:
                    copies[c, "l", s + 1] = send(blockref, blockref, sleft.at[c, s], left_sem.at[c, s], left)
                copies[c, "sl", s] = send(blockref, blockref, ssib.at[c, half + s], sib_sem.at[c, half + s], sib)
    for (c, d, s), copy in copies.items():
        if d in ("s", "sr", "sl"):
            copy.wait_recv()
    for copy in started:
        copy.wait_send()
    for copy in locals_:
        copy.wait()


def all_gather_blk(arrays, blks, collective_id, vmem=False):
    chips = blks // 2
    count = len(arrays)
    plans = [pieces_of(a.shape) for a in arrays]
    n = sum(len(p) for p in plans)
    half = chips // 2
    shapes = [
        jax.ShapeDtypeStruct((a.shape[0], blks) + a.shape[1:] if a.ndim == 3 else (blks,) + a.shape, a.dtype)
        for a in arrays
    ]
    dma = pltpu.SemaphoreType.DMA
    space = pltpu.VMEM if vmem else pl.ANY
    return pl.pallas_call(
        functools.partial(ag_kernel, count, chips, plans),
        out_shape=shapes,
        in_specs=[pl.BlockSpec(memory_space=space)] * count,
        out_specs=[pl.BlockSpec(memory_space=space)] * count,
        scratch_shapes=[
            dma((n, half)), dma((n, half)), dma((n, 2 * half + 1)),
            dma((n, half)), dma((n, half)), dma((n, 2 * half + 1)), dma((n,)),
        ],
        compiler_params=pltpu.CompilerParams(collective_id=collective_id, has_side_effects=True,
            vmem_limit_bytes=(60 << 20) if vmem else None),
    )(*arrays)


def rs_kernel(count, chips, plans, *refs):
    xs, outs = refs[:count], refs[count : 2 * count]
    rest = refs[2 * count :]
    n = sum(len(p) for p in plans)
    ys, rs, ls = rest[:n], rest[n : 2 * n], rest[2 * n : 3 * n]
    right_sem, left_sem, sib_sem, sright, sleft, ssib = rest[3 * n :]
    blk, core, at, sib = ring_info(chips)
    right, left = at(1), at(-1)
    barrier = pltpu.get_barrier_semaphore()
    for other in (right, left, sib):
        pl.semaphore_signal(barrier, inc=1, device_id={"blk": other}, device_id_type=MESH)
    pl.semaphore_wait(barrier, 3)
    half = chips // 2
    started = []

    def send(src, dst, ssem, rsem, dev):
        copy = pltpu.make_async_remote_copy(
            src_ref=src, dst_ref=dst, send_sem=ssem, recv_sem=rsem,
            device_id={"blk": dev}, device_id_type=MESH)
        copy.start()
        started.append(copy)
        return copy

    chunks = []
    for k in range(count):
        for i, piece in enumerate(plans[k]):
            chunks.append((len(chunks), k, piece, half - (i % 2), half - 1 + (i % 2)))
    order = []
    for d in range(half, 0, -1):
        order += [d, -d] if d < half else [d]
    order.append(0)
    sibs = {}
    for j, d in enumerate(order):
        there = at(d) + 1 - 2 * core
        for c, k, piece, rh, lh in chunks:
            sibs[c, d] = send(part_out(xs[k], piece, there), ys[c].at[j], ssib.at[c, j], sib_sem.at[c, j], sib)
    ready = set()

    def blocks(rows, body):
        step = 16 if rows % 16 == 0 else rows

        @pl.loop(0, rows // step)
        def _(i):
            body(pl.ds(pl.multiple_of(i * step, step), step))

    def mine(c, k, piece, d):
        j = order.index(d)
        if (c, d) not in ready:
            sibs[c, d].wait_recv()
            ready.add((c, d))
        return j

    copies = {}

    def join(c, k, piece, d, into, recv):
        j = mine(c, k, piece, d)
        x = part_out(xs[k], piece, at(d))
        rows = x.shape[0]

        def body(w):
            total = x[w].astype(jnp.float32) + ys[c][j, w].astype(jnp.float32)
            if recv is not None:
                total = total + recv[w].astype(jnp.float32)
            into[w] = total.astype(into.dtype)

        blocks(rows, body)

    for s in range(1, half + 1):
        for c, k, piece, rh, lh in chunks:
            for way, hops, buf, sem, ssem, dev in (
                (1, rh, rs[c], right_sem, sright, right),
                (-1, lh, ls[c], left_sem, sleft, left),
            ):
                if s > hops:
                    continue
                if s == 1:
                    j = order.index(way * hops if way * hops in order else hops)
                    join(c, k, piece, order[j], ys[c].at[j], None)
                    src = ys[c].at[j]
                else:
                    copies[c, way, s - 1].wait_recv()
                    d = way * (hops - s + 1)
                    src = buf.at[s - 2]
                    join(c, k, piece, d, src, src)
                copies[c, way, s] = send(src, buf.at[s - 1], ssem.at[c, s - 1], sem.at[c, s - 1], dev)
    for c, k, piece, rh, lh in chunks:
        if rh >= 1:
            copies[c, 1, rh].wait_recv()
        if lh >= 1:
            copies[c, -1, lh].wait_recv()
        j = mine(c, k, piece, 0)
        x = part_out(xs[k], piece, blk)
        target = part_in(outs[k], piece)

        def body(w, x=x, c=c, j=j, rh=rh, lh=lh, target=target):
            total = x[w].astype(jnp.float32) + ys[c][j, w].astype(jnp.float32)
            if rh >= 1:
                total = total + rs[c][rh - 1, w].astype(jnp.float32)
            if lh >= 1:
                total = total + ls[c][lh - 1, w].astype(jnp.float32)
            target[w] = total.astype(target.dtype)

        blocks(x.shape[0], body)
    for copy in started:
        copy.wait_send()


def reduce_scatter_blk(arrays, blks, collective_id, out_dtypes):
    chips = blks // 2
    half = chips // 2
    count = len(arrays)
    shapes = [a.shape[1:] if a.ndim == 3 else (2,) + a.shape[2:] for a in arrays]
    plans = [pieces_of(s) for s in shapes]
    dma = pltpu.SemaphoreType.DMA
    ys, rs = [], []
    for s, plan in zip(shapes, plans):
        for start, size in plan:
            rows = s[1] if size is None else size
            ys.append(pltpu.VMEM((chips, rows, s[-1]), jnp.bfloat16))
            rs.append(pltpu.VMEM((half, rows, s[-1]), jnp.bfloat16))
    n = len(ys)
    return pl.pallas_call(
        functools.partial(rs_kernel, count, chips, plans),
        out_shape=[jax.ShapeDtypeStruct(s, t) for s, t in zip(shapes, out_dtypes)],
        in_specs=[pl.BlockSpec(memory_space=pltpu.VMEM)] * count,
        out_specs=[pl.BlockSpec(memory_space=pltpu.VMEM)] * count,
        scratch_shapes=ys + rs + rs + [
            dma((n, half)), dma((n, half)), dma((n, chips)),
            dma((n, half)), dma((n, half)), dma((n, chips)),
        ],
        compiler_params=pltpu.CompilerParams(collective_id=collective_id, has_side_effects=True,
            vmem_limit_bytes=60 << 20),
    )(*arrays)


H = 12
KVH = 4
HD = 128
TOP = 6
PIECE = 128
EPS = 1e-05
NEG = -1e30
F32 = jnp.float32
BF16 = jnp.bfloat16


def dot(a, b):
    return jnp.dot(a, b, preferred_element_type=F32)


def dot_first(a, b):
    return lax.dot_general(a, b, (((0,), (0,)), ((), ())), preferred_element_type=F32)


def dot_last(a, b):
    return lax.dot_general(a, b, (((1,), (1,)), ((), ())), preferred_element_type=F32)


def inv_scale(values):
    return lax.rsqrt(jnp.mean(values * values, axis=1, keepdims=True) + EPS)


def norm_back(values, scaler, gain, upstream):
    normed = values * scaler
    gain_grad = jnp.sum(upstream * normed, axis=0)
    scaled = upstream * gain
    grad = scaler * (scaled - normed * jnp.mean(scaled * normed, axis=1, keepdims=True))
    return grad, gain_grad


def gated_grad(act_grad, gate, lift):
    sig = jax.nn.sigmoid(gate)
    return jnp.concatenate(
        [act_grad * lift * sig * (1.0 + gate * (1.0 - sig)), act_grad * gate * sig], axis=1
    ).astype(BF16)


def swap(array):
    return lax.ppermute(array, "head", [(0, 1), (1, 0)])


def key_span(places_ref, ends_ref, i):
    place = places_ref[i]
    start = jnp.int32(0)
    for e in range(ends_ref.shape[0]):
        start = jnp.where(ends_ref[e] <= place * PIECE, ends_ref[e], start)
    return start // PIECE, place


def key_chunk(slots_ref, first, pieces, *refs):
    last = slots_ref.shape[0] - 1
    slots = [slots_ref[jnp.clip(first + k, 0, last)] for k in range(pieces)]
    return slots, [jnp.concatenate([ref[s] for s in slots], axis=0) for ref in refs]


def stacked(ref, i, repeats):
    return jnp.concatenate(
        [ref[pl.ds(i * PIECE, PIECE), pl.ds(r * HD, HD)] for r in range(repeats)], axis=0)


def seen(ends_ref, place, first, keys, cols):
    own = place * PIECE + lax.broadcasted_iota(jnp.int32, (1, cols), 1) % PIECE
    start = jnp.zeros((1, cols), jnp.int32)
    for e in range(ends_ref.shape[0]):
        start = jnp.where(ends_ref[e] <= own, ends_ref[e], start)
    there = first * PIECE + lax.broadcasted_iota(jnp.int32, (keys, 1), 0)
    return (there <= own) & (there >= start)


CHUNK = 4


def forward_kernel(repeats, slots_ref, places_ref, ends_ref, q_ref, k_ref, v_ref, low_ref, full_ref, lse_ref):
    cols = repeats * PIECE
    for i in range(q_ref.shape[0] // PIECE):
        lo, place = key_span(places_ref, ends_ref, i)
        q = stacked(q_ref, i, repeats)

        def step(n, carry, lo=lo, place=place, q=q):
            top, total, acc = carry
            first = lo + n * CHUNK
            _, (k, v) = key_chunk(slots_ref, first, CHUNK, k_ref, v_ref)
            scores = dot_last(k, q) * HD**-0.5
            scores = jnp.where(seen(ends_ref, place, first, CHUNK * PIECE, cols), scores, NEG)
            new = jnp.maximum(top, jnp.max(scores, axis=0, keepdims=True))
            weights = jnp.exp(scores - new)
            factor = jnp.exp(top - new)
            total = total * factor + jnp.sum(weights, axis=0, keepdims=True)
            return new, total, acc * factor + dot_first(v, weights.astype(BF16))

        top, total, acc = lax.fori_loop(
            0, (place - lo) // CHUNK + 1, step,
            (jnp.full((1, cols), NEG, F32), jnp.zeros((1, cols), F32), jnp.zeros((HD, cols), F32)))
        out = jnp.swapaxes(acc / total, 0, 1)
        lse_ref[0, pl.ds(i, 1), :] = top + jnp.log(total)
        for r in range(repeats):
            part = out[r * PIECE : (r + 1) * PIECE]
            full_ref[pl.ds(i * PIECE, PIECE), pl.ds(r * HD, HD)] = part
            low_ref[pl.ds(i * PIECE, PIECE), pl.ds(r * HD, HD)] = part.astype(BF16)


def attention_forward(query, kv, where):
    rows, pieces = query.shape[0], kv.shape[0]
    groups = kv.shape[2] // (2 * HD)
    wide = query.shape[1] // groups
    repeats = wide // HD
    spec = pl.BlockSpec((rows, wide), lambda g, *_: (0, g))
    return pl.pallas_call(
        functools.partial(forward_kernel, repeats),
        grid_spec=pltpu.PrefetchScalarGridSpec(
            num_scalar_prefetch=3,
            grid=(groups,),
            in_specs=[
                spec,
                pl.BlockSpec((pieces, PIECE, HD), lambda g, *_: (0, 0, g)),
                pl.BlockSpec((pieces, PIECE, HD), lambda g, *_: (0, 0, groups + g)),
            ],
            out_specs=[spec, spec, pl.BlockSpec((1, rows // PIECE, repeats * PIECE), lambda g, *_: (g, 0, 0))],
        ),
        out_shape=[
            jax.ShapeDtypeStruct(query.shape, BF16),
            jax.ShapeDtypeStruct(query.shape, F32),
            jax.ShapeDtypeStruct((groups, rows // PIECE, repeats * PIECE), F32),
        ],
        compiler_params=pltpu.CompilerParams(vmem_limit_bytes=48 << 20),
    )(*where, query, kv, kv)


def backward_kernel(
    repeats, slots_ref, places_ref, ends_ref, q_ref, k_ref, v_ref, full_ref, grad_ref, lse_ref,
    dq_ref, dk_ref, dv_ref, key_acc, value_acc,
):
    cols = repeats * PIECE
    key_acc[...] = jnp.zeros_like(key_acc)
    value_acc[...] = jnp.zeros_like(value_acc)
    for i in range(q_ref.shape[0] // PIECE):
        lo, place = key_span(places_ref, ends_ref, i)
        q, grad = stacked(q_ref, i, repeats), stacked(grad_ref, i, repeats)
        product = grad.astype(F32) * stacked(full_ref, i, repeats)
        delta = jnp.sum(jnp.swapaxes(product, 0, 1), axis=0, keepdims=True)
        lse = lse_ref[0, pl.ds(i, 1), :]

        def step(n, dq, lo=lo, place=place, q=q, grad=grad, delta=delta, lse=lse):
            first = lo + n * CHUNK
            slots, (k, v) = key_chunk(slots_ref, first, CHUNK, k_ref, v_ref)
            scores = dot_last(k, q) * HD**-0.5
            weights = jnp.where(
                seen(ends_ref, place, first, CHUNK * PIECE, cols), jnp.exp(scores - lse), 0.0)
            back = (weights * (dot_last(v, grad) - delta)).astype(BF16)
            dk = dot(back, q)
            dv = dot(weights.astype(BF16), grad)
            for j, s in enumerate(slots):
                key_acc[s] += dk[j * PIECE : (j + 1) * PIECE]
                value_acc[s] += dv[j * PIECE : (j + 1) * PIECE]
            return dq + dot_first(k, back)

        dq = lax.fori_loop(0, (place - lo) // CHUNK + 1, step, jnp.zeros((HD, cols), F32))
        out = (jnp.swapaxes(dq, 0, 1) * HD**-0.5).astype(BF16)
        for r in range(repeats):
            dq_ref[pl.ds(i * PIECE, PIECE), pl.ds(r * HD, HD)] = out[r * PIECE : (r + 1) * PIECE]
    dk_ref[...] = (key_acc[...] * HD**-0.5).astype(BF16)
    dv_ref[...] = value_acc[...].astype(BF16)


def attention_backward(query, kv, full, lse, grad, where):
    rows, pieces = query.shape[0], kv.shape[0]
    groups = kv.shape[2] // (2 * HD)
    wide = query.shape[1] // groups
    repeats = wide // HD
    spec = pl.BlockSpec((rows, wide), lambda g, *_: (0, g))
    block = pl.BlockSpec((pieces, PIECE, HD), lambda g, *_: (0, 0, g))
    half = jax.ShapeDtypeStruct((pieces, PIECE, groups * HD), BF16)
    return pl.pallas_call(
        functools.partial(backward_kernel, repeats),
        grid_spec=pltpu.PrefetchScalarGridSpec(
            num_scalar_prefetch=3,
            grid=(groups,),
            in_specs=[
                spec, block, pl.BlockSpec((pieces, PIECE, HD), lambda g, *_: (0, 0, groups + g)), spec, spec,
                pl.BlockSpec((1, rows // PIECE, repeats * PIECE), lambda g, *_: (g, 0, 0)),
            ],
            out_specs=[spec, block, block],
            scratch_shapes=[pltpu.VMEM((pieces, PIECE, HD), F32)] * 2,
        ),
        out_shape=[jax.ShapeDtypeStruct(query.shape, BF16), half, half],
        compiler_params=pltpu.CompilerParams(vmem_limit_bytes=60 << 20),
    )(*where, query, kv, kv, full, grad, lse)


def tiles(total, size, body):
    if total == size:
        body(pl.ds(0, size))
    else:

        @pl.loop(0, total // size)
        def _(i):
            body(pl.ds(pl.multiple_of(i * size, size), size))


def shifted(c, by):
    if isinstance(c.start, int):
        return pl.ds(c.start + by, c.size)
    return pl.ds(pl.multiple_of(c.start + by, c.size), c.size)


def expert_kernel(
    chips, experts, ext_ref, up_own, up_other, down_own, down_other, cot_ref,
    shared_up, shared_down, cot_pair, cot_own, resid, gates, turned, low, full_out,
    output, hidden_grad, mixed_grad, out_part, up_part, down_part, din, dout, row_part, norm_pair, other_down,
    home_ref, routed_ref, din_ref, dout_ref, shared_act, shared_dab, hid, from_back, from_sum,
    in_ref, out_ref, ext, cot, rows_x, rows_dy, rows_act, rows_dab, both, result, back, deal, gate, take, take_gate,
    own_d, own_o, stage_d, stage_o, sib_d, sib_o, right_d, right_o, left_d, left_o,
    copy_sem, cot_sem, ag_r, ag_l, ag_sr, ag_sl, ss_r, ss_l, ss_sr, ss_sl,
    ex_sem, ss_ex, rs_r, rs_l, ss_rr, ss_rl, weight_sem, pair_sem, load_sem, y_send, y_recv,
):
    blk, core, at, sib = ring_info(chips)
    h = lax.axis_index("head")
    right, left = at(1), at(-1)
    half = chips // 2
    rows, wide = ext_ref.shape
    width = in_ref.shape[0]
    hidden = out_ref.shape[0]
    slots = rows_x.shape[0] // chips
    cut = rows // 2
    upper, lower = pl.ds(0, cut), pl.ds(cut, cut)

    barrier = pltpu.get_barrier_semaphore()
    for other in (right, left, sib):
        pl.semaphore_signal(barrier, inc=1, device_id={"blk": other}, device_id_type=MESH)
    pl.semaphore_signal(barrier, inc=1, device_id={"head": 1 - h}, device_id_type=MESH)
    pl.semaphore_wait(barrier, 4)

    def remote(src, dst, ssem, rsem, dev):
        return pltpu.make_async_remote_copy(
            src_ref=src, dst_ref=dst, send_sem=ssem, recv_sem=rsem,
            device_id={"blk": dev}, device_id_type=MESH)

    def hop_right(part, k, s):
        ref = ext.at[at(1 - s), part]
        return remote(ref, ref, ss_r.at[k, s], ag_r.at[k, s], right)

    def hop_left(part, k, s):
        ref = ext.at[at(s - 1), part]
        return remote(ref, ref, ss_l.at[k, s], ag_l.at[k, s], left)

    def over_right(part, k, s):
        ref = ext.at[at(-s), part]
        return remote(ref, ref, ss_sr.at[k, s], ag_sr.at[k, s], sib)

    def over_left(part, k, s):
        ref = ext.at[at(s), part]
        return remote(ref, ref, ss_sl.at[k, s], ag_sl.at[k, s], sib)

    def place_of(g, j):
        return at(-g) if j == 0 else at(g)

    def cot_copy(g, j):
        there = place_of(g, j)
        slot = lax.rem(g, 2)
        return pltpu.make_async_copy(
            cot_ref.at[pl.ds(there - core, 2)], cot.at[slot, j], cot_sem.at[slot, j])

    def exchange_d(g, j):
        return remote(stage_d.at[j], sib_d.at[lax.div(place_of(g, j), 2)], ss_ex.at[0, j, g], ex_sem.at[0, j, g], sib)

    def exchange_o(g, j):
        return remote(stage_o.at[j], sib_o.at[lax.div(place_of(g, j), 2)], ss_ex.at[1, j, g], ex_sem.at[1, j, g], sib)

    mine = pltpu.make_async_copy(ext_ref, ext.at[blk], copy_sem)
    mine.start()
    cot_copy(0, 0).start()
    weights = []
    for i, (up, down) in ((h, (up_own, down_own)), (1 - h, (up_other, down_other))):
        size = up.shape[0]
        start = pl.multiple_of(i * size, size)
        weights.append((up, in_ref.at[pl.ds(start, size)]))
        weights.append((down, out_ref.at[:, pl.ds(start, size)]))
    weights = [pltpu.make_async_copy(a, b, weight_sem.at[i]) for i, (a, b) in enumerate(weights)]
    for copy in weights:
        copy.start()
    mine.wait()
    for k, part in ((0, upper), (1, lower)):
        hop_right(part, k, 1).start()
        hop_left(part, k, 1).start()
        over_right(part, k, 0).start()
    own_norm = ext.at[blk, :, pl.ds(0, width)]
    keep = pltpu.make_async_copy(own_norm, norm_pair.at[h], pair_sem.at[0])
    keep.start()
    swapped = pltpu.make_async_remote_copy(
        src_ref=own_norm, dst_ref=norm_pair.at[h], send_sem=pair_sem.at[1], recv_sem=pair_sem.at[2],
        device_id={"head": 1 - h}, device_id_type=MESH)
    swapped.start()
    for copy in weights:
        copy.wait()

    lane = lax.broadcasted_iota(jnp.int32, (2 * rows, 128), 1)
    token_row = lax.broadcasted_iota(jnp.int32, (2 * rows, 2 * rows), 0)
    token_col = lax.broadcasted_iota(jnp.int32, (2 * rows, 2 * rows), 1)
    same = (token_row < rows) == (token_col < rows)
    triangle = jnp.where((token_row > token_col) & same, 1.0, 0.0).astype(BF16)
    offset = jnp.float32(slots // 2)
    shift_col = jnp.where(lax.broadcasted_iota(jnp.int32, (2 * rows, 1), 0) < rows, 0.0, offset)
    shift_row = jnp.where(lax.broadcasted_iota(jnp.int32, (1, 2 * rows), 1) < rows, 0.0, offset)
    slot_id = lax.broadcasted_iota(jnp.int32, (slots, 2 * rows), 0).astype(F32)
    lane_row = lax.broadcasted_iota(jnp.int32, (128, 128), 0)
    pick_mask = jnp.where(lane_row == experts + blk, 1.0, 0.0).astype(BF16)
    pick_gate = jnp.where(lane_row == blk, 1.0, 0.0).astype(BF16)
    lane_col = lax.broadcasted_iota(jnp.int32, (8, 128), 1)
    mask_row = jnp.where(lane_col == experts + blk, 1.0, 0.0).astype(BF16)
    gate_row = jnp.where(lane_col == blk, 1.0, 0.0).astype(BF16)

    def arrive(s):
        last = isinstance(s, int) and s == half
        hop_right(upper, 0, s).wait_recv()
        if not last:
            hop_right(upper, 0, s + 1).start()
        over_right(upper, 0, s).start()
        hop_left(lower, 1, s).wait_recv()
        if not last:
            hop_left(lower, 1, s + 1).start()
        over_left(lower, 1, s).start()
        if last:
            return
        hop_right(lower, 1, s).wait_recv()

        @pl.when(s < half - 1)
        def _():
            hop_right(lower, 1, s + 1).start()

        over_right(lower, 1, s).start()
        hop_left(upper, 0, s).wait_recv()

        @pl.when(s < half - 1)
        def _():
            hop_left(upper, 0, s + 1).start()

        over_left(upper, 0, s).start()

    def work(g, count, base, first):
        turn = lax.rem(g, 2)
        size = count * slots
        group = pl.ds(base, size)
        part = pl.ds(0, size)
        firsts = [place_of(g, j) - core for j in range(count)]
        for j in range(count):
            lanes = ext[pl.ds(firsts[j], 2), :, pl.ds(width, 128)].reshape(2 * rows, 128)
            chosen = dot(lanes, pick_mask)
            rank = dot(triangle, chosen.astype(BF16))
            spread = jnp.where((rank + shift_col == lane.astype(F32)) & (chosen > 0.5), 1.0, 0.0).astype(BF16)
            deal[j] = spread.reshape(2, rows, 128)
            gate[j] = dot(lanes, pick_gate).reshape(2, rows, 128)
            chosen_row = dot_last(mask_row, lanes)
            rank_row = dot_last(chosen_row.astype(BF16), triangle)
            weight_row = dot_last(gate_row, lanes)
            taken = jnp.where((rank_row[:1] + shift_row == slot_id) & (chosen_row[:1] > 0.5), 1.0, 0.0)
            take[j] = taken.astype(BF16)
            take_gate[j] = (taken * weight_row[:1]).astype(BF16)
        for j in range(count):
            cot_copy(g, j).wait()
            where = pl.ds(pl.multiple_of(base + j * slots, slots), slots)

            def pick_rows(c, j=j, where=where):
                rows_x[where, c] = dot(
                    take[j], ext[pl.ds(firsts[j], 2), :, c].reshape(2 * rows, c.size)).astype(BF16)
                rows_dy[where, c] = dot(take_gate[j], cot[turn, j, :, :, c].reshape(2 * rows, c.size)).astype(BF16)

            for t in range(2):
                pick_rows(pl.ds(t * (width // 2), width // 2))

        def hidden_tile(c):
            high = shifted(c, hidden)
            x = rows_x[group]
            gate_part = dot(x, in_ref[:, c])
            lift = dot(x, in_ref[:, high])
            both[part, c] = gate_part
            both[part, high] = lift
            rows_act[group, c] = (jax.nn.silu(gate_part) * lift).astype(BF16)

        for t in range(2):
            hidden_tile(pl.ds(t * (hidden // 2), hidden // 2))

        def result_tile(c):
            result[part, c] = dot(rows_act[group], out_ref[:, c]).astype(BF16)

        for t in range(2):
            result_tile(pl.ds(t * (width // 2), width // 2))

        def grad_tile(c):
            high = shifted(c, hidden)
            da = dot_last(rows_dy[group], out_ref[c, :])
            gate_part, lift = both[part, c], both[part, high]
            sig = jax.nn.sigmoid(gate_part)
            rows_dab[group, c] = (da * lift * sig * (1.0 + gate_part * (1.0 - sig))).astype(BF16)
            rows_dab[group, high] = (da * gate_part * sig).astype(BF16)

        for t in range(2):
            grad_tile(pl.ds(t * (hidden // 2), hidden // 2))

        def back_tile(c):
            back[part, c] = dot_last(rows_dab[group], in_ref[c, :]).astype(BF16)

        for t in range(2):
            back_tile(pl.ds(t * (width // 2), width // 2))
        if first is not None:

            @pl.when(first)
            def _():
                for j in range(2):
                    exchange_d(g - 1, j).wait_send()
                    exchange_o(g - 1, j).wait_send()

            @pl.when(jnp.logical_not(first))
            def _():
                exchange_d(g - 1, 0).wait_send()
                exchange_o(g - 1, 0).wait_send()

        for j in range(count):
            chip = lax.div(firsts[j], 2)
            for which, to_d, to_o in (
                (core, own_d.at[chip], own_o.at[chip]),
                (1 - core, stage_d.at[j], stage_o.at[j]),
            ):
                from_slots = pl.ds(j * slots, slots)
                dealer = deal[j, which]
                share = gate[j, which]
                total = jnp.zeros((rows, 1), F32)
                for t in range(width // 512):
                    c = pl.ds(t * 512, 512)
                    home_rows = dot(dealer, result[from_slots, c])
                    to_o[:, c] = (home_rows * share[:, :1]).astype(BF16)
                    total = total + jnp.sum(
                        home_rows * cot[turn, j, which, :, c].astype(F32), axis=1, keepdims=True)
                    to_d[:, c] = dot(dealer, back[from_slots, c]).astype(BF16)
                high = total.astype(BF16).astype(F32)
                own_lane = lane[:rows]
                lanes = jnp.where(own_lane == blk, high, jnp.where(own_lane == experts + blk, total - high, 0.0))
                to_d[:, pl.ds(width, 128)] = lanes.astype(BF16)
            exchange_d(g, j).start()
            exchange_o(g, j).start()

    over_right(upper, 0, 0).wait_recv()
    over_right(lower, 1, 0).wait_recv()
    cot_copy(1, 0).start()
    cot_copy(1, 1).start()
    work(0, 1, 0, None)

    @pl.loop(1, half)
    def _(g):
        arrive(g)
        over_right(upper, 0, g).wait_recv()
        over_right(lower, 1, g).wait_recv()
        over_left(lower, 1, g).wait_recv()
        over_left(upper, 0, g).wait_recv()
        cot_copy(g + 1, 0).start()

        @pl.when(g < half - 1)
        def _():
            cot_copy(g + 1, 1).start()

        work(g, 2, pl.multiple_of(slots + (g - 1) * 2 * slots, slots), g > 1)

    arrive(half)
    over_right(upper, 0, half).wait_recv()
    over_left(lower, 1, half).wait_recv()
    work(half, 1, (2 * half - 1) * slots, True)

    arrays = ((0, own_d, sib_d, right_d, left_d, home_ref), (1, own_o, sib_o, right_o, left_o, routed_ref))
    arrived = set()

    def join(a, own, other, d, part, into, received):
        g, j = (d, 1) if 0 < d < half else (abs(d), 0)
        if (a, g, j) not in arrived:
            arrived.add((a, g, j))
            (exchange_d, exchange_o)[a](g, j).wait_recv()
        chip = lax.div(at(d), 2)

        def add(c):
            total = own[chip, c].astype(F32) + other[chip, c].astype(F32)
            for ref in received:
                total = total + ref[c].astype(F32)
            into[c] = total.astype(into.dtype)

        @pl.loop(0, cut // 16)
        def _(i):
            add(pl.ds(pl.multiple_of(part.start + i * 16, 16), 16))

    def pass_right(a, src, buf, k, part, s):
        return remote(src.at[part], buf.at[s - 1, part], ss_rr.at[a, k, s], rs_r.at[a, k, s], right)

    def pass_left(a, src, buf, k, part, s):
        return remote(src.at[part], buf.at[s - 1, part], ss_rl.at[a, k, s], rs_l.at[a, k, s], left)

    ways = (
        (0, upper, 1, half), (1, lower, -1, half), (1, lower, 1, half - 1), (0, upper, -1, half - 1),
    )
    sent = []

    def scatter_step(a, s):
        _, own, other, to_right, to_left, _ = arrays[a]
        for k, part, way, hops in ways:
            if s > hops:
                continue
            make, buf = (pass_right, to_right) if way > 0 else (pass_left, to_left)
            d = way * (hops - s + 1)
            if d == -half:
                d = half
            if s == 1:
                src = own.at[lax.div(at(d), 2)]
                join(a, own, other, d, part, src, ())
            else:
                src = buf.at[s - 2]
                make(a, src, buf, k, part, s - 1).wait_recv()
                join(a, own, other, d, part, src, (src,))
            copy = make(a, src, buf, k, part, s)
            copy.start()
            sent.append(copy)

    def scatter_finish(a):
        _, own, other, to_right, to_left, into = arrays[a]
        for k, part in ((0, upper), (1, lower)):
            last_right, last_left = half - k, half - 1 + k
            pass_right(a, own.at[0], to_right, k, part, last_right).wait_recv()
            pass_left(a, own.at[0], to_left, k, part, last_left).wait_recv()
            join(a, own, other, 0, part, into, (to_right.at[last_right - 1], to_left.at[last_left - 1]))

    loads = 0

    def move(src, dst):
        nonlocal loads
        copy = pltpu.make_async_copy(src, dst, load_sem.at[loads])
        loads += 1
        copy.start()
        return copy

    def cross(i, src, dst):
        return pltpu.make_async_remote_copy(
            src_ref=src, dst_ref=dst, send_sem=y_send.at[i], recv_sem=y_recv.at[i],
            device_id={"head": 1 - h}, device_id_type=MESH)

    theirs = pl.ds(pl.multiple_of((1 - h) * rows, rows), rows)
    ours = pl.ds(pl.multiple_of(h * rows, rows), rows)
    keep.wait()
    swapped.wait()
    shared_loads = [
        move(shared_up, in_ref), move(shared_down, out_ref), move(cot_pair, back),
        move(norm_pair.at[0], result.at[pl.ds(0, rows)]), move(norm_pair.at[1], result.at[pl.ds(rows, rows)])]
    scatter_step(0, 1)

    def weight_in(c):
        din_ref[c, :] = dot_first(rows_x[:, c], rows_dab[...]).astype(BF16)

    tiles(width, 256, weight_in)
    din_out = move(din_ref, din)
    load_out = move(full_out, rows_x.at[pl.ds(0, low.shape[1])])
    scatter_step(0, 2)
    scatter_step(1, 1)

    for copy in shared_loads:
        copy.wait()

    def shared_tile(c):
        high = shifted(c, hidden)
        gate_part = dot(result[...], in_ref[:, c])
        lift = dot(result[...], in_ref[:, high])
        sig = jax.nn.sigmoid(gate_part)
        shared_act[:, c] = (gate_part * sig * lift).astype(BF16)
        da = dot_last(back[...], out_ref[c, :])
        shared_dab[:, c] = (da * lift * sig * (1.0 + gate_part * (1.0 - sig))).astype(BF16)
        shared_dab[:, high] = (da * gate_part * sig).astype(BF16)

    tiles(hidden, 256, shared_tile)
    to_back, to_sum = cot.at[0, 0, 0], cot.at[0, 0, 1]

    def back_part(c):
        to_back[:, c] = dot_last(shared_dab[theirs, :], in_ref[c, :]).astype(BF16)

    tiles(width, 512, back_part)
    swap_back = cross(0, to_back, from_back)
    swap_back.start()

    def weight_out(c):
        dout_ref[c, :] = dot_first(rows_act[:, c], rows_dy[...]).astype(BF16)

    tiles(hidden, 256, weight_out)
    dout_out = move(dout_ref, dout)
    scatter_step(0, 3)
    scatter_step(1, 2)

    def sum_part(c):
        to_sum[:, c] = dot(shared_act[theirs, :], out_ref[:, c]).astype(BF16)

    tiles(width, 512, sum_part)
    swap_sum = cross(1, to_sum, from_sum)
    swap_sum.start()
    din_out.wait()
    dout_out.wait()
    swap_down = cross(3, dout.at[:, pl.ds(pl.multiple_of((1 - h) * (width // 2), 128), width // 2)], other_down)
    swap_down.start()

    def shared_in(c):
        din_ref[c, :] = dot_first(result[:, c], shared_dab[...]).astype(BF16)

    tiles(width, 256, shared_in)
    up_out = move(din_ref, up_part)
    scatter_step(0, 4)
    scatter_step(1, 3)

    def shared_out(c):
        dout_ref[c, :] = dot_first(shared_act[:, c], back[...]).astype(BF16)

    tiles(hidden, 256, shared_out)
    down_out = move(dout_ref, down_part)
    swap_back.wait_recv()
    scatter_finish(0)

    lanes = home_ref[:, pl.ds(width, 128)].astype(BF16)
    row_id = lax.broadcasted_iota(jnp.int32, (128, 128), 0)
    col_id = lax.broadcasted_iota(jnp.int32, (128, 128), 1)
    fold = jnp.where((row_id == col_id) | (row_id == col_id + experts), 1.0, 0.0).astype(BF16)
    weighted = gates[...] * dot(lanes, fold)
    logit_grad = (weighted - gates[...] * jnp.sum(weighted, axis=1, keepdims=True)).astype(BF16)
    short = logit_grad[:, : turned.shape[0]]

    def norm_part(c):
        hidden_grad[:, c] = (
            home_ref[:, c] + from_back[:, c].astype(F32) + dot_last(shared_dab[ours, :], in_ref[c, :])
            + dot(short, turned[:, c].astype(BF16)))
        row_part[:, c] = dot_first(logit_grad, ext[blk, :, c])

    tiles(width, 512, norm_part)

    def norm_rows(n, total):
        part = pl.ds(pl.multiple_of(n * 32, 32), 32)
        x, up = resid[part, :], hidden_grad[part, :]
        scaler = lax.rsqrt(jnp.mean(x * x, axis=1, keepdims=True) + EPS)
        normed = x * scaler
        scaled = up * turned[pl.ds(experts + 1, 1), :]
        grad = cot_own[part, :].astype(F32) + scaler * (
            scaled - normed * jnp.mean(scaled * normed, axis=1, keepdims=True))
        hidden_grad[part, :] = grad
        hid[h, part, :] = grad.astype(BF16)
        return total + jnp.sum(up * normed, axis=0, keepdims=True)

    gain = lax.fori_loop(0, rows // 32, norm_rows, jnp.zeros((1, width), F32))
    swap_hid = cross(2, hid.at[h], hid.at[h])
    swap_hid.start()
    row_part[pl.ds(experts + 1, 1), :] = gain
    load_out.wait()
    inner = low.shape[1]
    full = rows_x.at[pl.ds(0, inner)]

    def mixed_tile(who, where):
        for t in range(inner // 256):
            c = pl.ds(t * 256, 256)
            mixed_grad[where, c] = dot_last(hid[who], full[c, :]).astype(BF16)

    mixed_tile(h, ours)
    scatter_step(1, 4)
    swap_hid.wait_recv()
    mixed_tile(1 - h, theirs)

    def out_tile(c):
        rows_dy[c, :] = (
            dot_first(low[pl.ds(0, rows), c], hid[0]) + dot_first(low[pl.ds(rows, rows), c], hid[1])).astype(BF16)

    for t in range(inner // 256):
        out_tile(pl.ds(t * 256, 256))
    part_out = move(rows_dy.at[pl.ds(0, inner)], out_part)
    swap_sum.wait_recv()
    scatter_finish(1)

    def output_tile(c):
        output[:, c] = (
            resid[:, c] + routed_ref[:, c] + from_sum[:, c].astype(F32)
            + dot(shared_act[ours, :], out_ref[:, c])).astype(BF16)

    tiles(width, 512, output_tile)
    for copy in (swap_back, swap_sum, swap_hid, swap_down):
        copy.wait_send()
    swap_down.wait_recv()
    for copy in (up_out, down_out, part_out):
        copy.wait()
    for copy in sent:
        copy.wait_send()
    exchange_d(half, 0).wait_send()
    exchange_o(half, 0).wait_send()
    for k, part in ((0, upper), (1, lower)):
        over_right(part, k, 0).wait_send()
        for s in range(1, half + 1):
            if s <= half - k:
                hop_right(part, k, s).wait_send()
                over_right(part, k, s).wait_send()
            if s <= half - 1 + k:
                hop_left(part, k, s).wait_send()
                over_left(part, k, s).wait_send()


def experts_fused(
    ext, weights, cot_all, shared, cot_pair, cot_own, resid, gates, turned, low, full_out, blks, capacity, collective_id,
):
    chips, half = blks // 2, blks // 4
    rows, wide = ext.shape
    width, hidden = 2 * weights[0].shape[0], weights[2].shape[0]
    count = blks * capacity
    group = 4 * capacity
    inner = low.shape[1]
    dma = pltpu.SemaphoreType.DMA
    vmem = pl.BlockSpec(memory_space=pltpu.VMEM)
    anywhere = pl.BlockSpec(memory_space=pl.ANY)

    def bf16(*shape):
        return pltpu.VMEM(shape, BF16)

    def f32(*shape):
        return pltpu.VMEM(shape, F32)

    out = [
        ((rows, width), BF16, vmem), ((rows, width), F32, vmem), ((2 * rows, inner), BF16, vmem),
        ((inner, width), BF16, anywhere), ((width, 2 * hidden), BF16, anywhere), ((hidden, width), BF16, anywhere),
        ((width, 2 * hidden), BF16, anywhere), ((hidden, width), BF16, anywhere), ((128, width), F32, vmem),
        ((2, rows, width), BF16, anywhere), ((hidden, width // 2), BF16, anywhere),
    ]
    return pl.pallas_call(
        functools.partial(expert_kernel, chips, blks),
        out_shape=[jax.ShapeDtypeStruct(s, t) for s, t, _ in out],
        in_specs=[anywhere] * 9 + [vmem] * 5 + [anywhere],
        out_specs=[space for _, _, space in out],
        scratch_shapes=[
            f32(rows, wide), f32(rows, width), bf16(width, 2 * hidden), bf16(hidden, width),
            bf16(2 * rows, hidden), bf16(2 * rows, 2 * hidden), bf16(2, rows, width), bf16(rows, width), bf16(rows, width),
            bf16(width, 2 * hidden), bf16(hidden, width),
            bf16(blks, rows, wide), bf16(2, 2, 2, rows, width),
            bf16(count, width), bf16(count, width), bf16(count, hidden), bf16(count, 2 * hidden),
            f32(group, 2 * hidden), bf16(group, width), bf16(group, width),
            bf16(2, 2, rows, 128), f32(2, 2, rows, 128), bf16(2, 128, 2 * rows), bf16(2, 128, 2 * rows),
            bf16(chips, rows, wide), bf16(chips, rows, width), bf16(2, rows, wide), bf16(2, rows, width),
            bf16(chips, rows, wide), bf16(chips, rows, width),
            bf16(half, rows, wide), bf16(half, rows, width), bf16(half, rows, wide), bf16(half, rows, width),
            dma(()), dma((2, 2)),
        ] + [dma((2, half + 1))] * 8 + [dma((2, 2, half + 1))] * 2 + [dma((2, 2, half + 1))] * 4
        + [dma((4,)), dma((3,)), dma((11,)), dma((4,)), dma((4,))],
        compiler_params=pltpu.CompilerParams(
            collective_id=collective_id, has_side_effects=True, vmem_limit_bytes=63 << 20),
    )(ext, *weights, cot_all, *shared, cot_pair, cot_own, resid, gates, turned, low, full_out)


class Ring:
    def __init__(self, info, chips, chunks, first, sems):
        self.blk, self.at, self.sib = info
        self.half = chips // 2
        self.chunks, self.first = chunks, first
        self.send_r, self.recv_r, self.send_l, self.recv_l, self.send_s, self.recv_s = sems

    def hops(self, c):
        return self.half - c % 2, self.half - 1 + c % 2

    def copy(self, ref, ssem, rsem, dev):
        return pltpu.make_async_remote_copy(
            src_ref=ref, dst_ref=ref, send_sem=ssem, recv_sem=rsem,
            device_id={"blk": dev}, device_id_type=MESH)

    def right(self, c, s):
        i = self.first + c
        return self.copy(self.chunks[c](self.at(1 - s)), self.send_r.at[i, s], self.recv_r.at[i, s], self.at(1))

    def left(self, c, s):
        i = self.first + c
        return self.copy(self.chunks[c](self.at(s - 1)), self.send_l.at[i, s], self.recv_l.at[i, s], self.at(-1))

    def over(self, c, d):
        i, k = self.first + c, d + self.half
        return self.copy(self.chunks[c](self.at(d)), self.send_s.at[i, k], self.recv_s.at[i, k], self.sib)

    def start(self, c):
        self.right(c, 1).start()
        self.left(c, 1).start()
        self.over(c, 0).start()

    def step(self, s):
        for c in range(len(self.chunks)):
            rh, lh = self.hops(c)
            if s <= rh:
                self.right(c, s).wait_recv()
                if s < rh:
                    self.right(c, s + 1).start()
                self.over(c, -s).start()
            if s <= lh:
                self.left(c, s).wait_recv()
                if s < lh:
                    self.left(c, s + 1).start()
                self.over(c, s).start()

    def end(self):
        for c in range(len(self.chunks)):
            rh, lh = self.hops(c)
            for d in range(-rh, lh + 1):
                self.over(c, d).wait_recv()

    def flush(self):
        for c in range(len(self.chunks)):
            rh, lh = self.hops(c)
            for s in range(1, rh + 1):
                self.right(c, s).wait_send()
            for s in range(1, lh + 1):
                self.left(c, s).wait_send()
            for d in range(-rh, lh + 1):
                self.over(c, d).wait_send()


def front_kernel(
    chips, experts,
    slots_ref, places_ref, ends_ref, lanes_ref, tokens, cotangent, w_query, w_key, w_value, small, w_out,
    shared_up, shared_down, expert_up, expert_down,
    n1_out, query_out, kv_out, first_out, out_out, up_w, down_w, cot, cot_pair, expert_in, expert_out,
    low_out, full_out, lse, resid, ext, gates, short,
    n1, query, kv, first_w, out_w, low, full, turned, pair, to_other, from_other,
    send_r, recv_r, send_l, recv_l, send_s, recv_s, own_sem, y_send, y_recv, store_sem,
):
    h = lax.axis_index("head")
    blk, core, at, sib = ring_info(chips)
    half = chips // 2
    rows, width = tokens.shape
    qw, kw = w_query.shape[1] // 2, w_key.shape[1] // 2
    sw = shared_up.shape[1] // 4
    barrier = pltpu.get_barrier_semaphore()
    for other in (at(1), at(-1), sib):
        pl.semaphore_signal(barrier, inc=1, device_id={"blk": other}, device_id_type=MESH)
    pl.semaphore_signal(barrier, inc=1, device_id={"head": 1 - h}, device_id_type=MESH)
    pl.semaphore_wait(barrier, 4)

    def lanes_of(start, size):
        return pl.ds(pl.multiple_of(start, 128), size)

    def halves(i, j):
        return [
            (w_query.at[:, lanes_of(i * qw, qw)], first_w.at[j, blk, :, pl.ds(0, qw)]),
            (w_key.at[:, lanes_of(i * kw, kw)], first_w.at[j, blk, :, pl.ds(qw, kw)]),
            (w_value.at[:, lanes_of(i * kw, kw)], first_w.at[j, blk, :, pl.ds(qw + kw, kw)]),
            (small, first_w.at[j, blk, :, pl.ds(qw + 2 * kw, small.shape[1])]),
            (tokens, pair.at[j]),
            (shared_up.at[:, lanes_of(i * sw, sw)], up_w.at[j, blk, :, pl.ds(0, sw)]),
            (shared_up.at[:, lanes_of((2 + i) * sw, sw)], up_w.at[j, blk, :, pl.ds(sw, sw)]),
            (cotangent, cot_pair.at[j]),
        ]

    whole = [(expert_up, expert_in), (expert_down, expert_out)]

    stores = []

    def store(src, dst):
        copy = pltpu.make_async_copy(src, dst, store_sem.at[len(stores)])
        copy.start()
        stores.append(copy)

    own = [pltpu.make_async_copy(a, b, own_sem.at[i]) for i, (a, b) in enumerate(halves(h, h))]
    own.append(pltpu.make_async_copy(w_out, out_w.at[blk], own_sem.at[len(own)]))
    own.append(pltpu.make_async_copy(shared_down, down_w.at[blk], own_sem.at[len(own)]))
    own.append(pltpu.make_async_copy(cotangent, cot.at[blk], own_sem.at[len(own)]))
    swaps = [
        pltpu.make_async_remote_copy(
            src_ref=a, dst_ref=b, send_sem=y_send.at[i], recv_sem=y_recv.at[i],
            device_id={"head": 1 - h}, device_id_type=MESH)
        for i, (a, b) in enumerate(halves(1 - h, h) + whole)
    ]
    for i in range(5):
        swaps[i].start()
    for i in (0, 1, 2, 3, 8, 4):
        own[i].start()

    info = (blk, at, sib)
    sems = (send_r, recv_r, send_l, recv_l, send_s, recv_s)

    def row_cuts(ref, *sizes):
        start, chunks = 0, []
        for size in sizes:
            chunks.append(lambda b, start=start, size=size: ref.at[b, pl.ds(start, size)])
            start += size
        return chunks

    ring_w = Ring(info, chips, [lambda b: first_w.at[h, b], lambda b: first_w.at[1 - h, b]], 0, sems)
    out_rows, down_rows = w_out.shape[0], shared_down.shape[0]
    ring_o = Ring(info, chips, row_cuts(out_w, 32, out_rows - 32), 2, sems)
    ring_kv = Ring(info, chips, [lambda b: kv.at[2 * b], lambda b: kv.at[2 * b + 1]], 4, sems)
    ring_u = Ring(info, chips, [lambda b: up_w.at[h, b], lambda b: up_w.at[1 - h, b]], 6, sems)
    ring_d = Ring(info, chips, row_cuts(down_w, down_rows // 2, down_rows // 2), 8, sems)
    ring_c = Ring(info, chips, row_cuts(cot, rows // 2, rows // 2), 10, sems)

    for i in (0, 1, 2, 3):
        own[i].wait()
    ring_w.start(0)
    own[8].wait()
    for i in range(4):
        swaps[i].wait_recv()
    ring_w.start(1)
    ring_o.start(0)
    ring_o.start(1)
    for i in (5, 6, 9, 10, 7):
        own[i].start()
    for i in range(5, 10):
        swaps[i].start()
    for s in range(1, half + 1):
        ring_w.step(s)
        ring_o.step(s)
    ring_w.end()
    store(first_w, first_out)
    own[4].wait()
    swaps[4].wait_recv()

    small_cols = first_w[:, :, :, pl.ds(qw + 2 * kw, 128)].reshape(width, 128)
    turned[...] = jnp.swapaxes(small_cols.astype(F32), 0, 1)
    short[...] = turned[pl.ds(0, short.shape[0]), :]

    @pl.loop(0, 2 * rows // 64)
    def _(i):
        x = pair[lax.div(i, rows // 64), pl.ds(pl.multiple_of(lax.rem(i, rows // 64) * 64, 64), 64), :].astype(F32)
        scaled = x * lax.rsqrt(jnp.mean(x * x, axis=1, keepdims=True) + EPS) * turned[pl.ds(experts, 1), :]
        n1[pl.ds(pl.multiple_of(i * 64, 64), 64), :] = scaled.astype(BF16)

    def project(start, size):
        weights = first_w[:, :, :, pl.ds(start, size)].reshape(width, size)
        return dot(n1[...], weights).astype(BF16)

    for t in range(2 * kw // 256):
        part = project(qw + t * 256, 256)
        for i in range(2):
            kv[2 * blk + i, :, pl.ds(t * 256, 256)] = part[i * rows : (i + 1) * rows]
    ring_kv.start(0)
    ring_kv.start(1)
    for t in range(qw // 256):
        query[:, pl.ds(t * 256, 256)] = project(t * 256, 256)
    for i in (5, 6, 9, 10):
        own[i].wait()
    swaps[5].wait_recv()
    swaps[6].wait_recv()
    for s in range(1, half + 1):
        ring_kv.step(s)
        if s == half - 1:
            for ring in (ring_u, ring_d, ring_c):
                ring.start(0)
                ring.start(1)
    ring_kv.end()
    store(kv, kv_out)
    store(n1, n1_out)
    store(query, query_out)

    groups, repeats = kw // HD, qw // kw
    cols = repeats * PIECE
    pieces = slots_ref.shape[0]
    need = pieces // 2 + 1
    chunk = 6
    chunks = -(-need // chunk)
    later = [(ring_u, 1), (ring_d, 1), (ring_c, 1), (ring_u, 2), (ring_d, 2), (ring_c, 2)]
    turns = 0
    for i in range(2):
        place = places_ref[i]
        for g in range(groups):
            q = jnp.concatenate(
                [query[pl.ds(i * PIECE, PIECE), pl.ds((g * repeats + r) * HD, HD)] for r in range(repeats)], axis=0)

            def step(n, carry, place=place, g=g, q=q):
                top, total, acc = carry
                first = place + 1 - chunks * chunk + n * chunk
                _, (k, v) = key_chunk(
                    slots_ref, first, chunk, kv.at[:, :, pl.ds(g * HD, HD)], kv.at[:, :, pl.ds((groups + g) * HD, HD)])
                scores = dot_last(k, q) * HD**-0.5
                scores = jnp.where(seen(ends_ref, place, first, chunk * PIECE, cols), scores, NEG)
                new = jnp.maximum(top, jnp.max(scores, axis=0, keepdims=True))
                weights = jnp.exp(scores - new)
                factor = jnp.exp(top - new)
                total = total * factor + jnp.sum(weights, axis=0, keepdims=True)
                return new, total, acc * factor + dot_first(v, weights.astype(BF16))

            top, total, acc = lax.fori_loop(
                0, chunks, step,
                (jnp.full((1, cols), NEG, F32), jnp.zeros((1, cols), F32), jnp.zeros((HD, cols), F32)))
            out = jnp.swapaxes(acc / total, 0, 1)
            lse[g, pl.ds(i, 1), :] = top + jnp.log(total)
            for r in range(repeats):
                part = out[r * PIECE : (r + 1) * PIECE]
                full[pl.ds(i * PIECE, PIECE), pl.ds((g * repeats + r) * HD, HD)] = part
                low[pl.ds(i * PIECE, PIECE), pl.ds((g * repeats + r) * HD, HD)] = part.astype(BF16)
            turns += 1
            if turns % 2 == 0:
                for ring, s in later[:3]:
                    ring.step(s)
                later = later[3:]

    ring_o.end()
    store(out_w, out_out)
    store(low, low_out)
    store(full, full_out)
    theirs = pl.ds(pl.multiple_of((1 - h) * rows, rows), rows)
    ours = pl.ds(pl.multiple_of(h * rows, rows), rows)

    def mixed(where, c):
        return dot(low[where, :], out_w[:, :, c].reshape(qw, c.size))

    for t in range(width // 512):
        c = pl.ds(t * 512, 512)
        to_other[:, c] = mixed(theirs, c).astype(BF16)
    swap_mixed = pltpu.make_async_remote_copy(
        src_ref=to_other, dst_ref=from_other, send_sem=y_send.at[10], recv_sem=y_recv.at[10],
        device_id={"head": 1 - h}, device_id_type=MESH)
    swap_mixed.start()
    for t in range(width // 512):
        c = pl.ds(t * 512, 512)
        resid[:, c] = pair[h, :, c].astype(F32) + mixed(ours, c)
    for ring in (ring_u, ring_d, ring_c):
        ring.step(3)
    swap_mixed.wait_recv()

    @pl.loop(0, rows // 32)
    def _(i):
        part = pl.ds(pl.multiple_of(i * 32, 32), 32)
        x = resid[part, :] + from_other[part, :].astype(F32)
        resid[part, :] = x
        scaled = x * lax.rsqrt(jnp.mean(x * x, axis=1, keepdims=True) + EPS) * turned[pl.ds(experts + 1, 1), :]
        ext[part, pl.ds(0, width)] = scaled.astype(BF16)

    logits = dot_last(ext[:, pl.ds(0, width)], turned[...].astype(BF16))
    mask = lanes_ref[:, pl.ds(0, 128)]
    masked = jnp.where(mask > 0.5, logits, NEG)
    raised = jnp.where(mask > 0.5, jnp.exp(masked - jnp.max(masked, axis=1, keepdims=True)), 0.0)
    probs = raised / jnp.sum(raised, axis=1, keepdims=True)
    gates[...] = probs
    ext[:, pl.ds(width, 128)] = (probs + lanes_ref[:, pl.ds(128, 128)]).astype(BF16)
    for ring in (ring_u, ring_d, ring_c):
        ring.step(4)
    own[7].wait()
    for i in (7, 8, 9):
        swaps[i].wait_recv()
    for ring in (ring_u, ring_d, ring_c):
        ring.end()
    for ring in (ring_w, ring_o, ring_kv, ring_u, ring_d, ring_c):
        ring.flush()
    for copy in swaps:
        copy.wait_send()
    swap_mixed.wait_send()
    for copy in stores:
        copy.wait()


def front_fused(
    tokens, cotangent, where, mask, w_query, w_key, w_value, small, w_out, shared_up, shared_down,
    expert_up, expert_down, blks, collective_id,
):
    chips, half = blks // 2, blks // 4
    rows, width = tokens.shape
    dense = w_query.shape[0]
    qw, kw, sw = w_query.shape[1] // 2, w_key.shape[1] // 2, shared_up.shape[1] // 4
    groups, repeats = kw // HD, qw // kw
    lanes = jnp.concatenate(
        [jnp.pad(mask, ((0, 0), (0, 128 - blks))), jnp.pad(mask, ((0, 0), (blks, 128 - 2 * blks)))], axis=1).astype(F32)
    dma = pltpu.SemaphoreType.DMA
    vmem = pl.BlockSpec(memory_space=pltpu.VMEM)
    anywhere = pl.BlockSpec(memory_space=pl.ANY)
    smem = pl.BlockSpec(memory_space=pltpu.SMEM)
    out = [
        ((2 * rows, width), BF16, anywhere), ((2 * rows, qw), BF16, anywhere), ((2 * blks, rows, 2 * kw), BF16, anywhere),
        ((2, blks, dense, qw + 2 * kw + small.shape[1]), BF16, anywhere), ((blks, w_out.shape[0], width), BF16, anywhere),
        ((2, blks, dense, 2 * sw), BF16, anywhere), ((blks, shared_down.shape[0], width), BF16, anywhere),
        ((blks, rows, width), BF16, anywhere), ((2, rows, width), BF16, anywhere),
        (expert_up.shape, BF16, anywhere), (expert_down.shape, BF16, anywhere),
        ((2 * rows, qw), BF16, anywhere), ((2 * rows, qw), F32, anywhere), ((groups, 2, repeats * PIECE), F32, vmem),
        ((rows, width), F32, vmem), ((rows, width + 128), BF16, vmem), ((rows, 128), F32, vmem), ((blks + 8, width), F32, vmem),
    ]
    ring = [dma((12, half + 1))] * 4 + [dma((12, 2 * half + 1))] * 2
    (
        n1, query, kv, first_w, out_w, up_w, down_w, cot, cot_pair, expert_in, expert_out,
        low, full, lse, resid, ext, gates, turned,
    ) = pl.pallas_call(
        functools.partial(front_kernel, chips, blks),
        out_shape=[jax.ShapeDtypeStruct(s, t) for s, t, _ in out],
        in_specs=[smem] * 3 + [vmem, anywhere, vmem] + [anywhere] * 5 + [vmem] * 2 + [anywhere] * 2,
        out_specs=[space for _, _, space in out],
        scratch_shapes=[pltpu.VMEM(out[i][0], out[i][1]) for i in (0, 1, 2, 3, 4, 11, 12)] + [
            pltpu.VMEM((128, width), F32), pltpu.VMEM((2, rows, width), BF16), pltpu.VMEM((rows, width), BF16), pltpu.VMEM((rows, width), BF16)]
        + ring + [dma((11,)), dma((11,)), dma((11,)), dma((7,))],
        compiler_params=pltpu.CompilerParams(
            collective_id=collective_id, has_side_effects=True, vmem_limit_bytes=56 << 20),
    )(*where, lanes, tokens, cotangent, w_query, w_key, w_value, small, w_out, shared_up, shared_down, expert_up, expert_down)
    return (
        n1, query, kv, first_w.reshape(width, -1)[:, : qw + 2 * kw], out_w.reshape(-1, width),
        up_w.reshape(width, -1), down_w.reshape(-1, width), cot, cot_pair.reshape(2 * rows, width),
        expert_in, expert_out, low, full, lse, resid, ext, gates,
        None, None, None, (first_w, turned))


class Scatter:
    def __init__(self, info, chips, chunks, first, sems):
        self.core, self.at, self.sib = info
        self.half = chips // 2
        self.chunks, self.first = chunks, first
        self.ex_s, self.ex_r, self.right_s, self.right_r, self.left_s, self.left_r = sems
        self.there, self.sent = set(), []

    def remote(self, src, dst, ssem, rsem, dev):
        return pltpu.make_async_remote_copy(
            src_ref=src, dst_ref=dst, send_sem=ssem, recv_sem=rsem,
            device_id={"blk": dev}, device_id_type=MESH)

    def over(self, c, d):
        own, other = self.chunks[c][:2]
        i, k = self.first + c, d + self.half
        place = self.at(d)
        return self.remote(
            own(place + 1 - 2 * self.core), other.at[lax.div(place, 2)], self.ex_s.at[i, k], self.ex_r.at[i, k], self.sib)

    def exchange(self):
        for d in sorted(range(1 - self.half, self.half + 1), key=lambda d: (-abs(d), -d)):
            for c in range(len(self.chunks)):
                copy = self.over(c, d)
                copy.start()
                self.sent.append(copy)

    def join(self, c, d, into, received):
        own, other = self.chunks[c][:2]
        if (c, d) not in self.there:
            self.there.add((c, d))
            self.over(c, d).wait_recv()
        place = self.at(d)
        mine, theirs = own(place), other.at[lax.div(place, 2)]
        rows = mine.shape[0]

        @pl.loop(0, rows // 16)
        def _(i):
            w = pl.ds(pl.multiple_of(i * 16, 16), 16)
            total = mine[w].astype(F32) + theirs[w].astype(F32)
            for ref in received:
                total = total + ref[w].astype(F32)
            into[w] = total.astype(into.dtype)

    def hop(self, c, way, src, s):
        i = self.first + c
        if way > 0:
            return self.remote(
                src, self.chunks[c][2].at[s - 1], self.right_s.at[i, s], self.right_r.at[i, s], self.at(1))
        return self.remote(
            src, self.chunks[c][3].at[s - 1], self.left_s.at[i, s], self.left_r.at[i, s], self.at(-1))

    def hops(self, c, way):
        return self.half - c % 2 if way > 0 else self.half - 1 + c % 2

    def step(self, s):
        for c, (own, _, right, left) in enumerate(self.chunks):
            for way in (1, -1):
                hops = self.hops(c, way)
                if s > hops:
                    continue
                d = way * (hops - s + 1)
                d = self.half if d == -self.half else d
                if s == 1:
                    src = self.chunks[c][1].at[lax.div(self.at(d), 2)]
                    self.join(c, d, src, ())
                else:
                    src = (right if way > 0 else left).at[s - 2]
                    self.hop(c, way, src, s - 1).wait_recv()
                    self.join(c, d, src, (src,))
                copy = self.hop(c, way, src, s)
                copy.start()
                self.sent.append(copy)

    def finish(self, outs):
        for c, (own, _, right, left) in enumerate(self.chunks):
            lasts = []
            for way, buf in ((1, right), (-1, left)):
                hops = self.hops(c, way)
                self.hop(c, way, own(self.at(0)), hops).wait_recv()
                lasts.append(buf.at[hops - 1])
            self.join(c, 0, outs[c], lasts)

    def flush(self):
        for copy in self.sent:
            copy.wait_send()


def tail_kernel(
    chips, experts,
    *refs,
):
    count = 14
    ins, (din,) = refs[:12], refs[12:13]
    input_grad, query_grad, key_grad, value_grad, out_grad, up_grad, down_grad, small_grad, other_up = refs[13:22]
    held = refs[22:34]
    dk, dv, dq, n1, first_w, tokens, hidden_grad, turned, out_part, up_part, down_part, row_part = held
    (
        kv_sum, qkv_part, qkv_sum, up_sum, small_part, small_sum, to_other, from_other, qkv_from, up_from, small_from,
    ) = refs[34:45]
    rest = refs[45:]
    h = lax.axis_index("head")
    blk, core, at, sib = ring_info(chips)
    half = chips // 2
    rows, width = tokens.shape
    qw, kw = dq.shape[1], dk.shape[2]
    top = qw + 2 * kw
    dense = first_w.shape[2]
    sw = up_part.shape[3] // 2
    others, rights, lefts = rest[:count], rest[count : 2 * count], rest[2 * count : 3 * count]
    sems, (y_send, y_recv, load_sem) = rest[3 * count : 3 * count + 6], rest[3 * count + 6 :]
    loads = [pltpu.make_async_copy(a, b, load_sem.at[i]) for i, (a, b) in enumerate(zip(ins, held))]
    for i in (0, 1, 9, 8, 10, 2, 4, 3, 5, 6, 7, 11):
        loads[i].start()
    barrier = pltpu.get_barrier_semaphore()
    for other in (at(1), at(-1), sib):
        pl.semaphore_signal(barrier, inc=1, device_id={"blk": other}, device_id_type=MESH)
    pl.semaphore_signal(barrier, inc=1, device_id={"head": 1 - h}, device_id_type=MESH)
    pl.semaphore_wait(barrier, 4)

    def cross(i, src, dst):
        return pltpu.make_async_remote_copy(
            src_ref=src, dst_ref=dst, send_sem=y_send.at[i], recv_sem=y_recv.at[i],
            device_id={"head": 1 - h}, device_id_type=MESH)

    info = (core, at, sib)

    def scatter(first, owns):
        chunks = [(own, others[first + i], rights[first + i], lefts[first + i]) for i, own in enumerate(owns)]
        return Scatter(info, chips, chunks, first, sems)

    def pieces_at(ref, i):
        return lambda b: ref.at[2 * b + i]

    def source_at(ref, i):
        return lambda b: ref.at[i, b]

    def rows_at(ref, start, size):
        return lambda b: ref.at[b, pl.ds(start, size)]

    out_rows, down_rows = out_part.shape[1], down_part.shape[1]
    kv_ring = scatter(0, [pieces_at(dk, 0), pieces_at(dk, 1), pieces_at(dv, 0), pieces_at(dv, 1)])
    rest_ring = scatter(4, [
        source_at(up_part, 0), source_at(up_part, 1), rows_at(out_part, 0, 32), rows_at(out_part, 32, out_rows - 32),
        rows_at(down_part, 0, down_rows // 2), rows_at(down_part, down_rows // 2, down_rows // 2)])
    qkv_ring = scatter(10, [source_at(qkv_part, 0), source_at(qkv_part, 1)])
    small_ring = scatter(12, [source_at(small_part, 0), source_at(small_part, 1)])

    loads[0].wait()
    loads[1].wait()
    kv_ring.exchange()
    size = width // 2
    swap_up = cross(0, din.at[pl.ds(pl.multiple_of((1 - h) * size, 128), size)], other_up)
    swap_up.start()
    for i in (8, 9, 10):
        loads[i].wait()
    rest_ring.exchange()
    for s in range(1, half + 1):
        kv_ring.step(s)
        if s % 2 == 0:
            rest_ring.step(s // 2)
    kv_ring.finish([kv_sum.at[i, pl.ds(j * rows, rows)] for i in range(2) for j in range(2)])

    for i in (2, 3, 4, 5, 6, 7, 11):
        loads[i].wait()
    theirs = pl.ds(pl.multiple_of((1 - h) * rows, rows), rows)
    ours = pl.ds(pl.multiple_of(h * rows, rows), rows)
    step = 8 * dense

    def norm_grad(where, i, t):
        def part(a, first, n):
            return dot_last(a, first_w[i, pl.ds(t * 8, 8), :, pl.ds(first, n)].reshape(step, n))

        return part(dq[where, :], 0, qw) + part(kv_sum[0, where, :], qw, kw) + part(kv_sum[1, where, :], qw + kw, kw)

    spans = [(i, t, pl.ds(i * (width // 2) + t * step, step)) for i in range(2) for t in range(width // (2 * step))]
    for i, t, c in spans:
        to_other[:, c] = norm_grad(theirs, i, t).astype(BF16)
    swap_norm = cross(1, to_other, from_other)
    swap_norm.start()
    for i, t, c in spans:
        lhs = n1[:, c]
        for first, n, rhs in ((0, qw, dq[...]), (qw, kw, kv_sum[0]), (qw + kw, kw, kv_sum[1])):
            part = dot_first(lhs, rhs).astype(BF16)
            qkv_part[i, pl.ds(t * 8, 8), :, pl.ds(first, n)] = part.reshape(8, dense, n)
    qkv_ring.exchange()
    rest_ring.step(3)
    qkv_ring.step(1)
    for i, t, c in spans:
        input_grad[:, c] = norm_grad(ours, i, t)
    swap_norm.wait_recv()
    rest_ring.step(4)
    qkv_ring.step(2)

    def norm_rows(n, total):
        part = pl.ds(pl.multiple_of(n * 32, 32), 32)
        x = tokens[part, :].astype(F32)
        up = input_grad[part, :] + from_other[part, :].astype(F32)
        scaler = lax.rsqrt(jnp.mean(x * x, axis=1, keepdims=True) + EPS)
        normed = x * scaler
        scaled = up * turned[pl.ds(experts, 1), :]
        back = scaler * (scaled - normed * jnp.mean(scaled * normed, axis=1, keepdims=True))
        input_grad[part, :] = hidden_grad[part, :] + back
        return total + jnp.sum(up * normed, axis=0, keepdims=True)

    gain = lax.fori_loop(0, rows // 32, norm_rows, jnp.zeros((1, width), F32))
    ids = lax.broadcasted_iota(jnp.int32, (128, 1), 0)
    turned_part = jnp.swapaxes(row_part[...] + jnp.where(ids == experts, gain, 0.0), 0, 1)
    small_part[...] = turned_part.astype(BF16).reshape(small_part.shape)
    small_ring.exchange()
    small_ring.step(1)
    qkv_ring.step(3)
    small_ring.step(2)
    up_views = [up_sum.at[0], up_sum.at[1]]
    rest_ring.finish(up_views + [
        out_grad.at[pl.ds(0, 32)], out_grad.at[pl.ds(32, out_rows - 32)],
        down_grad.at[pl.ds(0, down_rows // 2)], down_grad.at[pl.ds(down_rows // 2, down_rows // 2)]])
    swap_sum = cross(2, up_sum.at[1 - h], up_from)
    swap_sum.start()
    qkv_ring.step(4)
    small_ring.step(3)
    qkv_ring.finish([qkv_sum.at[0], qkv_sum.at[1]])
    swap_qkv = cross(3, qkv_sum.at[1 - h], qkv_from)
    swap_qkv.start()
    small_ring.step(4)
    small_ring.finish([small_sum.at[0], small_sum.at[1]])
    swap_small = cross(4, small_sum.at[1 - h], small_from)
    swap_small.start()

    def place(ref, source, first, n, base=0):
        for who, part in ((h, source[0]), (1 - h, source[1])):
            ref[:, pl.ds(pl.multiple_of(base + who * n, 128), n)] = part[:, pl.ds(first, n)].astype(F32)

    swap_sum.wait_recv()
    ups = (up_sum.at[h], up_from)
    place(up_grad, ups, 0, sw)
    place(up_grad, ups, sw, sw, 2 * sw)
    swap_qkv.wait_recv()
    sums = (qkv_sum.at[h], qkv_from)
    place(query_grad, sums, 0, qw)
    place(key_grad, sums, qw, kw)
    place(value_grad, sums, qw + kw, kw)
    swap_small.wait_recv()
    small_grad[...] = small_sum[h] + small_from[...]
    for ring in (kv_ring, rest_ring, qkv_ring, small_ring):
        ring.flush()
    for copy in (swap_norm, swap_up, swap_sum, swap_qkv, swap_small):
        copy.wait_send()
    swap_up.wait_recv()


def tail_fused(
    dk, dv, dq, n1, first_w, tokens, hidden_grad, turned, out_part, up_part, down_part, row_part, din,
    blks, collective_id,
):
    chips, half = blks // 2, blks // 4
    rows, width = tokens.shape
    qw, kw = dq.shape[1], dk.shape[2]
    top = qw + 2 * kw
    dense = first_w.shape[2]
    out_rows, down_rows, up_wide = out_part.shape[1], down_part.shape[1], up_part.shape[3]
    dma = pltpu.SemaphoreType.DMA
    vmem = pl.BlockSpec(memory_space=pltpu.VMEM)
    anywhere = pl.BlockSpec(memory_space=pl.ANY)
    shapes = [(rows, kw)] * 4 + [(dense, up_wide)] * 2 + [(32, width), (out_rows - 32, width)]
    shapes += [(down_rows // 2, width)] * 2 + [(dense, top)] * 2 + [(dense, 128)] * 2
    others = [pltpu.VMEM((chips,) + s, BF16) for s in shapes]
    slots = [pltpu.VMEM((half,) + s, BF16) for s in shapes]
    n = len(shapes)
    held = (dk, dv, dq, n1, first_w, tokens, hidden_grad, turned, out_part, up_part, down_part, row_part)

    def f32(*shape):
        return jax.ShapeDtypeStruct(shape, F32)

    def low(*shape):
        return pltpu.VMEM(shape, BF16)

    return pl.pallas_call(
        functools.partial(tail_kernel, chips, blks),
        out_shape=[
            f32(rows, width), f32(dense, 2 * qw), f32(dense, 2 * kw), f32(dense, 2 * kw), f32(out_rows, width),
            f32(dense, 2 * up_wide), f32(down_rows, width), f32(dense, 128),
            jax.ShapeDtypeStruct((din.shape[0] // 2, din.shape[1]), BF16),
        ],
        in_specs=[anywhere] * 13,
        out_specs=[vmem] * 8 + [anywhere],
        scratch_shapes=[pltpu.VMEM(a.shape, a.dtype) for a in held] + [
            low(2, 2 * rows, kw), low(2, blks, dense, top), low(2, dense, top), low(2, dense, up_wide),
            low(2, blks, dense, 128), pltpu.VMEM((2, dense, 128), F32), low(rows, width), low(rows, width),
            low(dense, top), low(dense, up_wide), pltpu.VMEM((dense, 128), F32),
        ] + others + slots + slots + [dma((n, 2 * half + 1))] * 2 + [dma((n, half + 1))] * 4 + [dma((5,)), dma((5,)), dma((12,))],
        compiler_params=pltpu.CompilerParams(
            collective_id=collective_id, has_side_effects=True, vmem_limit_bytes=62 << 20),
    )(*held, din)


def experts_plain(own_ext, weights, cot_all, blks, capacity, collective_id):
    h, b = lax.axis_index("head"), lax.axis_index("blk")
    own_up, other_up, own_down, other_down = weights
    expert_in = pair(own_up, other_up).reshape(2 * own_up.shape[0], -1)
    expert_out = jnp.where(
        h == 0,
        jnp.concatenate([own_down, other_down], axis=1),
        jnp.concatenate([other_down, own_down], axis=1),
    )
    normed = own_ext[:, : expert_in.shape[0]]
    normed_pair = pair(normed, swap(normed))
    experts, width = blks, expert_in.shape[0]
    rows = own_ext.shape[0]
    ext = all_gather_blk([own_ext], blks, collective_id)[0]
    norm_all = ext[:, :, :width]
    gate_here = lax.dynamic_index_in_dim(ext, width + b, 2, keepdims=False).astype(F32)
    mask_here = lax.dynamic_index_in_dim(ext, width + experts + b, 2, keepdims=False).astype(F32)
    rank = jnp.cumsum(mask_here, axis=1) - mask_here
    slots = jnp.arange(capacity, dtype=F32)
    deal = ((rank[:, None, :] == slots[None, :, None]) & (mask_here[:, None, :] > 0)).astype(BF16)
    deal_gate = deal * gate_here[:, None, :].astype(BF16)

    def to_slots(dealer, array):
        moved = jnp.einsum("bst,btd->bsd", dealer, array, preferred_element_type=F32)
        return moved.astype(BF16).reshape(blks * capacity, width)

    def to_rows(dealer, array):
        return jnp.einsum(
            "bst,bsd->btd", dealer, array.reshape(blks, capacity, width), preferred_element_type=F32)

    expert_rows = to_slots(deal, norm_all)
    both = dot(expert_rows, expert_in)
    ew = expert_out.shape[0]
    gate_part, up_part = both[:, :ew], both[:, ew:]
    activated = (jax.nn.silu(gate_part) * up_part).astype(BF16)
    result = dot(activated, expert_out).astype(BF16)
    result_rows = to_rows(deal, result)
    gate_grad = jnp.sum(result_rows * cot_all.astype(F32), axis=2, keepdims=True)
    routed = (result_rows * gate_here[:, :, None]).astype(BF16)
    slot_grad = to_slots(deal_gate, cot_all)
    act_grad = dot_last(slot_grad, expert_out)
    both_grad = gated_grad(act_grad, gate_part, up_part)
    rows_back = to_rows(deal, dot_last(both_grad, expert_in).astype(BF16)).astype(BF16)
    lane = jnp.arange(128 * (-(-2 * experts // 128)), dtype=jnp.int32)
    grad_high = gate_grad.astype(BF16)
    grad_low = (gate_grad - grad_high.astype(F32)).astype(BF16)
    grad_lanes = jnp.where(lane == b, grad_high, jnp.where(lane == b + experts, grad_low, jnp.zeros((), BF16)))
    dwn = dot_first(activated, slot_grad).astype(BF16)
    dup = dot_first(expert_rows, both_grad).astype(BF16)
    home = reduce_scatter_blk([jnp.concatenate([rows_back, grad_lanes], axis=2)], blks, collective_id + 1, [F32])[0]
    routed_sum = reduce_scatter_blk([routed], blks, collective_id + 2, [F32])[0]
    return home, routed_sum, dup, dwn, normed_pair


def pair(own, other):
    return jnp.where(lax.axis_index("head") == 0, jnp.stack([own, other]), jnp.stack([other, own]))


def half(w, i, parts=1):
    size = w.shape[1] // (2 * parts)
    cut = lax.dynamic_slice_in_dim(w.reshape(w.shape[0], parts, 2 * size), i * size, size, 2)
    return cut.reshape(w.shape[0], parts * size)


def pick(stacked, i):
    return lax.dynamic_index_in_dim(stacked, i, 0, keepdims=False)


def front_plain(
    tokens, cotangent, where, mask, w_query, w_key, w_value, small, w_out, shared_up, shared_down,
    expert_up, expert_down, blks, collective_id,
):
    h = lax.axis_index("head")
    rows, width = tokens.shape
    experts = blks

    def columns(i):
        return jnp.concatenate([half(w_query, i), half(w_key, i), half(w_value, i)], axis=1)

    first = pair(
        jnp.concatenate([columns(h), small], axis=1),
        swap(jnp.concatenate([columns(1 - h), small], axis=1)),
    )
    tokens_pair = pair(tokens, swap(tokens))
    cotangent_pair = pair(cotangent, swap(cotangent)).reshape(2 * rows, width)
    up_pair = pair(half(shared_up, h, 2), swap(half(shared_up, 1 - h, 2)))
    other_up, other_down = swap(expert_up), swap(expert_down)
    gathered = all_gather_blk([first], blks, collective_id)[0].reshape(width, -1)
    qw = w_query.shape[1] // 2
    kw = w_key.shape[1] // 2
    full_qkv = gathered[:, : qw + 2 * kw]
    full_router = gathered[:, qw + 2 * kw : qw + 2 * kw + experts]
    gain_first = gathered[:, qw + 2 * kw + experts].astype(F32)
    gain_second = gathered[:, qw + 2 * kw + experts + 1].astype(F32)

    inputs_pair = tokens_pair.reshape(2 * rows, width).astype(F32)
    normed_one = (inputs_pair * inv_scale(inputs_pair) * gain_first).astype(BF16)
    qkv = dot(normed_one, full_qkv).astype(BF16)
    query = qkv[:, :qw]
    kv = all_gather_blk([qkv[:, qw:]], blks, collective_id + 1)[0].reshape(-1, PIECE, 2 * kw)

    attended, attended_full, lse = attention_forward(query, kv, where)

    up_all, out_all, down_all, cot_all = all_gather_blk([up_pair, w_out, shared_down, cotangent], blks, collective_id + 2)
    full_up = up_all.reshape(width, -1)
    full_out = out_all.reshape(-1, width)
    full_down = down_all.reshape(-1, width)

    mixed = dot(attended, full_out).reshape(2, rows, width)
    inputs = tokens.astype(F32)
    resid = inputs + (pick(mixed, h) + swap(pick(mixed, 1 - h).astype(BF16)).astype(F32))
    scaler_two = inv_scale(resid)
    normed_two = (resid * scaler_two * gain_second).astype(BF16)

    logits = dot(normed_two, full_router)
    masked = jnp.where(mask, logits, NEG)
    raised = jnp.where(mask, jnp.exp(masked - jnp.max(masked, axis=1, keepdims=True)), 0.0)
    gates = raised / jnp.sum(raised, axis=1, keepdims=True)
    extra = jnp.concatenate(
        [gates.astype(BF16), mask.astype(BF16), jnp.zeros((rows, -2 * experts % 128), BF16)], axis=1)
    ext = jnp.concatenate([normed_two, extra], axis=1)
    return (
        normed_one, query, kv, full_qkv, full_out, full_up, full_down, cot_all, cotangent_pair, other_up, other_down,
        attended, attended_full, lse, resid, ext, gates, full_router.T, gain_first, gain_second, None)


def shards(
    tokens, cotangent, seq_lengths, piece_order, routes, norm1_gain, w_query, w_key, w_value, w_out,
    norm2_gain, w_router, shared_up, shared_down, expert_up, expert_down,
):
    blks = lax.axis_size("blk")
    h, b = lax.axis_index("head"), lax.axis_index("blk")
    rows, width = tokens.shape
    experts = blks
    capacity = rows * TOP * 4 // (3 * blks)
    dense_rows = w_query.shape[0]

    small = jnp.concatenate(
        [w_router, norm1_gain[:, None], norm2_gain[:, None],
         jnp.zeros((dense_rows, -(experts + 2) % 128), BF16)], axis=1)
    lanes = small.shape[1]
    places = jnp.swapaxes(piece_order.reshape(2, blks), 0, 1).reshape(-1)
    order = jnp.arange(2 * blks, dtype=jnp.int32)
    slots = jnp.sum(jnp.where(places[None, :] == order[:, None], order[None, :], 0), axis=1)
    where = (slots, lax.dynamic_slice_in_dim(places, 2 * b, 2), jnp.cumsum(seq_lengths))
    hot = routes[:, :, None] == jnp.arange(experts, dtype=jnp.int32)[None, None, :]
    mask = jnp.any(hot, axis=1)
    fits = blks == 16 and rows == 128 and 2 * capacity == 128 and width % 768 == 0 and dense_rows == 48
    front = front_fused if fits else front_plain
    (
        normed_one, query, kv, full_qkv, full_out, full_up, full_down, cot_all, cotangent_pair, other_up, other_down,
        attended, attended_full, lse, resid, ext, gates, router_rows, gain_first, gain_second, kept,
    ) = front(
        tokens, cotangent, where, mask, w_query, w_key, w_value, small, w_out, shared_up, shared_down,
        expert_up[0], expert_down[0], blks, 0)
    qw, kw = w_query.shape[1] // 2, w_key.shape[1] // 2
    shared_width = full_down.shape[0]
    inputs = tokens.astype(F32)
    if fits:
        (
            output, hidden_grad, mixed_grad, out_part, shared_up_part, shared_down_part, dup, dwn, row_part, _, add_down,
        ) = experts_fused(
            ext, (expert_up[0], other_up, expert_down[0], other_down), cot_all, (full_up, full_down), cotangent_pair,
            cotangent, resid, gates, kept[1], attended, full_out, blks, capacity, 3)
        query_grad, *kv_parts = attention_backward(query, kv, attended_full, lse, mixed_grad, where)
        (
            input_grad, w_query_grad, w_key_grad, w_value_grad, out_sum, up_grad, down_sum, small_sum, add_up,
        ) = tail_fused(
            *kv_parts, query_grad, normed_one, kept[0], tokens, hidden_grad, kept[1],
            out_part.reshape(blks, dense_rows, width),
            shared_up_part.reshape(2, blks, dense_rows, -1),
            shared_down_part.reshape(blks, -1, width), row_part, dup, blks, 6)
        size = width // 2
        expert_up_grad = lax.dynamic_slice_in_dim(dup, h * size, size, 0).astype(F32) + add_up.astype(F32)
        expert_down_grad = lax.dynamic_slice_in_dim(dwn, h * size, size, 1).astype(F32) + add_down.astype(F32)
        return (
            output, input_grad, small_sum[:, experts], w_query_grad, w_key_grad, w_value_grad,
            out_sum, small_sum[:, experts + 1], small_sum[:, :experts], up_grad, down_sum,
            expert_up_grad[None], expert_down_grad[None],
        )
    scaler_two = inv_scale(resid)
    normed_two = ext[:, :width]

    home, routed_sum, dup, dwn, normed_pair = experts_plain(
        ext, (expert_up[0], other_up, expert_down[0], other_down), cot_all, blks, capacity, 3)
    normed_pair = normed_pair.reshape(2 * rows, width)
    shared_both = dot(normed_pair, full_up)
    shared_gate, shared_lift = shared_both[:, :shared_width], shared_both[:, shared_width:]
    shared_act = (jax.nn.silu(shared_gate) * shared_lift).astype(BF16)
    shared_sum = dot(shared_act, full_down).reshape(2, rows, width)
    shared_down_part = dot_first(shared_act, cotangent_pair)
    shared_grad = gated_grad(dot_last(cotangent_pair, full_down), shared_gate, shared_lift)
    shared_up_part = dot_first(normed_pair, shared_grad)
    shared_back = dot_last(shared_grad, full_up).reshape(2, rows, width)
    output = (
        resid + routed_sum + pick(shared_sum, h) + swap(pick(shared_sum, 1 - h).astype(BF16)).astype(F32)
    ).astype(BF16)

    dgate = home[:, width : width + experts] + home[:, width + experts : width + 2 * experts]
    weighted = gates * dgate
    logit_grad = (weighted - gates * jnp.sum(weighted, axis=1, keepdims=True)).astype(BF16)
    norm_two_grad = (
        home[:, :width] + dot(logit_grad, router_rows)
        + pick(shared_back, h) + swap(pick(shared_back, 1 - h).astype(BF16)).astype(F32)
    )
    back, gain_two_part = norm_back(resid, scaler_two, gain_second, norm_two_grad)
    hidden_grad = cotangent.astype(F32) + back
    hidden_low = hidden_grad.astype(BF16)
    hidden_pair = pair(hidden_low, swap(hidden_low)).reshape(2 * rows, width)
    out_part = dot_first(attended, hidden_pair)
    mixed_grad = dot_last(hidden_pair, full_out).astype(BF16)
    query_grad, *kv_parts = attention_backward(query, kv, attended_full, lse, mixed_grad, where)
    router_part = dot_first(normed_two, logit_grad)
    dup, dwn, query_grad = lax.optimization_barrier((dup, dwn, query_grad))
    dup = dup.reshape(2, width // 2, -1)
    dwn = jnp.stack([dwn[:, : width // 2], dwn[:, width // 2 :]])
    expert_up_grad = pick(dup, h).astype(F32) + swap(pick(dup, 1 - h)).astype(F32)
    expert_down_grad = pick(dwn, h).astype(F32) + swap(pick(dwn, 1 - h)).astype(F32)
    kv_grads = reduce_scatter_blk([part.reshape(blks, 2 * rows, kw) for part in kv_parts], blks, 6, [BF16] * 2)
    qkv_grad = jnp.concatenate([query_grad, *kv_grads], axis=1)
    norm_one_part = dot_last(qkv_grad, full_qkv).reshape(2, rows, width)
    norm_one_grad = pick(norm_one_part, h) + swap(pick(norm_one_part, 1 - h).astype(BF16)).astype(F32)
    extra_grad, gain_one_part = norm_back(inputs, inv_scale(inputs), gain_first, norm_one_grad)
    input_grad = hidden_grad + extra_grad
    qkv_part = dot_first(normed_one, qkv_grad)
    small_part = jnp.concatenate(
        [router_part, gain_one_part[:, None], gain_two_part[:, None],
         jnp.zeros((width, lanes - experts - 2), F32)], axis=1)

    def by_rows(part):
        return part.astype(BF16).reshape(2, blks, dense_rows, -1)

    qkv_sum, up_sum, out_sum, down_sum, small_sum = reduce_scatter_blk(
        [by_rows(qkv_part), by_rows(shared_up_part),
         out_part.astype(BF16).reshape(blks, dense_rows, width),
         shared_down_part.astype(BF16).reshape(blks, -1, width), by_rows(small_part)],
        blks, 7, [BF16, BF16, F32, F32, F32])
    there = swap(jnp.concatenate([pick(qkv_sum, 1 - h), pick(up_sum, 1 - h)], axis=1)).astype(F32)
    here = jnp.concatenate([pick(qkv_sum, h), pick(up_sum, h)], axis=1).astype(F32)
    small_sum = pick(small_sum, h) + swap(pick(small_sum, 1 - h))

    def whole(start, size):
        return jnp.where(
            h == 0,
            jnp.concatenate([here[:, start : start + size], there[:, start : start + size]], axis=1),
            jnp.concatenate([there[:, start : start + size], here[:, start : start + size]], axis=1))

    top = qw + 2 * kw
    sw = shared_width
    up_grad = jnp.concatenate([whole(top, sw), whole(top + sw, sw)], axis=1)
    return (
        output, input_grad, small_sum[:, experts], whole(0, qw), whole(qw, kw), whole(qw + kw, kw),
        out_sum, small_sum[:, experts + 1], small_sum[:, :experts], up_grad, down_sum,
        expert_up_grad[None], expert_down_grad[None],
    )


def solution(mesh):
    both = P(("head", "blk"), None)
    flat = P(("head", "blk"))
    up, down = P("blk", "head", None), P("blk", None, "head")
    return jax.shard_map(
        shards,
        mesh=mesh,
        in_specs=(both, both, P(), P(), both, flat, both, both, both, both, flat, both, both, both, up, down),
        out_specs=(both, both, flat, both, both, both, both, flat, both, both, both, up, down),
        check_vma=False,
    )
```

```python
import functools

import jax
import jax.numpy as jnp
from jax import lax
from jax.experimental import pallas as pl
from jax.experimental.pallas import tpu as pltpu
from jax.sharding import PartitionSpec as P

MESH = pl.DeviceIdType.MESH


def ring_place(chip, chips):
    odd = chip % 2
    return (chip // 2) * (1 - odd) + (chips - 1 - chip // 2) * odd


def ring_chip(place, chips):
    high = place // (chips // 2)
    return 2 * place * (1 - high) + (2 * (chips - 1 - place) + 1) * high


def ring_info(chips):
    blk = lax.axis_index("blk")
    chip, core = blk // 2, blk % 2
    place = ring_place(chip, chips)

    def at(step):
        return ring_chip((place + step + chips) % chips, chips) * 2 + core

    return blk, core, at, blk + 1 - 2 * core


def pieces_of(shape):
    if len(shape) == 3:
        return [(0, None), (1, None)]
    rows = shape[0]
    if rows >= 32 and rows % 16 == 0:
        cut = (rows // 2 + 15) // 16 * 16
        return [(0, cut), (cut, rows - cut)]
    return [(0, rows)]


def part_in(ref, piece):
    start, size = piece
    return ref.at[start] if size is None else ref.at[pl.ds(start, size)]


def part_out(ref, piece, b):
    start, size = piece
    return ref.at[start, b] if size is None else ref.at[b, pl.ds(start, size)]


def ag_kernel(count, chips, plans, *refs):
    ins, outs = refs[:count], refs[count : 2 * count]
    right_sem, left_sem, sib_sem, sright, sleft, ssib, own_sem = refs[2 * count :]
    blk, core, at, sib = ring_info(chips)
    right, left = at(1), at(-1)
    barrier = pltpu.get_barrier_semaphore()
    for other in (right, left, sib):
        pl.semaphore_signal(barrier, inc=1, device_id={"blk": other}, device_id_type=MESH)
    pl.semaphore_wait(barrier, 3)
    half = chips // 2
    started = []

    def send(src, dst, ssem, rsem, dev):
        copy = pltpu.make_async_remote_copy(
            src_ref=src, dst_ref=dst, send_sem=ssem, recv_sem=rsem,
            device_id={"blk": dev}, device_id_type=MESH)
        copy.start()
        started.append(copy)
        return copy

    chunks = []
    for k in range(count):
        for i, piece in enumerate(plans[k]):
            chunks.append((len(chunks), k, piece, half - (i % 2), half - 1 + (i % 2)))
    copies = {}
    locals_ = []
    for c, k, piece, rh, lh in chunks:
        src = part_in(ins[k], piece)
        dst = part_out(outs[k], piece, blk)
        if rh >= 1:
            copies[c, "r", 1] = send(src, dst, sright.at[c, 0], right_sem.at[c, 0], right)
        if lh >= 1:
            copies[c, "l", 1] = send(src, dst, sleft.at[c, 0], left_sem.at[c, 0], left)
        copies[c, "s", 0] = send(src, dst, ssib.at[c, 0], sib_sem.at[c, 0], sib)
        own = pltpu.make_async_copy(src, dst, own_sem.at[c])
        own.start()
        locals_.append(own)
    for s in range(1, half + 1):
        for c, k, piece, rh, lh in chunks:
            if s <= rh:
                copies[c, "r", s].wait_recv()
                b = at(-s)
                blockref = part_out(outs[k], piece, b)
                if s < rh:
                    copies[c, "r", s + 1] = send(blockref, blockref, sright.at[c, s], right_sem.at[c, s], right)
                copies[c, "sr", s] = send(blockref, blockref, ssib.at[c, s], sib_sem.at[c, s], sib)
            if s <= lh:
                copies[c, "l", s].wait_recv()
                b = at(s)
                blockref = part_out(outs[k], piece, b)
                if s < lh:
                    copies[c, "l", s + 1] = send(blockref, blockref, sleft.at[c, s], left_sem.at[c, s], left)
                copies[c, "sl", s] = send(blockref, blockref, ssib.at[c, half + s], sib_sem.at[c, half + s], sib)
    for (c, d, s), copy in copies.items():
        if d in ("s", "sr", "sl"):
            copy.wait_recv()
    for copy in started:
        copy.wait_send()
    for copy in locals_:
        copy.wait()


def all_gather_blk(arrays, blks, collective_id, vmem=False):
    chips = blks // 2
    count = len(arrays)
    plans = [pieces_of(a.shape) for a in arrays]
    n = sum(len(p) for p in plans)
    half = chips // 2
    shapes = [
        jax.ShapeDtypeStruct((a.shape[0], blks) + a.shape[1:] if a.ndim == 3 else (blks,) + a.shape, a.dtype)
        for a in arrays
    ]
    dma = pltpu.SemaphoreType.DMA
    space = pltpu.VMEM if vmem else pl.ANY
    return pl.pallas_call(
        functools.partial(ag_kernel, count, chips, plans),
        out_shape=shapes,
        in_specs=[pl.BlockSpec(memory_space=space)] * count,
        out_specs=[pl.BlockSpec(memory_space=space)] * count,
        scratch_shapes=[
            dma((n, half)), dma((n, half)), dma((n, 2 * half + 1)),
            dma((n, half)), dma((n, half)), dma((n, 2 * half + 1)), dma((n,)),
        ],
        compiler_params=pltpu.CompilerParams(collective_id=collective_id, has_side_effects=True,
            vmem_limit_bytes=(60 << 20) if vmem else None),
    )(*arrays)


def rs_kernel(count, chips, plans, *refs):
    xs, outs = refs[:count], refs[count : 2 * count]
    rest = refs[2 * count :]
    n = sum(len(p) for p in plans)
    ys, rs, ls = rest[:n], rest[n : 2 * n], rest[2 * n : 3 * n]
    right_sem, left_sem, sib_sem, sright, sleft, ssib = rest[3 * n :]
    blk, core, at, sib = ring_info(chips)
    right, left = at(1), at(-1)
    barrier = pltpu.get_barrier_semaphore()
    for other in (right, left, sib):
        pl.semaphore_signal(barrier, inc=1, device_id={"blk": other}, device_id_type=MESH)
    pl.semaphore_wait(barrier, 3)
    half = chips // 2
    started = []

    def send(src, dst, ssem, rsem, dev):
        copy = pltpu.make_async_remote_copy(
            src_ref=src, dst_ref=dst, send_sem=ssem, recv_sem=rsem,
            device_id={"blk": dev}, device_id_type=MESH)
        copy.start()
        started.append(copy)
        return copy

    chunks = []
    for k in range(count):
        for i, piece in enumerate(plans[k]):
            chunks.append((len(chunks), k, piece, half - (i % 2), half - 1 + (i % 2)))
    order = []
    for d in range(half, 0, -1):
        order += [d, -d] if d < half else [d]
    order.append(0)
    sibs = {}
    for j, d in enumerate(order):
        there = at(d) + 1 - 2 * core
        for c, k, piece, rh, lh in chunks:
            sibs[c, d] = send(part_out(xs[k], piece, there), ys[c].at[j], ssib.at[c, j], sib_sem.at[c, j], sib)
    ready = set()

    def blocks(rows, body):
        step = 16 if rows % 16 == 0 else rows

        @pl.loop(0, rows // step)
        def _(i):
            body(pl.ds(pl.multiple_of(i * step, step), step))

    def mine(c, k, piece, d):
        j = order.index(d)
        if (c, d) not in ready:
            sibs[c, d].wait_recv()
            ready.add((c, d))
        return j

    copies = {}

    def join(c, k, piece, d, into, recv):
        j = mine(c, k, piece, d)
        x = part_out(xs[k], piece, at(d))
        rows = x.shape[0]

        def body(w):
            total = x[w].astype(jnp.float32) + ys[c][j, w].astype(jnp.float32)
            if recv is not None:
                total = total + recv[w].astype(jnp.float32)
            into[w] = total.astype(into.dtype)

        blocks(rows, body)

    for s in range(1, half + 1):
        for c, k, piece, rh, lh in chunks:
            for way, hops, buf, sem, ssem, dev in (
                (1, rh, rs[c], right_sem, sright, right),
                (-1, lh, ls[c], left_sem, sleft, left),
            ):
                if s > hops:
                    continue
                if s == 1:
                    j = order.index(way * hops if way * hops in order else hops)
                    join(c, k, piece, order[j], ys[c].at[j], None)
                    src = ys[c].at[j]
                else:
                    copies[c, way, s - 1].wait_recv()
                    d = way * (hops - s + 1)
                    src = buf.at[s - 2]
                    join(c, k, piece, d, src, src)
                copies[c, way, s] = send(src, buf.at[s - 1], ssem.at[c, s - 1], sem.at[c, s - 1], dev)
    for c, k, piece, rh, lh in chunks:
        if rh >= 1:
            copies[c, 1, rh].wait_recv()
        if lh >= 1:
            copies[c, -1, lh].wait_recv()
        j = mine(c, k, piece, 0)
        x = part_out(xs[k], piece, blk)
        target = part_in(outs[k], piece)

        def body(w, x=x, c=c, j=j, rh=rh, lh=lh, target=target):
            total = x[w].astype(jnp.float32) + ys[c][j, w].astype(jnp.float32)
            if rh >= 1:
                total = total + rs[c][rh - 1, w].astype(jnp.float32)
            if lh >= 1:
                total = total + ls[c][lh - 1, w].astype(jnp.float32)
            target[w] = total.astype(target.dtype)

        blocks(x.shape[0], body)
    for copy in started:
        copy.wait_send()


def reduce_scatter_blk(arrays, blks, collective_id, out_dtypes):
    chips = blks // 2
    half = chips // 2
    count = len(arrays)
    shapes = [a.shape[1:] if a.ndim == 3 else (2,) + a.shape[2:] for a in arrays]
    plans = [pieces_of(s) for s in shapes]
    dma = pltpu.SemaphoreType.DMA
    ys, rs = [], []
    for s, plan in zip(shapes, plans):
        for start, size in plan:
            rows = s[1] if size is None else size
            ys.append(pltpu.VMEM((chips, rows, s[-1]), jnp.bfloat16))
            rs.append(pltpu.VMEM((half, rows, s[-1]), jnp.bfloat16))
    n = len(ys)
    return pl.pallas_call(
        functools.partial(rs_kernel, count, chips, plans),
        out_shape=[jax.ShapeDtypeStruct(s, t) for s, t in zip(shapes, out_dtypes)],
        in_specs=[pl.BlockSpec(memory_space=pltpu.VMEM)] * count,
        out_specs=[pl.BlockSpec(memory_space=pltpu.VMEM)] * count,
        scratch_shapes=ys + rs + rs + [
            dma((n, half)), dma((n, half)), dma((n, chips)),
            dma((n, half)), dma((n, half)), dma((n, chips)),
        ],
        compiler_params=pltpu.CompilerParams(collective_id=collective_id, has_side_effects=True,
            vmem_limit_bytes=60 << 20),
    )(*arrays)


H = 12
KVH = 4
HD = 128
TOP = 6
PIECE = 128
EPS = 1e-05
NEG = -1e30
F32 = jnp.float32
BF16 = jnp.bfloat16


def dot(a, b):
    return jnp.dot(a, b, preferred_element_type=F32)


def dot_first(a, b):
    return lax.dot_general(a, b, (((0,), (0,)), ((), ())), preferred_element_type=F32)


def dot_last(a, b):
    return lax.dot_general(a, b, (((1,), (1,)), ((), ())), preferred_element_type=F32)


def inv_scale(values):
    return lax.rsqrt(jnp.mean(values * values, axis=1, keepdims=True) + EPS)


def norm_back(values, scaler, gain, upstream):
    normed = values * scaler
    gain_grad = jnp.sum(upstream * normed, axis=0)
    scaled = upstream * gain
    grad = scaler * (scaled - normed * jnp.mean(scaled * normed, axis=1, keepdims=True))
    return grad, gain_grad


def gated_grad(act_grad, gate, lift):
    sig = jax.nn.sigmoid(gate)
    return jnp.concatenate(
        [act_grad * lift * sig * (1.0 + gate * (1.0 - sig)), act_grad * gate * sig], axis=1
    ).astype(BF16)


def swap(array):
    return lax.ppermute(array, "head", [(0, 1), (1, 0)])


def ends_of(lengths_ref):
    end, ends = jnp.int32(0), []
    for e in range(lengths_ref.shape[0]):
        end = end + lengths_ref[e]
        ends.append(end)
    return ends


def key_span(place, lengths_ref):
    start = jnp.int32(0)
    for end in ends_of(lengths_ref):
        start = jnp.where(end <= place * PIECE, end, start)
    return start // PIECE


def key_chunk(slots_ref, first, pieces, *refs):
    last = slots_ref.shape[0] - 1
    slots = [slots_ref[jnp.clip(first + k, 0, last)] for k in range(pieces)]
    return slots, [jnp.concatenate([ref[s] for s in slots], axis=0) for ref in refs]


def stacked(ref, i, repeats):
    return jnp.concatenate(
        [ref[pl.ds(i * PIECE, PIECE), pl.ds(r * HD, HD)] for r in range(repeats)], axis=0)


def seen(lengths_ref, place, first, keys, cols):
    own = place * PIECE + lax.broadcasted_iota(jnp.int32, (1, cols), 1) % PIECE
    start = jnp.zeros((1, cols), jnp.int32)
    for end in ends_of(lengths_ref):
        start = jnp.where(end <= own, end, start)
    there = first * PIECE + lax.broadcasted_iota(jnp.int32, (keys, 1), 0)
    return (there <= own) & (there >= start)


CHUNK = 4


def forward_kernel(repeats, slots_ref, places_ref, lengths_ref, q_ref, k_ref, v_ref, low_ref, full_ref, lse_ref):
    cols = repeats * PIECE
    for i in range(q_ref.shape[0] // PIECE):
        place = places_ref[i]
        lo = key_span(place, lengths_ref)
        q = stacked(q_ref, i, repeats)

        def step(n, carry, lo=lo, place=place, q=q):
            top, total, acc = carry
            first = lo + n * CHUNK
            _, (k, v) = key_chunk(slots_ref, first, CHUNK, k_ref, v_ref)
            scores = dot_last(k, q) * HD**-0.5
            scores = jnp.where(seen(lengths_ref, place, first, CHUNK * PIECE, cols), scores, NEG)
            new = jnp.maximum(top, jnp.max(scores, axis=0, keepdims=True))
            weights = jnp.exp(scores - new)
            factor = jnp.exp(top - new)
            total = total * factor + jnp.sum(weights, axis=0, keepdims=True)
            return new, total, acc * factor + dot_first(v, weights.astype(BF16))

        top, total, acc = lax.fori_loop(
            0, (place - lo) // CHUNK + 1, step,
            (jnp.full((1, cols), NEG, F32), jnp.zeros((1, cols), F32), jnp.zeros((HD, cols), F32)))
        out = jnp.swapaxes(acc / total, 0, 1)
        lse_ref[0, pl.ds(i, 1), :] = top + jnp.log(total)
        for r in range(repeats):
            part = out[r * PIECE : (r + 1) * PIECE]
            full_ref[pl.ds(i * PIECE, PIECE), pl.ds(r * HD, HD)] = part
            low_ref[pl.ds(i * PIECE, PIECE), pl.ds(r * HD, HD)] = part.astype(BF16)


def attention_forward(query, kv, where):
    rows, pieces = query.shape[0], kv.shape[0]
    groups = kv.shape[2] // (2 * HD)
    wide = query.shape[1] // groups
    repeats = wide // HD
    spec = pl.BlockSpec((rows, wide), lambda g, *_: (0, g))
    return pl.pallas_call(
        functools.partial(forward_kernel, repeats),
        grid_spec=pltpu.PrefetchScalarGridSpec(
            num_scalar_prefetch=3,
            grid=(groups,),
            in_specs=[
                spec,
                pl.BlockSpec((pieces, PIECE, HD), lambda g, *_: (0, 0, g)),
                pl.BlockSpec((pieces, PIECE, HD), lambda g, *_: (0, 0, groups + g)),
            ],
            out_specs=[spec, spec, pl.BlockSpec((1, rows // PIECE, repeats * PIECE), lambda g, *_: (g, 0, 0))],
        ),
        out_shape=[
            jax.ShapeDtypeStruct(query.shape, BF16),
            jax.ShapeDtypeStruct(query.shape, F32),
            jax.ShapeDtypeStruct((groups, rows // PIECE, repeats * PIECE), F32),
        ],
        compiler_params=pltpu.CompilerParams(vmem_limit_bytes=48 << 20),
    )(*where, query, kv, kv)


def backward_kernel(
    repeats, slots_ref, places_ref, lengths_ref, q_ref, k_ref, v_ref, full_ref, grad_ref, lse_ref,
    dq_ref, dk_ref, dv_ref, key_acc, value_acc,
):
    cols = repeats * PIECE
    key_acc[...] = jnp.zeros_like(key_acc)
    value_acc[...] = jnp.zeros_like(value_acc)
    for i in range(q_ref.shape[0] // PIECE):
        place = places_ref[i]
        lo = key_span(place, lengths_ref)
        q, grad = stacked(q_ref, i, repeats), stacked(grad_ref, i, repeats)
        product = grad.astype(F32) * stacked(full_ref, i, repeats)
        delta = jnp.sum(jnp.swapaxes(product, 0, 1), axis=0, keepdims=True)
        lse = lse_ref[0, pl.ds(i, 1), :]

        def step(n, dq, lo=lo, place=place, q=q, grad=grad, delta=delta, lse=lse):
            first = lo + n * CHUNK
            slots, (k, v) = key_chunk(slots_ref, first, CHUNK, k_ref, v_ref)
            scores = dot_last(k, q) * HD**-0.5
            weights = jnp.where(
                seen(lengths_ref, place, first, CHUNK * PIECE, cols), jnp.exp(scores - lse), 0.0)
            back = (weights * (dot_last(v, grad) - delta)).astype(BF16)
            dk = dot(back, q)
            dv = dot(weights.astype(BF16), grad)
            for j, s in enumerate(slots):
                key_acc[s] += dk[j * PIECE : (j + 1) * PIECE]
                value_acc[s] += dv[j * PIECE : (j + 1) * PIECE]
            return dq + dot_first(k, back)

        dq = lax.fori_loop(0, (place - lo) // CHUNK + 1, step, jnp.zeros((HD, cols), F32))
        out = (jnp.swapaxes(dq, 0, 1) * HD**-0.5).astype(BF16)
        for r in range(repeats):
            dq_ref[pl.ds(i * PIECE, PIECE), pl.ds(r * HD, HD)] = out[r * PIECE : (r + 1) * PIECE]
    dk_ref[...] = (key_acc[...] * HD**-0.5).astype(BF16)
    dv_ref[...] = value_acc[...].astype(BF16)


def attention_backward(query, kv, full, lse, grad, where):
    rows, pieces = query.shape[0], kv.shape[0]
    groups = kv.shape[2] // (2 * HD)
    wide = query.shape[1] // groups
    repeats = wide // HD
    spec = pl.BlockSpec((rows, wide), lambda g, *_: (0, g))
    block = pl.BlockSpec((pieces, PIECE, HD), lambda g, *_: (0, 0, g))
    half = jax.ShapeDtypeStruct((pieces, PIECE, groups * HD), BF16)
    return pl.pallas_call(
        functools.partial(backward_kernel, repeats),
        grid_spec=pltpu.PrefetchScalarGridSpec(
            num_scalar_prefetch=3,
            grid=(groups,),
            in_specs=[
                spec, block, pl.BlockSpec((pieces, PIECE, HD), lambda g, *_: (0, 0, groups + g)), spec, spec,
                pl.BlockSpec((1, rows // PIECE, repeats * PIECE), lambda g, *_: (g, 0, 0)),
            ],
            out_specs=[spec, block, block],
            scratch_shapes=[pltpu.VMEM((pieces, PIECE, HD), F32)] * 2,
        ),
        out_shape=[jax.ShapeDtypeStruct(query.shape, BF16), half, half],
        compiler_params=pltpu.CompilerParams(vmem_limit_bytes=60 << 20),
    )(*where, query, kv, kv, full, grad, lse)


def tiles(total, size, body):
    if total == size:
        body(pl.ds(0, size))
    else:

        @pl.loop(0, total // size)
        def _(i):
            body(pl.ds(pl.multiple_of(i * size, size), size))


def shifted(c, by):
    if isinstance(c.start, int):
        return pl.ds(c.start + by, c.size)
    return pl.ds(pl.multiple_of(c.start + by, c.size), c.size)


def expert_kernel(
    chips, experts, ext_ref, up_own, up_other, down_own, down_other, cot_ref,
    shared_up, shared_down, cot_pair, cot_own, resid, gates, turned, low, full_out,
    output, hidden_grad, mixed_grad, out_part, up_part, down_part, din, dout, row_part, norm_pair, other_down,
    home_ref, routed_ref, din_ref, dout_ref, shared_act, shared_dab, hid, from_back, from_sum,
    in_ref, out_ref, ext, cot, rows_x, rows_dy, rows_act, rows_dab, both, result, back, deal, gate, take, take_gate,
    own_d, own_o, stage_d, stage_o, sib_d, sib_o, right_d, right_o, left_d, left_o,
    copy_sem, cot_sem, ag_r, ag_l, ag_sr, ag_sl, ss_r, ss_l, ss_sr, ss_sl,
    ex_sem, ss_ex, rs_r, rs_l, ss_rr, ss_rl, weight_sem, pair_sem, load_sem, y_send, y_recv,
):
    blk, core, at, sib = ring_info(chips)
    h = lax.axis_index("head")
    right, left = at(1), at(-1)
    half = chips // 2
    rows, wide = ext_ref.shape
    width = in_ref.shape[0]
    hidden = out_ref.shape[0]
    slots = rows_x.shape[0] // chips
    cut = rows // 2
    upper, lower = pl.ds(0, cut), pl.ds(cut, cut)

    barrier = pltpu.get_barrier_semaphore()
    for other in (right, left, sib):
        pl.semaphore_signal(barrier, inc=1, device_id={"blk": other}, device_id_type=MESH)
    pl.semaphore_signal(barrier, inc=1, device_id={"head": 1 - h}, device_id_type=MESH)
    pl.semaphore_wait(barrier, 4)

    def remote(src, dst, ssem, rsem, dev):
        return pltpu.make_async_remote_copy(
            src_ref=src, dst_ref=dst, send_sem=ssem, recv_sem=rsem,
            device_id={"blk": dev}, device_id_type=MESH)

    def hop_right(part, k, s):
        ref = ext.at[at(1 - s), part]
        return remote(ref, ref, ss_r.at[k, s], ag_r.at[k, s], right)

    def hop_left(part, k, s):
        ref = ext.at[at(s - 1), part]
        return remote(ref, ref, ss_l.at[k, s], ag_l.at[k, s], left)

    def over_right(part, k, s):
        ref = ext.at[at(-s), part]
        return remote(ref, ref, ss_sr.at[k, s], ag_sr.at[k, s], sib)

    def over_left(part, k, s):
        ref = ext.at[at(s), part]
        return remote(ref, ref, ss_sl.at[k, s], ag_sl.at[k, s], sib)

    def place_of(g, j):
        return at(-g) if j == 0 else at(g)

    def cot_copy(g, j):
        there = place_of(g, j)
        slot = lax.rem(g, 2)
        return pltpu.make_async_copy(
            cot_ref.at[pl.ds(there - core, 2)], cot.at[slot, j], cot_sem.at[slot, j])

    def exchange_d(g, j):
        return remote(stage_d.at[j], sib_d.at[lax.div(place_of(g, j), 2)], ss_ex.at[0, j, g], ex_sem.at[0, j, g], sib)

    def exchange_o(g, j):
        return remote(stage_o.at[j], sib_o.at[lax.div(place_of(g, j), 2)], ss_ex.at[1, j, g], ex_sem.at[1, j, g], sib)

    mine = pltpu.make_async_copy(ext_ref, ext.at[blk], copy_sem)
    mine.start()
    cot_copy(0, 0).start()
    weights = []
    for i, (up, down) in ((h, (up_own, down_own)), (1 - h, (up_other, down_other))):
        size = up.shape[0]
        start = pl.multiple_of(i * size, size)
        weights.append((up, in_ref.at[pl.ds(start, size)]))
        weights.append((down, out_ref.at[:, pl.ds(start, size)]))
    weights = [pltpu.make_async_copy(a, b, weight_sem.at[i]) for i, (a, b) in enumerate(weights)]
    for copy in weights:
        copy.start()
    mine.wait()
    for k, part in ((0, upper), (1, lower)):
        hop_right(part, k, 1).start()
        hop_left(part, k, 1).start()
        over_right(part, k, 0).start()
    own_norm = ext.at[blk, :, pl.ds(0, width)]
    keep = pltpu.make_async_copy(own_norm, norm_pair.at[h], pair_sem.at[0])
    keep.start()
    swapped = pltpu.make_async_remote_copy(
        src_ref=own_norm, dst_ref=norm_pair.at[h], send_sem=pair_sem.at[1], recv_sem=pair_sem.at[2],
        device_id={"head": 1 - h}, device_id_type=MESH)
    swapped.start()
    for copy in weights:
        copy.wait()

    lane = lax.broadcasted_iota(jnp.int32, (2 * rows, 128), 1)
    token_row = lax.broadcasted_iota(jnp.int32, (2 * rows, 2 * rows), 0)
    token_col = lax.broadcasted_iota(jnp.int32, (2 * rows, 2 * rows), 1)
    same = (token_row < rows) == (token_col < rows)
    triangle = jnp.where((token_row > token_col) & same, 1.0, 0.0).astype(BF16)
    offset = jnp.float32(slots // 2)
    shift_col = jnp.where(lax.broadcasted_iota(jnp.int32, (2 * rows, 1), 0) < rows, 0.0, offset)
    shift_row = jnp.where(lax.broadcasted_iota(jnp.int32, (1, 2 * rows), 1) < rows, 0.0, offset)
    slot_id = lax.broadcasted_iota(jnp.int32, (slots, 2 * rows), 0).astype(F32)
    lane_row = lax.broadcasted_iota(jnp.int32, (128, 128), 0)
    pick_mask = jnp.where(lane_row == experts + blk, 1.0, 0.0).astype(BF16)
    pick_gate = jnp.where(lane_row == blk, 1.0, 0.0).astype(BF16)
    lane_col = lax.broadcasted_iota(jnp.int32, (8, 128), 1)
    mask_row = jnp.where(lane_col == experts + blk, 1.0, 0.0).astype(BF16)
    gate_row = jnp.where(lane_col == blk, 1.0, 0.0).astype(BF16)

    def arrive(s):
        last = isinstance(s, int) and s == half
        hop_right(upper, 0, s).wait_recv()
        if not last:
            hop_right(upper, 0, s + 1).start()
        over_right(upper, 0, s).start()
        hop_left(lower, 1, s).wait_recv()
        if not last:
            hop_left(lower, 1, s + 1).start()
        over_left(lower, 1, s).start()
        if last:
            return
        hop_right(lower, 1, s).wait_recv()

        @pl.when(s < half - 1)
        def _():
            hop_right(lower, 1, s + 1).start()

        over_right(lower, 1, s).start()
        hop_left(upper, 0, s).wait_recv()

        @pl.when(s < half - 1)
        def _():
            hop_left(upper, 0, s + 1).start()

        over_left(upper, 0, s).start()

    def work(g, count, base, first):
        turn = lax.rem(g, 2)
        size = count * slots
        group = pl.ds(base, size)
        part = pl.ds(0, size)
        firsts = [place_of(g, j) - core for j in range(count)]
        for j in range(count):
            lanes = ext[pl.ds(firsts[j], 2), :, pl.ds(width, 128)].reshape(2 * rows, 128)
            chosen = dot(lanes, pick_mask)
            rank = dot(triangle, chosen.astype(BF16))
            spread = jnp.where((rank + shift_col == lane.astype(F32)) & (chosen > 0.5), 1.0, 0.0).astype(BF16)
            deal[j] = spread.reshape(2, rows, 128)
            gate[j] = dot(lanes, pick_gate).reshape(2, rows, 128)
            chosen_row = dot_last(mask_row, lanes)
            rank_row = dot_last(chosen_row.astype(BF16), triangle)
            weight_row = dot_last(gate_row, lanes)
            taken = jnp.where((rank_row[:1] + shift_row == slot_id) & (chosen_row[:1] > 0.5), 1.0, 0.0)
            take[j] = taken.astype(BF16)
            take_gate[j] = (taken * weight_row[:1]).astype(BF16)
        for j in range(count):
            cot_copy(g, j).wait()
            where = pl.ds(pl.multiple_of(base + j * slots, slots), slots)

            def pick_rows(c, j=j, where=where):
                rows_x[where, c] = dot(
                    take[j], ext[pl.ds(firsts[j], 2), :, c].reshape(2 * rows, c.size)).astype(BF16)
                rows_dy[where, c] = dot(take_gate[j], cot[turn, j, :, :, c].reshape(2 * rows, c.size)).astype(BF16)

            for t in range(2):
                pick_rows(pl.ds(t * (width // 2), width // 2))

        def hidden_tile(c):
            high = shifted(c, hidden)
            x = rows_x[group]
            gate_part = dot(x, in_ref[:, c])
            lift = dot(x, in_ref[:, high])
            both[part, c] = gate_part
            both[part, high] = lift
            rows_act[group, c] = (jax.nn.silu(gate_part) * lift).astype(BF16)

        for t in range(2):
            hidden_tile(pl.ds(t * (hidden // 2), hidden // 2))

        def result_tile(c):
            result[part, c] = dot(rows_act[group], out_ref[:, c]).astype(BF16)

        for t in range(2):
            result_tile(pl.ds(t * (width // 2), width // 2))

        def grad_tile(c):
            high = shifted(c, hidden)
            da = dot_last(rows_dy[group], out_ref[c, :])
            gate_part, lift = both[part, c], both[part, high]
            sig = jax.nn.sigmoid(gate_part)
            rows_dab[group, c] = (da * lift * sig * (1.0 + gate_part * (1.0 - sig))).astype(BF16)
            rows_dab[group, high] = (da * gate_part * sig).astype(BF16)

        for t in range(2):
            grad_tile(pl.ds(t * (hidden // 2), hidden // 2))

        def back_tile(c):
            back[part, c] = dot_last(rows_dab[group], in_ref[c, :]).astype(BF16)

        for t in range(2):
            back_tile(pl.ds(t * (width // 2), width // 2))
        if first is not None:

            @pl.when(first)
            def _():
                for j in range(2):
                    exchange_d(g - 1, j).wait_send()
                    exchange_o(g - 1, j).wait_send()

            @pl.when(jnp.logical_not(first))
            def _():
                exchange_d(g - 1, 0).wait_send()
                exchange_o(g - 1, 0).wait_send()

        for j in range(count):
            chip = lax.div(firsts[j], 2)
            for which, to_d, to_o in (
                (core, own_d.at[chip], own_o.at[chip]),
                (1 - core, stage_d.at[j], stage_o.at[j]),
            ):
                from_slots = pl.ds(j * slots, slots)
                dealer = deal[j, which]
                share = gate[j, which]
                total = jnp.zeros((rows, 1), F32)
                for t in range(width // 512):
                    c = pl.ds(t * 512, 512)
                    home_rows = dot(dealer, result[from_slots, c])
                    to_o[:, c] = (home_rows * share[:, :1]).astype(BF16)
                    total = total + jnp.sum(
                        home_rows * cot[turn, j, which, :, c].astype(F32), axis=1, keepdims=True)
                    to_d[:, c] = dot(dealer, back[from_slots, c]).astype(BF16)
                high = total.astype(BF16).astype(F32)
                own_lane = lane[:rows]
                lanes = jnp.where(own_lane == blk, high, jnp.where(own_lane == experts + blk, total - high, 0.0))
                to_d[:, pl.ds(width, 128)] = lanes.astype(BF16)
            exchange_d(g, j).start()
            exchange_o(g, j).start()

    over_right(upper, 0, 0).wait_recv()
    over_right(lower, 1, 0).wait_recv()
    cot_copy(1, 0).start()
    cot_copy(1, 1).start()
    work(0, 1, 0, None)

    @pl.loop(1, half)
    def _(g):
        arrive(g)
        over_right(upper, 0, g).wait_recv()
        over_right(lower, 1, g).wait_recv()
        over_left(lower, 1, g).wait_recv()
        over_left(upper, 0, g).wait_recv()
        cot_copy(g + 1, 0).start()

        @pl.when(g < half - 1)
        def _():
            cot_copy(g + 1, 1).start()

        work(g, 2, pl.multiple_of(slots + (g - 1) * 2 * slots, slots), g > 1)

    arrive(half)
    over_right(upper, 0, half).wait_recv()
    over_left(lower, 1, half).wait_recv()
    work(half, 1, (2 * half - 1) * slots, True)

    arrays = ((0, own_d, sib_d, right_d, left_d, home_ref), (1, own_o, sib_o, right_o, left_o, routed_ref))
    arrived = set()

    def join(a, own, other, d, part, into, received):
        g, j = (d, 1) if 0 < d < half else (abs(d), 0)
        if (a, g, j) not in arrived:
            arrived.add((a, g, j))
            (exchange_d, exchange_o)[a](g, j).wait_recv()
        chip = lax.div(at(d), 2)

        def add(c):
            total = own[chip, c].astype(F32) + other[chip, c].astype(F32)
            for ref in received:
                total = total + ref[c].astype(F32)
            into[c] = total.astype(into.dtype)

        @pl.loop(0, cut // 16)
        def _(i):
            add(pl.ds(pl.multiple_of(part.start + i * 16, 16), 16))

    def pass_right(a, src, buf, k, part, s):
        return remote(src.at[part], buf.at[s - 1, part], ss_rr.at[a, k, s], rs_r.at[a, k, s], right)

    def pass_left(a, src, buf, k, part, s):
        return remote(src.at[part], buf.at[s - 1, part], ss_rl.at[a, k, s], rs_l.at[a, k, s], left)

    ways = (
        (0, upper, 1, half), (1, lower, -1, half), (1, lower, 1, half - 1), (0, upper, -1, half - 1),
    )
    sent = []

    def scatter_step(a, s):
        _, own, other, to_right, to_left, _ = arrays[a]
        for k, part, way, hops in ways:
            if s > hops:
                continue
            make, buf = (pass_right, to_right) if way > 0 else (pass_left, to_left)
            d = way * (hops - s + 1)
            if d == -half:
                d = half
            if s == 1:
                src = own.at[lax.div(at(d), 2)]
                join(a, own, other, d, part, src, ())
            else:
                src = buf.at[s - 2]
                make(a, src, buf, k, part, s - 1).wait_recv()
                join(a, own, other, d, part, src, (src,))
            copy = make(a, src, buf, k, part, s)
            copy.start()
            sent.append(copy)

    def scatter_finish(a):
        _, own, other, to_right, to_left, into = arrays[a]
        for k, part in ((0, upper), (1, lower)):
            last_right, last_left = half - k, half - 1 + k
            pass_right(a, own.at[0], to_right, k, part, last_right).wait_recv()
            pass_left(a, own.at[0], to_left, k, part, last_left).wait_recv()
            join(a, own, other, 0, part, into, (to_right.at[last_right - 1], to_left.at[last_left - 1]))

    loads = 0

    def move(src, dst):
        nonlocal loads
        copy = pltpu.make_async_copy(src, dst, load_sem.at[loads])
        loads += 1
        copy.start()
        return copy

    def cross(i, src, dst):
        return pltpu.make_async_remote_copy(
            src_ref=src, dst_ref=dst, send_sem=y_send.at[i], recv_sem=y_recv.at[i],
            device_id={"head": 1 - h}, device_id_type=MESH)

    theirs = pl.ds(pl.multiple_of((1 - h) * rows, rows), rows)
    ours = pl.ds(pl.multiple_of(h * rows, rows), rows)
    keep.wait()
    swapped.wait()
    shared_loads = [
        move(shared_up, in_ref), move(shared_down, out_ref), move(cot_pair, back),
        move(norm_pair.at[0], result.at[pl.ds(0, rows)]), move(norm_pair.at[1], result.at[pl.ds(rows, rows)])]
    scatter_step(0, 1)

    def weight_in(c):
        din_ref[c, :] = dot_first(rows_x[:, c], rows_dab[...]).astype(BF16)

    tiles(width, 256, weight_in)
    din_out = move(din_ref, din)
    load_out = move(full_out, rows_x.at[pl.ds(0, low.shape[1])])
    scatter_step(0, 2)

    for copy in shared_loads:
        copy.wait()

    def shared_tile(c):
        high = shifted(c, hidden)
        gate_part = dot(result[...], in_ref[:, c])
        lift = dot(result[...], in_ref[:, high])
        sig = jax.nn.sigmoid(gate_part)
        shared_act[:, c] = (gate_part * sig * lift).astype(BF16)
        da = dot_last(back[...], out_ref[c, :])
        shared_dab[:, c] = (da * lift * sig * (1.0 + gate_part * (1.0 - sig))).astype(BF16)
        shared_dab[:, high] = (da * gate_part * sig).astype(BF16)

    tiles(hidden, 256, shared_tile)
    to_back, to_sum = cot.at[0, 0, 0], cot.at[0, 0, 1]

    def back_part(c):
        to_back[:, c] = dot_last(shared_dab[theirs, :], in_ref[c, :]).astype(BF16)

    tiles(width, 512, back_part)
    swap_back = cross(0, to_back, from_back)
    swap_back.start()

    def weight_out(c):
        dout_ref[c, :] = dot_first(rows_act[:, c], rows_dy[...]).astype(BF16)

    tiles(hidden, 256, weight_out)
    dout_out = move(dout_ref, dout)
    scatter_step(0, 3)
    scatter_step(1, 1)

    def sum_part(c):
        to_sum[:, c] = dot(shared_act[theirs, :], out_ref[:, c]).astype(BF16)

    tiles(width, 512, sum_part)
    swap_sum = cross(1, to_sum, from_sum)
    swap_sum.start()
    din_out.wait()
    dout_out.wait()
    swap_down = cross(3, dout.at[:, pl.ds(pl.multiple_of((1 - h) * (width // 2), 128), width // 2)], other_down)
    swap_down.start()

    def shared_in(c):
        din_ref[c, :] = dot_first(result[:, c], shared_dab[...]).astype(BF16)

    tiles(width, 256, shared_in)
    up_out = move(din_ref, up_part)
    scatter_step(0, 4)
    scatter_step(1, 2)

    def shared_out(c):
        dout_ref[c, :] = dot_first(shared_act[:, c], back[...]).astype(BF16)

    tiles(hidden, 256, shared_out)
    down_out = move(dout_ref, down_part)
    swap_back.wait_recv()
    scatter_finish(0)

    lanes = home_ref[:, pl.ds(width, 128)].astype(BF16)
    row_id = lax.broadcasted_iota(jnp.int32, (128, 128), 0)
    col_id = lax.broadcasted_iota(jnp.int32, (128, 128), 1)
    fold = jnp.where((row_id == col_id) | (row_id == col_id + experts), 1.0, 0.0).astype(BF16)
    weighted = gates[...] * dot(lanes, fold)
    logit_grad = (weighted - gates[...] * jnp.sum(weighted, axis=1, keepdims=True)).astype(BF16)
    short = logit_grad[:, : turned.shape[0]]

    def norm_part(c):
        hidden_grad[:, c] = (
            home_ref[:, c] + from_back[:, c].astype(F32) + dot_last(shared_dab[ours, :], in_ref[c, :])
            + dot(short, turned[:, c].astype(BF16)))
        row_part[:, c] = dot_first(logit_grad, ext[blk, :, c])

    tiles(width, 512, norm_part)

    def norm_rows(n, total):
        part = pl.ds(pl.multiple_of(n * 32, 32), 32)
        x, up = resid[part, :], hidden_grad[part, :]
        scaler = lax.rsqrt(jnp.mean(x * x, axis=1, keepdims=True) + EPS)
        normed = x * scaler
        scaled = up * turned[pl.ds(experts + 1, 1), :]
        grad = cot_own[part, :].astype(F32) + scaler * (
            scaled - normed * jnp.mean(scaled * normed, axis=1, keepdims=True))
        hidden_grad[part, :] = grad
        hid[h, part, :] = grad.astype(BF16)
        return total + jnp.sum(up * normed, axis=0, keepdims=True)

    gain = lax.fori_loop(0, rows // 32, norm_rows, jnp.zeros((1, width), F32))
    swap_hid = cross(2, hid.at[h], hid.at[h])
    swap_hid.start()
    scatter_step(1, 3)
    row_part[pl.ds(experts + 1, 1), :] = gain
    load_out.wait()
    inner = low.shape[1]
    full = rows_x.at[pl.ds(0, inner)]

    def mixed_tile(who, where):
        for t in range(inner // 256):
            c = pl.ds(t * 256, 256)
            mixed_grad[where, c] = dot_last(hid[who], full[c, :]).astype(BF16)

    mixed_tile(h, ours)
    scatter_step(1, 4)
    swap_hid.wait_recv()
    mixed_tile(1 - h, theirs)

    def out_tile(c):
        rows_dy[c, :] = (
            dot_first(low[pl.ds(0, rows), c], hid[0]) + dot_first(low[pl.ds(rows, rows), c], hid[1])).astype(BF16)

    for t in range(inner // 256):
        out_tile(pl.ds(t * 256, 256))
    part_out = move(rows_dy.at[pl.ds(0, inner)], out_part)
    swap_sum.wait_recv()
    scatter_finish(1)

    def output_tile(c):
        output[:, c] = (
            resid[:, c] + routed_ref[:, c] + from_sum[:, c].astype(F32)
            + dot(shared_act[ours, :], out_ref[:, c])).astype(BF16)

    tiles(width, 512, output_tile)
    for copy in (swap_back, swap_sum, swap_hid, swap_down):
        copy.wait_send()
    swap_down.wait_recv()
    for copy in (up_out, down_out, part_out):
        copy.wait()
    for copy in sent:
        copy.wait_send()
    exchange_d(half, 0).wait_send()
    exchange_o(half, 0).wait_send()
    for k, part in ((0, upper), (1, lower)):
        over_right(part, k, 0).wait_send()
        for s in range(1, half + 1):
            if s <= half - k:
                hop_right(part, k, s).wait_send()
                over_right(part, k, s).wait_send()
            if s <= half - 1 + k:
                hop_left(part, k, s).wait_send()
                over_left(part, k, s).wait_send()


def experts_fused(
    ext, weights, cot_all, shared, cot_pair, cot_own, resid, gates, turned, low, full_out, blks, capacity, collective_id,
):
    chips, half = blks // 2, blks // 4
    rows, wide = ext.shape
    width, hidden = 2 * weights[0].shape[0], weights[2].shape[0]
    count = blks * capacity
    group = 4 * capacity
    inner = low.shape[1]
    dma = pltpu.SemaphoreType.DMA
    vmem = pl.BlockSpec(memory_space=pltpu.VMEM)
    anywhere = pl.BlockSpec(memory_space=pl.ANY)

    def bf16(*shape):
        return pltpu.VMEM(shape, BF16)

    def f32(*shape):
        return pltpu.VMEM(shape, F32)

    out = [
        ((rows, width), BF16, vmem), ((rows, width), F32, vmem), ((2 * rows, inner), BF16, vmem),
        ((inner, width), BF16, anywhere), ((width, 2 * hidden), BF16, anywhere), ((hidden, width), BF16, anywhere),
        ((width, 2 * hidden), BF16, anywhere), ((hidden, width), BF16, anywhere), ((128, width), F32, vmem),
        ((2, rows, width), BF16, anywhere), ((hidden, width // 2), BF16, anywhere),
    ]
    return pl.pallas_call(
        functools.partial(expert_kernel, chips, blks),
        out_shape=[jax.ShapeDtypeStruct(s, t) for s, t, _ in out],
        in_specs=[anywhere] * 9 + [vmem] * 5 + [anywhere],
        out_specs=[space for _, _, space in out],
        scratch_shapes=[
            f32(rows, wide), f32(rows, width), bf16(width, 2 * hidden), bf16(hidden, width),
            bf16(2 * rows, hidden), bf16(2 * rows, 2 * hidden), bf16(2, rows, width), bf16(rows, width), bf16(rows, width),
            bf16(width, 2 * hidden), bf16(hidden, width),
            bf16(blks, rows, wide), bf16(2, 2, 2, rows, width),
            bf16(count, width), bf16(count, width), bf16(count, hidden), bf16(count, 2 * hidden),
            f32(group, 2 * hidden), bf16(group, width), bf16(group, width),
            bf16(2, 2, rows, 128), f32(2, 2, rows, 128), bf16(2, 128, 2 * rows), bf16(2, 128, 2 * rows),
            bf16(chips, rows, wide), bf16(chips, rows, width), bf16(2, rows, wide), bf16(2, rows, width),
            bf16(chips, rows, wide), bf16(chips, rows, width),
            bf16(half, rows, wide), bf16(half, rows, width), bf16(half, rows, wide), bf16(half, rows, width),
            dma(()), dma((2, 2)),
        ] + [dma((2, half + 1))] * 8 + [dma((2, 2, half + 1))] * 2 + [dma((2, 2, half + 1))] * 4
        + [dma((4,)), dma((3,)), dma((11,)), dma((4,)), dma((4,))],
        compiler_params=pltpu.CompilerParams(
            collective_id=collective_id, has_side_effects=True, vmem_limit_bytes=63 << 20),
    )(ext, *weights, cot_all, *shared, cot_pair, cot_own, resid, gates, turned, low, full_out)


class Ring:
    def __init__(self, info, chips, chunks, first, sems):
        self.blk, self.at, self.sib = info
        self.half = chips // 2
        self.chunks, self.first = chunks, first
        self.send_r, self.recv_r, self.send_l, self.recv_l, self.send_s, self.recv_s = sems

    def hops(self, c):
        return self.half - c % 2, self.half - 1 + c % 2

    def copy(self, ref, ssem, rsem, dev):
        return pltpu.make_async_remote_copy(
            src_ref=ref, dst_ref=ref, send_sem=ssem, recv_sem=rsem,
            device_id={"blk": dev}, device_id_type=MESH)

    def right(self, c, s):
        i = self.first + c
        return self.copy(self.chunks[c](self.at(1 - s)), self.send_r.at[i, s], self.recv_r.at[i, s], self.at(1))

    def left(self, c, s):
        i = self.first + c
        return self.copy(self.chunks[c](self.at(s - 1)), self.send_l.at[i, s], self.recv_l.at[i, s], self.at(-1))

    def over(self, c, d):
        i, k = self.first + c, d + self.half
        return self.copy(self.chunks[c](self.at(d)), self.send_s.at[i, k], self.recv_s.at[i, k], self.sib)

    def start(self, c):
        self.right(c, 1).start()
        self.left(c, 1).start()
        self.over(c, 0).start()

    def step(self, s):
        for c in range(len(self.chunks)):
            rh, lh = self.hops(c)
            if s <= rh:
                self.right(c, s).wait_recv()
                if s < rh:
                    self.right(c, s + 1).start()
                self.over(c, -s).start()
            if s <= lh:
                self.left(c, s).wait_recv()
                if s < lh:
                    self.left(c, s + 1).start()
                self.over(c, s).start()

    def end(self):
        for c in range(len(self.chunks)):
            rh, lh = self.hops(c)
            for d in range(-rh, lh + 1):
                self.over(c, d).wait_recv()

    def flush(self):
        for c in range(len(self.chunks)):
            rh, lh = self.hops(c)
            for s in range(1, rh + 1):
                self.right(c, s).wait_send()
            for s in range(1, lh + 1):
                self.left(c, s).wait_send()
            for d in range(-rh, lh + 1):
                self.over(c, d).wait_send()


def front_kernel(
    chips, experts,
    order_ref, lengths_ref, routes, router, gain_one, gain_two, tokens, cotangent, w_query, w_key, w_value, w_out,
    shared_up, shared_down, expert_up, expert_down,
    n1_out, query_out, kv_out, first_out, out_out, up_w, down_w, cot, cot_pair, expert_in, expert_out,
    low_out, full_out, lse, resid, ext, gates, short, slots_ref,
    small, n1, query, kv, first_w, out_w, low, full, turned, pair, to_other, from_other,
    send_r, recv_r, send_l, recv_l, send_s, recv_s, own_sem, y_send, y_recv, store_sem,
):
    h = lax.axis_index("head")
    blk, core, at, sib = ring_info(chips)
    half = chips // 2
    rows, width = tokens.shape
    qw, kw = w_query.shape[1] // 2, w_key.shape[1] // 2
    sw = shared_up.shape[1] // 4
    barrier = pltpu.get_barrier_semaphore()
    for other in (at(1), at(-1), sib):
        pl.semaphore_signal(barrier, inc=1, device_id={"blk": other}, device_id_type=MESH)
    pl.semaphore_signal(barrier, inc=1, device_id={"head": 1 - h}, device_id_type=MESH)
    pl.semaphore_wait(barrier, 4)

    wide = lax.broadcasted_iota(jnp.int32, (experts, 128), 1)
    column = lax.broadcasted_iota(jnp.int32, (experts, 128), 0)
    block = dot_first(router[...], jnp.where(wide == column, 1.0, 0.0).astype(BF16))
    for n, gain in ((0, gain_one), (1, gain_two)):
        spot = jnp.where(lax.broadcasted_iota(jnp.int32, (1, 128), 1) == experts + n, 1.0, 0.0).astype(BF16)
        block = block + dot_first(gain[...], spot)
    small[...] = block.astype(BF16)

    def lanes_of(start, size):
        return pl.ds(pl.multiple_of(start, 128), size)

    def halves(i, j):
        return [
            (w_query.at[:, lanes_of(i * qw, qw)], first_w.at[j, blk, :, pl.ds(0, qw)]),
            (w_key.at[:, lanes_of(i * kw, kw)], first_w.at[j, blk, :, pl.ds(qw, kw)]),
            (w_value.at[:, lanes_of(i * kw, kw)], first_w.at[j, blk, :, pl.ds(qw + kw, kw)]),
            (small, first_w.at[j, blk, :, pl.ds(qw + 2 * kw, small.shape[1])]),
            (tokens, pair.at[j]),
            (shared_up.at[:, lanes_of(i * sw, sw)], up_w.at[j, blk, :, pl.ds(0, sw)]),
            (shared_up.at[:, lanes_of((2 + i) * sw, sw)], up_w.at[j, blk, :, pl.ds(sw, sw)]),
            (cotangent, cot_pair.at[j]),
        ]

    whole = [(expert_up, expert_in), (expert_down, expert_out)]

    stores = []

    def store(src, dst):
        copy = pltpu.make_async_copy(src, dst, store_sem.at[len(stores)])
        copy.start()
        stores.append(copy)

    own = [pltpu.make_async_copy(a, b, own_sem.at[i]) for i, (a, b) in enumerate(halves(h, h))]
    own.append(pltpu.make_async_copy(w_out, out_w.at[blk], own_sem.at[len(own)]))
    own.append(pltpu.make_async_copy(shared_down, down_w.at[blk], own_sem.at[len(own)]))
    own.append(pltpu.make_async_copy(cotangent, cot.at[blk], own_sem.at[len(own)]))
    swaps = [
        pltpu.make_async_remote_copy(
            src_ref=a, dst_ref=b, send_sem=y_send.at[i], recv_sem=y_recv.at[i],
            device_id={"head": 1 - h}, device_id_type=MESH)
        for i, (a, b) in enumerate(halves(1 - h, h) + whole)
    ]
    for i in range(5):
        swaps[i].start()
    for i in (0, 1, 2, 3, 8, 4):
        own[i].start()

    info = (blk, at, sib)
    sems = (send_r, recv_r, send_l, recv_l, send_s, recv_s)

    def row_cuts(ref, *sizes):
        start, chunks = 0, []
        for size in sizes:
            chunks.append(lambda b, start=start, size=size: ref.at[b, pl.ds(start, size)])
            start += size
        return chunks

    ring_w = Ring(info, chips, [lambda b: first_w.at[h, b], lambda b: first_w.at[1 - h, b]], 0, sems)
    out_rows, down_rows = w_out.shape[0], shared_down.shape[0]
    ring_o = Ring(info, chips, row_cuts(out_w, 32, out_rows - 32), 2, sems)
    ring_kv = Ring(info, chips, [lambda b: kv.at[2 * b], lambda b: kv.at[2 * b + 1]], 4, sems)
    ring_u = Ring(info, chips, [lambda b: up_w.at[h, b], lambda b: up_w.at[1 - h, b]], 6, sems)
    ring_d = Ring(info, chips, row_cuts(down_w, down_rows // 2, down_rows // 2), 8, sems)
    ring_c = Ring(info, chips, row_cuts(cot, rows // 2, rows // 2), 10, sems)

    for i in (0, 1, 2, 3):
        own[i].wait()
    ring_w.start(0)
    own[10].start()
    own[10].wait()
    ring_c.start(0)
    ring_c.start(1)
    own[8].wait()
    for i in range(4):
        swaps[i].wait_recv()
    ring_w.start(1)
    ring_o.start(0)
    ring_o.start(1)
    for i in (5, 6, 9, 7):
        own[i].start()
    for i in range(5, 10):
        swaps[i].start()
    for s in range(1, half + 1):
        ring_w.step(s)
        ring_o.step(s)
    ring_c.step(1)
    ring_w.end()
    store(first_w, first_out)
    own[4].wait()
    swaps[4].wait_recv()

    @pl.loop(0, slots_ref.shape[0])
    def _(j):
        slot = jnp.int32(0)
        for n in range(order_ref.shape[0]):
            there = 2 * (n % (2 * chips)) + n // (2 * chips)
            slot = jnp.maximum(slot, jnp.where(order_ref[n] == j, there, 0))
        slots_ref[j] = slot

    small_cols = first_w[:, :, :, pl.ds(qw + 2 * kw, 128)].reshape(width, 128)
    turned[...] = jnp.swapaxes(small_cols.astype(F32), 0, 1)
    short[...] = turned[pl.ds(0, short.shape[0]), :]

    @pl.loop(0, 2 * rows // 64)
    def _(i):
        x = pair[lax.div(i, rows // 64), pl.ds(pl.multiple_of(lax.rem(i, rows // 64) * 64, 64), 64), :].astype(F32)
        scaled = x * lax.rsqrt(jnp.mean(x * x, axis=1, keepdims=True) + EPS) * turned[pl.ds(experts, 1), :]
        n1[pl.ds(pl.multiple_of(i * 64, 64), 64), :] = scaled.astype(BF16)

    def project(start, size):
        weights = first_w[:, :, :, pl.ds(start, size)].reshape(width, size)
        return dot(n1[...], weights).astype(BF16)

    for t in range(2 * kw // 256):
        part = project(qw + t * 256, 256)
        for i in range(2):
            kv[2 * blk + i, :, pl.ds(t * 256, 256)] = part[i * rows : (i + 1) * rows]
    ring_kv.start(0)
    ring_kv.start(1)
    for t in range(qw // 256):
        query[:, pl.ds(t * 256, 256)] = project(t * 256, 256)
    for i in (5, 6, 9):
        own[i].wait()
    swaps[5].wait_recv()
    swaps[6].wait_recv()
    for s in range(1, half + 1):
        ring_kv.step(s)
        if s == half - 1:
            ring_c.step(2)
            for ring in (ring_u, ring_d):
                ring.start(0)
                ring.start(1)
    ring_kv.end()
    store(kv, kv_out)
    store(n1, n1_out)
    store(query, query_out)

    groups, repeats = kw // HD, qw // kw
    cols = repeats * PIECE
    pieces = slots_ref.shape[0]
    need = pieces // 2 + 1
    chunk = 6
    chunks = -(-need // chunk)
    later = [(ring_u, 1), (ring_d, 1), (ring_c, 3), (ring_u, 2), (ring_d, 2), (ring_c, 4)]
    turns = 0
    for i in range(2):
        place = order_ref[i * 2 * chips + blk]
        for g in range(groups):
            q = jnp.concatenate(
                [query[pl.ds(i * PIECE, PIECE), pl.ds((g * repeats + r) * HD, HD)] for r in range(repeats)], axis=0)

            def step(n, carry, place=place, g=g, q=q):
                top, total, acc = carry
                first = place + 1 - chunks * chunk + n * chunk
                _, (k, v) = key_chunk(
                    slots_ref, first, chunk, kv.at[:, :, pl.ds(g * HD, HD)], kv.at[:, :, pl.ds((groups + g) * HD, HD)])
                scores = dot_last(k, q) * HD**-0.5
                scores = jnp.where(seen(lengths_ref, place, first, chunk * PIECE, cols), scores, NEG)
                new = jnp.maximum(top, jnp.max(scores, axis=0, keepdims=True))
                weights = jnp.exp(scores - new)
                factor = jnp.exp(top - new)
                total = total * factor + jnp.sum(weights, axis=0, keepdims=True)
                return new, total, acc * factor + dot_first(v, weights.astype(BF16))

            top, total, acc = lax.fori_loop(
                0, chunks, step,
                (jnp.full((1, cols), NEG, F32), jnp.zeros((1, cols), F32), jnp.zeros((HD, cols), F32)))
            out = jnp.swapaxes(acc / total, 0, 1)
            lse[g, pl.ds(i, 1), :] = top + jnp.log(total)
            for r in range(repeats):
                part = out[r * PIECE : (r + 1) * PIECE]
                full[pl.ds(i * PIECE, PIECE), pl.ds((g * repeats + r) * HD, HD)] = part
                low[pl.ds(i * PIECE, PIECE), pl.ds((g * repeats + r) * HD, HD)] = part.astype(BF16)
            turns += 1
            if turns % 2 == 0:
                for ring, s in later[:3]:
                    ring.step(s)
                later = later[3:]

    ring_o.end()
    store(out_w, out_out)
    store(low, low_out)
    store(full, full_out)
    theirs = pl.ds(pl.multiple_of((1 - h) * rows, rows), rows)
    ours = pl.ds(pl.multiple_of(h * rows, rows), rows)

    def mixed(where, c):
        return dot(low[where, :], out_w[:, :, c].reshape(qw, c.size))

    for t in range(width // 512):
        c = pl.ds(t * 512, 512)
        to_other[:, c] = mixed(theirs, c).astype(BF16)
    swap_mixed = pltpu.make_async_remote_copy(
        src_ref=to_other, dst_ref=from_other, send_sem=y_send.at[10], recv_sem=y_recv.at[10],
        device_id={"head": 1 - h}, device_id_type=MESH)
    swap_mixed.start()
    for t in range(width // 512):
        c = pl.ds(t * 512, 512)
        resid[:, c] = pair[h, :, c].astype(F32) + mixed(ours, c)
    for ring in (ring_u, ring_d):
        ring.step(3)
    swap_mixed.wait_recv()

    @pl.loop(0, rows // 32)
    def _(i):
        part = pl.ds(pl.multiple_of(i * 32, 32), 32)
        x = resid[part, :] + from_other[part, :].astype(F32)
        resid[part, :] = x
        scaled = x * lax.rsqrt(jnp.mean(x * x, axis=1, keepdims=True) + EPS) * turned[pl.ds(experts + 1, 1), :]
        ext[part, pl.ds(0, width)] = scaled.astype(BF16)

    logits = dot_last(ext[:, pl.ds(0, width)], turned[...].astype(BF16))
    lane = lax.broadcasted_iota(jnp.int32, (128, rows), 0)
    masks = jnp.zeros((128, rows), F32)
    for r in range(routes.shape[0]):
        named = routes[r : r + 1, :]
        masks = jnp.where((lane == named) | (lane == named + experts), 1.0, masks)
    masks = jnp.swapaxes(masks, 0, 1)
    low_lane = lax.broadcasted_iota(jnp.int32, (rows, 128), 1) < experts
    mask = jnp.where(low_lane, masks, 0.0)
    shifted_mask = jnp.where(low_lane, 0.0, masks)
    masked = jnp.where(mask > 0.5, logits, NEG)
    raised = jnp.where(mask > 0.5, jnp.exp(masked - jnp.max(masked, axis=1, keepdims=True)), 0.0)
    probs = raised / jnp.sum(raised, axis=1, keepdims=True)
    gates[...] = probs
    ext[:, pl.ds(width, 128)] = (probs + shifted_mask).astype(BF16)
    for ring in (ring_u, ring_d):
        ring.step(4)
    own[7].wait()
    for i in (7, 8, 9):
        swaps[i].wait_recv()
    for ring in (ring_u, ring_d, ring_c):
        ring.end()
    for ring in (ring_w, ring_o, ring_kv, ring_u, ring_d, ring_c):
        ring.flush()
    for copy in swaps:
        copy.wait_send()
    swap_mixed.wait_send()
    for copy in stores:
        copy.wait()


def front_fused(
    tokens, cotangent, piece_order, seq_lengths, routes, w_query, w_key, w_value, w_router, gain_one, gain_two, w_out,
    shared_up, shared_down, expert_up, expert_down, blks, collective_id,
):
    chips, half = blks // 2, blks // 4
    rows, width = tokens.shape
    dense = w_query.shape[0]
    qw, kw, sw = w_query.shape[1] // 2, w_key.shape[1] // 2, shared_up.shape[1] // 4
    groups, repeats = kw // HD, qw // kw
    dma = pltpu.SemaphoreType.DMA
    vmem = pl.BlockSpec(memory_space=pltpu.VMEM)
    anywhere = pl.BlockSpec(memory_space=pl.ANY)
    smem = pl.BlockSpec(memory_space=pltpu.SMEM)
    out = [
        ((2 * rows, width), BF16, anywhere), ((2 * rows, qw), BF16, anywhere), ((2 * blks, rows, 2 * kw), BF16, anywhere),
        ((2, blks, dense, qw + 2 * kw + 128), BF16, anywhere), ((blks, w_out.shape[0], width), BF16, anywhere),
        ((2, blks, dense, 2 * sw), BF16, anywhere), ((blks, shared_down.shape[0], width), BF16, anywhere),
        ((blks, rows, width), BF16, anywhere), ((2, rows, width), BF16, anywhere),
        (expert_up.shape, BF16, anywhere), (expert_down.shape, BF16, anywhere),
        ((2 * rows, qw), BF16, anywhere), ((2 * rows, qw), F32, anywhere), ((groups, 2, repeats * PIECE), F32, vmem),
        ((rows, width), F32, vmem), ((rows, width + 128), BF16, vmem), ((rows, 128), F32, vmem), ((blks + 8, width), F32, vmem),
        ((2 * blks,), jnp.int32, smem),
    ]
    ring = [dma((12, half + 1))] * 4 + [dma((12, 2 * half + 1))] * 2
    (
        n1, query, kv, first_w, out_w, up_w, down_w, cot, cot_pair, expert_in, expert_out,
        low, full, lse, resid, ext, gates, turned, slots,
    ) = pl.pallas_call(
        functools.partial(front_kernel, chips, blks),
        out_shape=[jax.ShapeDtypeStruct(s, t) for s, t, _ in out],
        in_specs=[smem] * 2 + [vmem] * 4 + [anywhere, vmem] + [anywhere] * 4 + [vmem] * 2 + [anywhere] * 2,
        out_specs=[space for _, _, space in out],
        scratch_shapes=[pltpu.VMEM((dense, 128), BF16)] + [pltpu.VMEM(out[i][0], out[i][1]) for i in (0, 1, 2, 3, 4, 11, 12)] + [
            pltpu.VMEM((128, width), F32), pltpu.VMEM((2, rows, width), BF16), pltpu.VMEM((rows, width), BF16), pltpu.VMEM((rows, width), BF16)]
        + ring + [dma((11,)), dma((11,)), dma((11,)), dma((7,))],
        compiler_params=pltpu.CompilerParams(
            collective_id=collective_id, has_side_effects=True, vmem_limit_bytes=56 << 20),
    )(
        piece_order, seq_lengths, routes.T, w_router.T, gain_one[None], gain_two[None], tokens, cotangent,
        w_query, w_key, w_value, w_out, shared_up, shared_down, expert_up, expert_down)
    return (
        n1, query, kv, first_w.reshape(width, -1)[:, : qw + 2 * kw], out_w.reshape(-1, width),
        up_w.reshape(width, -1), down_w.reshape(-1, width), cot, cot_pair.reshape(2 * rows, width),
        expert_in, expert_out, low, full, lse, resid, ext, gates,
        None, None, None, (first_w, turned, slots))


class Scatter:
    def __init__(self, info, chips, chunks, first, sems):
        self.core, self.at, self.sib = info
        self.half = chips // 2
        self.chunks, self.first = chunks, first
        self.ex_s, self.ex_r, self.right_s, self.right_r, self.left_s, self.left_r = sems
        self.there, self.sent = set(), []

    def remote(self, src, dst, ssem, rsem, dev):
        return pltpu.make_async_remote_copy(
            src_ref=src, dst_ref=dst, send_sem=ssem, recv_sem=rsem,
            device_id={"blk": dev}, device_id_type=MESH)

    def over(self, c, d):
        own, other = self.chunks[c][:2]
        i, k = self.first + c, d + self.half
        place = self.at(d)
        return self.remote(
            own(place + 1 - 2 * self.core), other.at[lax.div(place, 2)], self.ex_s.at[i, k], self.ex_r.at[i, k], self.sib)

    def exchange(self):
        for d in sorted(range(1 - self.half, self.half + 1), key=lambda d: (-abs(d), -d)):
            for c in range(len(self.chunks)):
                copy = self.over(c, d)
                copy.start()
                self.sent.append(copy)

    def join(self, c, d, into, received):
        own, other = self.chunks[c][:2]
        if (c, d) not in self.there:
            self.there.add((c, d))
            self.over(c, d).wait_recv()
        place = self.at(d)
        mine, theirs = own(place), other.at[lax.div(place, 2)]
        rows = mine.shape[0]

        @pl.loop(0, rows // 16)
        def _(i):
            w = pl.ds(pl.multiple_of(i * 16, 16), 16)
            total = mine[w].astype(F32) + theirs[w].astype(F32)
            for ref in received:
                total = total + ref[w].astype(F32)
            into[w] = total.astype(into.dtype)

    def hop(self, c, way, src, s):
        i = self.first + c
        if way > 0:
            return self.remote(
                src, self.chunks[c][2].at[s - 1], self.right_s.at[i, s], self.right_r.at[i, s], self.at(1))
        return self.remote(
            src, self.chunks[c][3].at[s - 1], self.left_s.at[i, s], self.left_r.at[i, s], self.at(-1))

    def hops(self, c, way):
        return self.half - c % 2 if way > 0 else self.half - 1 + c % 2

    def step(self, s):
        for c, (own, _, right, left) in enumerate(self.chunks):
            for way in (1, -1):
                hops = self.hops(c, way)
                if s > hops:
                    continue
                d = way * (hops - s + 1)
                d = self.half if d == -self.half else d
                if s == 1:
                    src = self.chunks[c][1].at[lax.div(self.at(d), 2)]
                    self.join(c, d, src, ())
                else:
                    src = (right if way > 0 else left).at[s - 2]
                    self.hop(c, way, src, s - 1).wait_recv()
                    self.join(c, d, src, (src,))
                copy = self.hop(c, way, src, s)
                copy.start()
                self.sent.append(copy)

    def finish(self, outs):
        for c, (own, _, right, left) in enumerate(self.chunks):
            lasts = []
            for way, buf in ((1, right), (-1, left)):
                hops = self.hops(c, way)
                self.hop(c, way, own(self.at(0)), hops).wait_recv()
                lasts.append(buf.at[hops - 1])
            self.join(c, 0, outs[c], lasts)

    def flush(self):
        for copy in self.sent:
            copy.wait_send()


def tail_kernel(
    chips, experts,
    *refs,
):
    count = 14
    ins, (din,) = refs[:12], refs[12:13]
    input_grad, query_grad, key_grad, value_grad, out_grad, up_grad, down_grad, small_grad, other_up = refs[13:22]
    held = refs[22:34]
    dk, dv, dq, n1, first_w, tokens, hidden_grad, turned, out_part, up_part, down_part, row_part = held
    (
        kv_sum, qkv_part, qkv_sum, up_sum, small_part, small_sum, to_other, from_other, qkv_from, up_from, small_from,
    ) = refs[34:45]
    rest = refs[45:]
    h = lax.axis_index("head")
    blk, core, at, sib = ring_info(chips)
    half = chips // 2
    rows, width = tokens.shape
    qw, kw = dq.shape[1], dk.shape[2]
    top = qw + 2 * kw
    dense = first_w.shape[2]
    sw = up_part.shape[3] // 2
    others, rights, lefts = rest[:count], rest[count : 2 * count], rest[2 * count : 3 * count]
    sems, (y_send, y_recv, load_sem) = rest[3 * count : 3 * count + 6], rest[3 * count + 6 :]
    loads = [pltpu.make_async_copy(a, b, load_sem.at[i]) for i, (a, b) in enumerate(zip(ins, held))]
    for i in (0, 1, 9, 8, 10, 2, 4, 3, 5, 6, 7, 11):
        loads[i].start()
    barrier = pltpu.get_barrier_semaphore()
    for other in (at(1), at(-1), sib):
        pl.semaphore_signal(barrier, inc=1, device_id={"blk": other}, device_id_type=MESH)
    pl.semaphore_signal(barrier, inc=1, device_id={"head": 1 - h}, device_id_type=MESH)
    pl.semaphore_wait(barrier, 4)

    def cross(i, src, dst):
        return pltpu.make_async_remote_copy(
            src_ref=src, dst_ref=dst, send_sem=y_send.at[i], recv_sem=y_recv.at[i],
            device_id={"head": 1 - h}, device_id_type=MESH)

    info = (core, at, sib)

    def scatter(first, owns):
        chunks = [(own, others[first + i], rights[first + i], lefts[first + i]) for i, own in enumerate(owns)]
        return Scatter(info, chips, chunks, first, sems)

    def pieces_at(ref, i):
        return lambda b: ref.at[2 * b + i]

    def source_at(ref, i):
        return lambda b: ref.at[i, b]

    def rows_at(ref, start, size):
        return lambda b: ref.at[b, pl.ds(start, size)]

    out_rows, down_rows = out_part.shape[1], down_part.shape[1]
    kv_ring = scatter(0, [pieces_at(dk, 0), pieces_at(dk, 1), pieces_at(dv, 0), pieces_at(dv, 1)])
    rest_ring = scatter(4, [
        source_at(up_part, 0), source_at(up_part, 1), rows_at(out_part, 0, 32), rows_at(out_part, 32, out_rows - 32),
        rows_at(down_part, 0, down_rows // 2), rows_at(down_part, down_rows // 2, down_rows // 2)])
    qkv_ring = scatter(10, [source_at(qkv_part, 0), source_at(qkv_part, 1)])
    small_ring = scatter(12, [source_at(small_part, 0), source_at(small_part, 1)])

    loads[0].wait()
    loads[1].wait()
    kv_ring.exchange()
    size = width // 2
    swap_up = cross(0, din.at[pl.ds(pl.multiple_of((1 - h) * size, 128), size)], other_up)
    swap_up.start()
    for i in (8, 9, 10):
        loads[i].wait()
    rest_ring.exchange()
    for s in range(1, half + 1):
        kv_ring.step(s)
        if s % 2 == 0:
            rest_ring.step(s // 2)
    kv_ring.finish([kv_sum.at[i, pl.ds(j * rows, rows)] for i in range(2) for j in range(2)])

    for i in (2, 3, 4, 5, 6, 7, 11):
        loads[i].wait()
    theirs = pl.ds(pl.multiple_of((1 - h) * rows, rows), rows)
    ours = pl.ds(pl.multiple_of(h * rows, rows), rows)
    step = 8 * dense

    def norm_grad(where, i, t):
        def part(a, first, n):
            return dot_last(a, first_w[i, pl.ds(t * 8, 8), :, pl.ds(first, n)].reshape(step, n))

        return part(dq[where, :], 0, qw) + part(kv_sum[0, where, :], qw, kw) + part(kv_sum[1, where, :], qw + kw, kw)

    spans = [(i, t, pl.ds(i * (width // 2) + t * step, step)) for i in range(2) for t in range(width // (2 * step))]
    for i, t, c in spans:
        to_other[:, c] = norm_grad(theirs, i, t).astype(BF16)
    swap_norm = cross(1, to_other, from_other)
    swap_norm.start()
    for i, t, c in spans:
        lhs = n1[:, c]
        for first, n, rhs in ((0, qw, dq[...]), (qw, kw, kv_sum[0]), (qw + kw, kw, kv_sum[1])):
            part = dot_first(lhs, rhs).astype(BF16)
            qkv_part[i, pl.ds(t * 8, 8), :, pl.ds(first, n)] = part.reshape(8, dense, n)
    qkv_ring.exchange()
    rest_ring.step(3)
    qkv_ring.step(1)
    for i, t, c in spans:
        input_grad[:, c] = norm_grad(ours, i, t)
    swap_norm.wait_recv()
    rest_ring.step(4)
    qkv_ring.step(2)

    def norm_rows(n, total):
        part = pl.ds(pl.multiple_of(n * 32, 32), 32)
        x = tokens[part, :].astype(F32)
        up = input_grad[part, :] + from_other[part, :].astype(F32)
        scaler = lax.rsqrt(jnp.mean(x * x, axis=1, keepdims=True) + EPS)
        normed = x * scaler
        scaled = up * turned[pl.ds(experts, 1), :]
        back = scaler * (scaled - normed * jnp.mean(scaled * normed, axis=1, keepdims=True))
        input_grad[part, :] = hidden_grad[part, :] + back
        return total + jnp.sum(up * normed, axis=0, keepdims=True)

    gain = lax.fori_loop(0, rows // 32, norm_rows, jnp.zeros((1, width), F32))
    ids = lax.broadcasted_iota(jnp.int32, (128, 1), 0)
    turned_part = jnp.swapaxes(row_part[...] + jnp.where(ids == experts, gain, 0.0), 0, 1)
    small_part[...] = turned_part.astype(BF16).reshape(small_part.shape)
    small_ring.exchange()
    small_ring.step(1)
    qkv_ring.step(3)
    small_ring.step(2)
    up_views = [up_sum.at[0], up_sum.at[1]]
    rest_ring.finish(up_views + [
        out_grad.at[pl.ds(0, 32)], out_grad.at[pl.ds(32, out_rows - 32)],
        down_grad.at[pl.ds(0, down_rows // 2)], down_grad.at[pl.ds(down_rows // 2, down_rows // 2)]])
    swap_sum = cross(2, up_sum.at[1 - h], up_from)
    swap_sum.start()
    qkv_ring.step(4)
    small_ring.step(3)
    qkv_ring.finish([qkv_sum.at[0], qkv_sum.at[1]])
    swap_qkv = cross(3, qkv_sum.at[1 - h], qkv_from)
    swap_qkv.start()
    small_ring.step(4)
    small_ring.finish([small_sum.at[0], small_sum.at[1]])
    swap_small = cross(4, small_sum.at[1 - h], small_from)
    swap_small.start()

    def place(ref, source, first, n, base=0):
        for who, part in ((h, source[0]), (1 - h, source[1])):
            ref[:, pl.ds(pl.multiple_of(base + who * n, 128), n)] = part[:, pl.ds(first, n)].astype(F32)

    swap_sum.wait_recv()
    ups = (up_sum.at[h], up_from)
    place(up_grad, ups, 0, sw)
    place(up_grad, ups, sw, sw, 2 * sw)
    swap_qkv.wait_recv()
    sums = (qkv_sum.at[h], qkv_from)
    place(query_grad, sums, 0, qw)
    place(key_grad, sums, qw, kw)
    place(value_grad, sums, qw + kw, kw)
    swap_small.wait_recv()
    small_grad[...] = small_sum[h] + small_from[...]
    for ring in (kv_ring, rest_ring, qkv_ring, small_ring):
        ring.flush()
    for copy in (swap_norm, swap_up, swap_sum, swap_qkv, swap_small):
        copy.wait_send()
    swap_up.wait_recv()


def tail_fused(
    dk, dv, dq, n1, first_w, tokens, hidden_grad, turned, out_part, up_part, down_part, row_part, din,
    blks, collective_id,
):
    chips, half = blks // 2, blks // 4
    rows, width = tokens.shape
    qw, kw = dq.shape[1], dk.shape[2]
    top = qw + 2 * kw
    dense = first_w.shape[2]
    out_rows, down_rows, up_wide = out_part.shape[1], down_part.shape[1], up_part.shape[3]
    dma = pltpu.SemaphoreType.DMA
    vmem = pl.BlockSpec(memory_space=pltpu.VMEM)
    anywhere = pl.BlockSpec(memory_space=pl.ANY)
    shapes = [(rows, kw)] * 4 + [(dense, up_wide)] * 2 + [(32, width), (out_rows - 32, width)]
    shapes += [(down_rows // 2, width)] * 2 + [(dense, top)] * 2 + [(dense, 128)] * 2
    others = [pltpu.VMEM((chips,) + s, BF16) for s in shapes]
    slots = [pltpu.VMEM((half,) + s, BF16) for s in shapes]
    n = len(shapes)
    held = (dk, dv, dq, n1, first_w, tokens, hidden_grad, turned, out_part, up_part, down_part, row_part)

    def f32(*shape):
        return jax.ShapeDtypeStruct(shape, F32)

    def low(*shape):
        return pltpu.VMEM(shape, BF16)

    return pl.pallas_call(
        functools.partial(tail_kernel, chips, blks),
        out_shape=[
            f32(rows, width), f32(dense, 2 * qw), f32(dense, 2 * kw), f32(dense, 2 * kw), f32(out_rows, width),
            f32(dense, 2 * up_wide), f32(down_rows, width), f32(dense, 128),
            jax.ShapeDtypeStruct((din.shape[0] // 2, din.shape[1]), BF16),
        ],
        in_specs=[anywhere] * 13,
        out_specs=[vmem] * 8 + [anywhere],
        scratch_shapes=[pltpu.VMEM(a.shape, a.dtype) for a in held] + [
            low(2, 2 * rows, kw), low(2, blks, dense, top), low(2, dense, top), low(2, dense, up_wide),
            low(2, blks, dense, 128), pltpu.VMEM((2, dense, 128), F32), low(rows, width), low(rows, width),
            low(dense, top), low(dense, up_wide), pltpu.VMEM((dense, 128), F32),
        ] + others + slots + slots + [dma((n, 2 * half + 1))] * 2 + [dma((n, half + 1))] * 4 + [dma((5,)), dma((5,)), dma((12,))],
        compiler_params=pltpu.CompilerParams(
            collective_id=collective_id, has_side_effects=True, vmem_limit_bytes=62 << 20),
    )(*held, din)


def experts_plain(own_ext, weights, cot_all, blks, capacity, collective_id):
    h, b = lax.axis_index("head"), lax.axis_index("blk")
    own_up, other_up, own_down, other_down = weights
    expert_in = pair(own_up, other_up).reshape(2 * own_up.shape[0], -1)
    expert_out = jnp.where(
        h == 0,
        jnp.concatenate([own_down, other_down], axis=1),
        jnp.concatenate([other_down, own_down], axis=1),
    )
    normed = own_ext[:, : expert_in.shape[0]]
    normed_pair = pair(normed, swap(normed))
    experts, width = blks, expert_in.shape[0]
    rows = own_ext.shape[0]
    ext = all_gather_blk([own_ext], blks, collective_id)[0]
    norm_all = ext[:, :, :width]
    gate_here = lax.dynamic_index_in_dim(ext, width + b, 2, keepdims=False).astype(F32)
    mask_here = lax.dynamic_index_in_dim(ext, width + experts + b, 2, keepdims=False).astype(F32)
    rank = jnp.cumsum(mask_here, axis=1) - mask_here
    slots = jnp.arange(capacity, dtype=F32)
    deal = ((rank[:, None, :] == slots[None, :, None]) & (mask_here[:, None, :] > 0)).astype(BF16)
    deal_gate = deal * gate_here[:, None, :].astype(BF16)

    def to_slots(dealer, array):
        moved = jnp.einsum("bst,btd->bsd", dealer, array, preferred_element_type=F32)
        return moved.astype(BF16).reshape(blks * capacity, width)

    def to_rows(dealer, array):
        return jnp.einsum(
            "bst,bsd->btd", dealer, array.reshape(blks, capacity, width), preferred_element_type=F32)

    expert_rows = to_slots(deal, norm_all)
    both = dot(expert_rows, expert_in)
    ew = expert_out.shape[0]
    gate_part, up_part = both[:, :ew], both[:, ew:]
    activated = (jax.nn.silu(gate_part) * up_part).astype(BF16)
    result = dot(activated, expert_out).astype(BF16)
    result_rows = to_rows(deal, result)
    gate_grad = jnp.sum(result_rows * cot_all.astype(F32), axis=2, keepdims=True)
    routed = (result_rows * gate_here[:, :, None]).astype(BF16)
    slot_grad = to_slots(deal_gate, cot_all)
    act_grad = dot_last(slot_grad, expert_out)
    both_grad = gated_grad(act_grad, gate_part, up_part)
    rows_back = to_rows(deal, dot_last(both_grad, expert_in).astype(BF16)).astype(BF16)
    lane = jnp.arange(128 * (-(-2 * experts // 128)), dtype=jnp.int32)
    grad_high = gate_grad.astype(BF16)
    grad_low = (gate_grad - grad_high.astype(F32)).astype(BF16)
    grad_lanes = jnp.where(lane == b, grad_high, jnp.where(lane == b + experts, grad_low, jnp.zeros((), BF16)))
    dwn = dot_first(activated, slot_grad).astype(BF16)
    dup = dot_first(expert_rows, both_grad).astype(BF16)
    home = reduce_scatter_blk([jnp.concatenate([rows_back, grad_lanes], axis=2)], blks, collective_id + 1, [F32])[0]
    routed_sum = reduce_scatter_blk([routed], blks, collective_id + 2, [F32])[0]
    return home, routed_sum, dup, dwn, normed_pair


def pair(own, other):
    return jnp.where(lax.axis_index("head") == 0, jnp.stack([own, other]), jnp.stack([other, own]))


def half(w, i, parts=1):
    size = w.shape[1] // (2 * parts)
    cut = lax.dynamic_slice_in_dim(w.reshape(w.shape[0], parts, 2 * size), i * size, size, 2)
    return cut.reshape(w.shape[0], parts * size)


def pick(stacked, i):
    return lax.dynamic_index_in_dim(stacked, i, 0, keepdims=False)


def front_plain(
    tokens, cotangent, where, mask, w_query, w_key, w_value, small, w_out, shared_up, shared_down,
    expert_up, expert_down, blks, collective_id,
):
    h = lax.axis_index("head")
    rows, width = tokens.shape
    experts = blks

    def columns(i):
        return jnp.concatenate([half(w_query, i), half(w_key, i), half(w_value, i)], axis=1)

    first = pair(
        jnp.concatenate([columns(h), small], axis=1),
        swap(jnp.concatenate([columns(1 - h), small], axis=1)),
    )
    tokens_pair = pair(tokens, swap(tokens))
    cotangent_pair = pair(cotangent, swap(cotangent)).reshape(2 * rows, width)
    up_pair = pair(half(shared_up, h, 2), swap(half(shared_up, 1 - h, 2)))
    other_up, other_down = swap(expert_up), swap(expert_down)
    gathered = all_gather_blk([first], blks, collective_id)[0].reshape(width, -1)
    qw = w_query.shape[1] // 2
    kw = w_key.shape[1] // 2
    full_qkv = gathered[:, : qw + 2 * kw]
    full_router = gathered[:, qw + 2 * kw : qw + 2 * kw + experts]
    gain_first = gathered[:, qw + 2 * kw + experts].astype(F32)
    gain_second = gathered[:, qw + 2 * kw + experts + 1].astype(F32)

    inputs_pair = tokens_pair.reshape(2 * rows, width).astype(F32)
    normed_one = (inputs_pair * inv_scale(inputs_pair) * gain_first).astype(BF16)
    qkv = dot(normed_one, full_qkv).astype(BF16)
    query = qkv[:, :qw]
    kv = all_gather_blk([qkv[:, qw:]], blks, collective_id + 1)[0].reshape(-1, PIECE, 2 * kw)

    attended, attended_full, lse = attention_forward(query, kv, where)

    up_all, out_all, down_all, cot_all = all_gather_blk([up_pair, w_out, shared_down, cotangent], blks, collective_id + 2)
    full_up = up_all.reshape(width, -1)
    full_out = out_all.reshape(-1, width)
    full_down = down_all.reshape(-1, width)

    mixed = dot(attended, full_out).reshape(2, rows, width)
    inputs = tokens.astype(F32)
    resid = inputs + (pick(mixed, h) + swap(pick(mixed, 1 - h).astype(BF16)).astype(F32))
    scaler_two = inv_scale(resid)
    normed_two = (resid * scaler_two * gain_second).astype(BF16)

    logits = dot(normed_two, full_router)
    masked = jnp.where(mask, logits, NEG)
    raised = jnp.where(mask, jnp.exp(masked - jnp.max(masked, axis=1, keepdims=True)), 0.0)
    gates = raised / jnp.sum(raised, axis=1, keepdims=True)
    extra = jnp.concatenate(
        [gates.astype(BF16), mask.astype(BF16), jnp.zeros((rows, -2 * experts % 128), BF16)], axis=1)
    ext = jnp.concatenate([normed_two, extra], axis=1)
    return (
        normed_one, query, kv, full_qkv, full_out, full_up, full_down, cot_all, cotangent_pair, other_up, other_down,
        attended, attended_full, lse, resid, ext, gates, full_router.T, gain_first, gain_second, None)


def finish_kernel(experts, count, h_ref, up_own, up_other, down_own, down_other, small, *refs):
    up_out, down_out, router_out, one_out, two_out = refs[count : count + 5]
    up_out[...] = up_own[...].astype(F32) + up_other[...].astype(F32)
    down_out[...] = down_own[...].astype(F32) + down_other[...].astype(F32)

    @pl.when(pl.program_id(0) == 0)
    def _():
        for source, target in zip(refs[:count], refs[count + 5 :]):
            target[...] = source[...]
        turned = jnp.swapaxes(small[...], 0, 1)
        router_out[...] = turned[:experts]
        one_out[...] = turned[experts : experts + 1]
        two_out[...] = turned[experts + 1 : experts + 2]


def finish_fused(h, dup, add_up, dwn, add_down, small, experts, others):
    steps = 4
    up_rows, down_rows = add_up.shape[0] // steps, add_down.shape[0] // steps
    up = pl.BlockSpec((up_rows, add_up.shape[1]), lambda i, *_: (i, 0))
    down = pl.BlockSpec((down_rows, add_down.shape[1]), lambda i, *_: (i, 0))
    dense = small.shape[0]
    made = [(add_up.shape, F32), (add_down.shape, F32), ((experts, dense), F32), ((1, dense), F32), ((1, dense), F32)]

    def still(shape):
        return pl.BlockSpec(shape, lambda i, *_: (0, 0))

    rest = [still(a.shape) for a in others]
    return pl.pallas_call(
        functools.partial(finish_kernel, experts, len(others)),
        grid_spec=pltpu.PrefetchScalarGridSpec(
            num_scalar_prefetch=1,
            grid=(steps,),
            in_specs=[
                pl.BlockSpec((up_rows, add_up.shape[1]), lambda i, h: (h[0] * steps + i, 0)), up,
                pl.BlockSpec((down_rows, add_down.shape[1]), lambda i, h: (i, h[0])), down,
                still(small.shape),
            ] + rest,
            out_specs=[up, down] + [still(s) for s, _ in made[2:]] + rest,
        ),
        out_shape=[jax.ShapeDtypeStruct(s, t) for s, t in made + [(a.shape, a.dtype) for a in others]],
        compiler_params=pltpu.CompilerParams(vmem_limit_bytes=63 << 20),
    )(h.reshape(1), dup, add_up, dwn, add_down, small, *others)


def shards(
    tokens, cotangent, seq_lengths, piece_order, routes, norm1_gain, w_query, w_key, w_value, w_out,
    norm2_gain, w_router, shared_up, shared_down, expert_up, expert_down,
):
    blks = lax.axis_size("blk")
    h, b = lax.axis_index("head"), lax.axis_index("blk")
    rows, width = tokens.shape
    experts = blks
    capacity = rows * TOP * 4 // (3 * blks)
    dense_rows = w_query.shape[0]

    fits = blks == 16 and rows == 128 and 2 * capacity == 128 and width % 768 == 0 and dense_rows == 48
    if fits:
        got = front_fused(
            tokens, cotangent, piece_order, seq_lengths, routes, w_query, w_key, w_value, w_router, norm1_gain,
            norm2_gain, w_out, shared_up, shared_down, expert_up[0], expert_down[0], blks, 0)
        slots = got[-1][2]
    else:
        small = jnp.concatenate(
            [w_router, norm1_gain[:, None], norm2_gain[:, None],
             jnp.zeros((dense_rows, -(experts + 2) % 128), BF16)], axis=1)
        lanes = small.shape[1]
        places = jnp.swapaxes(piece_order.reshape(2, blks), 0, 1).reshape(-1)
        order = jnp.arange(2 * blks, dtype=jnp.int32)
        slots = jnp.sum(jnp.where(places[None, :] == order[:, None], order[None, :], 0), axis=1)
    own_places = lax.dynamic_slice_in_dim(piece_order.reshape(2, blks), b, 1, 1).reshape(2)
    where = (slots, own_places, seq_lengths)
    if not fits:
        hot = routes[:, :, None] == jnp.arange(experts, dtype=jnp.int32)[None, None, :]
        mask = jnp.any(hot, axis=1)
        got = front_plain(
            tokens, cotangent, where, mask, w_query, w_key, w_value, small, w_out, shared_up, shared_down,
            expert_up[0], expert_down[0], blks, 0)
    (
        normed_one, query, kv, full_qkv, full_out, full_up, full_down, cot_all, cotangent_pair, other_up, other_down,
        attended, attended_full, lse, resid, ext, gates, router_rows, gain_first, gain_second, kept,
    ) = got
    qw, kw = w_query.shape[1] // 2, w_key.shape[1] // 2
    shared_width = full_down.shape[0]
    inputs = tokens.astype(F32)
    if fits:
        (
            output, hidden_grad, mixed_grad, out_part, shared_up_part, shared_down_part, dup, dwn, row_part, _, add_down,
        ) = experts_fused(
            ext, (expert_up[0], other_up, expert_down[0], other_down), cot_all, (full_up, full_down), cotangent_pair,
            cotangent, resid, gates, kept[1], attended, full_out, blks, capacity, 3)
        query_grad, *kv_parts = attention_backward(query, kv, attended_full, lse, mixed_grad, where)
        (
            input_grad, w_query_grad, w_key_grad, w_value_grad, out_sum, up_grad, down_sum, small_sum, add_up,
        ) = tail_fused(
            *kv_parts, query_grad, normed_one, kept[0], tokens, hidden_grad, kept[1],
            out_part.reshape(blks, dense_rows, width),
            shared_up_part.reshape(2, blks, dense_rows, -1),
            shared_down_part.reshape(blks, -1, width), row_part, dup, blks, 6)
        (
            expert_up_grad, expert_down_grad, router_grad, gain_one_grad, gain_two_grad, output,
            input_grad, w_query_grad, w_key_grad, w_value_grad, out_sum, up_grad, down_sum,
        ) = finish_fused(
            h, dup, add_up, dwn, add_down, small_sum, experts,
            (output, input_grad, w_query_grad, w_key_grad, w_value_grad, out_sum, up_grad, down_sum))
        return (
            output, input_grad, gain_one_grad.reshape(-1), w_query_grad, w_key_grad, w_value_grad,
            out_sum, gain_two_grad.reshape(-1), router_grad.T, up_grad, down_sum,
            expert_up_grad[None], expert_down_grad[None],
        )
    scaler_two = inv_scale(resid)
    normed_two = ext[:, :width]

    home, routed_sum, dup, dwn, normed_pair = experts_plain(
        ext, (expert_up[0], other_up, expert_down[0], other_down), cot_all, blks, capacity, 3)
    normed_pair = normed_pair.reshape(2 * rows, width)
    shared_both = dot(normed_pair, full_up)
    shared_gate, shared_lift = shared_both[:, :shared_width], shared_both[:, shared_width:]
    shared_act = (jax.nn.silu(shared_gate) * shared_lift).astype(BF16)
    shared_sum = dot(shared_act, full_down).reshape(2, rows, width)
    shared_down_part = dot_first(shared_act, cotangent_pair)
    shared_grad = gated_grad(dot_last(cotangent_pair, full_down), shared_gate, shared_lift)
    shared_up_part = dot_first(normed_pair, shared_grad)
    shared_back = dot_last(shared_grad, full_up).reshape(2, rows, width)
    output = (
        resid + routed_sum + pick(shared_sum, h) + swap(pick(shared_sum, 1 - h).astype(BF16)).astype(F32)
    ).astype(BF16)

    dgate = home[:, width : width + experts] + home[:, width + experts : width + 2 * experts]
    weighted = gates * dgate
    logit_grad = (weighted - gates * jnp.sum(weighted, axis=1, keepdims=True)).astype(BF16)
    norm_two_grad = (
        home[:, :width] + dot(logit_grad, router_rows)
        + pick(shared_back, h) + swap(pick(shared_back, 1 - h).astype(BF16)).astype(F32)
    )
    back, gain_two_part = norm_back(resid, scaler_two, gain_second, norm_two_grad)
    hidden_grad = cotangent.astype(F32) + back
    hidden_low = hidden_grad.astype(BF16)
    hidden_pair = pair(hidden_low, swap(hidden_low)).reshape(2 * rows, width)
    out_part = dot_first(attended, hidden_pair)
    mixed_grad = dot_last(hidden_pair, full_out).astype(BF16)
    query_grad, *kv_parts = attention_backward(query, kv, attended_full, lse, mixed_grad, where)
    router_part = dot_first(normed_two, logit_grad)
    dup, dwn, query_grad = lax.optimization_barrier((dup, dwn, query_grad))
    dup = dup.reshape(2, width // 2, -1)
    dwn = jnp.stack([dwn[:, : width // 2], dwn[:, width // 2 :]])
    expert_up_grad = pick(dup, h).astype(F32) + swap(pick(dup, 1 - h)).astype(F32)
    expert_down_grad = pick(dwn, h).astype(F32) + swap(pick(dwn, 1 - h)).astype(F32)
    kv_grads = reduce_scatter_blk([part.reshape(blks, 2 * rows, kw) for part in kv_parts], blks, 6, [BF16] * 2)
    qkv_grad = jnp.concatenate([query_grad, *kv_grads], axis=1)
    norm_one_part = dot_last(qkv_grad, full_qkv).reshape(2, rows, width)
    norm_one_grad = pick(norm_one_part, h) + swap(pick(norm_one_part, 1 - h).astype(BF16)).astype(F32)
    extra_grad, gain_one_part = norm_back(inputs, inv_scale(inputs), gain_first, norm_one_grad)
    input_grad = hidden_grad + extra_grad
    qkv_part = dot_first(normed_one, qkv_grad)
    small_part = jnp.concatenate(
        [router_part, gain_one_part[:, None], gain_two_part[:, None],
         jnp.zeros((width, lanes - experts - 2), F32)], axis=1)

    def by_rows(part):
        return part.astype(BF16).reshape(2, blks, dense_rows, -1)

    qkv_sum, up_sum, out_sum, down_sum, small_sum = reduce_scatter_blk(
        [by_rows(qkv_part), by_rows(shared_up_part),
         out_part.astype(BF16).reshape(blks, dense_rows, width),
         shared_down_part.astype(BF16).reshape(blks, -1, width), by_rows(small_part)],
        blks, 7, [BF16, BF16, F32, F32, F32])
    there = swap(jnp.concatenate([pick(qkv_sum, 1 - h), pick(up_sum, 1 - h)], axis=1)).astype(F32)
    here = jnp.concatenate([pick(qkv_sum, h), pick(up_sum, h)], axis=1).astype(F32)
    small_sum = pick(small_sum, h) + swap(pick(small_sum, 1 - h))

    def whole(start, size):
        return jnp.where(
            h == 0,
            jnp.concatenate([here[:, start : start + size], there[:, start : start + size]], axis=1),
            jnp.concatenate([there[:, start : start + size], here[:, start : start + size]], axis=1))

    top = qw + 2 * kw
    sw = shared_width
    up_grad = jnp.concatenate([whole(top, sw), whole(top + sw, sw)], axis=1)
    return (
        output, input_grad, small_sum[:, experts], whole(0, qw), whole(qw, kw), whole(qw + kw, kw),
        out_sum, small_sum[:, experts + 1], small_sum[:, :experts], up_grad, down_sum,
        expert_up_grad[None], expert_down_grad[None],
    )


def solution(mesh):
    both = P(("head", "blk"), None)
    flat = P(("head", "blk"))
    up, down = P("blk", "head", None), P("blk", None, "head")
    return jax.shard_map(
        shards,
        mesh=mesh,
        in_specs=(both, both, P(), P(), both, flat, both, both, both, both, flat, both, both, both, up, down),
        out_specs=(both, both, flat, both, both, both, both, flat, both, both, both, up, down),
        check_vma=False,
    )
```

```python
import functools

import jax
import jax.numpy as jnp
from jax import lax
from jax.experimental import pallas as pl
from jax.experimental.pallas import tpu as pltpu
from jax.sharding import PartitionSpec as P

MESH = pl.DeviceIdType.MESH


def ring_place(chip, chips):
    odd = chip % 2
    return (chip // 2) * (1 - odd) + (chips - 1 - chip // 2) * odd


def ring_chip(place, chips):
    high = place // (chips // 2)
    return 2 * place * (1 - high) + (2 * (chips - 1 - place) + 1) * high


def ring_info(chips):
    blk = lax.axis_index("blk")
    chip, core = blk // 2, blk % 2
    place = ring_place(chip, chips)

    def at(step):
        return ring_chip((place + step + chips) % chips, chips) * 2 + core

    return blk, core, at, blk + 1 - 2 * core


def pieces_of(shape):
    if len(shape) == 3:
        return [(0, None), (1, None)]
    rows = shape[0]
    if rows >= 32 and rows % 16 == 0:
        cut = (rows // 2 + 15) // 16 * 16
        return [(0, cut), (cut, rows - cut)]
    return [(0, rows)]


def part_in(ref, piece):
    start, size = piece
    return ref.at[start] if size is None else ref.at[pl.ds(start, size)]


def part_out(ref, piece, b):
    start, size = piece
    return ref.at[start, b] if size is None else ref.at[b, pl.ds(start, size)]


def ag_kernel(count, chips, plans, *refs):
    ins, outs = refs[:count], refs[count : 2 * count]
    right_sem, left_sem, sib_sem, sright, sleft, ssib, own_sem = refs[2 * count :]
    blk, core, at, sib = ring_info(chips)
    right, left = at(1), at(-1)
    barrier = pltpu.get_barrier_semaphore()
    for other in (right, left, sib):
        pl.semaphore_signal(barrier, inc=1, device_id={"blk": other}, device_id_type=MESH)
    pl.semaphore_wait(barrier, 3)
    half = chips // 2
    started = []

    def send(src, dst, ssem, rsem, dev):
        copy = pltpu.make_async_remote_copy(
            src_ref=src, dst_ref=dst, send_sem=ssem, recv_sem=rsem,
            device_id={"blk": dev}, device_id_type=MESH)
        copy.start()
        started.append(copy)
        return copy

    chunks = []
    for k in range(count):
        for i, piece in enumerate(plans[k]):
            chunks.append((len(chunks), k, piece, half - (i % 2), half - 1 + (i % 2)))
    copies = {}
    locals_ = []
    for c, k, piece, rh, lh in chunks:
        src = part_in(ins[k], piece)
        dst = part_out(outs[k], piece, blk)
        if rh >= 1:
            copies[c, "r", 1] = send(src, dst, sright.at[c, 0], right_sem.at[c, 0], right)
        if lh >= 1:
            copies[c, "l", 1] = send(src, dst, sleft.at[c, 0], left_sem.at[c, 0], left)
        copies[c, "s", 0] = send(src, dst, ssib.at[c, 0], sib_sem.at[c, 0], sib)
        own = pltpu.make_async_copy(src, dst, own_sem.at[c])
        own.start()
        locals_.append(own)
    for s in range(1, half + 1):
        for c, k, piece, rh, lh in chunks:
            if s <= rh:
                copies[c, "r", s].wait_recv()
                b = at(-s)
                blockref = part_out(outs[k], piece, b)
                if s < rh:
                    copies[c, "r", s + 1] = send(blockref, blockref, sright.at[c, s], right_sem.at[c, s], right)
                copies[c, "sr", s] = send(blockref, blockref, ssib.at[c, s], sib_sem.at[c, s], sib)
            if s <= lh:
                copies[c, "l", s].wait_recv()
                b = at(s)
                blockref = part_out(outs[k], piece, b)
                if s < lh:
                    copies[c, "l", s + 1] = send(blockref, blockref, sleft.at[c, s], left_sem.at[c, s], left)
                copies[c, "sl", s] = send(blockref, blockref, ssib.at[c, half + s], sib_sem.at[c, half + s], sib)
    for (c, d, s), copy in copies.items():
        if d in ("s", "sr", "sl"):
            copy.wait_recv()
    for copy in started:
        copy.wait_send()
    for copy in locals_:
        copy.wait()


def all_gather_blk(arrays, blks, collective_id, vmem=False):
    chips = blks // 2
    count = len(arrays)
    plans = [pieces_of(a.shape) for a in arrays]
    n = sum(len(p) for p in plans)
    half = chips // 2
    shapes = [
        jax.ShapeDtypeStruct((a.shape[0], blks) + a.shape[1:] if a.ndim == 3 else (blks,) + a.shape, a.dtype)
        for a in arrays
    ]
    dma = pltpu.SemaphoreType.DMA
    space = pltpu.VMEM if vmem else pl.ANY
    return pl.pallas_call(
        functools.partial(ag_kernel, count, chips, plans),
        out_shape=shapes,
        in_specs=[pl.BlockSpec(memory_space=space)] * count,
        out_specs=[pl.BlockSpec(memory_space=space)] * count,
        scratch_shapes=[
            dma((n, half)), dma((n, half)), dma((n, 2 * half + 1)),
            dma((n, half)), dma((n, half)), dma((n, 2 * half + 1)), dma((n,)),
        ],
        compiler_params=pltpu.CompilerParams(collective_id=collective_id, has_side_effects=True,
            vmem_limit_bytes=(60 << 20) if vmem else None),
    )(*arrays)


def rs_kernel(count, chips, plans, *refs):
    xs, outs = refs[:count], refs[count : 2 * count]
    rest = refs[2 * count :]
    n = sum(len(p) for p in plans)
    ys, rs, ls = rest[:n], rest[n : 2 * n], rest[2 * n : 3 * n]
    right_sem, left_sem, sib_sem, sright, sleft, ssib = rest[3 * n :]
    blk, core, at, sib = ring_info(chips)
    right, left = at(1), at(-1)
    barrier = pltpu.get_barrier_semaphore()
    for other in (right, left, sib):
        pl.semaphore_signal(barrier, inc=1, device_id={"blk": other}, device_id_type=MESH)
    pl.semaphore_wait(barrier, 3)
    half = chips // 2
    started = []

    def send(src, dst, ssem, rsem, dev):
        copy = pltpu.make_async_remote_copy(
            src_ref=src, dst_ref=dst, send_sem=ssem, recv_sem=rsem,
            device_id={"blk": dev}, device_id_type=MESH)
        copy.start()
        started.append(copy)
        return copy

    chunks = []
    for k in range(count):
        for i, piece in enumerate(plans[k]):
            chunks.append((len(chunks), k, piece, half - (i % 2), half - 1 + (i % 2)))
    order = []
    for d in range(half, 0, -1):
        order += [d, -d] if d < half else [d]
    order.append(0)
    sibs = {}
    for j, d in enumerate(order):
        there = at(d) + 1 - 2 * core
        for c, k, piece, rh, lh in chunks:
            sibs[c, d] = send(part_out(xs[k], piece, there), ys[c].at[j], ssib.at[c, j], sib_sem.at[c, j], sib)
    ready = set()

    def blocks(rows, body):
        step = 16 if rows % 16 == 0 else rows

        @pl.loop(0, rows // step)
        def _(i):
            body(pl.ds(pl.multiple_of(i * step, step), step))

    def mine(c, k, piece, d):
        j = order.index(d)
        if (c, d) not in ready:
            sibs[c, d].wait_recv()
            ready.add((c, d))
        return j

    copies = {}

    def join(c, k, piece, d, into, recv):
        j = mine(c, k, piece, d)
        x = part_out(xs[k], piece, at(d))
        rows = x.shape[0]

        def body(w):
            total = x[w].astype(jnp.float32) + ys[c][j, w].astype(jnp.float32)
            if recv is not None:
                total = total + recv[w].astype(jnp.float32)
            into[w] = total.astype(into.dtype)

        blocks(rows, body)

    for s in range(1, half + 1):
        for c, k, piece, rh, lh in chunks:
            for way, hops, buf, sem, ssem, dev in (
                (1, rh, rs[c], right_sem, sright, right),
                (-1, lh, ls[c], left_sem, sleft, left),
            ):
                if s > hops:
                    continue
                if s == 1:
                    j = order.index(way * hops if way * hops in order else hops)
                    join(c, k, piece, order[j], ys[c].at[j], None)
                    src = ys[c].at[j]
                else:
                    copies[c, way, s - 1].wait_recv()
                    d = way * (hops - s + 1)
                    src = buf.at[s - 2]
                    join(c, k, piece, d, src, src)
                copies[c, way, s] = send(src, buf.at[s - 1], ssem.at[c, s - 1], sem.at[c, s - 1], dev)
    for c, k, piece, rh, lh in chunks:
        if rh >= 1:
            copies[c, 1, rh].wait_recv()
        if lh >= 1:
            copies[c, -1, lh].wait_recv()
        j = mine(c, k, piece, 0)
        x = part_out(xs[k], piece, blk)
        target = part_in(outs[k], piece)

        def body(w, x=x, c=c, j=j, rh=rh, lh=lh, target=target):
            total = x[w].astype(jnp.float32) + ys[c][j, w].astype(jnp.float32)
            if rh >= 1:
                total = total + rs[c][rh - 1, w].astype(jnp.float32)
            if lh >= 1:
                total = total + ls[c][lh - 1, w].astype(jnp.float32)
            target[w] = total.astype(target.dtype)

        blocks(x.shape[0], body)
    for copy in started:
        copy.wait_send()


def reduce_scatter_blk(arrays, blks, collective_id, out_dtypes):
    chips = blks // 2
    half = chips // 2
    count = len(arrays)
    shapes = [a.shape[1:] if a.ndim == 3 else (2,) + a.shape[2:] for a in arrays]
    plans = [pieces_of(s) for s in shapes]
    dma = pltpu.SemaphoreType.DMA
    ys, rs = [], []
    for s, plan in zip(shapes, plans):
        for start, size in plan:
            rows = s[1] if size is None else size
            ys.append(pltpu.VMEM((chips, rows, s[-1]), jnp.bfloat16))
            rs.append(pltpu.VMEM((half, rows, s[-1]), jnp.bfloat16))
    n = len(ys)
    return pl.pallas_call(
        functools.partial(rs_kernel, count, chips, plans),
        out_shape=[jax.ShapeDtypeStruct(s, t) for s, t in zip(shapes, out_dtypes)],
        in_specs=[pl.BlockSpec(memory_space=pltpu.VMEM)] * count,
        out_specs=[pl.BlockSpec(memory_space=pltpu.VMEM)] * count,
        scratch_shapes=ys + rs + rs + [
            dma((n, half)), dma((n, half)), dma((n, chips)),
            dma((n, half)), dma((n, half)), dma((n, chips)),
        ],
        compiler_params=pltpu.CompilerParams(collective_id=collective_id, has_side_effects=True,
            vmem_limit_bytes=60 << 20),
    )(*arrays)


H = 12
KVH = 4
HD = 128
TOP = 6
PIECE = 128
EPS = 1e-05
NEG = -1e30
F32 = jnp.float32
BF16 = jnp.bfloat16


def dot(a, b):
    return jnp.dot(a, b, preferred_element_type=F32)


def dot_first(a, b):
    return lax.dot_general(a, b, (((0,), (0,)), ((), ())), preferred_element_type=F32)


def dot_last(a, b):
    return lax.dot_general(a, b, (((1,), (1,)), ((), ())), preferred_element_type=F32)


def inv_scale(values):
    return lax.rsqrt(jnp.mean(values * values, axis=1, keepdims=True) + EPS)


def norm_back(values, scaler, gain, upstream):
    normed = values * scaler
    gain_grad = jnp.sum(upstream * normed, axis=0)
    scaled = upstream * gain
    grad = scaler * (scaled - normed * jnp.mean(scaled * normed, axis=1, keepdims=True))
    return grad, gain_grad


def gated_grad(act_grad, gate, lift):
    sig = jax.nn.sigmoid(gate)
    return jnp.concatenate(
        [act_grad * lift * sig * (1.0 + gate * (1.0 - sig)), act_grad * gate * sig], axis=1
    ).astype(BF16)


def swap(array):
    return lax.ppermute(array, "head", [(0, 1), (1, 0)])


def ends_of(lengths_ref):
    end, ends = jnp.int32(0), []
    for e in range(lengths_ref.shape[0]):
        end = end + lengths_ref[e]
        ends.append(end)
    return ends


def key_span(place, lengths_ref):
    start = jnp.int32(0)
    for end in ends_of(lengths_ref):
        start = jnp.where(end <= place * PIECE, end, start)
    return start // PIECE


def key_chunk(slots_ref, first, pieces, *refs):
    last = slots_ref.shape[0] - 1
    slots = [slots_ref[jnp.clip(first + k, 0, last)] for k in range(pieces)]
    return slots, [jnp.concatenate([ref[s] for s in slots], axis=0) for ref in refs]


def stacked(ref, i, repeats):
    return jnp.concatenate(
        [ref[pl.ds(i * PIECE, PIECE), pl.ds(r * HD, HD)] for r in range(repeats)], axis=0)


def seen(lengths_ref, place, first, keys, cols):
    own = place * PIECE + lax.broadcasted_iota(jnp.int32, (1, cols), 1) % PIECE
    start = jnp.zeros((1, cols), jnp.int32)
    for end in ends_of(lengths_ref):
        start = jnp.where(end <= own, end, start)
    there = first * PIECE + lax.broadcasted_iota(jnp.int32, (keys, 1), 0)
    return (there <= own) & (there >= start)


CHUNK = 4


def forward_kernel(repeats, slots_ref, places_ref, lengths_ref, q_ref, k_ref, v_ref, low_ref, full_ref, lse_ref):
    cols = repeats * PIECE
    for i in range(q_ref.shape[0] // PIECE):
        place = places_ref[i]
        lo = key_span(place, lengths_ref)
        q = stacked(q_ref, i, repeats)

        def step(n, carry, lo=lo, place=place, q=q):
            top, total, acc = carry
            first = lo + n * CHUNK
            _, (k, v) = key_chunk(slots_ref, first, CHUNK, k_ref, v_ref)
            scores = dot_last(k, q) * HD**-0.5
            scores = jnp.where(seen(lengths_ref, place, first, CHUNK * PIECE, cols), scores, NEG)
            new = jnp.maximum(top, jnp.max(scores, axis=0, keepdims=True))
            weights = jnp.exp(scores - new)
            factor = jnp.exp(top - new)
            total = total * factor + jnp.sum(weights, axis=0, keepdims=True)
            return new, total, acc * factor + dot_first(v, weights.astype(BF16))

        top, total, acc = lax.fori_loop(
            0, (place - lo) // CHUNK + 1, step,
            (jnp.full((1, cols), NEG, F32), jnp.zeros((1, cols), F32), jnp.zeros((HD, cols), F32)))
        out = jnp.swapaxes(acc / total, 0, 1)
        lse_ref[0, pl.ds(i, 1), :] = top + jnp.log(total)
        for r in range(repeats):
            part = out[r * PIECE : (r + 1) * PIECE]
            full_ref[pl.ds(i * PIECE, PIECE), pl.ds(r * HD, HD)] = part
            low_ref[pl.ds(i * PIECE, PIECE), pl.ds(r * HD, HD)] = part.astype(BF16)


def attention_forward(query, kv, where):
    rows, pieces = query.shape[0], kv.shape[0]
    groups = kv.shape[2] // (2 * HD)
    wide = query.shape[1] // groups
    repeats = wide // HD
    spec = pl.BlockSpec((rows, wide), lambda g, *_: (0, g))
    return pl.pallas_call(
        functools.partial(forward_kernel, repeats),
        grid_spec=pltpu.PrefetchScalarGridSpec(
            num_scalar_prefetch=3,
            grid=(groups,),
            in_specs=[
                spec,
                pl.BlockSpec((pieces, PIECE, HD), lambda g, *_: (0, 0, g)),
                pl.BlockSpec((pieces, PIECE, HD), lambda g, *_: (0, 0, groups + g)),
            ],
            out_specs=[spec, spec, pl.BlockSpec((1, rows // PIECE, repeats * PIECE), lambda g, *_: (g, 0, 0))],
        ),
        out_shape=[
            jax.ShapeDtypeStruct(query.shape, BF16),
            jax.ShapeDtypeStruct(query.shape, F32),
            jax.ShapeDtypeStruct((groups, rows // PIECE, repeats * PIECE), F32),
        ],
        compiler_params=pltpu.CompilerParams(vmem_limit_bytes=48 << 20),
    )(*where, query, kv, kv)


def backward_kernel(
    repeats, slots_ref, places_ref, lengths_ref, q_ref, k_ref, v_ref, full_ref, grad_ref, lse_ref,
    dq_ref, dk_ref, dv_ref, key_acc, value_acc,
):
    cols = repeats * PIECE
    key_acc[...] = jnp.zeros_like(key_acc)
    value_acc[...] = jnp.zeros_like(value_acc)
    for i in range(q_ref.shape[0] // PIECE):
        place = places_ref[i]
        lo = key_span(place, lengths_ref)
        q, grad = stacked(q_ref, i, repeats), stacked(grad_ref, i, repeats)
        product = grad.astype(F32) * stacked(full_ref, i, repeats)
        delta = jnp.sum(jnp.swapaxes(product, 0, 1), axis=0, keepdims=True)
        lse = lse_ref[0, pl.ds(i, 1), :]

        def step(n, dq, lo=lo, place=place, q=q, grad=grad, delta=delta, lse=lse):
            first = lo + n * CHUNK
            slots, (k, v) = key_chunk(slots_ref, first, CHUNK, k_ref, v_ref)
            scores = dot_last(k, q) * HD**-0.5
            weights = jnp.where(
                seen(lengths_ref, place, first, CHUNK * PIECE, cols), jnp.exp(scores - lse), 0.0)
            back = (weights * (dot_last(v, grad) - delta)).astype(BF16)
            dk = dot(back, q)
            dv = dot(weights.astype(BF16), grad)
            for j, s in enumerate(slots):
                key_acc[s] += dk[j * PIECE : (j + 1) * PIECE]
                value_acc[s] += dv[j * PIECE : (j + 1) * PIECE]
            return dq + dot_first(k, back)

        dq = lax.fori_loop(0, (place - lo) // CHUNK + 1, step, jnp.zeros((HD, cols), F32))
        out = (jnp.swapaxes(dq, 0, 1) * HD**-0.5).astype(BF16)
        for r in range(repeats):
            dq_ref[pl.ds(i * PIECE, PIECE), pl.ds(r * HD, HD)] = out[r * PIECE : (r + 1) * PIECE]
    dk_ref[...] = (key_acc[...] * HD**-0.5).astype(BF16)
    dv_ref[...] = value_acc[...].astype(BF16)


def attention_backward(query, kv, full, lse, grad, where):
    rows, pieces = query.shape[0], kv.shape[0]
    groups = kv.shape[2] // (2 * HD)
    wide = query.shape[1] // groups
    repeats = wide // HD
    spec = pl.BlockSpec((rows, wide), lambda g, *_: (0, g))
    block = pl.BlockSpec((pieces, PIECE, HD), lambda g, *_: (0, 0, g))
    half = jax.ShapeDtypeStruct((pieces, PIECE, groups * HD), BF16)
    return pl.pallas_call(
        functools.partial(backward_kernel, repeats),
        grid_spec=pltpu.PrefetchScalarGridSpec(
            num_scalar_prefetch=3,
            grid=(groups,),
            in_specs=[
                spec, block, pl.BlockSpec((pieces, PIECE, HD), lambda g, *_: (0, 0, groups + g)), spec, spec,
                pl.BlockSpec((1, rows // PIECE, repeats * PIECE), lambda g, *_: (g, 0, 0)),
            ],
            out_specs=[spec, block, block],
            scratch_shapes=[pltpu.VMEM((pieces, PIECE, HD), F32)] * 2,
        ),
        out_shape=[jax.ShapeDtypeStruct(query.shape, BF16), half, half],
        compiler_params=pltpu.CompilerParams(vmem_limit_bytes=60 << 20),
    )(*where, query, kv, kv, full, grad, lse)


def tiles(total, size, body):
    if total == size:
        body(pl.ds(0, size))
    else:

        @pl.loop(0, total // size)
        def _(i):
            body(pl.ds(pl.multiple_of(i * size, size), size))


def shifted(c, by):
    if isinstance(c.start, int):
        return pl.ds(c.start + by, c.size)
    return pl.ds(pl.multiple_of(c.start + by, c.size), c.size)


def expert_kernel(
    chips, experts, ext_ref, up_own, up_other, down_own, down_other, cot_ref,
    shared_up, shared_down, cot_pair, cot_own, resid, gates, turned, low, full_out,
    output, hidden_grad, mixed_grad, out_part, up_part, down_part, din, dout, row_part, norm_pair, other_down,
    home_ref, routed_ref, din_ref, dout_ref, shared_act, shared_dab, hid, from_back, from_sum,
    in_ref, out_ref, ext, cot, rows_x, rows_dy, rows_act, rows_dab, both, result, back, deal, gate, take, take_gate,
    own_d, own_o, stage_d, stage_o, sib_d, sib_o, right_d, right_o, left_d, left_o,
    copy_sem, cot_sem, ag_r, ag_l, ag_sr, ag_sl, ss_r, ss_l, ss_sr, ss_sl,
    ex_sem, ss_ex, rs_r, rs_l, ss_rr, ss_rl, weight_sem, pair_sem, load_sem, y_send, y_recv,
):
    blk, core, at, sib = ring_info(chips)
    h = lax.axis_index("head")
    right, left = at(1), at(-1)
    half = chips // 2
    rows, wide = ext_ref.shape
    width = in_ref.shape[0]
    hidden = out_ref.shape[0]
    slots = rows_x.shape[0] // chips
    cut = rows // 2
    upper, lower = pl.ds(0, cut), pl.ds(cut, cut)

    barrier = pltpu.get_barrier_semaphore()
    for other in (right, left, sib):
        pl.semaphore_signal(barrier, inc=1, device_id={"blk": other}, device_id_type=MESH)
    pl.semaphore_signal(barrier, inc=1, device_id={"head": 1 - h}, device_id_type=MESH)
    pl.semaphore_wait(barrier, 4)

    def remote(src, dst, ssem, rsem, dev):
        return pltpu.make_async_remote_copy(
            src_ref=src, dst_ref=dst, send_sem=ssem, recv_sem=rsem,
            device_id={"blk": dev}, device_id_type=MESH)

    def hop_right(part, k, s):
        ref = ext.at[at(1 - s), part]
        return remote(ref, ref, ss_r.at[k, s], ag_r.at[k, s], right)

    def hop_left(part, k, s):
        ref = ext.at[at(s - 1), part]
        return remote(ref, ref, ss_l.at[k, s], ag_l.at[k, s], left)

    def over_right(part, k, s):
        ref = ext.at[at(-s), part]
        return remote(ref, ref, ss_sr.at[k, s], ag_sr.at[k, s], sib)

    def over_left(part, k, s):
        ref = ext.at[at(s), part]
        return remote(ref, ref, ss_sl.at[k, s], ag_sl.at[k, s], sib)

    def place_of(g, j):
        return at(-g) if j == 0 else at(g)

    def cot_copy(g, j):
        there = place_of(g, j)
        slot = lax.rem(g, 2)
        return pltpu.make_async_copy(
            cot_ref.at[pl.ds(there - core, 2)], cot.at[slot, j], cot_sem.at[slot, j])

    def exchange_d(g, j):
        return remote(stage_d.at[j], sib_d.at[lax.div(place_of(g, j), 2)], ss_ex.at[0, j, g], ex_sem.at[0, j, g], sib)

    def exchange_o(g, j):
        return remote(stage_o.at[j], sib_o.at[lax.div(place_of(g, j), 2)], ss_ex.at[1, j, g], ex_sem.at[1, j, g], sib)

    mine = pltpu.make_async_copy(ext_ref, ext.at[blk], copy_sem)
    mine.start()
    cot_copy(0, 0).start()
    weights = []
    for i, (up, down) in ((h, (up_own, down_own)), (1 - h, (up_other, down_other))):
        size = up.shape[0]
        start = pl.multiple_of(i * size, size)
        weights.append((up, in_ref.at[pl.ds(start, size)]))
        weights.append((down, out_ref.at[:, pl.ds(start, size)]))
    weights = [pltpu.make_async_copy(a, b, weight_sem.at[i]) for i, (a, b) in enumerate(weights)]
    for copy in weights:
        copy.start()
    mine.wait()
    for k, part in ((0, upper), (1, lower)):
        hop_right(part, k, 1).start()
        hop_left(part, k, 1).start()
        over_right(part, k, 0).start()
    own_norm = ext.at[blk, :, pl.ds(0, width)]
    keep = pltpu.make_async_copy(own_norm, norm_pair.at[h], pair_sem.at[0])
    keep.start()
    swapped = pltpu.make_async_remote_copy(
        src_ref=own_norm, dst_ref=norm_pair.at[h], send_sem=pair_sem.at[1], recv_sem=pair_sem.at[2],
        device_id={"head": 1 - h}, device_id_type=MESH)
    swapped.start()
    for copy in weights:
        copy.wait()

    lane = lax.broadcasted_iota(jnp.int32, (2 * rows, 128), 1)
    token_row = lax.broadcasted_iota(jnp.int32, (2 * rows, 2 * rows), 0)
    token_col = lax.broadcasted_iota(jnp.int32, (2 * rows, 2 * rows), 1)
    same = (token_row < rows) == (token_col < rows)
    triangle = jnp.where((token_row > token_col) & same, 1.0, 0.0).astype(BF16)
    offset = jnp.float32(slots // 2)
    shift_col = jnp.where(lax.broadcasted_iota(jnp.int32, (2 * rows, 1), 0) < rows, 0.0, offset)
    shift_row = jnp.where(lax.broadcasted_iota(jnp.int32, (1, 2 * rows), 1) < rows, 0.0, offset)
    slot_id = lax.broadcasted_iota(jnp.int32, (slots, 2 * rows), 0).astype(F32)
    lane_row = lax.broadcasted_iota(jnp.int32, (128, 128), 0)
    pick_mask = jnp.where(lane_row == experts + blk, 1.0, 0.0).astype(BF16)
    pick_gate = jnp.where(lane_row == blk, 1.0, 0.0).astype(BF16)
    lane_col = lax.broadcasted_iota(jnp.int32, (8, 128), 1)
    mask_row = jnp.where(lane_col == experts + blk, 1.0, 0.0).astype(BF16)
    gate_row = jnp.where(lane_col == blk, 1.0, 0.0).astype(BF16)

    def arrive(s):
        last = isinstance(s, int) and s == half
        hop_right(upper, 0, s).wait_recv()
        if not last:
            hop_right(upper, 0, s + 1).start()
        over_right(upper, 0, s).start()
        hop_left(lower, 1, s).wait_recv()
        if not last:
            hop_left(lower, 1, s + 1).start()
        over_left(lower, 1, s).start()
        if last:
            return
        hop_right(lower, 1, s).wait_recv()

        @pl.when(s < half - 1)
        def _():
            hop_right(lower, 1, s + 1).start()

        over_right(lower, 1, s).start()
        hop_left(upper, 0, s).wait_recv()

        @pl.when(s < half - 1)
        def _():
            hop_left(upper, 0, s + 1).start()

        over_left(upper, 0, s).start()

    def work(g, count, base, first):
        turn = lax.rem(g, 2)
        size = count * slots
        group = pl.ds(base, size)
        part = pl.ds(0, size)
        firsts = [place_of(g, j) - core for j in range(count)]
        for j in range(count):
            lanes = ext[pl.ds(firsts[j], 2), :, pl.ds(width, 128)].reshape(2 * rows, 128)
            chosen = dot(lanes, pick_mask)
            rank = dot(triangle, chosen.astype(BF16))
            spread = jnp.where((rank + shift_col == lane.astype(F32)) & (chosen > 0.5), 1.0, 0.0).astype(BF16)
            deal[j] = spread.reshape(2, rows, 128)
            gate[j] = dot(lanes, pick_gate).reshape(2, rows, 128)
            chosen_row = dot_last(mask_row, lanes)
            rank_row = dot_last(chosen_row.astype(BF16), triangle)
            weight_row = dot_last(gate_row, lanes)
            taken = jnp.where((rank_row[:1] + shift_row == slot_id) & (chosen_row[:1] > 0.5), 1.0, 0.0)
            take[j] = taken.astype(BF16)
            take_gate[j] = (taken * weight_row[:1]).astype(BF16)
        for j in range(count):
            cot_copy(g, j).wait()
            where = pl.ds(pl.multiple_of(base + j * slots, slots), slots)

            def pick_rows(c, j=j, where=where):
                rows_x[where, c] = dot(
                    take[j], ext[pl.ds(firsts[j], 2), :, c].reshape(2 * rows, c.size)).astype(BF16)
                rows_dy[where, c] = dot(take_gate[j], cot[turn, j, :, :, c].reshape(2 * rows, c.size)).astype(BF16)

            for t in range(2):
                pick_rows(pl.ds(t * (width // 2), width // 2))

        def hidden_tile(c):
            high = shifted(c, hidden)
            x = rows_x[group]
            gate_part = dot(x, in_ref[:, c])
            lift = dot(x, in_ref[:, high])
            both[part, c] = gate_part
            both[part, high] = lift
            rows_act[group, c] = (jax.nn.silu(gate_part) * lift).astype(BF16)

        for t in range(2):
            hidden_tile(pl.ds(t * (hidden // 2), hidden // 2))

        def result_tile(c):
            result[part, c] = dot(rows_act[group], out_ref[:, c]).astype(BF16)

        for t in range(2):
            result_tile(pl.ds(t * (width // 2), width // 2))

        def grad_tile(c):
            high = shifted(c, hidden)
            da = dot_last(rows_dy[group], out_ref[c, :])
            gate_part, lift = both[part, c], both[part, high]
            sig = jax.nn.sigmoid(gate_part)
            rows_dab[group, c] = (da * lift * sig * (1.0 + gate_part * (1.0 - sig))).astype(BF16)
            rows_dab[group, high] = (da * gate_part * sig).astype(BF16)

        for t in range(2):
            grad_tile(pl.ds(t * (hidden // 2), hidden // 2))

        def back_tile(c):
            back[part, c] = dot_last(rows_dab[group], in_ref[c, :]).astype(BF16)

        for t in range(2):
            back_tile(pl.ds(t * (width // 2), width // 2))
        if first is not None:

            @pl.when(first)
            def _():
                for j in range(2):
                    exchange_d(g - 1, j).wait_send()
                    exchange_o(g - 1, j).wait_send()

            @pl.when(jnp.logical_not(first))
            def _():
                exchange_d(g - 1, 0).wait_send()
                exchange_o(g - 1, 0).wait_send()

        for j in range(count):
            chip = lax.div(firsts[j], 2)
            for which, to_d, to_o in (
                (core, own_d.at[chip], own_o.at[chip]),
                (1 - core, stage_d.at[j], stage_o.at[j]),
            ):
                from_slots = pl.ds(j * slots, slots)
                dealer = deal[j, which]
                share = gate[j, which]
                total = jnp.zeros((rows, 1), F32)
                for t in range(width // 512):
                    c = pl.ds(t * 512, 512)
                    home_rows = dot(dealer, result[from_slots, c])
                    to_o[:, c] = (home_rows * share[:, :1]).astype(BF16)
                    total = total + jnp.sum(
                        home_rows * cot[turn, j, which, :, c].astype(F32), axis=1, keepdims=True)
                    to_d[:, c] = dot(dealer, back[from_slots, c]).astype(BF16)
                high = total.astype(BF16).astype(F32)
                own_lane = lane[:rows]
                lanes = jnp.where(own_lane == blk, high, jnp.where(own_lane == experts + blk, total - high, 0.0))
                to_d[:, pl.ds(width, 128)] = lanes.astype(BF16)
            exchange_d(g, j).start()
            exchange_o(g, j).start()

    arrays = ((0, own_d, sib_d, right_d, left_d, home_ref), (1, own_o, sib_o, right_o, left_o, routed_ref))
    arrived = set()

    def join(a, own, other, d, part, into, received):
        g, j = (d, 1) if 0 < d < half else (abs(d), 0)
        if (a, g, j) not in arrived:
            arrived.add((a, g, j))
            (exchange_d, exchange_o)[a](g, j).wait_recv()
        chip = lax.div(at(d), 2)

        def add(c):
            total = own[chip, c].astype(F32) + other[chip, c].astype(F32)
            for ref in received:
                total = total + ref[c].astype(F32)
            into[c] = total.astype(into.dtype)

        @pl.loop(0, cut // 16)
        def _(i):
            add(pl.ds(pl.multiple_of(part.start + i * 16, 16), 16))

    def pass_right(a, src, buf, k, part, s):
        return remote(src.at[part], buf.at[s - 1, part], ss_rr.at[a, k, s], rs_r.at[a, k, s], right)

    def pass_left(a, src, buf, k, part, s):
        return remote(src.at[part], buf.at[s - 1, part], ss_rl.at[a, k, s], rs_l.at[a, k, s], left)

    ways = (
        (0, upper, 1, half), (1, lower, -1, half), (1, lower, 1, half - 1), (0, upper, -1, half - 1),
    )
    sent = []

    def scatter_step(a, s, ways=ways):
        _, own, other, to_right, to_left, _ = arrays[a]
        for k, part, way, hops in ways:
            if s > hops:
                continue
            make, buf = (pass_right, to_right) if way > 0 else (pass_left, to_left)
            d = way * (hops - s + 1)
            if d == -half:
                d = half
            if s == 1:
                src = own.at[lax.div(at(d), 2)]
                join(a, own, other, d, part, src, ())
            else:
                src = buf.at[s - 2]
                make(a, src, buf, k, part, s - 1).wait_recv()
                join(a, own, other, d, part, src, (src,))
            copy = make(a, src, buf, k, part, s)
            copy.start()
            sent.append(copy)

    over_right(upper, 0, 0).wait_recv()
    over_right(lower, 1, 0).wait_recv()
    cot_copy(1, 0).start()
    cot_copy(1, 1).start()
    work(0, 1, 0, None)

    @pl.loop(1, half)
    def _(g):
        arrive(g)
        over_right(upper, 0, g).wait_recv()
        over_right(lower, 1, g).wait_recv()
        over_left(lower, 1, g).wait_recv()
        over_left(upper, 0, g).wait_recv()
        cot_copy(g + 1, 0).start()

        @pl.when(g < half - 1)
        def _():
            cot_copy(g + 1, 1).start()

        work(g, 2, pl.multiple_of(slots + (g - 1) * 2 * slots, slots), g > 1)

    arrive(half)
    over_right(upper, 0, half).wait_recv()
    over_left(lower, 1, half).wait_recv()
    scatter_step(0, 1, ways[2:])
    work(half, 1, (2 * half - 1) * slots, True)

    def scatter_finish(a):
        _, own, other, to_right, to_left, into = arrays[a]
        for k, part in ((0, upper), (1, lower)):
            last_right, last_left = half - k, half - 1 + k
            pass_right(a, own.at[0], to_right, k, part, last_right).wait_recv()
            pass_left(a, own.at[0], to_left, k, part, last_left).wait_recv()
            join(a, own, other, 0, part, into, (to_right.at[last_right - 1], to_left.at[last_left - 1]))

    loads = 0

    def move(src, dst):
        nonlocal loads
        copy = pltpu.make_async_copy(src, dst, load_sem.at[loads])
        loads += 1
        copy.start()
        return copy

    def cross(i, src, dst):
        return pltpu.make_async_remote_copy(
            src_ref=src, dst_ref=dst, send_sem=y_send.at[i], recv_sem=y_recv.at[i],
            device_id={"head": 1 - h}, device_id_type=MESH)

    theirs = pl.ds(pl.multiple_of((1 - h) * rows, rows), rows)
    ours = pl.ds(pl.multiple_of(h * rows, rows), rows)
    keep.wait()
    swapped.wait()
    shared_loads = [
        move(shared_up, in_ref), move(shared_down, out_ref), move(cot_pair, back),
        move(norm_pair.at[0], result.at[pl.ds(0, rows)]), move(norm_pair.at[1], result.at[pl.ds(rows, rows)])]
    scatter_step(0, 1, ways[:2])

    def weight_in(c):
        din_ref[c, :] = dot_first(rows_x[:, c], rows_dab[...]).astype(BF16)

    tiles(width, 256, weight_in)
    din_out = move(din_ref, din)
    load_out = move(full_out, rows_x.at[pl.ds(0, low.shape[1])])
    scatter_step(0, 2)

    for copy in shared_loads:
        copy.wait()

    def shared_tile(c):
        high = shifted(c, hidden)
        gate_part = dot(result[...], in_ref[:, c])
        lift = dot(result[...], in_ref[:, high])
        sig = jax.nn.sigmoid(gate_part)
        shared_act[:, c] = (gate_part * sig * lift).astype(BF16)
        da = dot_last(back[...], out_ref[c, :])
        shared_dab[:, c] = (da * lift * sig * (1.0 + gate_part * (1.0 - sig))).astype(BF16)
        shared_dab[:, high] = (da * gate_part * sig).astype(BF16)

    tiles(hidden, 256, shared_tile)
    to_back, to_sum = cot.at[0, 0, 0], cot.at[0, 0, 1]

    def back_part(c):
        to_back[:, c] = dot_last(shared_dab[theirs, :], in_ref[c, :]).astype(BF16)

    tiles(width, 512, back_part)
    swap_back = cross(0, to_back, from_back)
    swap_back.start()

    def weight_out(c):
        dout_ref[c, :] = dot_first(rows_act[:, c], rows_dy[...]).astype(BF16)

    tiles(hidden, 256, weight_out)
    dout_out = move(dout_ref, dout)
    scatter_step(0, 3)
    scatter_step(1, 1)

    def sum_part(c):
        to_sum[:, c] = dot(shared_act[theirs, :], out_ref[:, c]).astype(BF16)

    tiles(width, 512, sum_part)
    swap_sum = cross(1, to_sum, from_sum)
    swap_sum.start()
    din_out.wait()
    dout_out.wait()
    swap_down = cross(3, dout.at[:, pl.ds(pl.multiple_of((1 - h) * (width // 2), 128), width // 2)], other_down)
    swap_down.start()

    def shared_in(c):
        din_ref[c, :] = dot_first(result[:, c], shared_dab[...]).astype(BF16)

    tiles(width, 256, shared_in)
    up_out = move(din_ref, up_part)
    scatter_step(0, 4)
    scatter_step(1, 2)

    def shared_out(c):
        dout_ref[c, :] = dot_first(shared_act[:, c], back[...]).astype(BF16)

    tiles(hidden, 256, shared_out)
    down_out = move(dout_ref, down_part)
    swap_back.wait_recv()
    scatter_finish(0)

    lanes = home_ref[:, pl.ds(width, 128)].astype(BF16)
    row_id = lax.broadcasted_iota(jnp.int32, (128, 128), 0)
    col_id = lax.broadcasted_iota(jnp.int32, (128, 128), 1)
    fold = jnp.where((row_id == col_id) | (row_id == col_id + experts), 1.0, 0.0).astype(BF16)
    weighted = gates[...] * dot(lanes, fold)
    logit_grad = (weighted - gates[...] * jnp.sum(weighted, axis=1, keepdims=True)).astype(BF16)
    short = logit_grad[:, : turned.shape[0]]

    def norm_part(c):
        hidden_grad[:, c] = (
            home_ref[:, c] + from_back[:, c].astype(F32) + dot_last(shared_dab[ours, :], in_ref[c, :])
            + dot(short, turned[:, c].astype(BF16)))
        row_part[:, c] = dot_first(logit_grad, ext[blk, :, c])

    tiles(width, 512, norm_part)

    def norm_rows(n, total):
        part = pl.ds(pl.multiple_of(n * 32, 32), 32)
        x, up = resid[part, :], hidden_grad[part, :]
        scaler = lax.rsqrt(jnp.mean(x * x, axis=1, keepdims=True) + EPS)
        normed = x * scaler
        scaled = up * turned[pl.ds(experts + 1, 1), :]
        grad = cot_own[part, :].astype(F32) + scaler * (
            scaled - normed * jnp.mean(scaled * normed, axis=1, keepdims=True))
        hidden_grad[part, :] = grad
        hid[h, part, :] = grad.astype(BF16)
        return total + jnp.sum(up * normed, axis=0, keepdims=True)

    gain = lax.fori_loop(0, rows // 32, norm_rows, jnp.zeros((1, width), F32))
    swap_hid = cross(2, hid.at[h], hid.at[h])
    swap_hid.start()
    scatter_step(1, 3)
    row_part[pl.ds(experts + 1, 1), :] = gain
    load_out.wait()
    inner = low.shape[1]
    full = rows_x.at[pl.ds(0, inner)]

    def mixed_tile(who, where):
        for t in range(inner // 256):
            c = pl.ds(t * 256, 256)
            mixed_grad[where, c] = dot_last(hid[who], full[c, :]).astype(BF16)

    mixed_tile(h, ours)
    scatter_step(1, 4)
    swap_hid.wait_recv()
    mixed_tile(1 - h, theirs)

    def out_tile(c):
        rows_dy[c, :] = (
            dot_first(low[pl.ds(0, rows), c], hid[0]) + dot_first(low[pl.ds(rows, rows), c], hid[1])).astype(BF16)

    for t in range(inner // 256):
        out_tile(pl.ds(t * 256, 256))
    part_out = move(rows_dy.at[pl.ds(0, inner)], out_part)
    swap_sum.wait_recv()
    scatter_finish(1)

    def output_tile(c):
        output[:, c] = (
            resid[:, c] + routed_ref[:, c] + from_sum[:, c].astype(F32)
            + dot(shared_act[ours, :], out_ref[:, c])).astype(BF16)

    tiles(width, 512, output_tile)
    for copy in (swap_back, swap_sum, swap_hid, swap_down):
        copy.wait_send()
    swap_down.wait_recv()
    for copy in (up_out, down_out, part_out):
        copy.wait()
    for copy in sent:
        copy.wait_send()
    exchange_d(half, 0).wait_send()
    exchange_o(half, 0).wait_send()
    for k, part in ((0, upper), (1, lower)):
        over_right(part, k, 0).wait_send()
        for s in range(1, half + 1):
            if s <= half - k:
                hop_right(part, k, s).wait_send()
                over_right(part, k, s).wait_send()
            if s <= half - 1 + k:
                hop_left(part, k, s).wait_send()
                over_left(part, k, s).wait_send()


def experts_fused(
    ext, weights, cot_all, shared, cot_pair, cot_own, resid, gates, turned, low, full_out, blks, capacity, collective_id,
):
    chips, half = blks // 2, blks // 4
    rows, wide = ext.shape
    width, hidden = 2 * weights[0].shape[0], weights[2].shape[0]
    count = blks * capacity
    group = 4 * capacity
    inner = low.shape[1]
    dma = pltpu.SemaphoreType.DMA
    vmem = pl.BlockSpec(memory_space=pltpu.VMEM)
    anywhere = pl.BlockSpec(memory_space=pl.ANY)

    def bf16(*shape):
        return pltpu.VMEM(shape, BF16)

    def f32(*shape):
        return pltpu.VMEM(shape, F32)

    out = [
        ((rows, width), BF16, vmem), ((rows, width), F32, vmem), ((2 * rows, inner), BF16, vmem),
        ((inner, width), BF16, anywhere), ((width, 2 * hidden), BF16, anywhere), ((hidden, width), BF16, anywhere),
        ((width, 2 * hidden), BF16, anywhere), ((hidden, width), BF16, anywhere), ((128, width), F32, vmem),
        ((2, rows, width), BF16, anywhere), ((hidden, width // 2), BF16, anywhere),
    ]
    return pl.pallas_call(
        functools.partial(expert_kernel, chips, blks),
        out_shape=[jax.ShapeDtypeStruct(s, t) for s, t, _ in out],
        in_specs=[anywhere] * 9 + [vmem] * 5 + [anywhere],
        out_specs=[space for _, _, space in out],
        scratch_shapes=[
            f32(rows, wide), f32(rows, width), bf16(width, 2 * hidden), bf16(hidden, width),
            bf16(2 * rows, hidden), bf16(2 * rows, 2 * hidden), bf16(2, rows, width), bf16(rows, width), bf16(rows, width),
            bf16(width, 2 * hidden), bf16(hidden, width),
            bf16(blks, rows, wide), bf16(2, 2, 2, rows, width),
            bf16(count, width), bf16(count, width), bf16(count, hidden), bf16(count, 2 * hidden),
            f32(group, 2 * hidden), bf16(group, width), bf16(group, width),
            bf16(2, 2, rows, 128), f32(2, 2, rows, 128), bf16(2, 128, 2 * rows), bf16(2, 128, 2 * rows),
            bf16(chips, rows, wide), bf16(chips, rows, width), bf16(2, rows, wide), bf16(2, rows, width),
            bf16(chips, rows, wide), bf16(chips, rows, width),
            bf16(half, rows, wide), bf16(half, rows, width), bf16(half, rows, wide), bf16(half, rows, width),
            dma(()), dma((2, 2)),
        ] + [dma((2, half + 1))] * 8 + [dma((2, 2, half + 1))] * 2 + [dma((2, 2, half + 1))] * 4
        + [dma((4,)), dma((3,)), dma((11,)), dma((4,)), dma((4,))],
        compiler_params=pltpu.CompilerParams(
            collective_id=collective_id, has_side_effects=True, vmem_limit_bytes=63 << 20),
    )(ext, *weights, cot_all, *shared, cot_pair, cot_own, resid, gates, turned, low, full_out)


class Ring:
    def __init__(self, info, chips, chunks, first, sems):
        self.blk, self.at, self.sib = info
        self.half = chips // 2
        self.chunks, self.first = chunks, first
        self.send_r, self.recv_r, self.send_l, self.recv_l, self.send_s, self.recv_s = sems

    def hops(self, c):
        return self.half - c % 2, self.half - 1 + c % 2

    def copy(self, ref, ssem, rsem, dev):
        return pltpu.make_async_remote_copy(
            src_ref=ref, dst_ref=ref, send_sem=ssem, recv_sem=rsem,
            device_id={"blk": dev}, device_id_type=MESH)

    def right(self, c, s):
        i = self.first + c
        return self.copy(self.chunks[c](self.at(1 - s)), self.send_r.at[i, s], self.recv_r.at[i, s], self.at(1))

    def left(self, c, s):
        i = self.first + c
        return self.copy(self.chunks[c](self.at(s - 1)), self.send_l.at[i, s], self.recv_l.at[i, s], self.at(-1))

    def over(self, c, d):
        i, k = self.first + c, d + self.half
        return self.copy(self.chunks[c](self.at(d)), self.send_s.at[i, k], self.recv_s.at[i, k], self.sib)

    def start(self, c):
        self.right(c, 1).start()
        self.left(c, 1).start()
        self.over(c, 0).start()

    def step(self, s):
        for c in range(len(self.chunks)):
            rh, lh = self.hops(c)
            if s <= rh:
                self.right(c, s).wait_recv()
                if s < rh:
                    self.right(c, s + 1).start()
                self.over(c, -s).start()
            if s <= lh:
                self.left(c, s).wait_recv()
                if s < lh:
                    self.left(c, s + 1).start()
                self.over(c, s).start()

    def end(self):
        for c in range(len(self.chunks)):
            rh, lh = self.hops(c)
            for d in range(-rh, lh + 1):
                self.over(c, d).wait_recv()

    def flush(self):
        for c in range(len(self.chunks)):
            rh, lh = self.hops(c)
            for s in range(1, rh + 1):
                self.right(c, s).wait_send()
            for s in range(1, lh + 1):
                self.left(c, s).wait_send()
            for d in range(-rh, lh + 1):
                self.over(c, d).wait_send()


def front_kernel(
    chips, experts,
    order_ref, lengths_ref, routes, router, gain_one, gain_two, tokens, cotangent, w_query, w_key, w_value, w_out,
    shared_up, shared_down, expert_up, expert_down,
    n1_out, query_out, kv_out, first_out, out_out, up_w, down_w, cot, cot_pair, expert_in, expert_out,
    low_out, full_out, lse, resid, ext, gates, short, slots_ref,
    small, n1, query, kv, first_w, out_w, low, full, turned, pair, to_other, from_other,
    send_r, recv_r, send_l, recv_l, send_s, recv_s, own_sem, y_send, y_recv, store_sem,
):
    h = lax.axis_index("head")
    blk, core, at, sib = ring_info(chips)
    half = chips // 2
    rows, width = tokens.shape
    qw, kw = w_query.shape[1] // 2, w_key.shape[1] // 2
    sw = shared_up.shape[1] // 4
    barrier = pltpu.get_barrier_semaphore()
    for other in (at(1), at(-1), sib):
        pl.semaphore_signal(barrier, inc=1, device_id={"blk": other}, device_id_type=MESH)
    pl.semaphore_signal(barrier, inc=1, device_id={"head": 1 - h}, device_id_type=MESH)
    pl.semaphore_wait(barrier, 4)

    wide = lax.broadcasted_iota(jnp.int32, (experts, 128), 1)
    column = lax.broadcasted_iota(jnp.int32, (experts, 128), 0)
    block = dot_first(router[...], jnp.where(wide == column, 1.0, 0.0).astype(BF16))
    for n, gain in ((0, gain_one), (1, gain_two)):
        spot = jnp.where(lax.broadcasted_iota(jnp.int32, (1, 128), 1) == experts + n, 1.0, 0.0).astype(BF16)
        block = block + dot_first(gain[...], spot)
    small[...] = block.astype(BF16)

    def lanes_of(start, size):
        return pl.ds(pl.multiple_of(start, 128), size)

    def halves(i, j):
        return [
            (w_query.at[:, lanes_of(i * qw, qw)], first_w.at[j, blk, :, pl.ds(0, qw)]),
            (w_key.at[:, lanes_of(i * kw, kw)], first_w.at[j, blk, :, pl.ds(qw, kw)]),
            (w_value.at[:, lanes_of(i * kw, kw)], first_w.at[j, blk, :, pl.ds(qw + kw, kw)]),
            (small, first_w.at[j, blk, :, pl.ds(qw + 2 * kw, small.shape[1])]),
            (tokens, pair.at[j]),
            (shared_up.at[:, lanes_of(i * sw, sw)], up_w.at[j, blk, :, pl.ds(0, sw)]),
            (shared_up.at[:, lanes_of((2 + i) * sw, sw)], up_w.at[j, blk, :, pl.ds(sw, sw)]),
            (cotangent, cot_pair.at[j]),
        ]

    whole = [(expert_up, expert_in), (expert_down, expert_out)]

    stores = []

    def store(src, dst):
        copy = pltpu.make_async_copy(src, dst, store_sem.at[len(stores)])
        copy.start()
        stores.append(copy)

    own = [pltpu.make_async_copy(a, b, own_sem.at[i]) for i, (a, b) in enumerate(halves(h, h))]
    own.append(pltpu.make_async_copy(w_out, out_w.at[blk], own_sem.at[len(own)]))
    own.append(pltpu.make_async_copy(shared_down, down_w.at[blk], own_sem.at[len(own)]))
    own.append(pltpu.make_async_copy(cotangent, cot.at[blk], own_sem.at[len(own)]))
    swaps = [
        pltpu.make_async_remote_copy(
            src_ref=a, dst_ref=b, send_sem=y_send.at[i], recv_sem=y_recv.at[i],
            device_id={"head": 1 - h}, device_id_type=MESH)
        for i, (a, b) in enumerate(halves(1 - h, h) + whole)
    ]
    for i in range(5):
        swaps[i].start()
    for i in (0, 1, 2, 3, 8, 4):
        own[i].start()

    info = (blk, at, sib)
    sems = (send_r, recv_r, send_l, recv_l, send_s, recv_s)

    def row_cuts(ref, *sizes):
        start, chunks = 0, []
        for size in sizes:
            chunks.append(lambda b, start=start, size=size: ref.at[b, pl.ds(start, size)])
            start += size
        return chunks

    ring_w = Ring(info, chips, [lambda b: first_w.at[h, b], lambda b: first_w.at[1 - h, b]], 0, sems)
    out_rows, down_rows = w_out.shape[0], shared_down.shape[0]
    ring_o = Ring(info, chips, row_cuts(out_w, 32, out_rows - 32), 2, sems)
    ring_kv = Ring(info, chips, [lambda b: kv.at[2 * b], lambda b: kv.at[2 * b + 1]], 4, sems)
    ring_u = Ring(info, chips, [lambda b: up_w.at[h, b], lambda b: up_w.at[1 - h, b]], 6, sems)
    ring_d = Ring(info, chips, row_cuts(down_w, down_rows // 2, down_rows // 2), 8, sems)
    ring_c = Ring(info, chips, row_cuts(cot, rows // 2, rows // 2), 10, sems)

    for i in (0, 1, 2, 3):
        own[i].wait()
    ring_w.start(0)
    own[10].start()
    own[10].wait()
    ring_c.start(0)
    ring_c.start(1)
    own[8].wait()
    for i in range(4):
        swaps[i].wait_recv()
    ring_w.start(1)
    ring_o.start(0)
    ring_o.start(1)
    for i in (5, 6, 9, 7):
        own[i].start()
    for i in range(5, 10):
        swaps[i].start()
    for s in range(1, half + 1):
        ring_w.step(s)
        ring_o.step(s)
    ring_c.step(1)
    ring_w.end()
    store(first_w, first_out)
    own[4].wait()
    swaps[4].wait_recv()

    @pl.loop(0, slots_ref.shape[0])
    def _(j):
        slot = jnp.int32(0)
        for n in range(order_ref.shape[0]):
            there = 2 * (n % (2 * chips)) + n // (2 * chips)
            slot = jnp.maximum(slot, jnp.where(order_ref[n] == j, there, 0))
        slots_ref[j] = slot

    small_cols = first_w[:, :, :, pl.ds(qw + 2 * kw, 128)].reshape(width, 128)
    turned[...] = jnp.swapaxes(small_cols.astype(F32), 0, 1)
    short[...] = turned[pl.ds(0, short.shape[0]), :]

    @pl.loop(0, 2 * rows // 64)
    def _(i):
        x = pair[lax.div(i, rows // 64), pl.ds(pl.multiple_of(lax.rem(i, rows // 64) * 64, 64), 64), :].astype(F32)
        scaled = x * lax.rsqrt(jnp.mean(x * x, axis=1, keepdims=True) + EPS) * turned[pl.ds(experts, 1), :]
        n1[pl.ds(pl.multiple_of(i * 64, 64), 64), :] = scaled.astype(BF16)

    def project(start, size):
        weights = first_w[:, :, :, pl.ds(start, size)].reshape(width, size)
        return dot(n1[...], weights).astype(BF16)

    for t in range(2 * kw // 256):
        part = project(qw + t * 256, 256)
        for i in range(2):
            kv[2 * blk + i, :, pl.ds(t * 256, 256)] = part[i * rows : (i + 1) * rows]
    ring_kv.start(0)
    ring_kv.start(1)
    for t in range(qw // 256):
        query[:, pl.ds(t * 256, 256)] = project(t * 256, 256)
    for i in (5, 6, 9):
        own[i].wait()
    swaps[5].wait_recv()
    swaps[6].wait_recv()
    for s in range(1, half + 1):
        ring_kv.step(s)
        if s == half - 1:
            ring_c.step(2)
            for ring in (ring_u, ring_d):
                ring.start(0)
                ring.start(1)
    ring_kv.end()
    store(kv, kv_out)
    store(n1, n1_out)
    store(query, query_out)

    groups, repeats = kw // HD, qw // kw
    cols = repeats * PIECE
    pieces = slots_ref.shape[0]
    need = pieces // 2 + 1
    chunk = 6
    chunks = -(-need // chunk)
    later = [(ring_u, 1), (ring_d, 1), (ring_c, 3), (ring_u, 2), (ring_d, 2), (ring_c, 4)]
    turns = 0
    for i in range(2):
        place = order_ref[i * 2 * chips + blk]
        for g in range(groups):
            q = jnp.concatenate(
                [query[pl.ds(i * PIECE, PIECE), pl.ds((g * repeats + r) * HD, HD)] for r in range(repeats)], axis=0)

            def step(n, carry, place=place, g=g, q=q):
                top, total, acc = carry
                first = place + 1 - chunks * chunk + n * chunk
                _, (k, v) = key_chunk(
                    slots_ref, first, chunk, kv.at[:, :, pl.ds(g * HD, HD)], kv.at[:, :, pl.ds((groups + g) * HD, HD)])
                scores = dot_last(k, q) * HD**-0.5
                scores = jnp.where(seen(lengths_ref, place, first, chunk * PIECE, cols), scores, NEG)
                new = jnp.maximum(top, jnp.max(scores, axis=0, keepdims=True))
                weights = jnp.exp(scores - new)
                factor = jnp.exp(top - new)
                total = total * factor + jnp.sum(weights, axis=0, keepdims=True)
                return new, total, acc * factor + dot_first(v, weights.astype(BF16))

            top, total, acc = lax.fori_loop(
                0, chunks, step,
                (jnp.full((1, cols), NEG, F32), jnp.zeros((1, cols), F32), jnp.zeros((HD, cols), F32)))
            out = jnp.swapaxes(acc / total, 0, 1)
            lse[g, pl.ds(i, 1), :] = top + jnp.log(total)
            for r in range(repeats):
                part = out[r * PIECE : (r + 1) * PIECE]
                full[pl.ds(i * PIECE, PIECE), pl.ds((g * repeats + r) * HD, HD)] = part
                low[pl.ds(i * PIECE, PIECE), pl.ds((g * repeats + r) * HD, HD)] = part.astype(BF16)
            turns += 1
            if turns % 2 == 0:
                for ring, s in later[:3]:
                    ring.step(s)
                later = later[3:]

    ring_o.end()
    store(out_w, out_out)
    store(low, low_out)
    store(full, full_out)
    theirs = pl.ds(pl.multiple_of((1 - h) * rows, rows), rows)
    ours = pl.ds(pl.multiple_of(h * rows, rows), rows)

    def mixed(where, c):
        return dot(low[where, :], out_w[:, :, c].reshape(qw, c.size))

    for t in range(width // 512):
        c = pl.ds(t * 512, 512)
        to_other[:, c] = mixed(theirs, c).astype(BF16)
    swap_mixed = pltpu.make_async_remote_copy(
        src_ref=to_other, dst_ref=from_other, send_sem=y_send.at[10], recv_sem=y_recv.at[10],
        device_id={"head": 1 - h}, device_id_type=MESH)
    swap_mixed.start()
    for t in range(width // 512):
        c = pl.ds(t * 512, 512)
        resid[:, c] = pair[h, :, c].astype(F32) + mixed(ours, c)
    for ring in (ring_u, ring_d):
        ring.step(3)
    swap_mixed.wait_recv()

    @pl.loop(0, rows // 32)
    def _(i):
        part = pl.ds(pl.multiple_of(i * 32, 32), 32)
        x = resid[part, :] + from_other[part, :].astype(F32)
        resid[part, :] = x
        scaled = x * lax.rsqrt(jnp.mean(x * x, axis=1, keepdims=True) + EPS) * turned[pl.ds(experts + 1, 1), :]
        ext[part, pl.ds(0, width)] = scaled.astype(BF16)

    logits = dot_last(ext[:, pl.ds(0, width)], turned[...].astype(BF16))
    lane = lax.broadcasted_iota(jnp.int32, (128, rows), 0)
    masks = jnp.zeros((128, rows), F32)
    for r in range(routes.shape[0]):
        named = routes[r : r + 1, :]
        masks = jnp.where((lane == named) | (lane == named + experts), 1.0, masks)
    masks = jnp.swapaxes(masks, 0, 1)
    low_lane = lax.broadcasted_iota(jnp.int32, (rows, 128), 1) < experts
    mask = jnp.where(low_lane, masks, 0.0)
    shifted_mask = jnp.where(low_lane, 0.0, masks)
    masked = jnp.where(mask > 0.5, logits, NEG)
    raised = jnp.where(mask > 0.5, jnp.exp(masked - jnp.max(masked, axis=1, keepdims=True)), 0.0)
    probs = raised / jnp.sum(raised, axis=1, keepdims=True)
    gates[...] = probs
    ext[:, pl.ds(width, 128)] = (probs + shifted_mask).astype(BF16)
    for ring in (ring_u, ring_d):
        ring.step(4)
    own[7].wait()
    for i in (7, 8, 9):
        swaps[i].wait_recv()
    for ring in (ring_u, ring_d, ring_c):
        ring.end()
    for ring in (ring_w, ring_o, ring_kv, ring_u, ring_d, ring_c):
        ring.flush()
    for copy in swaps:
        copy.wait_send()
    swap_mixed.wait_send()
    for copy in stores:
        copy.wait()


def front_fused(
    tokens, cotangent, piece_order, seq_lengths, routes, w_query, w_key, w_value, w_router, gain_one, gain_two, w_out,
    shared_up, shared_down, expert_up, expert_down, blks, collective_id,
):
    chips, half = blks // 2, blks // 4
    rows, width = tokens.shape
    dense = w_query.shape[0]
    qw, kw, sw = w_query.shape[1] // 2, w_key.shape[1] // 2, shared_up.shape[1] // 4
    groups, repeats = kw // HD, qw // kw
    dma = pltpu.SemaphoreType.DMA
    vmem = pl.BlockSpec(memory_space=pltpu.VMEM)
    anywhere = pl.BlockSpec(memory_space=pl.ANY)
    smem = pl.BlockSpec(memory_space=pltpu.SMEM)
    out = [
        ((2 * rows, width), BF16, anywhere), ((2 * rows, qw), BF16, anywhere), ((2 * blks, rows, 2 * kw), BF16, anywhere),
        ((2, blks, dense, qw + 2 * kw + 128), BF16, anywhere), ((blks, w_out.shape[0], width), BF16, anywhere),
        ((2, blks, dense, 2 * sw), BF16, anywhere), ((blks, shared_down.shape[0], width), BF16, anywhere),
        ((blks, rows, width), BF16, anywhere), ((2, rows, width), BF16, anywhere),
        (expert_up.shape, BF16, anywhere), (expert_down.shape, BF16, anywhere),
        ((2 * rows, qw), BF16, anywhere), ((2 * rows, qw), F32, anywhere), ((groups, 2, repeats * PIECE), F32, vmem),
        ((rows, width), F32, vmem), ((rows, width + 128), BF16, vmem), ((rows, 128), F32, vmem), ((blks + 8, width), F32, vmem),
        ((2 * blks,), jnp.int32, smem),
    ]
    ring = [dma((12, half + 1))] * 4 + [dma((12, 2 * half + 1))] * 2
    (
        n1, query, kv, first_w, out_w, up_w, down_w, cot, cot_pair, expert_in, expert_out,
        low, full, lse, resid, ext, gates, turned, slots,
    ) = pl.pallas_call(
        functools.partial(front_kernel, chips, blks),
        out_shape=[jax.ShapeDtypeStruct(s, t) for s, t, _ in out],
        in_specs=[smem] * 2 + [vmem] * 4 + [anywhere, vmem] + [anywhere] * 4 + [vmem] * 2 + [anywhere] * 2,
        out_specs=[space for _, _, space in out],
        scratch_shapes=[pltpu.VMEM((dense, 128), BF16)] + [pltpu.VMEM(out[i][0], out[i][1]) for i in (0, 1, 2, 3, 4, 11, 12)] + [
            pltpu.VMEM((128, width), F32), pltpu.VMEM((2, rows, width), BF16), pltpu.VMEM((rows, width), BF16), pltpu.VMEM((rows, width), BF16)]
        + ring + [dma((11,)), dma((11,)), dma((11,)), dma((7,))],
        compiler_params=pltpu.CompilerParams(
            collective_id=collective_id, has_side_effects=True, vmem_limit_bytes=56 << 20),
    )(
        piece_order, seq_lengths, routes.T, w_router.T, gain_one[None], gain_two[None], tokens, cotangent,
        w_query, w_key, w_value, w_out, shared_up, shared_down, expert_up, expert_down)
    return (
        n1, query, kv, first_w.reshape(width, -1)[:, : qw + 2 * kw], out_w.reshape(-1, width),
        up_w.reshape(width, -1), down_w.reshape(-1, width), cot, cot_pair.reshape(2 * rows, width),
        expert_in, expert_out, low, full, lse, resid, ext, gates,
        None, None, None, (first_w, turned, slots))


class Scatter:
    def __init__(self, info, chips, chunks, first, sems):
        self.core, self.at, self.sib = info
        self.half = chips // 2
        self.chunks, self.first = chunks, first
        self.ex_s, self.ex_r, self.right_s, self.right_r, self.left_s, self.left_r = sems
        self.there, self.sent = set(), []

    def remote(self, src, dst, ssem, rsem, dev):
        return pltpu.make_async_remote_copy(
            src_ref=src, dst_ref=dst, send_sem=ssem, recv_sem=rsem,
            device_id={"blk": dev}, device_id_type=MESH)

    def over(self, c, d):
        own, other = self.chunks[c][:2]
        i, k = self.first + c, d + self.half
        place = self.at(d)
        return self.remote(
            own(place + 1 - 2 * self.core), other.at[lax.div(place, 2)], self.ex_s.at[i, k], self.ex_r.at[i, k], self.sib)

    def exchange(self):
        for d in sorted(range(1 - self.half, self.half + 1), key=lambda d: (-abs(d), -d)):
            for c in range(len(self.chunks)):
                copy = self.over(c, d)
                copy.start()
                self.sent.append(copy)

    def join(self, c, d, into, received):
        own, other = self.chunks[c][:2]
        if (c, d) not in self.there:
            self.there.add((c, d))
            self.over(c, d).wait_recv()
        place = self.at(d)
        mine, theirs = own(place), other.at[lax.div(place, 2)]
        rows = mine.shape[0]

        @pl.loop(0, rows // 16)
        def _(i):
            w = pl.ds(pl.multiple_of(i * 16, 16), 16)
            total = mine[w].astype(F32) + theirs[w].astype(F32)
            for ref in received:
                total = total + ref[w].astype(F32)
            into[w] = total.astype(into.dtype)

    def hop(self, c, way, src, s):
        i = self.first + c
        if way > 0:
            return self.remote(
                src, self.chunks[c][2].at[s - 1], self.right_s.at[i, s], self.right_r.at[i, s], self.at(1))
        return self.remote(
            src, self.chunks[c][3].at[s - 1], self.left_s.at[i, s], self.left_r.at[i, s], self.at(-1))

    def hops(self, c, way):
        return self.half - c % 2 if way > 0 else self.half - 1 + c % 2

    def step(self, s):
        for c, (own, _, right, left) in enumerate(self.chunks):
            for way in (1, -1):
                hops = self.hops(c, way)
                if s > hops:
                    continue
                d = way * (hops - s + 1)
                d = self.half if d == -self.half else d
                if s == 1:
                    src = self.chunks[c][1].at[lax.div(self.at(d), 2)]
                    self.join(c, d, src, ())
                else:
                    src = (right if way > 0 else left).at[s - 2]
                    self.hop(c, way, src, s - 1).wait_recv()
                    self.join(c, d, src, (src,))
                copy = self.hop(c, way, src, s)
                copy.start()
                self.sent.append(copy)

    def finish(self, outs):
        for c, (own, _, right, left) in enumerate(self.chunks):
            lasts = []
            for way, buf in ((1, right), (-1, left)):
                hops = self.hops(c, way)
                self.hop(c, way, own(self.at(0)), hops).wait_recv()
                lasts.append(buf.at[hops - 1])
            self.join(c, 0, outs[c], lasts)

    def flush(self):
        for copy in self.sent:
            copy.wait_send()


def tail_kernel(
    chips, experts,
    *refs,
):
    count = 14
    ins, (din,) = refs[:12], refs[12:13]
    input_grad, query_grad, key_grad, value_grad, out_grad, up_grad, down_grad, small_grad, other_up = refs[13:22]
    held = refs[22:34]
    dk, dv, dq, n1, first_w, tokens, hidden_grad, turned, out_part, up_part, down_part, row_part = held
    (
        kv_sum, qkv_part, qkv_sum, up_sum, small_part, small_sum, to_other, from_other, qkv_from, up_from, small_from,
    ) = refs[34:45]
    rest = refs[45:]
    h = lax.axis_index("head")
    blk, core, at, sib = ring_info(chips)
    half = chips // 2
    rows, width = tokens.shape
    qw, kw = dq.shape[1], dk.shape[2]
    top = qw + 2 * kw
    dense = first_w.shape[2]
    sw = up_part.shape[3] // 2
    others, rights, lefts = rest[:count], rest[count : 2 * count], rest[2 * count : 3 * count]
    sems, (y_send, y_recv, load_sem) = rest[3 * count : 3 * count + 6], rest[3 * count + 6 :]
    loads = [pltpu.make_async_copy(a, b, load_sem.at[i]) for i, (a, b) in enumerate(zip(ins, held))]
    for i in (0, 1, 9, 8, 10, 2, 4, 3, 5, 6, 7, 11):
        loads[i].start()
    barrier = pltpu.get_barrier_semaphore()
    for other in (at(1), at(-1), sib):
        pl.semaphore_signal(barrier, inc=1, device_id={"blk": other}, device_id_type=MESH)
    pl.semaphore_signal(barrier, inc=1, device_id={"head": 1 - h}, device_id_type=MESH)
    pl.semaphore_wait(barrier, 4)

    def cross(i, src, dst):
        return pltpu.make_async_remote_copy(
            src_ref=src, dst_ref=dst, send_sem=y_send.at[i], recv_sem=y_recv.at[i],
            device_id={"head": 1 - h}, device_id_type=MESH)

    info = (core, at, sib)

    def scatter(first, owns):
        chunks = [(own, others[first + i], rights[first + i], lefts[first + i]) for i, own in enumerate(owns)]
        return Scatter(info, chips, chunks, first, sems)

    def pieces_at(ref, i):
        return lambda b: ref.at[2 * b + i]

    def source_at(ref, i):
        return lambda b: ref.at[i, b]

    def rows_at(ref, start, size):
        return lambda b: ref.at[b, pl.ds(start, size)]

    out_rows, down_rows = out_part.shape[1], down_part.shape[1]
    kv_ring = scatter(0, [pieces_at(dk, 0), pieces_at(dk, 1), pieces_at(dv, 0), pieces_at(dv, 1)])
    rest_ring = scatter(4, [
        source_at(up_part, 0), source_at(up_part, 1), rows_at(out_part, 0, 32), rows_at(out_part, 32, out_rows - 32),
        rows_at(down_part, 0, down_rows // 2), rows_at(down_part, down_rows // 2, down_rows // 2)])
    qkv_ring = scatter(10, [source_at(qkv_part, 0), source_at(qkv_part, 1)])
    small_ring = scatter(12, [source_at(small_part, 0), source_at(small_part, 1)])

    loads[0].wait()
    loads[1].wait()
    kv_ring.exchange()
    size = width // 2
    swap_up = cross(0, din.at[pl.ds(pl.multiple_of((1 - h) * size, 128), size)], other_up)
    swap_up.start()
    for i in (8, 9, 10):
        loads[i].wait()
    rest_ring.exchange()
    for s in range(1, half + 1):
        kv_ring.step(s)
        if s % 2 == 0:
            rest_ring.step(s // 2)
    kv_ring.finish([kv_sum.at[i, pl.ds(j * rows, rows)] for i in range(2) for j in range(2)])

    for i in (2, 3, 4, 5, 6, 7, 11):
        loads[i].wait()
    theirs = pl.ds(pl.multiple_of((1 - h) * rows, rows), rows)
    ours = pl.ds(pl.multiple_of(h * rows, rows), rows)
    step = 8 * dense

    def norm_grad(where, i, t):
        def part(a, first, n):
            return dot_last(a, first_w[i, pl.ds(t * 8, 8), :, pl.ds(first, n)].reshape(step, n))

        return part(dq[where, :], 0, qw) + part(kv_sum[0, where, :], qw, kw) + part(kv_sum[1, where, :], qw + kw, kw)

    spans = [(i, t, pl.ds(i * (width // 2) + t * step, step)) for i in range(2) for t in range(width // (2 * step))]
    for i, t, c in spans:
        to_other[:, c] = norm_grad(theirs, i, t).astype(BF16)
    swap_norm = cross(1, to_other, from_other)
    swap_norm.start()
    for i, t, c in spans:
        lhs = n1[:, c]
        for first, n, rhs in ((0, qw, dq[...]), (qw, kw, kv_sum[0]), (qw + kw, kw, kv_sum[1])):
            part = dot_first(lhs, rhs).astype(BF16)
            qkv_part[i, pl.ds(t * 8, 8), :, pl.ds(first, n)] = part.reshape(8, dense, n)
    qkv_ring.exchange()
    rest_ring.step(3)
    qkv_ring.step(1)
    for i, t, c in spans:
        input_grad[:, c] = norm_grad(ours, i, t)
    swap_norm.wait_recv()
    rest_ring.step(4)
    qkv_ring.step(2)

    def norm_rows(n, total):
        part = pl.ds(pl.multiple_of(n * 32, 32), 32)
        x = tokens[part, :].astype(F32)
        up = input_grad[part, :] + from_other[part, :].astype(F32)
        scaler = lax.rsqrt(jnp.mean(x * x, axis=1, keepdims=True) + EPS)
        normed = x * scaler
        scaled = up * turned[pl.ds(experts, 1), :]
        back = scaler * (scaled - normed * jnp.mean(scaled * normed, axis=1, keepdims=True))
        input_grad[part, :] = hidden_grad[part, :] + back
        return total + jnp.sum(up * normed, axis=0, keepdims=True)

    gain = lax.fori_loop(0, rows // 32, norm_rows, jnp.zeros((1, width), F32))
    ids = lax.broadcasted_iota(jnp.int32, (128, 1), 0)
    turned_part = jnp.swapaxes(row_part[...] + jnp.where(ids == experts, gain, 0.0), 0, 1)
    small_part[...] = turned_part.astype(BF16).reshape(small_part.shape)
    small_ring.exchange()
    small_ring.step(1)
    qkv_ring.step(3)
    small_ring.step(2)
    up_views = [up_sum.at[0], up_sum.at[1]]
    rest_ring.finish(up_views + [
        out_grad.at[pl.ds(0, 32)], out_grad.at[pl.ds(32, out_rows - 32)],
        down_grad.at[pl.ds(0, down_rows // 2)], down_grad.at[pl.ds(down_rows // 2, down_rows // 2)]])
    swap_sum = cross(2, up_sum.at[1 - h], up_from)
    swap_sum.start()
    qkv_ring.step(4)
    small_ring.step(3)
    qkv_ring.finish([qkv_sum.at[0], qkv_sum.at[1]])
    swap_qkv = cross(3, qkv_sum.at[1 - h], qkv_from)
    swap_qkv.start()
    small_ring.step(4)
    small_ring.finish([small_sum.at[0], small_sum.at[1]])
    swap_small = cross(4, small_sum.at[1 - h], small_from)
    swap_small.start()

    def place(ref, source, first, n, base=0):
        for who, part in ((h, source[0]), (1 - h, source[1])):
            ref[:, pl.ds(pl.multiple_of(base + who * n, 128), n)] = part[:, pl.ds(first, n)].astype(F32)

    swap_sum.wait_recv()
    ups = (up_sum.at[h], up_from)
    place(up_grad, ups, 0, sw)
    place(up_grad, ups, sw, sw, 2 * sw)
    swap_qkv.wait_recv()
    sums = (qkv_sum.at[h], qkv_from)
    place(query_grad, sums, 0, qw)
    place(key_grad, sums, qw, kw)
    place(value_grad, sums, qw + kw, kw)
    swap_small.wait_recv()
    small_grad[...] = small_sum[h] + small_from[...]
    for ring in (kv_ring, rest_ring, qkv_ring, small_ring):
        ring.flush()
    for copy in (swap_norm, swap_up, swap_sum, swap_qkv, swap_small):
        copy.wait_send()
    swap_up.wait_recv()


def tail_fused(
    dk, dv, dq, n1, first_w, tokens, hidden_grad, turned, out_part, up_part, down_part, row_part, din,
    blks, collective_id,
):
    chips, half = blks // 2, blks // 4
    rows, width = tokens.shape
    qw, kw = dq.shape[1], dk.shape[2]
    top = qw + 2 * kw
    dense = first_w.shape[2]
    out_rows, down_rows, up_wide = out_part.shape[1], down_part.shape[1], up_part.shape[3]
    dma = pltpu.SemaphoreType.DMA
    vmem = pl.BlockSpec(memory_space=pltpu.VMEM)
    anywhere = pl.BlockSpec(memory_space=pl.ANY)
    shapes = [(rows, kw)] * 4 + [(dense, up_wide)] * 2 + [(32, width), (out_rows - 32, width)]
    shapes += [(down_rows // 2, width)] * 2 + [(dense, top)] * 2 + [(dense, 128)] * 2
    others = [pltpu.VMEM((chips,) + s, BF16) for s in shapes]
    slots = [pltpu.VMEM((half,) + s, BF16) for s in shapes]
    n = len(shapes)
    held = (dk, dv, dq, n1, first_w, tokens, hidden_grad, turned, out_part, up_part, down_part, row_part)

    def f32(*shape):
        return jax.ShapeDtypeStruct(shape, F32)

    def low(*shape):
        return pltpu.VMEM(shape, BF16)

    return pl.pallas_call(
        functools.partial(tail_kernel, chips, blks),
        out_shape=[
            f32(rows, width), f32(dense, 2 * qw), f32(dense, 2 * kw), f32(dense, 2 * kw), f32(out_rows, width),
            f32(dense, 2 * up_wide), f32(down_rows, width), f32(dense, 128),
            jax.ShapeDtypeStruct((din.shape[0] // 2, din.shape[1]), BF16),
        ],
        in_specs=[anywhere] * 13,
        out_specs=[vmem] * 8 + [anywhere],
        scratch_shapes=[pltpu.VMEM(a.shape, a.dtype) for a in held] + [
            low(2, 2 * rows, kw), low(2, blks, dense, top), low(2, dense, top), low(2, dense, up_wide),
            low(2, blks, dense, 128), pltpu.VMEM((2, dense, 128), F32), low(rows, width), low(rows, width),
            low(dense, top), low(dense, up_wide), pltpu.VMEM((dense, 128), F32),
        ] + others + slots + slots + [dma((n, 2 * half + 1))] * 2 + [dma((n, half + 1))] * 4 + [dma((5,)), dma((5,)), dma((12,))],
        compiler_params=pltpu.CompilerParams(
            collective_id=collective_id, has_side_effects=True, vmem_limit_bytes=62 << 20),
    )(*held, din)


def experts_plain(own_ext, weights, cot_all, blks, capacity, collective_id):
    h, b = lax.axis_index("head"), lax.axis_index("blk")
    own_up, other_up, own_down, other_down = weights
    expert_in = pair(own_up, other_up).reshape(2 * own_up.shape[0], -1)
    expert_out = jnp.where(
        h == 0,
        jnp.concatenate([own_down, other_down], axis=1),
        jnp.concatenate([other_down, own_down], axis=1),
    )
    normed = own_ext[:, : expert_in.shape[0]]
    normed_pair = pair(normed, swap(normed))
    experts, width = blks, expert_in.shape[0]
    rows = own_ext.shape[0]
    ext = all_gather_blk([own_ext], blks, collective_id)[0]
    norm_all = ext[:, :, :width]
    gate_here = lax.dynamic_index_in_dim(ext, width + b, 2, keepdims=False).astype(F32)
    mask_here = lax.dynamic_index_in_dim(ext, width + experts + b, 2, keepdims=False).astype(F32)
    rank = jnp.cumsum(mask_here, axis=1) - mask_here
    slots = jnp.arange(capacity, dtype=F32)
    deal = ((rank[:, None, :] == slots[None, :, None]) & (mask_here[:, None, :] > 0)).astype(BF16)
    deal_gate = deal * gate_here[:, None, :].astype(BF16)

    def to_slots(dealer, array):
        moved = jnp.einsum("bst,btd->bsd", dealer, array, preferred_element_type=F32)
        return moved.astype(BF16).reshape(blks * capacity, width)

    def to_rows(dealer, array):
        return jnp.einsum(
            "bst,bsd->btd", dealer, array.reshape(blks, capacity, width), preferred_element_type=F32)

    expert_rows = to_slots(deal, norm_all)
    both = dot(expert_rows, expert_in)
    ew = expert_out.shape[0]
    gate_part, up_part = both[:, :ew], both[:, ew:]
    activated = (jax.nn.silu(gate_part) * up_part).astype(BF16)
    result = dot(activated, expert_out).astype(BF16)
    result_rows = to_rows(deal, result)
    gate_grad = jnp.sum(result_rows * cot_all.astype(F32), axis=2, keepdims=True)
    routed = (result_rows * gate_here[:, :, None]).astype(BF16)
    slot_grad = to_slots(deal_gate, cot_all)
    act_grad = dot_last(slot_grad, expert_out)
    both_grad = gated_grad(act_grad, gate_part, up_part)
    rows_back = to_rows(deal, dot_last(both_grad, expert_in).astype(BF16)).astype(BF16)
    lane = jnp.arange(128 * (-(-2 * experts // 128)), dtype=jnp.int32)
    grad_high = gate_grad.astype(BF16)
    grad_low = (gate_grad - grad_high.astype(F32)).astype(BF16)
    grad_lanes = jnp.where(lane == b, grad_high, jnp.where(lane == b + experts, grad_low, jnp.zeros((), BF16)))
    dwn = dot_first(activated, slot_grad).astype(BF16)
    dup = dot_first(expert_rows, both_grad).astype(BF16)
    home = reduce_scatter_blk([jnp.concatenate([rows_back, grad_lanes], axis=2)], blks, collective_id + 1, [F32])[0]
    routed_sum = reduce_scatter_blk([routed], blks, collective_id + 2, [F32])[0]
    return home, routed_sum, dup, dwn, normed_pair


def pair(own, other):
    return jnp.where(lax.axis_index("head") == 0, jnp.stack([own, other]), jnp.stack([other, own]))


def half(w, i, parts=1):
    size = w.shape[1] // (2 * parts)
    cut = lax.dynamic_slice_in_dim(w.reshape(w.shape[0], parts, 2 * size), i * size, size, 2)
    return cut.reshape(w.shape[0], parts * size)


def pick(stacked, i):
    return lax.dynamic_index_in_dim(stacked, i, 0, keepdims=False)


def front_plain(
    tokens, cotangent, where, mask, w_query, w_key, w_value, small, w_out, shared_up, shared_down,
    expert_up, expert_down, blks, collective_id,
):
    h = lax.axis_index("head")
    rows, width = tokens.shape
    experts = blks

    def columns(i):
        return jnp.concatenate([half(w_query, i), half(w_key, i), half(w_value, i)], axis=1)

    first = pair(
        jnp.concatenate([columns(h), small], axis=1),
        swap(jnp.concatenate([columns(1 - h), small], axis=1)),
    )
    tokens_pair = pair(tokens, swap(tokens))
    cotangent_pair = pair(cotangent, swap(cotangent)).reshape(2 * rows, width)
    up_pair = pair(half(shared_up, h, 2), swap(half(shared_up, 1 - h, 2)))
    other_up, other_down = swap(expert_up), swap(expert_down)
    gathered = all_gather_blk([first], blks, collective_id)[0].reshape(width, -1)
    qw = w_query.shape[1] // 2
    kw = w_key.shape[1] // 2
    full_qkv = gathered[:, : qw + 2 * kw]
    full_router = gathered[:, qw + 2 * kw : qw + 2 * kw + experts]
    gain_first = gathered[:, qw + 2 * kw + experts].astype(F32)
    gain_second = gathered[:, qw + 2 * kw + experts + 1].astype(F32)

    inputs_pair = tokens_pair.reshape(2 * rows, width).astype(F32)
    normed_one = (inputs_pair * inv_scale(inputs_pair) * gain_first).astype(BF16)
    qkv = dot(normed_one, full_qkv).astype(BF16)
    query = qkv[:, :qw]
    kv = all_gather_blk([qkv[:, qw:]], blks, collective_id + 1)[0].reshape(-1, PIECE, 2 * kw)

    attended, attended_full, lse = attention_forward(query, kv, where)

    up_all, out_all, down_all, cot_all = all_gather_blk([up_pair, w_out, shared_down, cotangent], blks, collective_id + 2)
    full_up = up_all.reshape(width, -1)
    full_out = out_all.reshape(-1, width)
    full_down = down_all.reshape(-1, width)

    mixed = dot(attended, full_out).reshape(2, rows, width)
    inputs = tokens.astype(F32)
    resid = inputs + (pick(mixed, h) + swap(pick(mixed, 1 - h).astype(BF16)).astype(F32))
    scaler_two = inv_scale(resid)
    normed_two = (resid * scaler_two * gain_second).astype(BF16)

    logits = dot(normed_two, full_router)
    masked = jnp.where(mask, logits, NEG)
    raised = jnp.where(mask, jnp.exp(masked - jnp.max(masked, axis=1, keepdims=True)), 0.0)
    gates = raised / jnp.sum(raised, axis=1, keepdims=True)
    extra = jnp.concatenate(
        [gates.astype(BF16), mask.astype(BF16), jnp.zeros((rows, -2 * experts % 128), BF16)], axis=1)
    ext = jnp.concatenate([normed_two, extra], axis=1)
    return (
        normed_one, query, kv, full_qkv, full_out, full_up, full_down, cot_all, cotangent_pair, other_up, other_down,
        attended, attended_full, lse, resid, ext, gates, full_router.T, gain_first, gain_second, None)


def finish_kernel(experts, count, h_ref, up_own, up_other, down_own, down_other, small, *refs):
    up_out, down_out, router_out, one_out, two_out = refs[count : count + 5]
    up_out[...] = up_own[...].astype(F32) + up_other[...].astype(F32)
    down_out[...] = down_own[...].astype(F32) + down_other[...].astype(F32)

    @pl.when(pl.program_id(0) == 0)
    def _():
        for source, target in zip(refs[:count], refs[count + 5 :]):
            target[...] = source[...]
        turned = jnp.swapaxes(small[...], 0, 1)
        router_out[...] = turned[:experts]
        one_out[...] = turned[experts : experts + 1]
        two_out[...] = turned[experts + 1 : experts + 2]


def finish_fused(h, dup, add_up, dwn, add_down, small, experts, others):
    steps = 4
    up_rows, down_rows = add_up.shape[0] // steps, add_down.shape[0] // steps
    up = pl.BlockSpec((up_rows, add_up.shape[1]), lambda i, *_: (i, 0))
    down = pl.BlockSpec((down_rows, add_down.shape[1]), lambda i, *_: (i, 0))
    dense = small.shape[0]
    made = [(add_up.shape, F32), (add_down.shape, F32), ((experts, dense), F32), ((1, dense), F32), ((1, dense), F32)]

    def still(shape):
        return pl.BlockSpec(shape, lambda i, *_: (0, 0))

    rest = [still(a.shape) for a in others]
    return pl.pallas_call(
        functools.partial(finish_kernel, experts, len(others)),
        grid_spec=pltpu.PrefetchScalarGridSpec(
            num_scalar_prefetch=1,
            grid=(steps,),
            in_specs=[
                pl.BlockSpec((up_rows, add_up.shape[1]), lambda i, h: (h[0] * steps + i, 0)), up,
                pl.BlockSpec((down_rows, add_down.shape[1]), lambda i, h: (i, h[0])), down,
                still(small.shape),
            ] + rest,
            out_specs=[up, down] + [still(s) for s, _ in made[2:]] + rest,
        ),
        out_shape=[jax.ShapeDtypeStruct(s, t) for s, t in made + [(a.shape, a.dtype) for a in others]],
        compiler_params=pltpu.CompilerParams(vmem_limit_bytes=63 << 20),
    )(h.reshape(1), dup, add_up, dwn, add_down, small, *others)


def shards(
    tokens, cotangent, seq_lengths, piece_order, routes, norm1_gain, w_query, w_key, w_value, w_out,
    norm2_gain, w_router, shared_up, shared_down, expert_up, expert_down,
):
    blks = lax.axis_size("blk")
    h, b = lax.axis_index("head"), lax.axis_index("blk")
    rows, width = tokens.shape
    experts = blks
    capacity = rows * TOP * 4 // (3 * blks)
    dense_rows = w_query.shape[0]

    fits = blks == 16 and rows == 128 and 2 * capacity == 128 and width % 768 == 0 and dense_rows == 48
    if fits:
        got = front_fused(
            tokens, cotangent, piece_order, seq_lengths, routes, w_query, w_key, w_value, w_router, norm1_gain,
            norm2_gain, w_out, shared_up, shared_down, expert_up[0], expert_down[0], blks, 0)
        slots = got[-1][2]
    else:
        small = jnp.concatenate(
            [w_router, norm1_gain[:, None], norm2_gain[:, None],
             jnp.zeros((dense_rows, -(experts + 2) % 128), BF16)], axis=1)
        lanes = small.shape[1]
        places = jnp.swapaxes(piece_order.reshape(2, blks), 0, 1).reshape(-1)
        order = jnp.arange(2 * blks, dtype=jnp.int32)
        slots = jnp.sum(jnp.where(places[None, :] == order[:, None], order[None, :], 0), axis=1)
    own_places = lax.dynamic_slice_in_dim(piece_order.reshape(2, blks), b, 1, 1).reshape(2)
    where = (slots, own_places, seq_lengths)
    if not fits:
        hot = routes[:, :, None] == jnp.arange(experts, dtype=jnp.int32)[None, None, :]
        mask = jnp.any(hot, axis=1)
        got = front_plain(
            tokens, cotangent, where, mask, w_query, w_key, w_value, small, w_out, shared_up, shared_down,
            expert_up[0], expert_down[0], blks, 0)
    (
        normed_one, query, kv, full_qkv, full_out, full_up, full_down, cot_all, cotangent_pair, other_up, other_down,
        attended, attended_full, lse, resid, ext, gates, router_rows, gain_first, gain_second, kept,
    ) = got
    qw, kw = w_query.shape[1] // 2, w_key.shape[1] // 2
    shared_width = full_down.shape[0]
    inputs = tokens.astype(F32)
    if fits:
        (
            output, hidden_grad, mixed_grad, out_part, shared_up_part, shared_down_part, dup, dwn, row_part, _, add_down,
        ) = experts_fused(
            ext, (expert_up[0], other_up, expert_down[0], other_down), cot_all, (full_up, full_down), cotangent_pair,
            cotangent, resid, gates, kept[1], attended, full_out, blks, capacity, 3)
        query_grad, *kv_parts = attention_backward(query, kv, attended_full, lse, mixed_grad, where)
        (
            input_grad, w_query_grad, w_key_grad, w_value_grad, out_sum, up_grad, down_sum, small_sum, add_up,
        ) = tail_fused(
            *kv_parts, query_grad, normed_one, kept[0], tokens, hidden_grad, kept[1],
            out_part.reshape(blks, dense_rows, width),
            shared_up_part.reshape(2, blks, dense_rows, -1),
            shared_down_part.reshape(blks, -1, width), row_part, dup, blks, 6)
        (
            expert_up_grad, expert_down_grad, router_grad, gain_one_grad, gain_two_grad, output,
            input_grad, w_query_grad, w_key_grad, w_value_grad, out_sum, up_grad, down_sum,
        ) = finish_fused(
            h, dup, add_up, dwn, add_down, small_sum, experts,
            (output, input_grad, w_query_grad, w_key_grad, w_value_grad, out_sum, up_grad, down_sum))
        return (
            output, input_grad, gain_one_grad.reshape(-1), w_query_grad, w_key_grad, w_value_grad,
            out_sum, gain_two_grad.reshape(-1), router_grad.T, up_grad, down_sum,
            expert_up_grad[None], expert_down_grad[None],
        )
    scaler_two = inv_scale(resid)
    normed_two = ext[:, :width]

    home, routed_sum, dup, dwn, normed_pair = experts_plain(
        ext, (expert_up[0], other_up, expert_down[0], other_down), cot_all, blks, capacity, 3)
    normed_pair = normed_pair.reshape(2 * rows, width)
    shared_both = dot(normed_pair, full_up)
    shared_gate, shared_lift = shared_both[:, :shared_width], shared_both[:, shared_width:]
    shared_act = (jax.nn.silu(shared_gate) * shared_lift).astype(BF16)
    shared_sum = dot(shared_act, full_down).reshape(2, rows, width)
    shared_down_part = dot_first(shared_act, cotangent_pair)
    shared_grad = gated_grad(dot_last(cotangent_pair, full_down), shared_gate, shared_lift)
    shared_up_part = dot_first(normed_pair, shared_grad)
    shared_back = dot_last(shared_grad, full_up).reshape(2, rows, width)
    output = (
        resid + routed_sum + pick(shared_sum, h) + swap(pick(shared_sum, 1 - h).astype(BF16)).astype(F32)
    ).astype(BF16)

    dgate = home[:, width : width + experts] + home[:, width + experts : width + 2 * experts]
    weighted = gates * dgate
    logit_grad = (weighted - gates * jnp.sum(weighted, axis=1, keepdims=True)).astype(BF16)
    norm_two_grad = (
        home[:, :width] + dot(logit_grad, router_rows)
        + pick(shared_back, h) + swap(pick(shared_back, 1 - h).astype(BF16)).astype(F32)
    )
    back, gain_two_part = norm_back(resid, scaler_two, gain_second, norm_two_grad)
    hidden_grad = cotangent.astype(F32) + back
    hidden_low = hidden_grad.astype(BF16)
    hidden_pair = pair(hidden_low, swap(hidden_low)).reshape(2 * rows, width)
    out_part = dot_first(attended, hidden_pair)
    mixed_grad = dot_last(hidden_pair, full_out).astype(BF16)
    query_grad, *kv_parts = attention_backward(query, kv, attended_full, lse, mixed_grad, where)
    router_part = dot_first(normed_two, logit_grad)
    dup, dwn, query_grad = lax.optimization_barrier((dup, dwn, query_grad))
    dup = dup.reshape(2, width // 2, -1)
    dwn = jnp.stack([dwn[:, : width // 2], dwn[:, width // 2 :]])
    expert_up_grad = pick(dup, h).astype(F32) + swap(pick(dup, 1 - h)).astype(F32)
    expert_down_grad = pick(dwn, h).astype(F32) + swap(pick(dwn, 1 - h)).astype(F32)
    kv_grads = reduce_scatter_blk([part.reshape(blks, 2 * rows, kw) for part in kv_parts], blks, 6, [BF16] * 2)
    qkv_grad = jnp.concatenate([query_grad, *kv_grads], axis=1)
    norm_one_part = dot_last(qkv_grad, full_qkv).reshape(2, rows, width)
    norm_one_grad = pick(norm_one_part, h) + swap(pick(norm_one_part, 1 - h).astype(BF16)).astype(F32)
    extra_grad, gain_one_part = norm_back(inputs, inv_scale(inputs), gain_first, norm_one_grad)
    input_grad = hidden_grad + extra_grad
    qkv_part = dot_first(normed_one, qkv_grad)
    small_part = jnp.concatenate(
        [router_part, gain_one_part[:, None], gain_two_part[:, None],
         jnp.zeros((width, lanes - experts - 2), F32)], axis=1)

    def by_rows(part):
        return part.astype(BF16).reshape(2, blks, dense_rows, -1)

    qkv_sum, up_sum, out_sum, down_sum, small_sum = reduce_scatter_blk(
        [by_rows(qkv_part), by_rows(shared_up_part),
         out_part.astype(BF16).reshape(blks, dense_rows, width),
         shared_down_part.astype(BF16).reshape(blks, -1, width), by_rows(small_part)],
        blks, 7, [BF16, BF16, F32, F32, F32])
    there = swap(jnp.concatenate([pick(qkv_sum, 1 - h), pick(up_sum, 1 - h)], axis=1)).astype(F32)
    here = jnp.concatenate([pick(qkv_sum, h), pick(up_sum, h)], axis=1).astype(F32)
    small_sum = pick(small_sum, h) + swap(pick(small_sum, 1 - h))

    def whole(start, size):
        return jnp.where(
            h == 0,
            jnp.concatenate([here[:, start : start + size], there[:, start : start + size]], axis=1),
            jnp.concatenate([there[:, start : start + size], here[:, start : start + size]], axis=1))

    top = qw + 2 * kw
    sw = shared_width
    up_grad = jnp.concatenate([whole(top, sw), whole(top + sw, sw)], axis=1)
    return (
        output, input_grad, small_sum[:, experts], whole(0, qw), whole(qw, kw), whole(qw + kw, kw),
        out_sum, small_sum[:, experts + 1], small_sum[:, :experts], up_grad, down_sum,
        expert_up_grad[None], expert_down_grad[None],
    )


def solution(mesh):
    both = P(("head", "blk"), None)
    flat = P(("head", "blk"))
    up, down = P("blk", "head", None), P("blk", None, "head")
    return jax.shard_map(
        shards,
        mesh=mesh,
        in_specs=(both, both, P(), P(), both, flat, both, both, both, both, flat, both, both, both, up, down),
        out_specs=(both, both, flat, both, both, both, both, flat, both, both, both, up, down),
        check_vma=False,
    )
```

```python
import functools

import jax
import jax.numpy as jnp
from jax import lax
from jax.experimental import pallas as pl
from jax.experimental.pallas import tpu as pltpu
from jax.sharding import PartitionSpec as P

MESH = pl.DeviceIdType.MESH


def ring_place(chip, chips):
    odd = chip % 2
    return (chip // 2) * (1 - odd) + (chips - 1 - chip // 2) * odd


def ring_chip(place, chips):
    high = place // (chips // 2)
    return 2 * place * (1 - high) + (2 * (chips - 1 - place) + 1) * high


def ring_info(chips):
    blk = lax.axis_index("blk")
    chip, core = blk // 2, blk % 2
    place = ring_place(chip, chips)

    def at(step):
        return ring_chip((place + step + chips) % chips, chips) * 2 + core

    return blk, core, at, blk + 1 - 2 * core


def pieces_of(shape):
    if len(shape) == 3:
        return [(0, None), (1, None)]
    rows = shape[0]
    if rows >= 32 and rows % 16 == 0:
        cut = (rows // 2 + 15) // 16 * 16
        return [(0, cut), (cut, rows - cut)]
    return [(0, rows)]


def part_in(ref, piece):
    start, size = piece
    return ref.at[start] if size is None else ref.at[pl.ds(start, size)]


def part_out(ref, piece, b):
    start, size = piece
    return ref.at[start, b] if size is None else ref.at[b, pl.ds(start, size)]


def ag_kernel(count, chips, plans, *refs):
    ins, outs = refs[:count], refs[count : 2 * count]
    right_sem, left_sem, sib_sem, sright, sleft, ssib, own_sem = refs[2 * count :]
    blk, core, at, sib = ring_info(chips)
    right, left = at(1), at(-1)
    barrier = pltpu.get_barrier_semaphore()
    for other in (right, left, sib):
        pl.semaphore_signal(barrier, inc=1, device_id={"blk": other}, device_id_type=MESH)
    pl.semaphore_wait(barrier, 3)
    half = chips // 2
    started = []

    def send(src, dst, ssem, rsem, dev):
        copy = pltpu.make_async_remote_copy(
            src_ref=src, dst_ref=dst, send_sem=ssem, recv_sem=rsem,
            device_id={"blk": dev}, device_id_type=MESH)
        copy.start()
        started.append(copy)
        return copy

    chunks = []
    for k in range(count):
        for i, piece in enumerate(plans[k]):
            chunks.append((len(chunks), k, piece, half - (i % 2), half - 1 + (i % 2)))
    copies = {}
    locals_ = []
    for c, k, piece, rh, lh in chunks:
        src = part_in(ins[k], piece)
        dst = part_out(outs[k], piece, blk)
        if rh >= 1:
            copies[c, "r", 1] = send(src, dst, sright.at[c, 0], right_sem.at[c, 0], right)
        if lh >= 1:
            copies[c, "l", 1] = send(src, dst, sleft.at[c, 0], left_sem.at[c, 0], left)
        copies[c, "s", 0] = send(src, dst, ssib.at[c, 0], sib_sem.at[c, 0], sib)
        own = pltpu.make_async_copy(src, dst, own_sem.at[c])
        own.start()
        locals_.append(own)
    for s in range(1, half + 1):
        for c, k, piece, rh, lh in chunks:
            if s <= rh:
                copies[c, "r", s].wait_recv()
                b = at(-s)
                blockref = part_out(outs[k], piece, b)
                if s < rh:
                    copies[c, "r", s + 1] = send(blockref, blockref, sright.at[c, s], right_sem.at[c, s], right)
                copies[c, "sr", s] = send(blockref, blockref, ssib.at[c, s], sib_sem.at[c, s], sib)
            if s <= lh:
                copies[c, "l", s].wait_recv()
                b = at(s)
                blockref = part_out(outs[k], piece, b)
                if s < lh:
                    copies[c, "l", s + 1] = send(blockref, blockref, sleft.at[c, s], left_sem.at[c, s], left)
                copies[c, "sl", s] = send(blockref, blockref, ssib.at[c, half + s], sib_sem.at[c, half + s], sib)
    for (c, d, s), copy in copies.items():
        if d in ("s", "sr", "sl"):
            copy.wait_recv()
    for copy in started:
        copy.wait_send()
    for copy in locals_:
        copy.wait()


def all_gather_blk(arrays, blks, collective_id, vmem=False):
    chips = blks // 2
    count = len(arrays)
    plans = [pieces_of(a.shape) for a in arrays]
    n = sum(len(p) for p in plans)
    half = chips // 2
    shapes = [
        jax.ShapeDtypeStruct((a.shape[0], blks) + a.shape[1:] if a.ndim == 3 else (blks,) + a.shape, a.dtype)
        for a in arrays
    ]
    dma = pltpu.SemaphoreType.DMA
    space = pltpu.VMEM if vmem else pl.ANY
    return pl.pallas_call(
        functools.partial(ag_kernel, count, chips, plans),
        out_shape=shapes,
        in_specs=[pl.BlockSpec(memory_space=space)] * count,
        out_specs=[pl.BlockSpec(memory_space=space)] * count,
        scratch_shapes=[
            dma((n, half)), dma((n, half)), dma((n, 2 * half + 1)),
            dma((n, half)), dma((n, half)), dma((n, 2 * half + 1)), dma((n,)),
        ],
        compiler_params=pltpu.CompilerParams(collective_id=collective_id, has_side_effects=True,
            vmem_limit_bytes=(60 << 20) if vmem else None),
    )(*arrays)


def rs_kernel(count, chips, plans, *refs):
    xs, outs = refs[:count], refs[count : 2 * count]
    rest = refs[2 * count :]
    n = sum(len(p) for p in plans)
    ys, rs, ls = rest[:n], rest[n : 2 * n], rest[2 * n : 3 * n]
    right_sem, left_sem, sib_sem, sright, sleft, ssib = rest[3 * n :]
    blk, core, at, sib = ring_info(chips)
    right, left = at(1), at(-1)
    barrier = pltpu.get_barrier_semaphore()
    for other in (right, left, sib):
        pl.semaphore_signal(barrier, inc=1, device_id={"blk": other}, device_id_type=MESH)
    pl.semaphore_wait(barrier, 3)
    half = chips // 2
    started = []

    def send(src, dst, ssem, rsem, dev):
        copy = pltpu.make_async_remote_copy(
            src_ref=src, dst_ref=dst, send_sem=ssem, recv_sem=rsem,
            device_id={"blk": dev}, device_id_type=MESH)
        copy.start()
        started.append(copy)
        return copy

    chunks = []
    for k in range(count):
        for i, piece in enumerate(plans[k]):
            chunks.append((len(chunks), k, piece, half - (i % 2), half - 1 + (i % 2)))
    order = []
    for d in range(half, 0, -1):
        order += [d, -d] if d < half else [d]
    order.append(0)
    sibs = {}
    for j, d in enumerate(order):
        there = at(d) + 1 - 2 * core
        for c, k, piece, rh, lh in chunks:
            sibs[c, d] = send(part_out(xs[k], piece, there), ys[c].at[j], ssib.at[c, j], sib_sem.at[c, j], sib)
    ready = set()

    def blocks(rows, body):
        step = 16 if rows % 16 == 0 else rows

        @pl.loop(0, rows // step)
        def _(i):
            body(pl.ds(pl.multiple_of(i * step, step), step))

    def mine(c, k, piece, d):
        j = order.index(d)
        if (c, d) not in ready:
            sibs[c, d].wait_recv()
            ready.add((c, d))
        return j

    copies = {}

    def join(c, k, piece, d, into, recv):
        j = mine(c, k, piece, d)
        x = part_out(xs[k], piece, at(d))
        rows = x.shape[0]

        def body(w):
            total = x[w].astype(jnp.float32) + ys[c][j, w].astype(jnp.float32)
            if recv is not None:
                total = total + recv[w].astype(jnp.float32)
            into[w] = total.astype(into.dtype)

        blocks(rows, body)

    for s in range(1, half + 1):
        for c, k, piece, rh, lh in chunks:
            for way, hops, buf, sem, ssem, dev in (
                (1, rh, rs[c], right_sem, sright, right),
                (-1, lh, ls[c], left_sem, sleft, left),
            ):
                if s > hops:
                    continue
                if s == 1:
                    j = order.index(way * hops if way * hops in order else hops)
                    join(c, k, piece, order[j], ys[c].at[j], None)
                    src = ys[c].at[j]
                else:
                    copies[c, way, s - 1].wait_recv()
                    d = way * (hops - s + 1)
                    src = buf.at[s - 2]
                    join(c, k, piece, d, src, src)
                copies[c, way, s] = send(src, buf.at[s - 1], ssem.at[c, s - 1], sem.at[c, s - 1], dev)
    for c, k, piece, rh, lh in chunks:
        if rh >= 1:
            copies[c, 1, rh].wait_recv()
        if lh >= 1:
            copies[c, -1, lh].wait_recv()
        j = mine(c, k, piece, 0)
        x = part_out(xs[k], piece, blk)
        target = part_in(outs[k], piece)

        def body(w, x=x, c=c, j=j, rh=rh, lh=lh, target=target):
            total = x[w].astype(jnp.float32) + ys[c][j, w].astype(jnp.float32)
            if rh >= 1:
                total = total + rs[c][rh - 1, w].astype(jnp.float32)
            if lh >= 1:
                total = total + ls[c][lh - 1, w].astype(jnp.float32)
            target[w] = total.astype(target.dtype)

        blocks(x.shape[0], body)
    for copy in started:
        copy.wait_send()


def reduce_scatter_blk(arrays, blks, collective_id, out_dtypes):
    chips = blks // 2
    half = chips // 2
    count = len(arrays)
    shapes = [a.shape[1:] if a.ndim == 3 else (2,) + a.shape[2:] for a in arrays]
    plans = [pieces_of(s) for s in shapes]
    dma = pltpu.SemaphoreType.DMA
    ys, rs = [], []
    for s, plan in zip(shapes, plans):
        for start, size in plan:
            rows = s[1] if size is None else size
            ys.append(pltpu.VMEM((chips, rows, s[-1]), jnp.bfloat16))
            rs.append(pltpu.VMEM((half, rows, s[-1]), jnp.bfloat16))
    n = len(ys)
    return pl.pallas_call(
        functools.partial(rs_kernel, count, chips, plans),
        out_shape=[jax.ShapeDtypeStruct(s, t) for s, t in zip(shapes, out_dtypes)],
        in_specs=[pl.BlockSpec(memory_space=pltpu.VMEM)] * count,
        out_specs=[pl.BlockSpec(memory_space=pltpu.VMEM)] * count,
        scratch_shapes=ys + rs + rs + [
            dma((n, half)), dma((n, half)), dma((n, chips)),
            dma((n, half)), dma((n, half)), dma((n, chips)),
        ],
        compiler_params=pltpu.CompilerParams(collective_id=collective_id, has_side_effects=True,
            vmem_limit_bytes=60 << 20),
    )(*arrays)


H = 12
KVH = 4
HD = 128
TOP = 6
PIECE = 128
EPS = 1e-05
NEG = -1e30
F32 = jnp.float32
BF16 = jnp.bfloat16


def dot(a, b):
    return jnp.dot(a, b, preferred_element_type=F32)


def dot_first(a, b):
    return lax.dot_general(a, b, (((0,), (0,)), ((), ())), preferred_element_type=F32)


def dot_last(a, b):
    return lax.dot_general(a, b, (((1,), (1,)), ((), ())), preferred_element_type=F32)


def inv_scale(values):
    return lax.rsqrt(jnp.mean(values * values, axis=1, keepdims=True) + EPS)


def norm_back(values, scaler, gain, upstream):
    normed = values * scaler
    gain_grad = jnp.sum(upstream * normed, axis=0)
    scaled = upstream * gain
    grad = scaler * (scaled - normed * jnp.mean(scaled * normed, axis=1, keepdims=True))
    return grad, gain_grad


def gated_grad(act_grad, gate, lift):
    sig = jax.nn.sigmoid(gate)
    return jnp.concatenate(
        [act_grad * lift * sig * (1.0 + gate * (1.0 - sig)), act_grad * gate * sig], axis=1
    ).astype(BF16)


def swap(array):
    return lax.ppermute(array, "head", [(0, 1), (1, 0)])


def ends_of(lengths_ref):
    end, ends = jnp.int32(0), []
    for e in range(lengths_ref.shape[0]):
        end = end + lengths_ref[e]
        ends.append(end)
    return ends


def key_span(place, lengths_ref):
    start = jnp.int32(0)
    for end in ends_of(lengths_ref):
        start = jnp.where(end <= place * PIECE, end, start)
    return start // PIECE


def key_chunk(slots_ref, first, pieces, *refs):
    last = slots_ref.shape[0] - 1
    slots = [slots_ref[jnp.clip(first + k, 0, last)] for k in range(pieces)]
    return slots, [jnp.concatenate([ref[s] for s in slots], axis=0) for ref in refs]


def stacked(ref, i, repeats):
    return jnp.concatenate(
        [ref[pl.ds(i * PIECE, PIECE), pl.ds(r * HD, HD)] for r in range(repeats)], axis=0)


def seen(lengths_ref, place, first, keys, cols):
    own = place * PIECE + lax.broadcasted_iota(jnp.int32, (1, cols), 1) % PIECE
    start = jnp.zeros((1, cols), jnp.int32)
    for end in ends_of(lengths_ref):
        start = jnp.where(end <= own, end, start)
    there = first * PIECE + lax.broadcasted_iota(jnp.int32, (keys, 1), 0)
    return (there <= own) & (there >= start)


CHUNK = 4


def forward_kernel(repeats, slots_ref, places_ref, lengths_ref, q_ref, k_ref, v_ref, low_ref, full_ref, lse_ref):
    cols = repeats * PIECE
    for i in range(q_ref.shape[0] // PIECE):
        place = places_ref[i]
        lo = key_span(place, lengths_ref)
        q = stacked(q_ref, i, repeats)

        def step(n, carry, lo=lo, place=place, q=q):
            top, total, acc = carry
            first = lo + n * CHUNK
            _, (k, v) = key_chunk(slots_ref, first, CHUNK, k_ref, v_ref)
            scores = dot_last(k, q) * HD**-0.5
            scores = jnp.where(seen(lengths_ref, place, first, CHUNK * PIECE, cols), scores, NEG)
            new = jnp.maximum(top, jnp.max(scores, axis=0, keepdims=True))
            weights = jnp.exp(scores - new)
            factor = jnp.exp(top - new)
            total = total * factor + jnp.sum(weights, axis=0, keepdims=True)
            return new, total, acc * factor + dot_first(v, weights.astype(BF16))

        top, total, acc = lax.fori_loop(
            0, (place - lo) // CHUNK + 1, step,
            (jnp.full((1, cols), NEG, F32), jnp.zeros((1, cols), F32), jnp.zeros((HD, cols), F32)))
        out = jnp.swapaxes(acc / total, 0, 1)
        lse_ref[0, pl.ds(i, 1), :] = top + jnp.log(total)
        for r in range(repeats):
            part = out[r * PIECE : (r + 1) * PIECE]
            full_ref[pl.ds(i * PIECE, PIECE), pl.ds(r * HD, HD)] = part
            low_ref[pl.ds(i * PIECE, PIECE), pl.ds(r * HD, HD)] = part.astype(BF16)


def attention_forward(query, kv, where):
    rows, pieces = query.shape[0], kv.shape[0]
    groups = kv.shape[2] // (2 * HD)
    wide = query.shape[1] // groups
    repeats = wide // HD
    spec = pl.BlockSpec((rows, wide), lambda g, *_: (0, g))
    return pl.pallas_call(
        functools.partial(forward_kernel, repeats),
        grid_spec=pltpu.PrefetchScalarGridSpec(
            num_scalar_prefetch=3,
            grid=(groups,),
            in_specs=[
                spec,
                pl.BlockSpec((pieces, PIECE, HD), lambda g, *_: (0, 0, g)),
                pl.BlockSpec((pieces, PIECE, HD), lambda g, *_: (0, 0, groups + g)),
            ],
            out_specs=[spec, spec, pl.BlockSpec((1, rows // PIECE, repeats * PIECE), lambda g, *_: (g, 0, 0))],
        ),
        out_shape=[
            jax.ShapeDtypeStruct(query.shape, BF16),
            jax.ShapeDtypeStruct(query.shape, F32),
            jax.ShapeDtypeStruct((groups, rows // PIECE, repeats * PIECE), F32),
        ],
        compiler_params=pltpu.CompilerParams(vmem_limit_bytes=48 << 20),
    )(*where, query, kv, kv)


def backward_kernel(
    repeats, slots_ref, places_ref, lengths_ref, q_ref, k_ref, v_ref, full_ref, grad_ref, lse_ref,
    dq_ref, dk_ref, dv_ref, key_acc, value_acc,
):
    cols = repeats * PIECE
    key_acc[...] = jnp.zeros_like(key_acc)
    value_acc[...] = jnp.zeros_like(value_acc)
    for i in range(q_ref.shape[0] // PIECE):
        place = places_ref[i]
        lo = key_span(place, lengths_ref)
        q, grad = stacked(q_ref, i, repeats), stacked(grad_ref, i, repeats)
        product = grad.astype(F32) * stacked(full_ref, i, repeats)
        delta = jnp.sum(jnp.swapaxes(product, 0, 1), axis=0, keepdims=True)
        lse = lse_ref[0, pl.ds(i, 1), :]

        def step(n, dq, lo=lo, place=place, q=q, grad=grad, delta=delta, lse=lse):
            first = lo + n * CHUNK
            slots, (k, v) = key_chunk(slots_ref, first, CHUNK, k_ref, v_ref)
            scores = dot_last(k, q) * HD**-0.5
            weights = jnp.where(
                seen(lengths_ref, place, first, CHUNK * PIECE, cols), jnp.exp(scores - lse), 0.0)
            back = (weights * (dot_last(v, grad) - delta)).astype(BF16)
            dk = dot(back, q)
            dv = dot(weights.astype(BF16), grad)
            for j, s in enumerate(slots):
                key_acc[s] += dk[j * PIECE : (j + 1) * PIECE]
                value_acc[s] += dv[j * PIECE : (j + 1) * PIECE]
            return dq + dot_first(k, back)

        dq = lax.fori_loop(0, (place - lo) // CHUNK + 1, step, jnp.zeros((HD, cols), F32))
        out = (jnp.swapaxes(dq, 0, 1) * HD**-0.5).astype(BF16)
        for r in range(repeats):
            dq_ref[pl.ds(i * PIECE, PIECE), pl.ds(r * HD, HD)] = out[r * PIECE : (r + 1) * PIECE]
    dk_ref[...] = (key_acc[...] * HD**-0.5).astype(BF16)
    dv_ref[...] = value_acc[...].astype(BF16)


def attention_backward(query, kv, full, lse, grad, where):
    rows, pieces = query.shape[0], kv.shape[0]
    groups = kv.shape[2] // (2 * HD)
    wide = query.shape[1] // groups
    repeats = wide // HD
    spec = pl.BlockSpec((rows, wide), lambda g, *_: (0, g))
    block = pl.BlockSpec((pieces, PIECE, HD), lambda g, *_: (0, 0, g))
    half = jax.ShapeDtypeStruct((pieces, PIECE, groups * HD), BF16)
    return pl.pallas_call(
        functools.partial(backward_kernel, repeats),
        grid_spec=pltpu.PrefetchScalarGridSpec(
            num_scalar_prefetch=3,
            grid=(groups,),
            in_specs=[
                spec, block, pl.BlockSpec((pieces, PIECE, HD), lambda g, *_: (0, 0, groups + g)), spec, spec,
                pl.BlockSpec((1, rows // PIECE, repeats * PIECE), lambda g, *_: (g, 0, 0)),
            ],
            out_specs=[spec, block, block],
            scratch_shapes=[pltpu.VMEM((pieces, PIECE, HD), F32)] * 2,
        ),
        out_shape=[jax.ShapeDtypeStruct(query.shape, BF16), half, half],
        compiler_params=pltpu.CompilerParams(vmem_limit_bytes=60 << 20),
    )(*where, query, kv, kv, full, grad, lse)


def tiles(total, size, body):
    if total == size:
        body(pl.ds(0, size))
    else:

        @pl.loop(0, total // size)
        def _(i):
            body(pl.ds(pl.multiple_of(i * size, size), size))


def shifted(c, by):
    if isinstance(c.start, int):
        return pl.ds(c.start + by, c.size)
    return pl.ds(pl.multiple_of(c.start + by, c.size), c.size)


def expert_kernel(
    chips, experts, ext_ref, up_own, up_other, down_own, down_other, cot_ref,
    shared_up, shared_down, cot_pair, cot_own, resid, gates, turned, low, full_out,
    output, hidden_grad, mixed_grad, out_part, up_part, down_part, din, dout, row_part, norm_pair, other_down,
    home_ref, routed_ref, din_ref, dout_ref, shared_act, shared_dab, hid, from_back, from_sum,
    in_ref, out_ref, ext, cot, rows_x, rows_dy, rows_act, rows_dab, both, result, back, deal, gate, take, take_gate,
    own_d, own_o, stage_d, stage_o, sib_d, sib_o, right_d, right_o, left_d, left_o,
    copy_sem, cot_sem, ag_r, ag_l, ag_sr, ag_sl, ss_r, ss_l, ss_sr, ss_sl,
    ex_sem, ss_ex, rs_r, rs_l, ss_rr, ss_rl, weight_sem, pair_sem, load_sem, y_send, y_recv,
):
    blk, core, at, sib = ring_info(chips)
    h = lax.axis_index("head")
    right, left = at(1), at(-1)
    half = chips // 2
    rows, wide = ext_ref.shape
    width = in_ref.shape[0]
    hidden = out_ref.shape[0]
    slots = rows_x.shape[0] // chips
    cut = rows // 2
    upper, lower = pl.ds(0, cut), pl.ds(cut, cut)

    barrier = pltpu.get_barrier_semaphore()
    for other in (right, left, sib):
        pl.semaphore_signal(barrier, inc=1, device_id={"blk": other}, device_id_type=MESH)
    pl.semaphore_signal(barrier, inc=1, device_id={"head": 1 - h}, device_id_type=MESH)
    pl.semaphore_wait(barrier, 4)

    def remote(src, dst, ssem, rsem, dev):
        return pltpu.make_async_remote_copy(
            src_ref=src, dst_ref=dst, send_sem=ssem, recv_sem=rsem,
            device_id={"blk": dev}, device_id_type=MESH)

    def hop_right(part, k, s):
        ref = ext.at[at(1 - s), part]
        return remote(ref, ref, ss_r.at[k, s], ag_r.at[k, s], right)

    def hop_left(part, k, s):
        ref = ext.at[at(s - 1), part]
        return remote(ref, ref, ss_l.at[k, s], ag_l.at[k, s], left)

    def over_right(part, k, s):
        ref = ext.at[at(-s), part]
        return remote(ref, ref, ss_sr.at[k, s], ag_sr.at[k, s], sib)

    def over_left(part, k, s):
        ref = ext.at[at(s), part]
        return remote(ref, ref, ss_sl.at[k, s], ag_sl.at[k, s], sib)

    def place_of(g, j):
        return at(-g) if j == 0 else at(g)

    def cot_copy(g, j):
        there = place_of(g, j)
        slot = lax.rem(g, 2)
        return pltpu.make_async_copy(
            cot_ref.at[pl.ds(there - core, 2)], cot.at[slot, j], cot_sem.at[slot, j])

    def exchange_d(g, j):
        return remote(stage_d.at[j], sib_d.at[lax.div(place_of(g, j), 2)], ss_ex.at[0, j, g], ex_sem.at[0, j, g], sib)

    def exchange_o(g, j):
        return remote(stage_o.at[j], sib_o.at[lax.div(place_of(g, j), 2)], ss_ex.at[1, j, g], ex_sem.at[1, j, g], sib)

    mine = pltpu.make_async_copy(ext_ref, ext.at[blk], copy_sem)
    mine.start()
    cot_copy(0, 0).start()
    weights = []
    for i, (up, down) in ((h, (up_own, down_own)), (1 - h, (up_other, down_other))):
        size = up.shape[0]
        start = pl.multiple_of(i * size, size)
        weights.append((up, in_ref.at[pl.ds(start, size)]))
        weights.append((down, out_ref.at[:, pl.ds(start, size)]))
    weights = [pltpu.make_async_copy(a, b, weight_sem.at[i]) for i, (a, b) in enumerate(weights)]
    for copy in weights:
        copy.start()
    mine.wait()
    for k, part in ((0, upper), (1, lower)):
        hop_right(part, k, 1).start()
        hop_left(part, k, 1).start()
        over_right(part, k, 0).start()
    own_norm = ext.at[blk, :, pl.ds(0, width)]
    keep = pltpu.make_async_copy(own_norm, norm_pair.at[h], pair_sem.at[0])
    keep.start()
    swapped = pltpu.make_async_remote_copy(
        src_ref=own_norm, dst_ref=norm_pair.at[h], send_sem=pair_sem.at[1], recv_sem=pair_sem.at[2],
        device_id={"head": 1 - h}, device_id_type=MESH)
    swapped.start()
    for copy in weights:
        copy.wait()

    lane = lax.broadcasted_iota(jnp.int32, (2 * rows, 128), 1)
    token_row = lax.broadcasted_iota(jnp.int32, (2 * rows, 2 * rows), 0)
    token_col = lax.broadcasted_iota(jnp.int32, (2 * rows, 2 * rows), 1)
    same = (token_row < rows) == (token_col < rows)
    triangle = jnp.where((token_row > token_col) & same, 1.0, 0.0).astype(BF16)
    offset = jnp.float32(slots // 2)
    shift_col = jnp.where(lax.broadcasted_iota(jnp.int32, (2 * rows, 1), 0) < rows, 0.0, offset)
    shift_row = jnp.where(lax.broadcasted_iota(jnp.int32, (1, 2 * rows), 1) < rows, 0.0, offset)
    slot_id = lax.broadcasted_iota(jnp.int32, (slots, 2 * rows), 0).astype(F32)
    lane_row = lax.broadcasted_iota(jnp.int32, (128, 128), 0)
    pick_mask = jnp.where(lane_row == experts + blk, 1.0, 0.0).astype(BF16)
    pick_gate = jnp.where(lane_row == blk, 1.0, 0.0).astype(BF16)
    lane_col = lax.broadcasted_iota(jnp.int32, (8, 128), 1)
    mask_row = jnp.where(lane_col == experts + blk, 1.0, 0.0).astype(BF16)
    gate_row = jnp.where(lane_col == blk, 1.0, 0.0).astype(BF16)

    def arrive(s):
        last = isinstance(s, int) and s == half
        hop_right(upper, 0, s).wait_recv()
        if not last:
            hop_right(upper, 0, s + 1).start()
        over_right(upper, 0, s).start()
        hop_left(lower, 1, s).wait_recv()
        if not last:
            hop_left(lower, 1, s + 1).start()
        over_left(lower, 1, s).start()
        if last:
            return
        hop_right(lower, 1, s).wait_recv()

        @pl.when(s < half - 1)
        def _():
            hop_right(lower, 1, s + 1).start()

        over_right(lower, 1, s).start()
        hop_left(upper, 0, s).wait_recv()

        @pl.when(s < half - 1)
        def _():
            hop_left(upper, 0, s + 1).start()

        over_left(upper, 0, s).start()

    def work(g, count, base, first):
        turn = lax.rem(g, 2)
        size = count * slots
        group = pl.ds(base, size)
        part = pl.ds(0, size)
        firsts = [place_of(g, j) - core for j in range(count)]
        for j in range(count):
            lanes = ext[pl.ds(firsts[j], 2), :, pl.ds(width, 128)].reshape(2 * rows, 128)
            chosen = dot(lanes, pick_mask)
            rank = dot(triangle, chosen.astype(BF16))
            spread = jnp.where((rank + shift_col == lane.astype(F32)) & (chosen > 0.5), 1.0, 0.0).astype(BF16)
            deal[j] = spread.reshape(2, rows, 128)
            gate[j] = dot(lanes, pick_gate).reshape(2, rows, 128)
            chosen_row = dot_last(mask_row, lanes)
            rank_row = dot_last(chosen_row.astype(BF16), triangle)
            weight_row = dot_last(gate_row, lanes)
            taken = jnp.where((rank_row[:1] + shift_row == slot_id) & (chosen_row[:1] > 0.5), 1.0, 0.0)
            take[j] = taken.astype(BF16)
            take_gate[j] = (taken * weight_row[:1]).astype(BF16)
        for j in range(count):
            cot_copy(g, j).wait()
            where = pl.ds(pl.multiple_of(base + j * slots, slots), slots)

            def pick_rows(c, j=j, where=where):
                rows_x[where, c] = dot(
                    take[j], ext[pl.ds(firsts[j], 2), :, c].reshape(2 * rows, c.size)).astype(BF16)
                rows_dy[where, c] = dot(take_gate[j], cot[turn, j, :, :, c].reshape(2 * rows, c.size)).astype(BF16)

            for t in range(2):
                pick_rows(pl.ds(t * (width // 2), width // 2))

        def hidden_tile(c):
            high = shifted(c, hidden)
            x = rows_x[group]
            gate_part = dot(x, in_ref[:, c])
            lift = dot(x, in_ref[:, high])
            both[part, c] = gate_part
            both[part, high] = lift
            rows_act[group, c] = (jax.nn.silu(gate_part) * lift).astype(BF16)

        for t in range(2):
            hidden_tile(pl.ds(t * (hidden // 2), hidden // 2))

        def result_tile(c):
            result[part, c] = dot(rows_act[group], out_ref[:, c]).astype(BF16)

        for t in range(2):
            result_tile(pl.ds(t * (width // 2), width // 2))

        def grad_tile(c):
            high = shifted(c, hidden)
            da = dot_last(rows_dy[group], out_ref[c, :])
            gate_part, lift = both[part, c], both[part, high]
            sig = jax.nn.sigmoid(gate_part)
            rows_dab[group, c] = (da * lift * sig * (1.0 + gate_part * (1.0 - sig))).astype(BF16)
            rows_dab[group, high] = (da * gate_part * sig).astype(BF16)

        for t in range(2):
            grad_tile(pl.ds(t * (hidden // 2), hidden // 2))

        def back_tile(c):
            back[part, c] = dot_last(rows_dab[group], in_ref[c, :]).astype(BF16)

        for t in range(2):
            back_tile(pl.ds(t * (width // 2), width // 2))
        if first is not None:

            @pl.when(first)
            def _():
                for j in range(2):
                    exchange_d(g - 1, j).wait_send()
                    exchange_o(g - 1, j).wait_send()

            @pl.when(jnp.logical_not(first))
            def _():
                exchange_d(g - 1, 0).wait_send()
                exchange_o(g - 1, 0).wait_send()

        for j in range(count):
            chip = lax.div(firsts[j], 2)
            for which, to_d, to_o in (
                (core, own_d.at[chip], own_o.at[chip]),
                (1 - core, stage_d.at[j], stage_o.at[j]),
            ):
                from_slots = pl.ds(j * slots, slots)
                dealer = deal[j, which]
                share = gate[j, which]
                total = jnp.zeros((rows, 1), F32)
                for t in range(width // 512):
                    c = pl.ds(t * 512, 512)
                    home_rows = dot(dealer, result[from_slots, c])
                    to_o[:, c] = (home_rows * share[:, :1]).astype(BF16)
                    total = total + jnp.sum(
                        home_rows * cot[turn, j, which, :, c].astype(F32), axis=1, keepdims=True)
                    to_d[:, c] = dot(dealer, back[from_slots, c]).astype(BF16)
                high = total.astype(BF16).astype(F32)
                own_lane = lane[:rows]
                lanes = jnp.where(own_lane == blk, high, jnp.where(own_lane == experts + blk, total - high, 0.0))
                to_d[:, pl.ds(width, 128)] = lanes.astype(BF16)
            exchange_d(g, j).start()
            exchange_o(g, j).start()

    arrays = ((0, own_d, sib_d, right_d, left_d, home_ref), (1, own_o, sib_o, right_o, left_o, routed_ref))
    arrived = set()

    def join(a, own, other, d, part, into, received):
        g, j = (d, 1) if 0 < d < half else (abs(d), 0)
        if (a, g, j) not in arrived:
            arrived.add((a, g, j))
            (exchange_d, exchange_o)[a](g, j).wait_recv()
        chip = lax.div(at(d), 2)

        def add(c):
            total = own[chip, c].astype(F32) + other[chip, c].astype(F32)
            for ref in received:
                total = total + ref[c].astype(F32)
            into[c] = total.astype(into.dtype)

        @pl.loop(0, cut // 16)
        def _(i):
            add(pl.ds(pl.multiple_of(part.start + i * 16, 16), 16))

    def pass_right(a, src, buf, k, part, s):
        return remote(src.at[part], buf.at[s - 1, part], ss_rr.at[a, k, s], rs_r.at[a, k, s], right)

    def pass_left(a, src, buf, k, part, s):
        return remote(src.at[part], buf.at[s - 1, part], ss_rl.at[a, k, s], rs_l.at[a, k, s], left)

    ways = (
        (0, upper, 1, half), (1, lower, -1, half), (1, lower, 1, half - 1), (0, upper, -1, half - 1),
    )
    sent = []

    def scatter_step(a, s, ways=ways):
        _, own, other, to_right, to_left, _ = arrays[a]
        for k, part, way, hops in ways:
            if s > hops:
                continue
            make, buf = (pass_right, to_right) if way > 0 else (pass_left, to_left)
            d = way * (hops - s + 1)
            if d == -half:
                d = half
            if s == 1:
                src = own.at[lax.div(at(d), 2)]
                join(a, own, other, d, part, src, ())
            else:
                src = buf.at[s - 2]
                make(a, src, buf, k, part, s - 1).wait_recv()
                join(a, own, other, d, part, src, (src,))
            copy = make(a, src, buf, k, part, s)
            copy.start()
            sent.append(copy)

    over_right(upper, 0, 0).wait_recv()
    over_right(lower, 1, 0).wait_recv()
    cot_copy(1, 0).start()
    cot_copy(1, 1).start()
    work(0, 1, 0, None)

    @pl.loop(1, half)
    def _(g):
        arrive(g)
        over_right(upper, 0, g).wait_recv()
        over_right(lower, 1, g).wait_recv()
        over_left(lower, 1, g).wait_recv()
        over_left(upper, 0, g).wait_recv()
        cot_copy(g + 1, 0).start()

        @pl.when(g < half - 1)
        def _():
            cot_copy(g + 1, 1).start()

        work(g, 2, pl.multiple_of(slots + (g - 1) * 2 * slots, slots), g > 1)

    arrive(half)
    over_right(upper, 0, half).wait_recv()
    over_left(lower, 1, half).wait_recv()
    scatter_step(0, 1, ways[2:])
    work(half, 1, (2 * half - 1) * slots, True)

    def scatter_finish(a):
        _, own, other, to_right, to_left, into = arrays[a]
        for k, part in ((0, upper), (1, lower)):
            last_right, last_left = half - k, half - 1 + k
            pass_right(a, own.at[0], to_right, k, part, last_right).wait_recv()
            pass_left(a, own.at[0], to_left, k, part, last_left).wait_recv()
            join(a, own, other, 0, part, into, (to_right.at[last_right - 1], to_left.at[last_left - 1]))

    loads = 0

    def move(src, dst):
        nonlocal loads
        copy = pltpu.make_async_copy(src, dst, load_sem.at[loads])
        loads += 1
        copy.start()
        return copy

    def cross(i, src, dst):
        return pltpu.make_async_remote_copy(
            src_ref=src, dst_ref=dst, send_sem=y_send.at[i], recv_sem=y_recv.at[i],
            device_id={"head": 1 - h}, device_id_type=MESH)

    theirs = pl.ds(pl.multiple_of((1 - h) * rows, rows), rows)
    ours = pl.ds(pl.multiple_of(h * rows, rows), rows)
    keep.wait()
    swapped.wait()
    shared_loads = [
        move(shared_up, in_ref), move(shared_down, out_ref), move(cot_pair, back),
        move(norm_pair.at[0], result.at[pl.ds(0, rows)]), move(norm_pair.at[1], result.at[pl.ds(rows, rows)])]
    scatter_step(0, 1, ways[:2])

    def weight_in(c):
        din_ref[c, :] = dot_first(rows_x[:, c], rows_dab[...]).astype(BF16)

    tiles(width, 256, weight_in)
    din_out = move(din_ref, din)
    load_out = move(full_out, rows_x.at[pl.ds(0, low.shape[1])])
    scatter_step(0, 2)

    for copy in shared_loads:
        copy.wait()

    def shared_tile(c):
        high = shifted(c, hidden)
        gate_part = dot(result[...], in_ref[:, c])
        lift = dot(result[...], in_ref[:, high])
        sig = jax.nn.sigmoid(gate_part)
        shared_act[:, c] = (gate_part * sig * lift).astype(BF16)
        da = dot_last(back[...], out_ref[c, :])
        shared_dab[:, c] = (da * lift * sig * (1.0 + gate_part * (1.0 - sig))).astype(BF16)
        shared_dab[:, high] = (da * gate_part * sig).astype(BF16)

    tiles(hidden, 256, shared_tile)
    to_back, to_sum = cot.at[0, 0, 0], cot.at[0, 0, 1]

    def back_part(c):
        to_back[:, c] = dot_last(shared_dab[theirs, :], in_ref[c, :]).astype(BF16)

    tiles(width, 512, back_part)
    swap_back = cross(0, to_back, from_back)
    swap_back.start()

    def weight_out(c):
        dout_ref[c, :] = dot_first(rows_act[:, c], rows_dy[...]).astype(BF16)

    tiles(hidden, 256, weight_out)
    dout_out = move(dout_ref, dout)
    scatter_step(0, 3)
    scatter_step(1, 1)

    def sum_part(c):
        to_sum[:, c] = dot(shared_act[theirs, :], out_ref[:, c]).astype(BF16)

    tiles(width, 512, sum_part)
    swap_sum = cross(1, to_sum, from_sum)
    swap_sum.start()
    din_out.wait()
    dout_out.wait()
    swap_down = cross(3, dout.at[:, pl.ds(pl.multiple_of((1 - h) * (width // 2), 128), width // 2)], other_down)
    swap_down.start()

    def shared_in(c):
        din_ref[c, :] = dot_first(result[:, c], shared_dab[...]).astype(BF16)

    tiles(width, 256, shared_in)
    up_out = move(din_ref, up_part)
    scatter_step(0, 4)
    scatter_step(1, 2)

    def shared_out(c):
        dout_ref[c, :] = dot_first(shared_act[:, c], back[...]).astype(BF16)

    tiles(hidden, 256, shared_out)
    down_out = move(dout_ref, down_part)
    swap_back.wait_recv()
    scatter_finish(0)

    lanes = home_ref[:, pl.ds(width, 128)].astype(BF16)
    row_id = lax.broadcasted_iota(jnp.int32, (128, 128), 0)
    col_id = lax.broadcasted_iota(jnp.int32, (128, 128), 1)
    fold = jnp.where((row_id == col_id) | (row_id == col_id + experts), 1.0, 0.0).astype(BF16)
    weighted = gates[...] * dot(lanes, fold)
    logit_grad = (weighted - gates[...] * jnp.sum(weighted, axis=1, keepdims=True)).astype(BF16)
    short = logit_grad[:, : turned.shape[0]]

    def norm_part(c):
        hidden_grad[:, c] = (
            home_ref[:, c] + from_back[:, c].astype(F32) + dot_last(shared_dab[ours, :], in_ref[c, :])
            + dot(short, turned[:, c].astype(BF16)))
        row_part[:, c] = dot_first(logit_grad, ext[blk, :, c])

    tiles(width, 512, norm_part)

    def norm_rows(n, total):
        part = pl.ds(n * 32, 32)
        x, up = resid[part, :], hidden_grad[part, :]
        scaler = lax.rsqrt(jnp.mean(x * x, axis=1, keepdims=True) + EPS)
        normed = x * scaler
        scaled = up * turned[pl.ds(experts + 1, 1), :]
        grad = cot_own[part, :].astype(F32) + scaler * (
            scaled - normed * jnp.mean(scaled * normed, axis=1, keepdims=True))
        hidden_grad[part, :] = grad
        hid[h, part, :] = grad.astype(BF16)
        return total + jnp.sum(up * normed, axis=0, keepdims=True)

    gain = jnp.zeros((1, width), F32)
    swap_hid = []
    for n in range(4):
        gain = norm_rows(n, gain)
        block = hid.at[h, pl.ds(n * 32, 32)]
        swap_hid.append(cross(4 + n, block, block))
        swap_hid[n].start()
    scatter_step(1, 3)
    row_part[pl.ds(experts + 1, 1), :] = gain
    load_out.wait()
    inner = low.shape[1]
    full = rows_x.at[pl.ds(0, inner)]

    def mixed_tile(who, where):
        for t in range(inner // 256):
            c = pl.ds(t * 256, 256)
            mixed_grad[where, c] = dot_last(hid[who], full[c, :]).astype(BF16)

    mixed_tile(h, ours)
    scatter_step(1, 4)
    for copy in swap_hid:
        copy.wait_recv()
    mixed_tile(1 - h, theirs)

    def out_tile(c):
        rows_dy[c, :] = (
            dot_first(low[pl.ds(0, rows), c], hid[0]) + dot_first(low[pl.ds(rows, rows), c], hid[1])).astype(BF16)

    for t in range(inner // 256):
        out_tile(pl.ds(t * 256, 256))
    part_out = move(rows_dy.at[pl.ds(0, inner)], out_part)
    swap_sum.wait_recv()
    scatter_finish(1)

    def output_tile(c):
        output[:, c] = (
            resid[:, c] + routed_ref[:, c] + from_sum[:, c].astype(F32)
            + dot(shared_act[ours, :], out_ref[:, c])).astype(BF16)

    tiles(width, 512, output_tile)
    for copy in (swap_back, swap_sum, swap_down, *swap_hid):
        copy.wait_send()
    swap_down.wait_recv()
    for copy in (up_out, down_out, part_out):
        copy.wait()
    for copy in sent:
        copy.wait_send()
    exchange_d(half, 0).wait_send()
    exchange_o(half, 0).wait_send()
    for k, part in ((0, upper), (1, lower)):
        over_right(part, k, 0).wait_send()
        for s in range(1, half + 1):
            if s <= half - k:
                hop_right(part, k, s).wait_send()
                over_right(part, k, s).wait_send()
            if s <= half - 1 + k:
                hop_left(part, k, s).wait_send()
                over_left(part, k, s).wait_send()


def experts_fused(
    ext, weights, cot_all, shared, cot_pair, cot_own, resid, gates, turned, low, full_out, blks, capacity, collective_id,
):
    chips, half = blks // 2, blks // 4
    rows, wide = ext.shape
    width, hidden = 2 * weights[0].shape[0], weights[2].shape[0]
    count = blks * capacity
    group = 4 * capacity
    inner = low.shape[1]
    dma = pltpu.SemaphoreType.DMA
    vmem = pl.BlockSpec(memory_space=pltpu.VMEM)
    anywhere = pl.BlockSpec(memory_space=pl.ANY)

    def bf16(*shape):
        return pltpu.VMEM(shape, BF16)

    def f32(*shape):
        return pltpu.VMEM(shape, F32)

    out = [
        ((rows, width), BF16, vmem), ((rows, width), F32, vmem), ((2 * rows, inner), BF16, vmem),
        ((inner, width), BF16, anywhere), ((width, 2 * hidden), BF16, anywhere), ((hidden, width), BF16, anywhere),
        ((width, 2 * hidden), BF16, anywhere), ((hidden, width), BF16, anywhere), ((128, width), F32, vmem),
        ((2, rows, width), BF16, anywhere), ((hidden, width // 2), BF16, anywhere),
    ]
    return pl.pallas_call(
        functools.partial(expert_kernel, chips, blks),
        out_shape=[jax.ShapeDtypeStruct(s, t) for s, t, _ in out],
        in_specs=[anywhere] * 9 + [vmem] * 5 + [anywhere],
        out_specs=[space for _, _, space in out],
        scratch_shapes=[
            f32(rows, wide), f32(rows, width), bf16(width, 2 * hidden), bf16(hidden, width),
            bf16(2 * rows, hidden), bf16(2 * rows, 2 * hidden), bf16(2, rows, width), bf16(rows, width), bf16(rows, width),
            bf16(width, 2 * hidden), bf16(hidden, width),
            bf16(blks, rows, wide), bf16(2, 2, 2, rows, width),
            bf16(count, width), bf16(count, width), bf16(count, hidden), bf16(count, 2 * hidden),
            f32(group, 2 * hidden), bf16(group, width), bf16(group, width),
            bf16(2, 2, rows, 128), f32(2, 2, rows, 128), bf16(2, 128, 2 * rows), bf16(2, 128, 2 * rows),
            bf16(chips, rows, wide), bf16(chips, rows, width), bf16(2, rows, wide), bf16(2, rows, width),
            bf16(chips, rows, wide), bf16(chips, rows, width),
            bf16(half, rows, wide), bf16(half, rows, width), bf16(half, rows, wide), bf16(half, rows, width),
            dma(()), dma((2, 2)),
        ] + [dma((2, half + 1))] * 8 + [dma((2, 2, half + 1))] * 2 + [dma((2, 2, half + 1))] * 4
        + [dma((4,)), dma((3,)), dma((11,)), dma((8,)), dma((8,))],
        compiler_params=pltpu.CompilerParams(
            collective_id=collective_id, has_side_effects=True, vmem_limit_bytes=63 << 20),
    )(ext, *weights, cot_all, *shared, cot_pair, cot_own, resid, gates, turned, low, full_out)


class Ring:
    def __init__(self, info, chips, chunks, first, sems):
        self.blk, self.at, self.sib = info
        self.half = chips // 2
        self.chunks, self.first = chunks, first
        self.send_r, self.recv_r, self.send_l, self.recv_l, self.send_s, self.recv_s = sems

    def hops(self, c):
        return self.half - c % 2, self.half - 1 + c % 2

    def copy(self, ref, ssem, rsem, dev):
        return pltpu.make_async_remote_copy(
            src_ref=ref, dst_ref=ref, send_sem=ssem, recv_sem=rsem,
            device_id={"blk": dev}, device_id_type=MESH)

    def right(self, c, s):
        i = self.first + c
        return self.copy(self.chunks[c](self.at(1 - s)), self.send_r.at[i, s], self.recv_r.at[i, s], self.at(1))

    def left(self, c, s):
        i = self.first + c
        return self.copy(self.chunks[c](self.at(s - 1)), self.send_l.at[i, s], self.recv_l.at[i, s], self.at(-1))

    def over(self, c, d):
        i, k = self.first + c, d + self.half
        return self.copy(self.chunks[c](self.at(d)), self.send_s.at[i, k], self.recv_s.at[i, k], self.sib)

    def start(self, c):
        self.right(c, 1).start()
        self.left(c, 1).start()
        self.over(c, 0).start()

    def step(self, s):
        for c in range(len(self.chunks)):
            rh, lh = self.hops(c)
            if s <= rh:
                self.right(c, s).wait_recv()
                if s < rh:
                    self.right(c, s + 1).start()
                self.over(c, -s).start()
            if s <= lh:
                self.left(c, s).wait_recv()
                if s < lh:
                    self.left(c, s + 1).start()
                self.over(c, s).start()

    def end(self):
        for c in range(len(self.chunks)):
            rh, lh = self.hops(c)
            for d in range(-rh, lh + 1):
                self.over(c, d).wait_recv()

    def flush(self):
        for c in range(len(self.chunks)):
            rh, lh = self.hops(c)
            for s in range(1, rh + 1):
                self.right(c, s).wait_send()
            for s in range(1, lh + 1):
                self.left(c, s).wait_send()
            for d in range(-rh, lh + 1):
                self.over(c, d).wait_send()


def front_kernel(
    chips, experts,
    order_ref, lengths_ref, routes, router, gain_one, gain_two, tokens, cotangent, w_query, w_key, w_value, w_out,
    shared_up, shared_down, expert_up, expert_down,
    n1_out, query_out, kv_out, first_out, out_out, up_w, down_w, cot, cot_pair, expert_in, expert_out,
    low_out, full_out, lse, resid, ext, gates, short, slots_ref,
    small, n1, query, kv, first_w, out_w, low, full, turned, pair, to_other, from_other,
    send_r, recv_r, send_l, recv_l, send_s, recv_s, own_sem, y_send, y_recv, store_sem,
):
    h = lax.axis_index("head")
    blk, core, at, sib = ring_info(chips)
    half = chips // 2
    rows, width = tokens.shape
    qw, kw = w_query.shape[1] // 2, w_key.shape[1] // 2
    sw = shared_up.shape[1] // 4
    barrier = pltpu.get_barrier_semaphore()
    for other in (at(1), at(-1), sib):
        pl.semaphore_signal(barrier, inc=1, device_id={"blk": other}, device_id_type=MESH)
    pl.semaphore_signal(barrier, inc=1, device_id={"head": 1 - h}, device_id_type=MESH)
    pl.semaphore_wait(barrier, 4)

    wide = lax.broadcasted_iota(jnp.int32, (experts, 128), 1)
    column = lax.broadcasted_iota(jnp.int32, (experts, 128), 0)
    block = dot_first(router[...], jnp.where(wide == column, 1.0, 0.0).astype(BF16))
    for n, gain in ((0, gain_one), (1, gain_two)):
        spot = jnp.where(lax.broadcasted_iota(jnp.int32, (1, 128), 1) == experts + n, 1.0, 0.0).astype(BF16)
        block = block + dot_first(gain[...], spot)
    small[...] = block.astype(BF16)

    def lanes_of(start, size):
        return pl.ds(pl.multiple_of(start, 128), size)

    def halves(i, j):
        return [
            (w_query.at[:, lanes_of(i * qw, qw)], first_w.at[j, blk, :, pl.ds(0, qw)]),
            (w_key.at[:, lanes_of(i * kw, kw)], first_w.at[j, blk, :, pl.ds(qw, kw)]),
            (w_value.at[:, lanes_of(i * kw, kw)], first_w.at[j, blk, :, pl.ds(qw + kw, kw)]),
            (small, first_w.at[j, blk, :, pl.ds(qw + 2 * kw, small.shape[1])]),
            (tokens, pair.at[j]),
            (shared_up.at[:, lanes_of(i * sw, sw)], up_w.at[j, blk, :, pl.ds(0, sw)]),
            (shared_up.at[:, lanes_of((2 + i) * sw, sw)], up_w.at[j, blk, :, pl.ds(sw, sw)]),
            (cotangent, cot_pair.at[j]),
        ]

    whole = [(expert_up, expert_in), (expert_down, expert_out)]

    stores = []

    def store(src, dst):
        copy = pltpu.make_async_copy(src, dst, store_sem.at[len(stores)])
        copy.start()
        stores.append(copy)

    own = [pltpu.make_async_copy(a, b, own_sem.at[i]) for i, (a, b) in enumerate(halves(h, h))]
    own.append(pltpu.make_async_copy(w_out, out_w.at[blk], own_sem.at[len(own)]))
    own.append(pltpu.make_async_copy(shared_down, down_w.at[blk], own_sem.at[len(own)]))
    own.append(pltpu.make_async_copy(cotangent, cot.at[blk], own_sem.at[len(own)]))
    swaps = [
        pltpu.make_async_remote_copy(
            src_ref=a, dst_ref=b, send_sem=y_send.at[i], recv_sem=y_recv.at[i],
            device_id={"head": 1 - h}, device_id_type=MESH)
        for i, (a, b) in enumerate(halves(1 - h, h) + whole)
    ]
    for i in range(5):
        swaps[i].start()
    for i in (0, 1, 2, 3, 8, 4):
        own[i].start()

    info = (blk, at, sib)
    sems = (send_r, recv_r, send_l, recv_l, send_s, recv_s)

    def row_cuts(ref, *sizes):
        start, chunks = 0, []
        for size in sizes:
            chunks.append(lambda b, start=start, size=size: ref.at[b, pl.ds(start, size)])
            start += size
        return chunks

    ring_w = Ring(info, chips, [lambda b: first_w.at[h, b], lambda b: first_w.at[1 - h, b]], 0, sems)
    out_rows, down_rows = w_out.shape[0], shared_down.shape[0]
    ring_o = Ring(info, chips, row_cuts(out_w, 32, out_rows - 32), 2, sems)
    ring_kv = Ring(info, chips, [lambda b: kv.at[2 * b], lambda b: kv.at[2 * b + 1]], 4, sems)
    ring_u = Ring(info, chips, [lambda b: up_w.at[h, b], lambda b: up_w.at[1 - h, b]], 6, sems)
    ring_d = Ring(info, chips, row_cuts(down_w, down_rows // 2, down_rows // 2), 8, sems)
    ring_c = Ring(info, chips, row_cuts(cot, rows // 2, rows // 2), 10, sems)

    for i in (0, 1, 2, 3):
        own[i].wait()
    ring_w.start(0)
    own[10].start()
    own[10].wait()
    ring_c.start(0)
    ring_c.start(1)
    own[8].wait()
    for i in range(4):
        swaps[i].wait_recv()
    ring_w.start(1)
    ring_o.start(0)
    ring_o.start(1)
    for i in (5, 6, 9, 7):
        own[i].start()
    for i in range(5, 10):
        swaps[i].start()
    for s in range(1, half + 1):
        ring_w.step(s)
        ring_o.step(s)
    ring_c.step(1)
    ring_w.end()
    store(first_w, first_out)
    own[4].wait()
    swaps[4].wait_recv()

    @pl.loop(0, slots_ref.shape[0])
    def _(j):
        slot = jnp.int32(0)
        for n in range(order_ref.shape[0]):
            there = 2 * (n % (2 * chips)) + n // (2 * chips)
            slot = jnp.maximum(slot, jnp.where(order_ref[n] == j, there, 0))
        slots_ref[j] = slot

    small_cols = first_w[:, :, :, pl.ds(qw + 2 * kw, 128)].reshape(width, 128)
    turned[...] = jnp.swapaxes(small_cols.astype(F32), 0, 1)
    short[...] = turned[pl.ds(0, short.shape[0]), :]

    @pl.loop(0, 2 * rows // 64)
    def _(i):
        x = pair[lax.div(i, rows // 64), pl.ds(pl.multiple_of(lax.rem(i, rows // 64) * 64, 64), 64), :].astype(F32)
        scaled = x * lax.rsqrt(jnp.mean(x * x, axis=1, keepdims=True) + EPS) * turned[pl.ds(experts, 1), :]
        n1[pl.ds(pl.multiple_of(i * 64, 64), 64), :] = scaled.astype(BF16)

    def project(start, size):
        weights = first_w[:, :, :, pl.ds(start, size)].reshape(width, size)
        return dot(n1[...], weights).astype(BF16)

    for t in range(2 * kw // 256):
        part = project(qw + t * 256, 256)
        for i in range(2):
            kv[2 * blk + i, :, pl.ds(t * 256, 256)] = part[i * rows : (i + 1) * rows]
    ring_kv.start(0)
    ring_kv.start(1)
    for t in range(qw // 256):
        query[:, pl.ds(t * 256, 256)] = project(t * 256, 256)
    for i in (5, 6, 9):
        own[i].wait()
    swaps[5].wait_recv()
    swaps[6].wait_recv()
    for s in range(1, half + 1):
        ring_kv.step(s)
        if s == half - 1:
            ring_c.step(2)
            for ring in (ring_u, ring_d):
                ring.start(0)
                ring.start(1)
    ring_kv.end()
    store(kv, kv_out)
    store(n1, n1_out)
    store(query, query_out)

    groups, repeats = kw // HD, qw // kw
    cols = repeats * PIECE
    pieces = slots_ref.shape[0]
    need = pieces // 2 + 1
    chunk = 6
    chunks = -(-need // chunk)
    later = [(ring_u, 1), (ring_d, 1), (ring_c, 3), (ring_u, 2), (ring_d, 2), (ring_c, 4)]
    turns = 0
    for i in range(2):
        place = order_ref[i * 2 * chips + blk]
        for g in range(groups):
            q = jnp.concatenate(
                [query[pl.ds(i * PIECE, PIECE), pl.ds((g * repeats + r) * HD, HD)] for r in range(repeats)], axis=0)

            def step(n, carry, place=place, g=g, q=q):
                top, total, acc = carry
                first = place + 1 - chunks * chunk + n * chunk
                _, (k, v) = key_chunk(
                    slots_ref, first, chunk, kv.at[:, :, pl.ds(g * HD, HD)], kv.at[:, :, pl.ds((groups + g) * HD, HD)])
                scores = dot_last(k, q) * HD**-0.5
                scores = jnp.where(seen(lengths_ref, place, first, chunk * PIECE, cols), scores, NEG)
                new = jnp.maximum(top, jnp.max(scores, axis=0, keepdims=True))
                weights = jnp.exp(scores - new)
                factor = jnp.exp(top - new)
                total = total * factor + jnp.sum(weights, axis=0, keepdims=True)
                return new, total, acc * factor + dot_first(v, weights.astype(BF16))

            top, total, acc = lax.fori_loop(
                0, chunks, step,
                (jnp.full((1, cols), NEG, F32), jnp.zeros((1, cols), F32), jnp.zeros((HD, cols), F32)))
            out = jnp.swapaxes(acc / total, 0, 1)
            lse[g, pl.ds(i, 1), :] = top + jnp.log(total)
            for r in range(repeats):
                part = out[r * PIECE : (r + 1) * PIECE]
                full[pl.ds(i * PIECE, PIECE), pl.ds((g * repeats + r) * HD, HD)] = part
                low[pl.ds(i * PIECE, PIECE), pl.ds((g * repeats + r) * HD, HD)] = part.astype(BF16)
            turns += 1
            if turns % 2 == 0:
                for ring, s in later[:3]:
                    ring.step(s)
                later = later[3:]

    ring_o.end()
    store(out_w, out_out)
    store(low, low_out)
    store(full, full_out)
    theirs = pl.ds(pl.multiple_of((1 - h) * rows, rows), rows)
    ours = pl.ds(pl.multiple_of(h * rows, rows), rows)

    def mixed(where, c):
        return dot(low[where, :], out_w[:, :, c].reshape(qw, c.size))

    for t in range(width // 512):
        c = pl.ds(t * 512, 512)
        to_other[:, c] = mixed(theirs, c).astype(BF16)
    swap_mixed = pltpu.make_async_remote_copy(
        src_ref=to_other, dst_ref=from_other, send_sem=y_send.at[10], recv_sem=y_recv.at[10],
        device_id={"head": 1 - h}, device_id_type=MESH)
    swap_mixed.start()
    for t in range(width // 512):
        c = pl.ds(t * 512, 512)
        resid[:, c] = pair[h, :, c].astype(F32) + mixed(ours, c)
    for ring in (ring_u, ring_d):
        ring.step(3)
    swap_mixed.wait_recv()

    @pl.loop(0, rows // 32)
    def _(i):
        part = pl.ds(pl.multiple_of(i * 32, 32), 32)
        x = resid[part, :] + from_other[part, :].astype(F32)
        resid[part, :] = x
        scaled = x * lax.rsqrt(jnp.mean(x * x, axis=1, keepdims=True) + EPS) * turned[pl.ds(experts + 1, 1), :]
        ext[part, pl.ds(0, width)] = scaled.astype(BF16)

    logits = dot_last(ext[:, pl.ds(0, width)], turned[...].astype(BF16))
    lane = lax.broadcasted_iota(jnp.int32, (128, rows), 0)
    masks = jnp.zeros((128, rows), F32)
    for r in range(routes.shape[0]):
        named = routes[r : r + 1, :]
        masks = jnp.where((lane == named) | (lane == named + experts), 1.0, masks)
    masks = jnp.swapaxes(masks, 0, 1)
    low_lane = lax.broadcasted_iota(jnp.int32, (rows, 128), 1) < experts
    mask = jnp.where(low_lane, masks, 0.0)
    shifted_mask = jnp.where(low_lane, 0.0, masks)
    masked = jnp.where(mask > 0.5, logits, NEG)
    raised = jnp.where(mask > 0.5, jnp.exp(masked - jnp.max(masked, axis=1, keepdims=True)), 0.0)
    probs = raised / jnp.sum(raised, axis=1, keepdims=True)
    gates[...] = probs
    ext[:, pl.ds(width, 128)] = (probs + shifted_mask).astype(BF16)
    for ring in (ring_u, ring_d):
        ring.step(4)
    own[7].wait()
    for i in (7, 8, 9):
        swaps[i].wait_recv()
    for ring in (ring_u, ring_d, ring_c):
        ring.end()
    for ring in (ring_w, ring_o, ring_kv, ring_u, ring_d, ring_c):
        ring.flush()
    for copy in swaps:
        copy.wait_send()
    swap_mixed.wait_send()
    for copy in stores:
        copy.wait()


def front_fused(
    tokens, cotangent, piece_order, seq_lengths, routes, w_query, w_key, w_value, w_router, gain_one, gain_two, w_out,
    shared_up, shared_down, expert_up, expert_down, blks, collective_id,
):
    chips, half = blks // 2, blks // 4
    rows, width = tokens.shape
    dense = w_query.shape[0]
    qw, kw, sw = w_query.shape[1] // 2, w_key.shape[1] // 2, shared_up.shape[1] // 4
    groups, repeats = kw // HD, qw // kw
    dma = pltpu.SemaphoreType.DMA
    vmem = pl.BlockSpec(memory_space=pltpu.VMEM)
    anywhere = pl.BlockSpec(memory_space=pl.ANY)
    smem = pl.BlockSpec(memory_space=pltpu.SMEM)
    out = [
        ((2 * rows, width), BF16, anywhere), ((2 * rows, qw), BF16, anywhere), ((2 * blks, rows, 2 * kw), BF16, anywhere),
        ((2, blks, dense, qw + 2 * kw + 128), BF16, anywhere), ((blks, w_out.shape[0], width), BF16, anywhere),
        ((2, blks, dense, 2 * sw), BF16, anywhere), ((blks, shared_down.shape[0], width), BF16, anywhere),
        ((blks, rows, width), BF16, anywhere), ((2, rows, width), BF16, anywhere),
        (expert_up.shape, BF16, anywhere), (expert_down.shape, BF16, anywhere),
        ((2 * rows, qw), BF16, anywhere), ((2 * rows, qw), F32, anywhere), ((groups, 2, repeats * PIECE), F32, vmem),
        ((rows, width), F32, vmem), ((rows, width + 128), BF16, vmem), ((rows, 128), F32, vmem), ((blks + 8, width), F32, vmem),
        ((2 * blks,), jnp.int32, smem),
    ]
    ring = [dma((12, half + 1))] * 4 + [dma((12, 2 * half + 1))] * 2
    (
        n1, query, kv, first_w, out_w, up_w, down_w, cot, cot_pair, expert_in, expert_out,
        low, full, lse, resid, ext, gates, turned, slots,
    ) = pl.pallas_call(
        functools.partial(front_kernel, chips, blks),
        out_shape=[jax.ShapeDtypeStruct(s, t) for s, t, _ in out],
        in_specs=[smem] * 2 + [vmem] * 4 + [anywhere, vmem] + [anywhere] * 4 + [vmem] * 2 + [anywhere] * 2,
        out_specs=[space for _, _, space in out],
        scratch_shapes=[pltpu.VMEM((dense, 128), BF16)] + [pltpu.VMEM(out[i][0], out[i][1]) for i in (0, 1, 2, 3, 4, 11, 12)] + [
            pltpu.VMEM((128, width), F32), pltpu.VMEM((2, rows, width), BF16), pltpu.VMEM((rows, width), BF16), pltpu.VMEM((rows, width), BF16)]
        + ring + [dma((11,)), dma((11,)), dma((11,)), dma((7,))],
        compiler_params=pltpu.CompilerParams(
            collective_id=collective_id, has_side_effects=True, vmem_limit_bytes=56 << 20),
    )(
        piece_order, seq_lengths, routes.T, w_router.T, gain_one[None], gain_two[None], tokens, cotangent,
        w_query, w_key, w_value, w_out, shared_up, shared_down, expert_up, expert_down)
    return (
        n1, query, kv, first_w.reshape(width, -1)[:, : qw + 2 * kw], out_w.reshape(-1, width),
        up_w.reshape(width, -1), down_w.reshape(-1, width), cot, cot_pair.reshape(2 * rows, width),
        expert_in, expert_out, low, full, lse, resid, ext, gates,
        None, None, None, (first_w, turned, slots))


class Scatter:
    def __init__(self, info, chips, chunks, first, sems):
        self.core, self.at, self.sib = info
        self.half = chips // 2
        self.chunks, self.first = chunks, first
        self.ex_s, self.ex_r, self.right_s, self.right_r, self.left_s, self.left_r = sems
        self.there, self.sent = set(), []

    def remote(self, src, dst, ssem, rsem, dev):
        return pltpu.make_async_remote_copy(
            src_ref=src, dst_ref=dst, send_sem=ssem, recv_sem=rsem,
            device_id={"blk": dev}, device_id_type=MESH)

    def over(self, c, d):
        own, other = self.chunks[c][:2]
        i, k = self.first + c, d + self.half
        place = self.at(d)
        return self.remote(
            own(place + 1 - 2 * self.core), other.at[lax.div(place, 2)], self.ex_s.at[i, k], self.ex_r.at[i, k], self.sib)

    def exchange(self):
        for d in sorted(range(1 - self.half, self.half + 1), key=lambda d: (-abs(d), -d)):
            for c in range(len(self.chunks)):
                copy = self.over(c, d)
                copy.start()
                self.sent.append(copy)

    def join(self, c, d, into, received):
        own, other = self.chunks[c][:2]
        if (c, d) not in self.there:
            self.there.add((c, d))
            self.over(c, d).wait_recv()
        place = self.at(d)
        mine, theirs = own(place), other.at[lax.div(place, 2)]
        rows = mine.shape[0]

        @pl.loop(0, rows // 16)
        def _(i):
            w = pl.ds(pl.multiple_of(i * 16, 16), 16)
            total = mine[w].astype(F32) + theirs[w].astype(F32)
            for ref in received:
                total = total + ref[w].astype(F32)
            into[w] = total.astype(into.dtype)

    def hop(self, c, way, src, s):
        i = self.first + c
        if way > 0:
            return self.remote(
                src, self.chunks[c][2].at[s - 1], self.right_s.at[i, s], self.right_r.at[i, s], self.at(1))
        return self.remote(
            src, self.chunks[c][3].at[s - 1], self.left_s.at[i, s], self.left_r.at[i, s], self.at(-1))

    def hops(self, c, way):
        return self.half - c % 2 if way > 0 else self.half - 1 + c % 2

    def step(self, s):
        for c, (own, _, right, left) in enumerate(self.chunks):
            for way in (1, -1):
                hops = self.hops(c, way)
                if s > hops:
                    continue
                d = way * (hops - s + 1)
                d = self.half if d == -self.half else d
                if s == 1:
                    src = self.chunks[c][1].at[lax.div(self.at(d), 2)]
                    self.join(c, d, src, ())
                else:
                    src = (right if way > 0 else left).at[s - 2]
                    self.hop(c, way, src, s - 1).wait_recv()
                    self.join(c, d, src, (src,))
                copy = self.hop(c, way, src, s)
                copy.start()
                self.sent.append(copy)

    def finish(self, outs):
        for c, (own, _, right, left) in enumerate(self.chunks):
            lasts = []
            for way, buf in ((1, right), (-1, left)):
                hops = self.hops(c, way)
                self.hop(c, way, own(self.at(0)), hops).wait_recv()
                lasts.append(buf.at[hops - 1])
            self.join(c, 0, outs[c], lasts)

    def flush(self):
        for copy in self.sent:
            copy.wait_send()


def tail_kernel(
    chips, experts,
    *refs,
):
    count = 14
    ins, (din,) = refs[:12], refs[12:13]
    input_grad, query_grad, key_grad, value_grad, out_grad, up_grad, down_grad, small_grad, other_up = refs[13:22]
    held = refs[22:34]
    dk, dv, dq, n1, first_w, tokens, hidden_grad, turned, out_part, up_part, down_part, row_part = held
    (
        kv_sum, qkv_part, qkv_sum, up_sum, small_part, small_sum, to_other, from_other, qkv_from, up_from, small_from,
    ) = refs[34:45]
    rest = refs[45:]
    h = lax.axis_index("head")
    blk, core, at, sib = ring_info(chips)
    half = chips // 2
    rows, width = tokens.shape
    qw, kw = dq.shape[1], dk.shape[2]
    top = qw + 2 * kw
    dense = first_w.shape[2]
    sw = up_part.shape[3] // 2
    others, rights, lefts = rest[:count], rest[count : 2 * count], rest[2 * count : 3 * count]
    sems, (y_send, y_recv, load_sem) = rest[3 * count : 3 * count + 6], rest[3 * count + 6 :]
    loads = [pltpu.make_async_copy(a, b, load_sem.at[i]) for i, (a, b) in enumerate(zip(ins, held))]
    for i in (0, 1, 9, 8, 10, 2, 4, 3, 5, 6, 7, 11):
        loads[i].start()
    barrier = pltpu.get_barrier_semaphore()
    for other in (at(1), at(-1), sib):
        pl.semaphore_signal(barrier, inc=1, device_id={"blk": other}, device_id_type=MESH)
    pl.semaphore_signal(barrier, inc=1, device_id={"head": 1 - h}, device_id_type=MESH)
    pl.semaphore_wait(barrier, 4)

    def cross(i, src, dst):
        return pltpu.make_async_remote_copy(
            src_ref=src, dst_ref=dst, send_sem=y_send.at[i], recv_sem=y_recv.at[i],
            device_id={"head": 1 - h}, device_id_type=MESH)

    info = (core, at, sib)

    def scatter(first, owns):
        chunks = [(own, others[first + i], rights[first + i], lefts[first + i]) for i, own in enumerate(owns)]
        return Scatter(info, chips, chunks, first, sems)

    def pieces_at(ref, i):
        return lambda b: ref.at[2 * b + i]

    def source_at(ref, i):
        return lambda b: ref.at[i, b]

    def rows_at(ref, start, size):
        return lambda b: ref.at[b, pl.ds(start, size)]

    out_rows, down_rows = out_part.shape[1], down_part.shape[1]
    kv_ring = scatter(0, [pieces_at(dk, 0), pieces_at(dk, 1), pieces_at(dv, 0), pieces_at(dv, 1)])
    rest_ring = scatter(4, [
        source_at(up_part, 0), source_at(up_part, 1), rows_at(out_part, 0, 32), rows_at(out_part, 32, out_rows - 32),
        rows_at(down_part, 0, down_rows // 2), rows_at(down_part, down_rows // 2, down_rows // 2)])
    qkv_ring = scatter(10, [source_at(qkv_part, 0), source_at(qkv_part, 1)])
    small_ring = scatter(12, [source_at(small_part, 0), source_at(small_part, 1)])

    loads[0].wait()
    loads[1].wait()
    kv_ring.exchange()
    size = width // 2
    swap_up = cross(0, din.at[pl.ds(pl.multiple_of((1 - h) * size, 128), size)], other_up)
    swap_up.start()
    for i in (8, 9, 10):
        loads[i].wait()
    rest_ring.exchange()
    for s in range(1, half + 1):
        kv_ring.step(s)
        if s % 2 == 0:
            rest_ring.step(s // 2)
    kv_ring.finish([kv_sum.at[i, pl.ds(j * rows, rows)] for i in range(2) for j in range(2)])

    for i in (2, 3, 4, 5, 6, 7, 11):
        loads[i].wait()
    theirs = pl.ds(pl.multiple_of((1 - h) * rows, rows), rows)
    ours = pl.ds(pl.multiple_of(h * rows, rows), rows)
    step = 8 * dense

    def norm_grad(where, i, t):
        def part(a, first, n):
            return dot_last(a, first_w[i, pl.ds(t * 8, 8), :, pl.ds(first, n)].reshape(step, n))

        return part(dq[where, :], 0, qw) + part(kv_sum[0, where, :], qw, kw) + part(kv_sum[1, where, :], qw + kw, kw)

    spans = [(i, t, pl.ds(i * (width // 2) + t * step, step)) for i in range(2) for t in range(width // (2 * step))]
    for i, t, c in spans:
        to_other[:, c] = norm_grad(theirs, i, t).astype(BF16)
    swap_norm = cross(1, to_other, from_other)
    swap_norm.start()
    for i, t, c in spans:
        lhs = n1[:, c]
        for first, n, rhs in ((0, qw, dq[...]), (qw, kw, kv_sum[0]), (qw + kw, kw, kv_sum[1])):
            part = dot_first(lhs, rhs).astype(BF16)
            qkv_part[i, pl.ds(t * 8, 8), :, pl.ds(first, n)] = part.reshape(8, dense, n)
    qkv_ring.exchange()
    rest_ring.step(3)
    qkv_ring.step(1)
    for i, t, c in spans:
        input_grad[:, c] = norm_grad(ours, i, t)
    swap_norm.wait_recv()
    rest_ring.step(4)
    qkv_ring.step(2)

    def norm_rows(n, total):
        part = pl.ds(pl.multiple_of(n * 32, 32), 32)
        x = tokens[part, :].astype(F32)
        up = input_grad[part, :] + from_other[part, :].astype(F32)
        scaler = lax.rsqrt(jnp.mean(x * x, axis=1, keepdims=True) + EPS)
        normed = x * scaler
        scaled = up * turned[pl.ds(experts, 1), :]
        back = scaler * (scaled - normed * jnp.mean(scaled * normed, axis=1, keepdims=True))
        input_grad[part, :] = hidden_grad[part, :] + back
        return total + jnp.sum(up * normed, axis=0, keepdims=True)

    gain = lax.fori_loop(0, rows // 32, norm_rows, jnp.zeros((1, width), F32))
    ids = lax.broadcasted_iota(jnp.int32, (128, 1), 0)
    turned_part = jnp.swapaxes(row_part[...] + jnp.where(ids == experts, gain, 0.0), 0, 1)
    small_part[...] = turned_part.astype(BF16).reshape(small_part.shape)
    small_ring.exchange()
    small_ring.step(1)
    qkv_ring.step(3)
    small_ring.step(2)
    up_views = [up_sum.at[0], up_sum.at[1]]
    rest_ring.finish(up_views + [
        out_grad.at[pl.ds(0, 32)], out_grad.at[pl.ds(32, out_rows - 32)],
        down_grad.at[pl.ds(0, down_rows // 2)], down_grad.at[pl.ds(down_rows // 2, down_rows // 2)]])
    swap_sum = cross(2, up_sum.at[1 - h], up_from)
    swap_sum.start()
    qkv_ring.step(4)
    small_ring.step(3)
    qkv_ring.finish([qkv_sum.at[0], qkv_sum.at[1]])
    swap_qkv = cross(3, qkv_sum.at[1 - h], qkv_from)
    swap_qkv.start()
    small_ring.step(4)
    small_ring.finish([small_sum.at[0], small_sum.at[1]])
    swap_small = cross(4, small_sum.at[1 - h], small_from)
    swap_small.start()

    def place(ref, source, first, n, base=0):
        for who, part in ((h, source[0]), (1 - h, source[1])):
            ref[:, pl.ds(pl.multiple_of(base + who * n, 128), n)] = part[:, pl.ds(first, n)].astype(F32)

    swap_sum.wait_recv()
    ups = (up_sum.at[h], up_from)
    place(up_grad, ups, 0, sw)
    place(up_grad, ups, sw, sw, 2 * sw)
    swap_qkv.wait_recv()
    sums = (qkv_sum.at[h], qkv_from)
    place(query_grad, sums, 0, qw)
    place(key_grad, sums, qw, kw)
    place(value_grad, sums, qw + kw, kw)
    swap_small.wait_recv()
    small_grad[...] = small_sum[h] + small_from[...]
    for ring in (kv_ring, rest_ring, qkv_ring, small_ring):
        ring.flush()
    for copy in (swap_norm, swap_up, swap_sum, swap_qkv, swap_small):
        copy.wait_send()
    swap_up.wait_recv()


def tail_fused(
    dk, dv, dq, n1, first_w, tokens, hidden_grad, turned, out_part, up_part, down_part, row_part, din,
    blks, collective_id,
):
    chips, half = blks // 2, blks // 4
    rows, width = tokens.shape
    qw, kw = dq.shape[1], dk.shape[2]
    top = qw + 2 * kw
    dense = first_w.shape[2]
    out_rows, down_rows, up_wide = out_part.shape[1], down_part.shape[1], up_part.shape[3]
    dma = pltpu.SemaphoreType.DMA
    vmem = pl.BlockSpec(memory_space=pltpu.VMEM)
    anywhere = pl.BlockSpec(memory_space=pl.ANY)
    shapes = [(rows, kw)] * 4 + [(dense, up_wide)] * 2 + [(32, width), (out_rows - 32, width)]
    shapes += [(down_rows // 2, width)] * 2 + [(dense, top)] * 2 + [(dense, 128)] * 2
    others = [pltpu.VMEM((chips,) + s, BF16) for s in shapes]
    slots = [pltpu.VMEM((half,) + s, BF16) for s in shapes]
    n = len(shapes)
    held = (dk, dv, dq, n1, first_w, tokens, hidden_grad, turned, out_part, up_part, down_part, row_part)

    def f32(*shape):
        return jax.ShapeDtypeStruct(shape, F32)

    def low(*shape):
        return pltpu.VMEM(shape, BF16)

    return pl.pallas_call(
        functools.partial(tail_kernel, chips, blks),
        out_shape=[
            f32(rows, width), f32(dense, 2 * qw), f32(dense, 2 * kw), f32(dense, 2 * kw), f32(out_rows, width),
            f32(dense, 2 * up_wide), f32(down_rows, width), f32(dense, 128),
            jax.ShapeDtypeStruct((din.shape[0] // 2, din.shape[1]), BF16),
        ],
        in_specs=[anywhere] * 13,
        out_specs=[vmem] * 8 + [anywhere],
        scratch_shapes=[pltpu.VMEM(a.shape, a.dtype) for a in held] + [
            low(2, 2 * rows, kw), low(2, blks, dense, top), low(2, dense, top), low(2, dense, up_wide),
            low(2, blks, dense, 128), pltpu.VMEM((2, dense, 128), F32), low(rows, width), low(rows, width),
            low(dense, top), low(dense, up_wide), pltpu.VMEM((dense, 128), F32),
        ] + others + slots + slots + [dma((n, 2 * half + 1))] * 2 + [dma((n, half + 1))] * 4 + [dma((5,)), dma((5,)), dma((12,))],
        compiler_params=pltpu.CompilerParams(
            collective_id=collective_id, has_side_effects=True, vmem_limit_bytes=62 << 20),
    )(*held, din)


def experts_plain(own_ext, weights, cot_all, blks, capacity, collective_id):
    h, b = lax.axis_index("head"), lax.axis_index("blk")
    own_up, other_up, own_down, other_down = weights
    expert_in = pair(own_up, other_up).reshape(2 * own_up.shape[0], -1)
    expert_out = jnp.where(
        h == 0,
        jnp.concatenate([own_down, other_down], axis=1),
        jnp.concatenate([other_down, own_down], axis=1),
    )
    normed = own_ext[:, : expert_in.shape[0]]
    normed_pair = pair(normed, swap(normed))
    experts, width = blks, expert_in.shape[0]
    rows = own_ext.shape[0]
    ext = all_gather_blk([own_ext], blks, collective_id)[0]
    norm_all = ext[:, :, :width]
    gate_here = lax.dynamic_index_in_dim(ext, width + b, 2, keepdims=False).astype(F32)
    mask_here = lax.dynamic_index_in_dim(ext, width + experts + b, 2, keepdims=False).astype(F32)
    rank = jnp.cumsum(mask_here, axis=1) - mask_here
    slots = jnp.arange(capacity, dtype=F32)
    deal = ((rank[:, None, :] == slots[None, :, None]) & (mask_here[:, None, :] > 0)).astype(BF16)
    deal_gate = deal * gate_here[:, None, :].astype(BF16)

    def to_slots(dealer, array):
        moved = jnp.einsum("bst,btd->bsd", dealer, array, preferred_element_type=F32)
        return moved.astype(BF16).reshape(blks * capacity, width)

    def to_rows(dealer, array):
        return jnp.einsum(
            "bst,bsd->btd", dealer, array.reshape(blks, capacity, width), preferred_element_type=F32)

    expert_rows = to_slots(deal, norm_all)
    both = dot(expert_rows, expert_in)
    ew = expert_out.shape[0]
    gate_part, up_part = both[:, :ew], both[:, ew:]
    activated = (jax.nn.silu(gate_part) * up_part).astype(BF16)
    result = dot(activated, expert_out).astype(BF16)
    result_rows = to_rows(deal, result)
    gate_grad = jnp.sum(result_rows * cot_all.astype(F32), axis=2, keepdims=True)
    routed = (result_rows * gate_here[:, :, None]).astype(BF16)
    slot_grad = to_slots(deal_gate, cot_all)
    act_grad = dot_last(slot_grad, expert_out)
    both_grad = gated_grad(act_grad, gate_part, up_part)
    rows_back = to_rows(deal, dot_last(both_grad, expert_in).astype(BF16)).astype(BF16)
    lane = jnp.arange(128 * (-(-2 * experts // 128)), dtype=jnp.int32)
    grad_high = gate_grad.astype(BF16)
    grad_low = (gate_grad - grad_high.astype(F32)).astype(BF16)
    grad_lanes = jnp.where(lane == b, grad_high, jnp.where(lane == b + experts, grad_low, jnp.zeros((), BF16)))
    dwn = dot_first(activated, slot_grad).astype(BF16)
    dup = dot_first(expert_rows, both_grad).astype(BF16)
    home = reduce_scatter_blk([jnp.concatenate([rows_back, grad_lanes], axis=2)], blks, collective_id + 1, [F32])[0]
    routed_sum = reduce_scatter_blk([routed], blks, collective_id + 2, [F32])[0]
    return home, routed_sum, dup, dwn, normed_pair


def pair(own, other):
    return jnp.where(lax.axis_index("head") == 0, jnp.stack([own, other]), jnp.stack([other, own]))


def half(w, i, parts=1):
    size = w.shape[1] // (2 * parts)
    cut = lax.dynamic_slice_in_dim(w.reshape(w.shape[0], parts, 2 * size), i * size, size, 2)
    return cut.reshape(w.shape[0], parts * size)


def pick(stacked, i):
    return lax.dynamic_index_in_dim(stacked, i, 0, keepdims=False)


def front_plain(
    tokens, cotangent, where, mask, w_query, w_key, w_value, small, w_out, shared_up, shared_down,
    expert_up, expert_down, blks, collective_id,
):
    h = lax.axis_index("head")
    rows, width = tokens.shape
    experts = blks

    def columns(i):
        return jnp.concatenate([half(w_query, i), half(w_key, i), half(w_value, i)], axis=1)

    first = pair(
        jnp.concatenate([columns(h), small], axis=1),
        swap(jnp.concatenate([columns(1 - h), small], axis=1)),
    )
    tokens_pair = pair(tokens, swap(tokens))
    cotangent_pair = pair(cotangent, swap(cotangent)).reshape(2 * rows, width)
    up_pair = pair(half(shared_up, h, 2), swap(half(shared_up, 1 - h, 2)))
    other_up, other_down = swap(expert_up), swap(expert_down)
    gathered = all_gather_blk([first], blks, collective_id)[0].reshape(width, -1)
    qw = w_query.shape[1] // 2
    kw = w_key.shape[1] // 2
    full_qkv = gathered[:, : qw + 2 * kw]
    full_router = gathered[:, qw + 2 * kw : qw + 2 * kw + experts]
    gain_first = gathered[:, qw + 2 * kw + experts].astype(F32)
    gain_second = gathered[:, qw + 2 * kw + experts + 1].astype(F32)

    inputs_pair = tokens_pair.reshape(2 * rows, width).astype(F32)
    normed_one = (inputs_pair * inv_scale(inputs_pair) * gain_first).astype(BF16)
    qkv = dot(normed_one, full_qkv).astype(BF16)
    query = qkv[:, :qw]
    kv = all_gather_blk([qkv[:, qw:]], blks, collective_id + 1)[0].reshape(-1, PIECE, 2 * kw)

    attended, attended_full, lse = attention_forward(query, kv, where)

    up_all, out_all, down_all, cot_all = all_gather_blk([up_pair, w_out, shared_down, cotangent], blks, collective_id + 2)
    full_up = up_all.reshape(width, -1)
    full_out = out_all.reshape(-1, width)
    full_down = down_all.reshape(-1, width)

    mixed = dot(attended, full_out).reshape(2, rows, width)
    inputs = tokens.astype(F32)
    resid = inputs + (pick(mixed, h) + swap(pick(mixed, 1 - h).astype(BF16)).astype(F32))
    scaler_two = inv_scale(resid)
    normed_two = (resid * scaler_two * gain_second).astype(BF16)

    logits = dot(normed_two, full_router)
    masked = jnp.where(mask, logits, NEG)
    raised = jnp.where(mask, jnp.exp(masked - jnp.max(masked, axis=1, keepdims=True)), 0.0)
    gates = raised / jnp.sum(raised, axis=1, keepdims=True)
    extra = jnp.concatenate(
        [gates.astype(BF16), mask.astype(BF16), jnp.zeros((rows, -2 * experts % 128), BF16)], axis=1)
    ext = jnp.concatenate([normed_two, extra], axis=1)
    return (
        normed_one, query, kv, full_qkv, full_out, full_up, full_down, cot_all, cotangent_pair, other_up, other_down,
        attended, attended_full, lse, resid, ext, gates, full_router.T, gain_first, gain_second, None)


def finish_kernel(experts, count, h_ref, up_own, up_other, down_own, down_other, small, *refs):
    up_out, down_out, router_out, one_out, two_out = refs[count : count + 5]
    up_out[...] = up_own[...].astype(F32) + up_other[...].astype(F32)
    down_out[...] = down_own[...].astype(F32) + down_other[...].astype(F32)

    @pl.when(pl.program_id(0) == 0)
    def _():
        for source, target in zip(refs[:count], refs[count + 5 :]):
            target[...] = source[...]
        turned = jnp.swapaxes(small[...], 0, 1)
        router_out[...] = turned[:experts]
        one_out[...] = turned[experts : experts + 1]
        two_out[...] = turned[experts + 1 : experts + 2]


def finish_fused(h, dup, add_up, dwn, add_down, small, experts, others):
    steps = 4
    up_rows, down_rows = add_up.shape[0] // steps, add_down.shape[0] // steps
    up = pl.BlockSpec((up_rows, add_up.shape[1]), lambda i, *_: (i, 0))
    down = pl.BlockSpec((down_rows, add_down.shape[1]), lambda i, *_: (i, 0))
    dense = small.shape[0]
    made = [(add_up.shape, F32), (add_down.shape, F32), ((experts, dense), F32), ((1, dense), F32), ((1, dense), F32)]

    def still(shape):
        return pl.BlockSpec(shape, lambda i, *_: (0, 0))

    rest = [still(a.shape) for a in others]
    return pl.pallas_call(
        functools.partial(finish_kernel, experts, len(others)),
        grid_spec=pltpu.PrefetchScalarGridSpec(
            num_scalar_prefetch=1,
            grid=(steps,),
            in_specs=[
                pl.BlockSpec((up_rows, add_up.shape[1]), lambda i, h: (h[0] * steps + i, 0)), up,
                pl.BlockSpec((down_rows, add_down.shape[1]), lambda i, h: (i, h[0])), down,
                still(small.shape),
            ] + rest,
            out_specs=[up, down] + [still(s) for s, _ in made[2:]] + rest,
        ),
        out_shape=[jax.ShapeDtypeStruct(s, t) for s, t in made + [(a.shape, a.dtype) for a in others]],
        compiler_params=pltpu.CompilerParams(vmem_limit_bytes=63 << 20),
    )(h.reshape(1), dup, add_up, dwn, add_down, small, *others)


def shards(
    tokens, cotangent, seq_lengths, piece_order, routes, norm1_gain, w_query, w_key, w_value, w_out,
    norm2_gain, w_router, shared_up, shared_down, expert_up, expert_down,
):
    blks = lax.axis_size("blk")
    h, b = lax.axis_index("head"), lax.axis_index("blk")
    rows, width = tokens.shape
    experts = blks
    capacity = rows * TOP * 4 // (3 * blks)
    dense_rows = w_query.shape[0]

    fits = blks == 16 and rows == 128 and 2 * capacity == 128 and width % 768 == 0 and dense_rows == 48
    if fits:
        got = front_fused(
            tokens, cotangent, piece_order, seq_lengths, routes, w_query, w_key, w_value, w_router, norm1_gain,
            norm2_gain, w_out, shared_up, shared_down, expert_up[0], expert_down[0], blks, 0)
        slots = got[-1][2]
    else:
        small = jnp.concatenate(
            [w_router, norm1_gain[:, None], norm2_gain[:, None],
             jnp.zeros((dense_rows, -(experts + 2) % 128), BF16)], axis=1)
        lanes = small.shape[1]
        places = jnp.swapaxes(piece_order.reshape(2, blks), 0, 1).reshape(-1)
        order = jnp.arange(2 * blks, dtype=jnp.int32)
        slots = jnp.sum(jnp.where(places[None, :] == order[:, None], order[None, :], 0), axis=1)
    own_places = lax.dynamic_slice_in_dim(piece_order.reshape(2, blks), b, 1, 1).reshape(2)
    where = (slots, own_places, seq_lengths)
    if not fits:
        hot = routes[:, :, None] == jnp.arange(experts, dtype=jnp.int32)[None, None, :]
        mask = jnp.any(hot, axis=1)
        got = front_plain(
            tokens, cotangent, where, mask, w_query, w_key, w_value, small, w_out, shared_up, shared_down,
            expert_up[0], expert_down[0], blks, 0)
    (
        normed_one, query, kv, full_qkv, full_out, full_up, full_down, cot_all, cotangent_pair, other_up, other_down,
        attended, attended_full, lse, resid, ext, gates, router_rows, gain_first, gain_second, kept,
    ) = got
    qw, kw = w_query.shape[1] // 2, w_key.shape[1] // 2
    shared_width = full_down.shape[0]
    inputs = tokens.astype(F32)
    if fits:
        (
            output, hidden_grad, mixed_grad, out_part, shared_up_part, shared_down_part, dup, dwn, row_part, _, add_down,
        ) = experts_fused(
            ext, (expert_up[0], other_up, expert_down[0], other_down), cot_all, (full_up, full_down), cotangent_pair,
            cotangent, resid, gates, kept[1], attended, full_out, blks, capacity, 3)
        query_grad, *kv_parts = attention_backward(query, kv, attended_full, lse, mixed_grad, where)
        (
            input_grad, w_query_grad, w_key_grad, w_value_grad, out_sum, up_grad, down_sum, small_sum, add_up,
        ) = tail_fused(
            *kv_parts, query_grad, normed_one, kept[0], tokens, hidden_grad, kept[1],
            out_part.reshape(blks, dense_rows, width),
            shared_up_part.reshape(2, blks, dense_rows, -1),
            shared_down_part.reshape(blks, -1, width), row_part, dup, blks, 6)
        (
            expert_up_grad, expert_down_grad, router_grad, gain_one_grad, gain_two_grad, output,
            input_grad, w_query_grad, w_key_grad, w_value_grad, out_sum, up_grad, down_sum,
        ) = finish_fused(
            h, dup, add_up, dwn, add_down, small_sum, experts,
            (output, input_grad, w_query_grad, w_key_grad, w_value_grad, out_sum, up_grad, down_sum))
        return (
            output, input_grad, gain_one_grad.reshape(-1), w_query_grad, w_key_grad, w_value_grad,
            out_sum, gain_two_grad.reshape(-1), router_grad.T, up_grad, down_sum,
            expert_up_grad[None], expert_down_grad[None],
        )
    scaler_two = inv_scale(resid)
    normed_two = ext[:, :width]

    home, routed_sum, dup, dwn, normed_pair = experts_plain(
        ext, (expert_up[0], other_up, expert_down[0], other_down), cot_all, blks, capacity, 3)
    normed_pair = normed_pair.reshape(2 * rows, width)
    shared_both = dot(normed_pair, full_up)
    shared_gate, shared_lift = shared_both[:, :shared_width], shared_both[:, shared_width:]
    shared_act = (jax.nn.silu(shared_gate) * shared_lift).astype(BF16)
    shared_sum = dot(shared_act, full_down).reshape(2, rows, width)
    shared_down_part = dot_first(shared_act, cotangent_pair)
    shared_grad = gated_grad(dot_last(cotangent_pair, full_down), shared_gate, shared_lift)
    shared_up_part = dot_first(normed_pair, shared_grad)
    shared_back = dot_last(shared_grad, full_up).reshape(2, rows, width)
    output = (
        resid + routed_sum + pick(shared_sum, h) + swap(pick(shared_sum, 1 - h).astype(BF16)).astype(F32)
    ).astype(BF16)

    dgate = home[:, width : width + experts] + home[:, width + experts : width + 2 * experts]
    weighted = gates * dgate
    logit_grad = (weighted - gates * jnp.sum(weighted, axis=1, keepdims=True)).astype(BF16)
    norm_two_grad = (
        home[:, :width] + dot(logit_grad, router_rows)
        + pick(shared_back, h) + swap(pick(shared_back, 1 - h).astype(BF16)).astype(F32)
    )
    back, gain_two_part = norm_back(resid, scaler_two, gain_second, norm_two_grad)
    hidden_grad = cotangent.astype(F32) + back
    hidden_low = hidden_grad.astype(BF16)
    hidden_pair = pair(hidden_low, swap(hidden_low)).reshape(2 * rows, width)
    out_part = dot_first(attended, hidden_pair)
    mixed_grad = dot_last(hidden_pair, full_out).astype(BF16)
    query_grad, *kv_parts = attention_backward(query, kv, attended_full, lse, mixed_grad, where)
    router_part = dot_first(normed_two, logit_grad)
    dup, dwn, query_grad = lax.optimization_barrier((dup, dwn, query_grad))
    dup = dup.reshape(2, width // 2, -1)
    dwn = jnp.stack([dwn[:, : width // 2], dwn[:, width // 2 :]])
    expert_up_grad = pick(dup, h).astype(F32) + swap(pick(dup, 1 - h)).astype(F32)
    expert_down_grad = pick(dwn, h).astype(F32) + swap(pick(dwn, 1 - h)).astype(F32)
    kv_grads = reduce_scatter_blk([part.reshape(blks, 2 * rows, kw) for part in kv_parts], blks, 6, [BF16] * 2)
    qkv_grad = jnp.concatenate([query_grad, *kv_grads], axis=1)
    norm_one_part = dot_last(qkv_grad, full_qkv).reshape(2, rows, width)
    norm_one_grad = pick(norm_one_part, h) + swap(pick(norm_one_part, 1 - h).astype(BF16)).astype(F32)
    extra_grad, gain_one_part = norm_back(inputs, inv_scale(inputs), gain_first, norm_one_grad)
    input_grad = hidden_grad + extra_grad
    qkv_part = dot_first(normed_one, qkv_grad)
    small_part = jnp.concatenate(
        [router_part, gain_one_part[:, None], gain_two_part[:, None],
         jnp.zeros((width, lanes - experts - 2), F32)], axis=1)

    def by_rows(part):
        return part.astype(BF16).reshape(2, blks, dense_rows, -1)

    qkv_sum, up_sum, out_sum, down_sum, small_sum = reduce_scatter_blk(
        [by_rows(qkv_part), by_rows(shared_up_part),
         out_part.astype(BF16).reshape(blks, dense_rows, width),
         shared_down_part.astype(BF16).reshape(blks, -1, width), by_rows(small_part)],
        blks, 7, [BF16, BF16, F32, F32, F32])
    there = swap(jnp.concatenate([pick(qkv_sum, 1 - h), pick(up_sum, 1 - h)], axis=1)).astype(F32)
    here = jnp.concatenate([pick(qkv_sum, h), pick(up_sum, h)], axis=1).astype(F32)
    small_sum = pick(small_sum, h) + swap(pick(small_sum, 1 - h))

    def whole(start, size):
        return jnp.where(
            h == 0,
            jnp.concatenate([here[:, start : start + size], there[:, start : start + size]], axis=1),
            jnp.concatenate([there[:, start : start + size], here[:, start : start + size]], axis=1))

    top = qw + 2 * kw
    sw = shared_width
    up_grad = jnp.concatenate([whole(top, sw), whole(top + sw, sw)], axis=1)
    return (
        output, input_grad, small_sum[:, experts], whole(0, qw), whole(qw, kw), whole(qw + kw, kw),
        out_sum, small_sum[:, experts + 1], small_sum[:, :experts], up_grad, down_sum,
        expert_up_grad[None], expert_down_grad[None],
    )


def solution(mesh):
    both = P(("head", "blk"), None)
    flat = P(("head", "blk"))
    up, down = P("blk", "head", None), P("blk", None, "head")
    return jax.shard_map(
        shards,
        mesh=mesh,
        in_specs=(both, both, P(), P(), both, flat, both, both, both, both, flat, both, both, both, up, down),
        out_specs=(both, both, flat, both, both, both, both, flat, both, both, both, up, down),
        check_vma=False,
    )
```
